32 devices in a mesh: dp: 16 (over z, y, core), fsdp: 2 (over x).
Axes of the slice: x: 2, y: 2, z: 4, core: 2. Of those that a mesh axis runs over, the one named last changes fastest.
Arguments:
- captions: bfloat16 [32, 128, 768], P(('dp', 'fsdp')), may hold values from -6 to 6
- tiles: bfloat16 [32, 196, 768], P(('dp', 'fsdp')), may hold values from -6 to 6
- tile_index: int32 [32, 4], P(('dp', 'fsdp')), may hold values from 0 to 1
- tile_valid: int32 [32, 4], P(('dp', 'fsdp')), may hold values from 0 to 1
- caption_len: int32 [32], P(('dp', 'fsdp')), may hold values from 32 to 128
- weights: bfloat16 [73984, 128], P('fsdp')
- first_moment: float32 [73984, 128], P(('dp', 'fsdp')), may hold values from -0.00024414062 to 0.00024414062
- second_moment: float32 [73984, 128], P(('dp', 'fsdp')), may hold values from 2e-11 to 5e-10
- d_out: bfloat16 [32, 128, 768], P(('dp', 'fsdp')), may hold values from -6 to 6
Outputs:
- output: bfloat16 [32, 128, 768], P(('dp', 'fsdp'))
- d_captions: float32 [32, 128, 768], P(('dp', 'fsdp'))
- d_tiles: float32 [32, 196, 768], P(('dp', 'fsdp'))
- grads: float32 [73984, 128], P(('dp', 'fsdp'))
- update: float32 [73984, 128], P(('dp', 'fsdp'))
- new_first: float32 [73984, 128], P(('dp', 'fsdp'))
- new_second: float32 [73984, 128], P(('dp', 'fsdp'))
- grad_norm: float32 [], replicated
- tensor_rms: float32 [21], replicated
The draws below stay inside these ranges and needn't reach their ends.
Inputs may be any that keep to these rules, and one draw needn't show every extreme that they name: `tile_index`: indices count the tiles of the caption's own dp index.
All inputs are finite; a program needn't handle non-finite values.
Results may differ from the reference program's by a relative error of at most 0.018.
Values may be sent and summed in bfloat16 or wider, within the bound.
A program may use at most 256 MiB of HBM per device.

```python
import math
import jax
import jax.numpy as jnp
import numpy as np
from jax import lax

D = 768
HEADS = 12
HEAD_DIM = 64
FF = 3072
CAP_LEN = 128
PATCH = 196
MAXT = 4
STEP = 10
CAPTIONS = 32
TILES = 32
GROUP_TILES = 2
PROWS = 73984
N_DP = 16


def layout_scales(model_width, hidden_width):
    narrow = 1.0 / math.sqrt(model_width)
    return [('norm_one_gain', model_width, 0.1, 1.0), ('norm_one_shift', model_width, 0.1, 0.0), ('self_qkv', 3 * model_width * model_width, narrow, 0.0), ('self_query_bias', model_width, 0.1, 0.0), ('self_value_bias', model_width, 0.1, 0.0), ('self_out', model_width * model_width, 3.0 * narrow, 0.0), ('self_out_bias', model_width, 0.1, 0.0), ('norm_two_gain', model_width, 0.1, 1.0), ('norm_two_shift', model_width, 0.1, 0.0), ('cross_query', model_width * model_width, narrow, 0.0), ('cross_query_bias', model_width, 0.1, 0.0), ('cross_kv', 2 * model_width * model_width, narrow, 0.0), ('cross_value_bias', model_width, 0.1, 0.0), ('cross_out', model_width * model_width, 6.0 * narrow, 0.0), ('cross_out_bias', model_width, 0.1, 0.0), ('norm_three_gain', model_width, 0.1, 1.0), ('norm_three_shift', model_width, 0.1, 0.0), ('mlp_up', model_width * hidden_width, narrow, 0.0), ('mlp_up_bias', hidden_width, 0.1, 0.0), ('mlp_down', hidden_width * model_width, 1.5 / math.sqrt(hidden_width), 0.0), ('mlp_down_bias', model_width, 0.1, 0.0)]


def draw_weights(key, part):
    row_ids = jnp.arange(PROWS)
    row_scale = jnp.zeros((PROWS,), jnp.float32)
    row_offset = jnp.zeros((PROWS,), jnp.float32)
    row_at = 0
    for seg_label, seg_entries, seg_scale, seg_offset in layout_scales(D, FF):
        seg_rows = seg_entries // 128
        inside = (row_ids >= row_at) & (row_ids < row_at + seg_rows)
        row_scale = jnp.where(inside, seg_scale, row_scale)
        row_offset = jnp.where(inside, seg_offset, row_offset)
        row_at = row_at + seg_rows
    base_values = jax.random.normal(key, (PROWS, 128), jnp.float32)
    return (base_values * row_scale[:, None] + row_offset[:, None]).astype(jnp.bfloat16)


def draw_tile_valid(key, part):
    coin_flips = jax.random.randint(key, (CAPTIONS, MAXT), 0, 2, dtype=jnp.int32)
    leading = (jnp.arange(MAXT) == 0)[None, :]
    return jnp.where(leading, 1, coin_flips).astype(jnp.int32)


def place_ends(drawn, own_key, least, top_value):
    place = [jax.random.randint(jax.random.fold_in(own_key, axis), (), 0, length) for axis, length in enumerate(drawn.shape)]
    longest = drawn.shape.index(max(drawn.shape))
    beside = place[:longest] + [(place[longest] + 1) % drawn.shape[longest]] + place[longest + 1:]
    return drawn.at[tuple(place)].set(least).at[tuple(beside)].set(top_value)


def block_scale(rng, shape, cuts, smallest, largest):
    factor_of = 1.0
    for dim, shards_of in cuts:
        steps = jax.random.uniform(jax.random.fold_in(jax.random.fold_in(rng, 6), dim), (shards_of,), jnp.float32, smallest / len(cuts), largest / len(cuts))
        factor_of = factor_of * jnp.repeat(jnp.exp(steps), shape[dim] // shards_of).reshape((-1,) + (1,) * (len(shape) - 1 - dim))
    return factor_of


def normal_values(own_key, dims, scale, reach, shards=(), held_as=jnp.bfloat16):
    gain = block_scale(own_key, dims, shards, -0.22, 0.18) if shards else 1.0
    entries = jax.random.normal(own_key, dims, jnp.float32) * scale * gain
    return jnp.minimum(jnp.maximum(entries, -reach), reach).astype(held_as)


def setup_inputs(seed: int = 0) -> dict:
    seeds = jax.random.split(jax.random.key(seed), 10)
    captions = normal_values(seeds[0], (CAPTIONS, CAP_LEN, D), 1.0, 6.0, ((0, 32),))
    tiles = normal_values(seeds[1], (TILES, PATCH, D), 1.0, 6.0, ((0, 32),))
    tile_index = place_ends(jax.random.randint(seeds[2], (CAPTIONS, MAXT), 0, GROUP_TILES), jax.random.fold_in(seeds[2], 1), 0, GROUP_TILES - 1).astype(jnp.int32)
    tile_valid = draw_tile_valid(jax.random.fold_in(seeds[9], 71), 0)
    caption_len = place_ends(jax.random.randint(seeds[4], (CAPTIONS,), CAP_LEN // 4, CAP_LEN + 1), jax.random.fold_in(seeds[4], 1), CAP_LEN // 4, CAP_LEN).astype(jnp.int32)
    weights = draw_weights(jax.random.fold_in(seeds[9], 71), 0)
    first_moment = normal_values(seeds[6], (PROWS, 128), (4e-5), 0.00024414062, ((0, 32),), jnp.float32)
    second_moment = jnp.clip(jnp.exp(math.log(4.999999858590343e-10) - 3.218876 * jax.random.uniform(seeds[7], (PROWS, 128), jnp.float32) ** block_scale(seeds[7], (PROWS, 128), ((0, 32),), -0.2, 0.2)), 1.9999999920083944e-11, 4.999999858590343e-10)
    d_out = normal_values(seeds[8], (CAPTIONS, CAP_LEN, D), 1.0, 6.0, ((0, 32),))
    return {"captions": captions, "tiles": tiles, "tile_index": tile_index, "tile_valid": tile_valid, "caption_len": caption_len, "weights": weights, "first_moment": first_moment, "second_moment": second_moment, "d_out": d_out}


EPS_NORM = 1e-05
CLIP_NORM = 1.0
BETA_ONE = 0.9
BETA_TWO = 0.999
LEARN_RATE = 0.01
DECAY_RATE = 0.1
ADAM_EPS = 1e-08
NEG_LARGE = -1e+30

@jax.custom_vjp
def low(v):
    return lax.optimization_barrier(v.astype(jnp.bfloat16)).astype(jnp.float32)

@jax.custom_vjp
def low_back(v):
    return v

def low_keep(v):
    return (low(v), None)

def low_pass(kept, grad):
    return (grad,)

def back_keep(v):
    return (v, None)

def back_low(kept, grad):
    return (low(grad),)
low.defvjp(low_keep, low_pass)
low_back.defvjp(back_keep, back_low)

def layout(model_width, hidden_width):
    return [('norm_one_gain', (model_width,), 0), ('norm_one_shift', (model_width,), 0), ('self_qkv', (model_width, 3 * model_width), 1), ('self_query_bias', (model_width,), 0), ('self_value_bias', (model_width,), 0), ('self_out', (model_width, model_width), 1), ('self_out_bias', (model_width,), 0), ('norm_two_gain', (model_width,), 0), ('norm_two_shift', (model_width,), 0), ('cross_query', (model_width, model_width), 1), ('cross_query_bias', (model_width,), 0), ('cross_kv', (model_width, 2 * model_width), 1), ('cross_value_bias', (model_width,), 0), ('cross_out', (model_width, model_width), 1), ('cross_out_bias', (model_width,), 0), ('norm_three_gain', (model_width,), 0), ('norm_three_shift', (model_width,), 0), ('mlp_up', (model_width, hidden_width), 1), ('mlp_up_bias', (hidden_width,), 0), ('mlp_down', (hidden_width, model_width), 1), ('mlp_down_bias', (model_width,), 0)]

def segment_table(model_width, hidden_width):
    seg_starts = []
    seg_ends = []
    decay_flags = []
    seg_entries = []
    row_at = 0
    for seg_label, seg_shape, seg_flag in layout(model_width, hidden_width):
        item_count = int(np.prod(seg_shape))
        seg_rows = item_count // 128
        seg_starts.append(row_at)
        seg_ends.append(row_at + seg_rows)
        decay_flags.append(seg_flag == 1)
        seg_entries.append(float(item_count))
        row_at = row_at + seg_rows
    return (np.array(seg_starts), np.array(seg_ends), np.array(decay_flags), np.array(seg_entries))

def unpack(flat_rows, model_width, hidden_width):
    vector = flat_rows.reshape(-1)
    tensors = {}
    offset = 0
    for seg_label, seg_shape, seg_flag in layout(model_width, hidden_width):
        item_count = int(np.prod(seg_shape))
        tensors[seg_label] = vector[offset:offset + item_count].reshape(seg_shape)
        offset = offset + item_count
    return tensors

def product(pattern, left_side, right_side):
    return jnp.einsum(pattern, left_side, right_side, precision=lax.Precision.HIGHEST)

def layer_norm(values, gain_term, offset_term):
    center = values - lax.optimization_barrier(jnp.mean(values, axis=-1, keepdims=True))
    spread = lax.optimization_barrier(jnp.mean(center * center, axis=-1, keepdims=True))
    return center * lax.rsqrt(spread + EPS_NORM) * gain_term + offset_term

def softmax_with_mask(scores, allowed):
    scores = jnp.where(allowed, scores, NEG_LARGE)
    highest = lax.optimization_barrier(jnp.max(scores, axis=-1, keepdims=True))
    exponent = jnp.exp(scores - highest)
    return exponent / lax.optimization_barrier(jnp.sum(exponent, axis=-1, keepdims=True))

def forward(flat_rows, caption_block, tile_block, index_block, valid_block, length_block):
    tensors = unpack(flat_rows, D, FF)
    caption_rows = caption_block.shape[0]
    zero_part = jnp.zeros((D,), flat_rows.dtype)
    heads_shape = (caption_rows, CAP_LEN, HEADS, HEAD_DIM)
    key_shape = (caption_rows, MAXT * PATCH, HEADS, HEAD_DIM)
    normed_one = low(layer_norm(caption_block, tensors['norm_one_gain'], tensors['norm_one_shift']))
    qkv_bias = jnp.concatenate([tensors['self_query_bias'], zero_part, tensors['self_value_bias']])
    packed_qkv = low(low_back(product('bld,de->ble', normed_one, tensors['self_qkv']) + qkv_bias))
    self_query = packed_qkv[..., :D].reshape(heads_shape)
    self_keys = packed_qkv[..., D:2 * D].reshape(heads_shape)
    self_values = packed_qkv[..., 2 * D:].reshape(heads_shape)
    positions = jnp.arange(CAP_LEN)
    causal = (positions[None, :] <= positions[:, None])[None, None]
    present = (positions[None, :] < length_block[:, None])[:, None, None, :]
    self_scores = low_back(product('bqhe,bkhe->bhqk', self_query, self_keys) * 0.125)
    self_probs = low(softmax_with_mask(self_scores, causal & present))
    self_mixed = low(low_back(product('bhqk,bkhe->bqhe', self_probs, self_values).reshape(caption_rows, CAP_LEN, D)))
    first_sum = caption_block + low_back(product('bld,de->ble', self_mixed, tensors['self_out']) + tensors['self_out_bias'])
    normed_two = low(layer_norm(first_sum, tensors['norm_two_gain'], tensors['norm_two_shift']))
    cross_queries = low(low_back(product('bld,de->ble', normed_two, tensors['cross_query']) + tensors['cross_query_bias'])).reshape(heads_shape)
    kv_bias = jnp.concatenate([zero_part, tensors['cross_value_bias']])
    tile_kv = low(low_back(product('tpd,de->tpe', tile_block, tensors['cross_kv']) + kv_bias))
    chosen = tile_kv[index_block]
    cross_keys = chosen[..., :D].reshape(key_shape)
    cross_values = chosen[..., D:].reshape(key_shape)
    usable = jnp.repeat(valid_block > 0, PATCH, axis=1)[:, None, None, :]
    cross_scores = low_back(product('bqhe,bkhe->bhqk', cross_queries, cross_keys) * 0.125)
    cross_probs = low(softmax_with_mask(cross_scores, usable))
    cross_mixed = low(low_back(product('bhqk,bkhe->bqhe', cross_probs, cross_values).reshape(caption_rows, CAP_LEN, D)))
    second = first_sum + low_back(product('bld,de->ble', cross_mixed, tensors['cross_out']) + tensors['cross_out_bias'])
    normed_three = low(layer_norm(second, tensors['norm_three_gain'], tensors['norm_three_shift']))
    preact = low_back(product('bld,df->blf', normed_three, tensors['mlp_up']) + tensors['mlp_up_bias'])
    activation = low(jax.nn.gelu(preact, approximate=False))
    return second + low_back(product('blf,fd->bld', activation, tensors['mlp_down']) + tensors['mlp_down_bias'])

def adam_step(gradients, member, decay_flags, old_weights, first_moment, second_moment, square_sums, seg_entries):
    grad_norm = jnp.sqrt(jnp.sum(square_sums))
    tensor_rms = jnp.sqrt(square_sums / jnp.asarray(seg_entries, dtype=square_sums.dtype))
    clip_scale = jnp.minimum(1.0, CLIP_NORM / (grad_norm + 1e-06))
    clipped = gradients * clip_scale
    new_first = BETA_ONE * first_moment + (1.0 - BETA_ONE) * clipped
    new_second = BETA_TWO * second_moment + (1.0 - BETA_TWO) * clipped * clipped
    first_hat = new_first / (1.0 - BETA_ONE ** STEP)
    second_hat = new_second / (1.0 - BETA_TWO ** STEP)
    decay_rows = jnp.any(member & decay_flags[None, :], axis=1)
    decayed = jnp.where(decay_rows[:, None], old_weights, 0.0)
    update = -LEARN_RATE * (first_hat / (jnp.sqrt(second_hat) + ADAM_EPS) + DECAY_RATE * decayed)
    return (update, new_first, new_second, grad_norm, tensor_rms)

def reference(captions, tiles, tile_index, tile_valid, caption_len, weights, first_moment, second_moment, d_out):
    flat_rows = weights.astype(jnp.float32)
    group_caps = CAPTIONS // N_DP
    group_tiles = TILES // N_DP
    caption_groups = captions.astype(jnp.float32).reshape(N_DP, group_caps, CAP_LEN, D)
    tile_groups = tiles.astype(jnp.float32).reshape(N_DP, group_tiles, PATCH, D)
    index_groups = tile_index.reshape(N_DP, group_caps, MAXT)
    valid_groups = tile_valid.reshape(N_DP, group_caps, MAXT)
    length_groups = caption_len.reshape(N_DP, group_caps)
    cotan_groups = d_out.astype(jnp.float32).reshape(N_DP, group_caps, CAP_LEN, D)

    def group_step(running, inputs):
        caption_in, tile_in, index_in, valid_in, length_in, cotan_in = inputs

        def closure(flat_in, caption_arg, tile_arg):
            return forward(flat_in, caption_arg, tile_arg, index_in, valid_in, length_in)
        result, pullback = jax.vjp(closure, flat_rows, caption_in, tile_in)
        flat_grad, caption_grad, tile_grad = pullback(cotan_in)
        return (running + flat_grad, (result.astype(jnp.bfloat16), caption_grad, tile_grad))
    gradients, stacked = lax.scan(group_step, jnp.zeros_like(flat_rows), (caption_groups, tile_groups, index_groups, valid_groups, length_groups, cotan_groups))
    outputs, caption_grads, tile_grads = stacked
    seg_starts, seg_ends, decay_flags, seg_entries = segment_table(D, FF)
    row_ids = jnp.arange(PROWS)
    member = (row_ids[:, None] >= seg_starts[None, :]) & (row_ids[:, None] < seg_ends[None, :])
    row_squares = lax.optimization_barrier(jnp.sum(gradients * gradients, axis=1))
    square_sums = lax.optimization_barrier(jnp.sum(jnp.where(member, row_squares[:, None], 0.0), axis=0))
    update, new_first, new_second, grad_norm, tensor_rms = adam_step(gradients, member, decay_flags, flat_rows, first_moment, second_moment, square_sums, seg_entries)
    return (outputs.reshape(CAPTIONS, CAP_LEN, D), caption_grads.reshape(CAPTIONS, CAP_LEN, D), tile_grads.reshape(TILES, PATCH, D), gradients, update, new_first, new_second, grad_norm, tensor_rms)
```

```python
import jax
import jax.numpy as jnp
import numpy as np
from jax import lax
from jax.experimental import pallas as pl
from jax.experimental.pallas import tpu as pltpu
from jax.sharding import PartitionSpec as P

HEADS = 12
HEAD_DIM = 64
FF = 3072
STEP = 10


EPS_NORM = 1e-05
CLIP_NORM = 1.0
BETA_ONE = 0.9
BETA_TWO = 0.999
LEARN_RATE = 0.01
DECAY_RATE = 0.1
ADAM_EPS = 1e-08
NEG_LARGE = -1e30
(NORM_ONE_GAIN, NORM_ONE_SHIFT, SELF_QKV, SELF_QUERY_BIAS, SELF_VALUE_BIAS, SELF_OUT, SELF_OUT_BIAS, NORM_TWO_GAIN, NORM_TWO_SHIFT, CROSS_QUERY, CROSS_QUERY_BIAS, CROSS_KV, CROSS_VALUE_BIAS, CROSS_OUT, CROSS_OUT_BIAS, NORM_THREE_GAIN, NORM_THREE_SHIFT, MLP_UP, MLP_UP_BIAS, MLP_DOWN, MLP_DOWN_BIAS) = range(21)
DP, FSDP = "dp", "fsdp"
BOTH = (DP, FSDP)
E_BHQK_BKHE_TO_BQHE = "bhqk,bkhe->bqhe"
E_BHQK_BQHE_TO_BKHE = "bhqk,bqhe->bkhe"
E_BLD_BLE_TO_DE = "bld,ble->de"
E_BLD_BLF_TO_DF = "bld,blf->df"
E_BLD_DE_TO_BLE = "bld,de->ble"
E_BLD_DF_TO_BLF = "bld,df->blf"
E_BLD_FD_TO_BLF = "bld,fd->blf"
E_BLE_DE_TO_BLD = "ble,de->bld"
E_BLF_BLD_TO_FD = "blf,bld->fd"
E_BLF_DF_TO_BLD = "blf,df->bld"
E_BLF_FD_TO_BLD = "blf,fd->bld"
E_BQHE_BKHE_TO_BHQK = "bqhe,bkhe->bhqk"
E_CSG_CSPE_TO_GPE = "csg,cspe->gpe"
E_TPD_DE_TO_TPE = "tpd,de->tpe"
E_TPD_TPE_TO_DE = "tpd,tpe->de"
E_TPE_DE_TO_TPD = "tpe,de->tpd"


def for_sending(x):
    return jax.tree.map(lambda a: a.astype(jnp.bfloat16) if a.dtype == jnp.float32 else a, x)


def layout(model_width, hidden_width):
    return [
        (NORM_ONE_GAIN, (model_width,), 0),
        (NORM_ONE_SHIFT, (model_width,), 0),
        (SELF_QKV, (model_width, 3 * model_width), 1),
        (SELF_QUERY_BIAS, (model_width,), 0),
        (SELF_VALUE_BIAS, (model_width,), 0),
        (SELF_OUT, (model_width, model_width), 1),
        (SELF_OUT_BIAS, (model_width,), 0),
        (NORM_TWO_GAIN, (model_width,), 0),
        (NORM_TWO_SHIFT, (model_width,), 0),
        (CROSS_QUERY, (model_width, model_width), 1),
        (CROSS_QUERY_BIAS, (model_width,), 0),
        (CROSS_KV, (model_width, 2 * model_width), 1),
        (CROSS_VALUE_BIAS, (model_width,), 0),
        (CROSS_OUT, (model_width, model_width), 1),
        (CROSS_OUT_BIAS, (model_width,), 0),
        (NORM_THREE_GAIN, (model_width,), 0),
        (NORM_THREE_SHIFT, (model_width,), 0),
        (MLP_UP, (model_width, hidden_width), 1),
        (MLP_UP_BIAS, (hidden_width,), 0),
        (MLP_DOWN, (hidden_width, model_width), 1),
        (MLP_DOWN_BIAS, (model_width,), 0),
    ]


def segment_table(model_width, hidden_width):
    seg_starts = []
    seg_ends = []
    decay_flags = []
    seg_entries = []
    row_at = 0
    for seg_label, seg_shape, seg_flag in layout(model_width, hidden_width):
        item_count = int(np.prod(seg_shape))
        seg_rows = item_count // 128
        seg_starts.append(row_at)
        seg_ends.append(row_at + seg_rows)
        decay_flags.append(seg_flag == 1)
        seg_entries.append(float(item_count))
        row_at = row_at + seg_rows
    return (np.array(seg_starts), np.array(seg_ends), np.array(decay_flags), np.array(seg_entries))


def unpack(flat_rows, model_width, hidden_width):
    vector = flat_rows.reshape(-1)
    tensors = {}
    offset = 0
    for seg_label, seg_shape, seg_flag in layout(model_width, hidden_width):
        item_count = int(np.prod(seg_shape))
        tensors[seg_label] = vector[offset : offset + item_count].reshape(seg_shape)
        offset = offset + item_count
    return tensors


def pack_rows(gradients, model_width, hidden_width, total_rows):
    pieces = [
        gradients[seg_label].reshape(-1, 128)
        for seg_label, seg_shape, seg_flag in layout(model_width, hidden_width)
    ]
    used_rows = sum((tensor_piece.shape[0] for tensor_piece in pieces))
    pieces.append(jnp.zeros((total_rows - used_rows, 128), jnp.float32))
    return jnp.concatenate(pieces, axis=0)


def product(pattern, left_side, right_side):
    return jnp.einsum(pattern, left_side, right_side, preferred_element_type=jnp.float32)


def as_float(tensors, seg_label):
    return tensors[seg_label].astype(jnp.float32)


def column_sums(values):
    return jnp.sum(values.astype(jnp.float32), axis=tuple(range(values.ndim - 1)))


def layer_norm(values, gain_term, offset_term):
    center = values - jnp.mean(values, axis=-1, keepdims=True)
    spread = jnp.mean(center * center, axis=-1, keepdims=True)
    return center * lax.rsqrt(spread + EPS_NORM) * gain_term + offset_term


def gelu_exact(pre_values):
    return jax.nn.gelu(pre_values, approximate=False)


def norm_back(values, tensors, gain, shift, normed_grad, gradients):
    norm_value, norm_pull = jax.vjp(
        layer_norm,
        values,
        as_float(tensors, gain),
        as_float(tensors, shift),
    )
    values_grad, gain_grad, offset_grad = norm_pull(normed_grad)
    gradients[gain] = gain_grad
    gradients[shift] = offset_grad
    return values_grad


def score_block(queries, key_head_split, allowed):
    scores = product(E_BQHE_BKHE_TO_BHQK, queries, key_head_split) * 0.125
    return jnp.where(allowed, scores, NEG_LARGE)


def softmax_forward(queries, key_head_split, allowed):
    scores = score_block(queries, key_head_split, allowed)
    highest = jnp.max(scores, axis=-1, keepdims=True)
    exponent = jnp.exp(scores - highest)
    row_total = jnp.sum(exponent, axis=-1, keepdims=True)
    return (exponent / row_total, highest + jnp.log(row_total))


def attention_backward_pass(queries, key_head_split, values, allowed, log_total, mixed_grad):
    probabilities = jnp.where(
        allowed, jnp.exp(score_block(queries, key_head_split, allowed) - log_total), 0.0
    )
    probs_grad = product(E_BQHE_BKHE_TO_BHQK, mixed_grad, values)
    values_grad = product(E_BHQK_BQHE_TO_BKHE, probabilities.astype(jnp.bfloat16), mixed_grad)
    inner_sum = jnp.sum(probabilities * probs_grad, axis=-1, keepdims=True)
    score_grad = (probabilities * (probs_grad - inner_sum)).astype(jnp.bfloat16)
    queries_grad = product(E_BHQK_BKHE_TO_BQHE, score_grad, key_head_split) * 0.125
    keys_grad = product(E_BHQK_BQHE_TO_BKHE, score_grad, queries) * 0.125
    return (queries_grad, keys_grad, values_grad)


def adam_step(
    gradients,
    member,
    decay_flags,
    old_weights,
    first_moment,
    second_moment,
    square_sums,
    seg_entries,
):
    grad_norm = jnp.sqrt(jnp.sum(square_sums))
    tensor_rms = jnp.sqrt(square_sums / jnp.asarray(seg_entries, dtype=square_sums.dtype))
    clip_scale = jnp.minimum(1.0, CLIP_NORM / (grad_norm + 1e-06))
    clipped = gradients * clip_scale
    new_first = BETA_ONE * first_moment + (1.0 - BETA_ONE) * clipped
    new_second = BETA_TWO * second_moment + (1.0 - BETA_TWO) * clipped * clipped
    first_hat = new_first / (1.0 - BETA_ONE**STEP)
    second_hat = new_second / (1.0 - BETA_TWO**STEP)
    decay_rows = jnp.any(member & decay_flags[None, :], axis=1)
    decayed = jnp.where(decay_rows[:, None], old_weights, 0.0)
    update = -LEARN_RATE * (first_hat / (jnp.sqrt(second_hat) + ADAM_EPS) + DECAY_RATE * decayed)
    return (update, new_first, new_second, grad_norm, tensor_rms)


def body(
    captions,
    tiles,
    tile_index,
    tile_valid,
    caption_len,
    weights,
    first_moment,
    second_moment,
    d_out,
):
    model_width = captions.shape[2]
    hidden_width = FF
    caption_rows = captions.shape[0]
    cap_length = captions.shape[1]
    patch_count = tiles.shape[1]
    own_tiles = tiles.shape[0]
    slot_count = tile_index.shape[1]
    group_size = lax.axis_size(FSDP)
    data_size = lax.axis_size(DP)
    total_rows = weights.shape[0] * group_size
    heads_shape = (caption_rows, cap_length, HEADS, HEAD_DIM)
    key_shape = (caption_rows, slot_count * patch_count, HEADS, HEAD_DIM)
    token_layout_form = (caption_rows, cap_length, model_width)
    tensors = unpack(lax.all_gather(weights, FSDP, axis=0, tiled=True), model_width, hidden_width)
    zero_part = jnp.zeros((model_width,), jnp.bfloat16)
    input_values = captions.astype(jnp.float32)
    normed_one = layer_norm(
        input_values, as_float(tensors, NORM_ONE_GAIN), as_float(tensors, NORM_ONE_SHIFT)
    ).astype(jnp.bfloat16)
    qkv_bias = jnp.concatenate(
        [tensors[SELF_QUERY_BIAS], zero_part, tensors[SELF_VALUE_BIAS]]
    ).astype(jnp.float32)
    packed_qkv = (product(E_BLD_DE_TO_BLE, normed_one, tensors[SELF_QKV]) + qkv_bias).astype(
        jnp.bfloat16
    )
    self_query = packed_qkv[..., :model_width].reshape(heads_shape)
    self_keys = packed_qkv[..., model_width : 2 * model_width].reshape(heads_shape)
    self_values = packed_qkv[..., 2 * model_width :].reshape(heads_shape)
    positions = jnp.arange(cap_length)
    causal = (positions[None, :] <= positions[:, None])[None, None]
    present = (positions[None, :] < caption_len[:, None])[:, None, None, :]
    self_allowed = causal & present
    self_probs, self_log = softmax_forward(self_query, self_keys, self_allowed)
    self_mixed = (
        product(E_BHQK_BKHE_TO_BQHE, self_probs.astype(jnp.bfloat16), self_values)
        .reshape(token_layout_form)
        .astype(jnp.bfloat16)
    )
    first_sum = (
        input_values
        + product(E_BLD_DE_TO_BLE, self_mixed, tensors[SELF_OUT])
        + as_float(tensors, SELF_OUT_BIAS)
    )
    normed_two = layer_norm(
        first_sum, as_float(tensors, NORM_TWO_GAIN), as_float(tensors, NORM_TWO_SHIFT)
    ).astype(jnp.bfloat16)
    cross_queries = (
        (
            product(E_BLD_DE_TO_BLE, normed_two, tensors[CROSS_QUERY])
            + as_float(tensors, CROSS_QUERY_BIAS)
        )
        .astype(jnp.bfloat16)
        .reshape(heads_shape)
    )
    kv_bias = jnp.concatenate([zero_part, tensors[CROSS_VALUE_BIAS]]).astype(jnp.float32)
    kv_weight = tensors[CROSS_KV]
    group_kv = (
        product(E_TPD_DE_TO_TPE, lax.all_gather(tiles, FSDP, axis=0, tiled=True), kv_weight)
        + kv_bias
    ).astype(jnp.bfloat16)
    chosen = jnp.stack(
        [
            jnp.stack(
                [
                    lax.dynamic_index_in_dim(group_kv, tile_index[c, s], 0, keepdims=False)
                    for s in range(slot_count)
                ]
            )
            for c in range(caption_rows)
        ]
    )
    cross_keys = chosen[..., :model_width].reshape(key_shape)
    cross_values = chosen[..., model_width:].reshape(key_shape)
    usable = jnp.repeat(tile_valid > 0, patch_count, axis=1)[:, None, None, :]
    cross_probs, cross_log = softmax_forward(cross_queries, cross_keys, usable)
    cross_mixed = (
        product(E_BHQK_BKHE_TO_BQHE, cross_probs.astype(jnp.bfloat16), cross_values)
        .reshape(token_layout_form)
        .astype(jnp.bfloat16)
    )
    second = (
        first_sum
        + product(E_BLD_DE_TO_BLE, cross_mixed, tensors[CROSS_OUT])
        + as_float(tensors, CROSS_OUT_BIAS)
    )
    normed_three = layer_norm(
        second, as_float(tensors, NORM_THREE_GAIN), as_float(tensors, NORM_THREE_SHIFT)
    ).astype(jnp.bfloat16)
    preact = product(E_BLD_DF_TO_BLF, normed_three, tensors[MLP_UP]) + as_float(
        tensors, MLP_UP_BIAS
    )
    activation = gelu_exact(preact).astype(jnp.bfloat16)
    result = (
        second
        + product(E_BLF_FD_TO_BLD, activation, tensors[MLP_DOWN])
        + as_float(tensors, MLP_DOWN_BIAS)
    ).astype(jnp.bfloat16)
    back_flat = lax.all_gather(weights, FSDP, axis=0, tiled=True)
    tensors = unpack(back_flat, model_width, hidden_width)
    gradients = {}
    out_grad = d_out.astype(jnp.float32)
    gradients[MLP_DOWN] = product(E_BLF_BLD_TO_FD, activation, d_out)
    gradients[MLP_DOWN_BIAS] = column_sums(d_out)
    activ_grad = product(E_BLD_FD_TO_BLF, d_out, tensors[MLP_DOWN])
    gelu_value, gelu_pull = jax.vjp(gelu_exact, preact)
    preact_grad = gelu_pull(activ_grad)[0].astype(jnp.bfloat16)
    gradients[MLP_UP] = product(E_BLD_BLF_TO_DF, normed_three, preact_grad)
    gradients[MLP_UP_BIAS] = column_sums(preact_grad)
    second_grad = out_grad + norm_back(
        second,
        tensors,
        NORM_THREE_GAIN,
        NORM_THREE_SHIFT,
        product(E_BLF_DF_TO_BLD, preact_grad, tensors[MLP_UP]),
        gradients,
    )
    cross_branch = second_grad.astype(jnp.bfloat16)
    gradients[CROSS_OUT] = product(E_BLD_BLE_TO_DE, cross_mixed, cross_branch)
    gradients[CROSS_OUT_BIAS] = column_sums(cross_branch)
    cmixed_grad = (
        product(E_BLE_DE_TO_BLD, cross_branch, tensors[CROSS_OUT])
        .astype(jnp.bfloat16)
        .reshape(heads_shape)
    )
    cquery_grad, ckeys_grad, cvalues_grad = attention_backward_pass(
        cross_queries, cross_keys, cross_values, usable, cross_log, cmixed_grad
    )
    cquery_low = cquery_grad.astype(jnp.bfloat16).reshape(token_layout_form)
    gradients[CROSS_QUERY] = product(E_BLD_BLE_TO_DE, normed_two, cquery_low)
    gradients[CROSS_QUERY_BIAS] = column_sums(cquery_low)
    first_grad = second_grad + norm_back(
        first_sum,
        tensors,
        NORM_TWO_GAIN,
        NORM_TWO_SHIFT,
        product(E_BLE_DE_TO_BLD, cquery_low, tensors[CROSS_QUERY]),
        gradients,
    )
    slot_layout_form = (caption_rows, slot_count, patch_count, model_width)
    slot_grad = jnp.concatenate(
        [ckeys_grad.reshape(slot_layout_form), cvalues_grad.reshape(slot_layout_form)], axis=-1
    )
    picked = (tile_index[:, :, None] == jnp.arange(group_kv.shape[0])[None, None, :]).astype(
        jnp.float32
    )
    group_grad = jnp.einsum(E_CSG_CSPE_TO_GPE, picked, slot_grad, precision=lax.Precision.HIGHEST)
    arrived = lax.all_to_all(
        group_grad.astype(jnp.bfloat16), FSDP, split_axis=0, concat_axis=0, tiled=True
    ).astype(group_grad.dtype)
    own_grad = jnp.sum(arrived.reshape((group_size, own_tiles) + arrived.shape[1:]), axis=0).astype(
        jnp.bfloat16
    )
    gradients[CROSS_KV] = product(E_TPD_TPE_TO_DE, tiles, own_grad)
    gradients[CROSS_VALUE_BIAS] = column_sums(own_grad[..., model_width:])
    tiles_grad = product(E_TPE_DE_TO_TPD, own_grad, tensors[CROSS_KV])
    self_branch = first_grad.astype(jnp.bfloat16)
    gradients[SELF_OUT] = product(E_BLD_BLE_TO_DE, self_mixed, self_branch)
    gradients[SELF_OUT_BIAS] = column_sums(self_branch)
    smixed_grad = (
        product(E_BLE_DE_TO_BLD, self_branch, tensors[SELF_OUT])
        .astype(jnp.bfloat16)
        .reshape(heads_shape)
    )
    self_query_gradient, self_key_gradient, self_value_gradient = attention_backward_pass(
        self_query, self_keys, self_values, self_allowed, self_log, smixed_grad
    )
    qkv_grad = jnp.concatenate(
        [
            self_query_gradient.reshape(token_layout_form),
            self_key_gradient.reshape(token_layout_form),
            self_value_gradient.reshape(token_layout_form),
        ],
        axis=-1,
    ).astype(jnp.bfloat16)
    gradients[SELF_QKV] = product(E_BLD_BLE_TO_DE, normed_one, qkv_grad)
    gradients[SELF_QUERY_BIAS] = column_sums(qkv_grad[..., :model_width])
    gradients[SELF_VALUE_BIAS] = column_sums(qkv_grad[..., 2 * model_width :])
    caption_grad = first_grad + norm_back(
        input_values,
        tensors,
        NORM_ONE_GAIN,
        NORM_ONE_SHIFT,
        product(E_BLE_DE_TO_BLD, qkv_grad, tensors[SELF_QKV]),
        gradients,
    )
    flat_grad = pack_rows(gradients, model_width, hidden_width, total_rows)
    shard_rows = total_rows // (data_size * group_size)
    received = lax.all_to_all(
        for_sending(flat_grad), DP, split_axis=0, concat_axis=0, tiled=True
    ).astype(flat_grad.dtype)
    data_grad = jnp.sum(received.reshape(data_size, group_size * shard_rows, 128), axis=0)
    shard_grad = lax.psum_scatter(
        data_grad.astype(jnp.bfloat16), FSDP, scatter_dimension=0, tiled=True
    ).astype(jnp.float32)
    begin_row = lax.axis_index(BOTH) * shard_rows
    seg_starts, seg_ends, decay_flags, seg_entries = segment_table(model_width, hidden_width)
    row_ids = begin_row + jnp.arange(shard_rows)
    member = (row_ids[:, None] >= seg_starts[None, :]) & (row_ids[:, None] < seg_ends[None, :])
    row_squares = jnp.sum(shard_grad * shard_grad, axis=1)
    part_sums = jnp.sum(jnp.where(member, row_squares[:, None], 0.0), axis=0)
    square_sums = lax.psum(part_sums, BOTH)
    old_weights = lax.dynamic_slice_in_dim(back_flat, begin_row, shard_rows, 0).astype(jnp.float32)
    update, new_first, new_second, grad_norm, tensor_rms = adam_step(
        shard_grad,
        member,
        decay_flags,
        old_weights,
        first_moment,
        second_moment,
        square_sums,
        seg_entries,
    )
    return (
        result,
        caption_grad,
        tiles_grad,
        shard_grad,
        update,
        new_first,
        new_second,
        grad_norm,
        tensor_rms,
    )


D = HEADS * HEAD_DIM
NZ = 4
TOK = 128
PATCH = 196
PATCH_SENT = 208
PATCH_SLOT = 256
KEYS = 2 * PATCH_SLOT
LEAD = 80
BF, F32 = jnp.bfloat16, jnp.float32
MESH = pl.DeviceIdType.MESH
SHARD, PIECES, PIECE = 2312, 5, 464
PADDED = PIECES * PIECE
WINDOW = 8 * SHARD
CARRY = 96
SEGS = 24
QKV_AT, WO_AT, UQ_AT, UKV_AT, UO_AT, WIDE = 0, 2304, 3072, 3840, 5376, 6144
W1_AT, W2_AT = 0, 3072
(V_G1, V_C1, V_BQKV, V_BO, V_G2, V_C2, V_UQ, V_BKV, V_UO, V_G3, V_C3, V_B1, V_B2) = range(13)


def row_starts():
    starts, at = {}, 0
    for label, shape, _ in layout(D, FF):
        starts[label] = at
        at += int(np.prod(shape)) // 128
    return starts


def mm(a, b):
    return lax.dot_general(a, b, (((1,), (0,)), ((), ())), preferred_element_type=F32)


def mm_nt(a, b):
    return lax.dot_general(a, b, (((1,), (1,)), ((), ())), preferred_element_type=F32)


def mm_tn(a, b):
    return lax.dot_general(a, b, (((0,), (0,)), ((), ())), preferred_element_type=F32)


def al(i, m):
    return pl.multiple_of(i * m, m)


def halves(pair):
    lane = lax.broadcasted_iota(jnp.int32, pair.shape, 1)
    zero = jnp.zeros_like(pair)
    return jnp.concatenate(
        [jnp.where(lane < HEAD_DIM, pair, zero), jnp.where(lane < HEAD_DIM, zero, pair)], axis=0
    )


def joined(stacked):
    n = stacked.shape[0] // 2
    lane = lax.broadcasted_iota(jnp.int32, (n, 128), 1)
    return jnp.where(lane < HEAD_DIM, stacked[:n], stacked[n:])


def normed(v):
    center = v - jnp.mean(v, axis=-1, keepdims=True)
    r = lax.rsqrt(jnp.mean(center * center, axis=-1, keepdims=True) + EPS_NORM)
    return center * r, r


def pair_kernel(
    cap, tiles, d_out, index, valid, length, weights,
    g_out, sums_out, old_out, out, dcap, dtile,
    fw, wide, gf, pc, ps, big1, big2, kv, dkvt, tl, tlT,
    xin, h1, am, h2, q2, a2, sb, rb, dy, t1, h1T, amT, h2T, a2T,
    x1, dx, acc, vec, meta, ob, pfx, pfx_in, carry, dcap_b, dtile_b,
    from_core, from_y, from_x, from_low, from_high, total, sq,
    wsem, gsem, send, recv, core_s, core_r, y_s, y_r, x_s, x_r, up_s, up_r, down_s, down_r, free, sum_s, sum_r,
):
    role = lax.axis_index(FSDP)
    other = 1 - role
    me = lax.axis_index(DP)
    my_z, my_y, my_core = me // 4, (me // 2) % 2, me % 2

    def at_dp(z, y, core):
        return {DP: z * 4 + y * 2 + core, FSDP: role}

    core_peer = at_dp(my_z, my_y, 1 - my_core)
    y_peer = at_dp(my_z, 1 - my_y, my_core)
    x_peer = {DP: me, FSDP: other}
    up_peer = at_dp(jnp.minimum(my_z + 1, NZ - 1), my_y, my_core)
    down_peer = at_dp(jnp.maximum(my_z - 1, 0), my_y, my_core)
    row0 = row_starts()

    cuts = [0, 13856, 18480, 23088, 32320, weights.shape[0]]
    loads = []
    for i in range(5):
        n = cuts[i + 1] - cuts[i]
        loads.append(
            pltpu.make_async_copy(
                weights.at[pl.ds(cuts[i], n)], fw.at[pl.ds(LEAD + cuts[i], n)], wsem.at[i]
            )
        )
    for c in loads:
        c.start()

    def to_other(src, dst, k):
        return pltpu.make_async_remote_copy(
            src_ref=src, dst_ref=dst, send_sem=send.at[k], recv_sem=recv.at[k],
            device_id=x_peer, device_id_type=MESH,
        )

    first, later = pl.ds(0, TOK), pl.ds(TOK, TOK)
    copies = dict(
        cap=to_other(cap, xin.at[later], 0),
        tile=to_other(tl.at[pl.ds(0, PATCH_SENT)], tl.at[pl.ds(PATCH_SLOT, PATCH_SENT)], 1),
        meta=to_other(meta.at[0], meta.at[1], 2),
        dy=to_other(d_out, dy.at[first], 3),
        lead=to_other(fw.at[pl.ds(weights.shape[0], LEAD)], fw.at[pl.ds(0, LEAD)], 4),
        x2=to_other(sb, rb, 5),
        dx2=to_other(sb, rb, 6),
        out=to_other(t1.at[first], ob, 7),
        pfx=to_other(pfx, pfx_in, 8),
        old=to_other(
            weights.at[pl.ds(pl.multiple_of(((2 * me + other) % 16) * SHARD - 8 * other, 16), PADDED)], old_out, 9
        ),
        dcap=to_other(dcap_b, dcap_b, 10),
        dtile=to_other(dtile_b, dtile_b, 11),
    )

    tl[...] = jnp.zeros_like(tl)
    tl[0:PATCH, :] = tiles[...]
    counts = []
    for g in range(2):
        named_by = jnp.int32(0)
        for s in range(index.shape[1]):
            named = jnp.where(index[0, s] == g, jnp.int32(1), jnp.int32(0))
            named_by = named_by + jnp.where(valid[0, s] > 0, named, jnp.int32(0))
        counts.append(named_by)
    rows8 = lax.broadcasted_iota(jnp.int32, (8, 128), 0)
    meta[0] = jnp.where(
        rows8 == 0, counts[0], jnp.where(rows8 == 1, counts[1], length[0])
    ).astype(F32)

    barrier = pltpu.get_barrier_semaphore()
    for peer in (core_peer, y_peer, x_peer):
        pl.semaphore_signal(barrier, inc=1, device_id=peer, device_id_type=MESH)
    for step in range(1, NZ):
        peer = at_dp((my_z + step) % NZ, my_y, my_core)
        pl.semaphore_signal(barrier, inc=1, device_id=peer, device_id_type=MESH)
    pl.semaphore_wait(barrier, 3 + NZ - 1)

    def vector(row, at, n, col=0):
        block = fw[pl.ds(at, n // 128), :].astype(F32)
        for j in range(n // 128):
            vec[row : row + 1, col + 128 * j : col + 128 * j + 128] = block[j : j + 1, :]

    def widen(at, k, col, rows=D):
        for j in range(k):
            wide[:, col + 128 * j : col + 128 * j + 128] = fw[pl.ds(at + j, rows, stride=k), :]

    def norm_forward(src, dst, g, c):
        @pl.loop(0, 4)
        def _(i):
            rows = pl.ds(al(i, 64), 64)
            n, _ = normed(src[rows, :].astype(F32))
            dst[rows, :] = (n * vec[g : g + 1, :D] + vec[c : c + 1, :D]).astype(BF)

    def norm_backward(src, dh, g, write, g_at, c_at, into):
        sums = (jnp.zeros((1, D), F32), jnp.zeros((1, D), F32))

        def step(i, carry):
            rows = pl.ds(al(i, 64), 64)
            n, r = normed(src[rows, :].astype(F32))
            d = dh[rows, :]
            dn = d * vec[g : g + 1, :D]
            dv = r * (
                dn - jnp.mean(dn, axis=-1, keepdims=True) - n * jnp.mean(dn * n, axis=-1, keepdims=True)
            )
            write(rows, dv)
            return (
                carry[0] + jnp.sum(d * n, axis=0, keepdims=True),
                carry[1] + jnp.sum(d, axis=0, keepdims=True),
            )

        gg, gc = lax.fori_loop(0, 4, step, sums)
        put_vector(g_at, gg, into)
        put_vector(c_at, gc, into)

    def put_vector(at, row, into=gf):
        for j in range(row.shape[1] // 128):
            into[at + j : at + j + 1, :] = row[:, 128 * j : 128 * j + 128]

    def column_total(ref, cols):
        return jnp.sum(ref[:, cols].astype(F32), axis=0, keepdims=True)

    def matrix_grad(at, k, lhs_t, rhs, transposed=False):
        @pl.loop(0, k // 2)
        def _(m):
            cols = pl.ds(al(m, 256), 256)
            res = mm_nt(lhs_t[...], rhs[cols, :]) if transposed else mm(lhs_t[...], rhs[:, cols])
            for half in range(2):
                gf[pl.ds(at + 2 * m + half, D, stride=k), :] = res[:, 128 * half : 128 * half + 128]

    def copy_to(peer, src, dst, ssem, rsem):
        return pltpu.make_async_remote_copy(
            src_ref=src, dst_ref=dst, send_sem=ssem, recv_sem=rsem, device_id=peer, device_id_type=MESH
        )

    def slot(w, s, core, y=0, x=0):
        return pl.multiple_of(((w * PIECES + s) * 8 + core * 4 + y * 2 + x) * PIECE, 16)

    class Scatter:
        def __init__(self, w, x):
            self.w, self.x = w, x

        def core(self, s):
            rows = pl.ds(slot(self.w, s, 1 - my_core), 4 * PIECE)
            return copy_to(core_peer, fw.at[rows], from_core.at[s], core_s.at[s], core_r.at[s])

        def y(self, s):
            rows = pl.ds(slot(self.w, s, my_core, 1 - my_y), 2 * PIECE)
            return copy_to(y_peer, fw.at[rows], from_y.at[s], y_s.at[s], y_r.at[s])

        def over(self, s):
            rows = pl.ds(slot(self.w, s, my_core, my_y, 1 - self.x), PIECE)
            return copy_to(x_peer, fw.at[rows], from_x.at[s], x_s.at[s], x_r.at[s])

        def held(self, s, h):
            if h == self.x:
                return fw.at[pl.ds(slot(self.w, s, my_core, my_y, self.x), PIECE)]
            return from_x.at[s]

        def up(self, s, h):
            return copy_to(up_peer, self.held(s, h), from_low.at[s, h], up_s.at[s, h], up_r.at[s, h])

        def down(self, s, h):
            return copy_to(down_peer, self.held(s, h), from_high.at[s, h], down_s.at[s, h], down_r.at[s, h])

        def cast(self, first_row):
            @pl.loop(0, PIECES)
            def _(s):
                for k in range(8):
                    j = (k & 2) * 2 + (k & 4) // 2 + (k & 1)
                    src = pl.ds(pl.multiple_of(first_row + j * SHARD + s * PIECE, 8), PIECE)
                    fw[pl.ds(pl.multiple_of(slot(self.w, s, 0) + k * PIECE, 16), PIECE), :] = gf[src, :].astype(BF)
                self.core(s).start()

        def add_core(self):
            @pl.loop(0, PIECES)
            def _(s):
                self.core(s).wait_recv()
                rows = pl.ds(slot(self.w, s, my_core), 4 * PIECE)
                fw[rows, :] = fw[rows, :] + from_core[s]

        def start_y(self):
            @pl.loop(0, PIECES)
            def _(s):
                self.y(s).start()

        def add_y(self, s):
            self.y(s).wait_recv()
            rows = pl.ds(slot(self.w, s, my_core, my_y), 2 * PIECE)
            fw[rows, :] = fw[rows, :] + from_y[s]
            self.over(s).start()

        def from_ends(self, s):
            self.over(s).wait_recv()
            for h in range(2):
                goal = 2 * h + self.w
                if goal > 0:
                    pl.when(my_z == 0)(self.up(s, h).start)
                if goal < NZ - 1:
                    pl.when(my_z == NZ - 1)(self.down(s, h).start)

        def relay(self, s):
            for h in range(2):
                goal = 2 * h + self.w
                mine = self.held(s, h)
                if goal > 1:

                    @pl.when((my_z > 0) & (my_z < goal))
                    def _():
                        self.up(s, h).wait_recv()
                        mine[...] = mine[...] + from_low[s, h]
                        self.up(s, h).start()

                if goal < NZ - 2:

                    @pl.when((my_z < NZ - 1) & (my_z > goal))
                    def _():
                        self.down(s, h).wait_recv()
                        mine[...] = mine[...] + from_high[s, h]
                        self.down(s, h).start()

        def collect(self, s):
            for h in range(2):
                goal = 2 * h + self.w

                @pl.when(my_z == goal)
                def _():
                    whole = self.held(s, h)[...].astype(F32)
                    if goal > 0:
                        self.up(s, h).wait_recv()
                        whole = whole + from_low[s, h].astype(F32)
                    if goal < NZ - 1:
                        self.down(s, h).wait_recv()
                        whole = whole + from_high[s, h].astype(F32)
                    total[pl.ds(pl.multiple_of(s * PIECE, 8), PIECE), :] = whole

        def sent(self):
            @pl.loop(0, PIECES)
            def _(s):
                self.core(s).wait_send()
                self.y(s).wait_send()
                self.over(s).wait_send()

        def sent_z(self):
            @pl.loop(0, PIECES)
            def _(s):
                for h in range(2):
                    goal = 2 * h + self.w
                    pl.when(my_z < goal)(self.up(s, h).wait_send)
                    pl.when(my_z > goal)(self.down(s, h).wait_send)

    def give(k, peer):
        pl.semaphore_signal(free.at[k], inc=1, device_id=peer, device_id_type=MESH)

    def take(k):
        pl.semaphore_wait(free.at[k], 1)

    def rest_of_scatter(one, zero):
        @pl.loop(0, PIECES)
        def _(s):
            one.add_y(s)

        give(1, y_peer)
        take(1)
        zero.start_y()

        pl.loop(0, PIECES)(one.from_ends)
        pl.loop(0, PIECES)(one.relay)
        pl.loop(0, PIECES)(one.collect)

        one.sent_z()
        give(2, x_peer)
        pl.when(my_z > 0)(lambda: give(3, down_peer))
        pl.when(my_z < NZ - 1)(lambda: give(4, up_peer))
        take(2)
        pl.when(my_z < NZ - 1)(lambda: take(3))
        pl.when(my_z > 0)(lambda: take(4))

        @pl.loop(0, PIECES)
        def _(s):
            zero.add_y(s)

            pl.when(s > 0)(lambda: zero.from_ends(s - 1))
            pl.when(s > 1)(lambda: zero.relay(s - 2))

        zero.from_ends(PIECES - 1)
        zero.relay(PIECES - 2)
        zero.relay(PIECES - 1)
        pl.loop(0, PIECES)(zero.collect)
        zero.sent()
        zero.sent_z()

    def square_sums():
        total[SHARD:, :] = jnp.zeros((total.shape[0] - SHARD, 128), F32)
        done = pltpu.make_async_copy(total.at[pl.ds(0, SHARD)], g_out, gsem)
        done.start()
        seg = lax.broadcasted_iota(jnp.int32, (SEGS, 1), 0)
        begin = jnp.full((SEGS, 1), 1 << 30, jnp.int32)
        end = begin
        for i, (a, b) in enumerate(zip(*segment_table(D, FF)[:2])):
            begin = jnp.where(seg == i, int(a), begin)
            end = jnp.where(seg == i, int(b), end)
        row = (me * 2 + role) * SHARD + lax.broadcasted_iota(jnp.int32, (SEGS, total.shape[0]), 1)
        member = jnp.where((row >= begin) & (row < end), 1.0, 0.0)
        squares = lax.dot_general(
            member, total[...] * total[...], (((1,), (0,)), ((), ())),
            precision=lax.Precision.HIGHEST, preferred_element_type=F32,
        )
        mine = jnp.broadcast_to(jnp.sum(squares, axis=1, keepdims=True), (SEGS, 128))
        for i, peer in enumerate((core_peer, y_peer, x_peer)):
            sq[2 * i] = mine
            swap = copy_to(peer, sq.at[2 * i], sq.at[2 * i + 1], sum_s.at[i], sum_r.at[i])
            swap.start()
            swap.wait()
            mine = mine + sq[2 * i + 1]
        sq[6] = mine
        sends = []
        for step in range(1, NZ):
            to = at_dp((my_z + step) % NZ, my_y, my_core)
            sends.append(copy_to(to, sq.at[6], sq.at[6 + step], sum_s.at[2 + step], sum_r.at[2 + step]))
            sends[-1].start()
        for c in sends:
            c.wait()
        whole = jnp.zeros((SEGS, 128), F32)
        for z in range(NZ):
            part = mine
            for step in range(1, NZ):
                part = jnp.where((my_z - step + NZ) % NZ == z, sq[6 + step], part)
            whole = whole + part
        sums_out[...] = whole
        done.wait()

    def attention_role():
        at = {k: LEAD + v for k, v in row0.items()}
        at0 = {k: CARRY + v for k, v in row0.items()}
        at1 = {k: CARRY - WINDOW + v for k, v in row0.items()}
        one, zero = Scatter(1, 0), Scatter(0, 0)
        xin[first, :] = cap[...]
        copies["dy"].start()
        loads[0].wait()
        vector(V_G1, at[NORM_ONE_GAIN], D)
        vector(V_C1, at[NORM_ONE_SHIFT], D)
        vec[V_BQKV : V_BQKV + 1, :] = jnp.zeros((1, FF), F32)
        vec[V_BKV : V_BKV + 1, :] = jnp.zeros((1, FF), F32)
        vector(V_BQKV, at[SELF_QUERY_BIAS], D)
        vector(V_BQKV, at[SELF_VALUE_BIAS], D, 2 * D)
        widen(at[SELF_QKV], 18, QKV_AT)
        for c in loads[1:]:
            c.wait()
        copies["lead"].start()
        vector(V_BO, at[SELF_OUT_BIAS], D)
        vector(V_G2, at[NORM_TWO_GAIN], D)
        vector(V_C2, at[NORM_TWO_SHIFT], D)
        vector(V_UQ, at[CROSS_QUERY_BIAS], D)
        vector(V_BKV, at[CROSS_VALUE_BIAS], D, D)
        vector(V_UO, at[CROSS_OUT_BIAS], D)
        widen(at[SELF_OUT], 6, WO_AT)
        widen(at[CROSS_QUERY], 6, UQ_AT)
        widen(at[CROSS_KV], 12, UKV_AT)
        widen(at[CROSS_OUT], 6, UO_AT)

        copies["cap"].wait_recv()
        norm_forward(xin, h1, V_G1, V_C1)

        @pl.loop(0, 3)
        def _(j):
            cols = pl.ds(al(j, D), D)
            big1[:, cols] = (mm(h1[...], wide[:, cols]) + vec[V_BQKV : V_BQKV + 1, cols]).astype(BF)

        copies["meta"].wait_recv()

        @pl.loop(0, 12)
        def _(i):
            c, p = i // 6, i % 6
            rows = pl.ds(al(c, TOK), TOK)
            qq = halves(big1[rows, pl.ds(al(p, 128), 128)]) * BF(0.125)
            k2 = big1[rows, pl.ds(al(p, 128) + D, 128)]
            v2 = big1[rows, pl.ds(al(p, 128) + 2 * D, 128)]
            s = mm_nt(qq, k2)
            row = lax.broadcasted_iota(jnp.int32, s.shape, 0) % TOK
            col = lax.broadcasted_iota(jnp.int32, s.shape, 1)
            present = col.astype(F32) < meta[c][2:3, :]
            s = jnp.where((col <= row) & present, s, NEG_LARGE)
            e = jnp.exp(s - jnp.max(s, axis=-1, keepdims=True))
            prob = (e / jnp.sum(e, axis=-1, keepdims=True)).astype(BF)
            ps[i] = prob
            am[rows, pl.ds(al(p, 128), 128)] = joined(mm(prob, v2)).astype(BF)

        x1[...] = xin[...].astype(F32) + mm(am[...], wide[:, WO_AT : WO_AT + D]) + vec[V_BO : V_BO + 1, :D]
        norm_forward(x1, h2, V_G2, V_C2)
        q2[...] = (mm(h2[...], wide[:, UQ_AT : UQ_AT + D]) + vec[V_UQ : V_UQ + 1, :D]).astype(BF)
        copies["tile"].wait_recv()

        @pl.loop(0, 2)
        def _(j):
            cols = pl.ds(al(j, D), D)
            kv[:, cols] = (
                mm(tl[...], wide[:, pl.ds(al(j, D) + UKV_AT, D)]) + vec[V_BKV : V_BKV + 1, cols]
            ).astype(BF)

        @pl.loop(0, 12)
        def _(i):
            p, c = i // 2, i % 2
            rows = pl.ds(al(c, TOK), TOK)
            qq = halves(q2[rows, pl.ds(al(p, 128), 128)]) * BF(0.125)
            s = mm_nt(qq, kv[:, pl.ds(al(p, 128), 128)])
            col = lax.broadcasted_iota(jnp.int32, (1, KEYS), 1)
            m = meta[c]
            c0 = jnp.concatenate([m[0:1, :]] * (KEYS // 128), axis=1)
            c1 = jnp.concatenate([m[1:2, :]] * (KEYS // 128), axis=1)
            count = jnp.where(col < PATCH, c0, jnp.where(col < PATCH_SLOT, 0.0, c1))
            count = jnp.where(col < PATCH_SLOT + PATCH, count, 0.0)
            s = jnp.where(count > 0.0, s, NEG_LARGE)
            e = jnp.exp(s - jnp.max(s, axis=-1, keepdims=True)) * count
            prob = (e / jnp.sum(e, axis=-1, keepdims=True)).astype(BF)
            pc[pl.ds(al(i, 2 * TOK), 2 * TOK), :] = prob
            a2[rows, pl.ds(al(p, 128), 128)] = joined(
                mm(prob, kv[:, pl.ds(al(p, 128) + D, 128)])
            ).astype(BF)

        sb[...] = (
            x1[...] + mm(a2[...], wide[:, UO_AT : UO_AT + D]) + vec[V_UO : V_UO + 1, :D]
        ).astype(BF)
        copies["x2"].start()
        copies["old"].start()

        h1T[...] = h1[...].T
        amT[...] = am[...].T
        h2T[...] = h2[...].T
        a2T[...] = a2[...].T
        tlT[...] = tl[...].T

        copies["dx2"].wait_recv()
        t1[...] = mm_nt(rb[...], wide[:, UO_AT : UO_AT + D]).astype(BF)
        put_vector(at1[CROSS_OUT_BIAS], column_total(rb, slice(None)))
        matrix_grad(at1[CROSS_OUT], 6, a2T, rb)

        @pl.loop(0, 6)
        def _(p):
            lanes, vlanes = pl.ds(al(p, 128), 128), pl.ds(al(p, 128) + D, 128)
            dk = dv = None
            for c in range(2):
                rows = pl.ds(c * TOK, TOK)
                qq = halves(q2[rows, lanes]) * BF(0.125)
                do = halves(t1[rows, lanes])
                prob = pc[pl.ds(al(2 * p + c, 2 * TOK), 2 * TOK), :]
                pf = prob.astype(F32)
                dp = mm_nt(do, kv[:, vlanes])
                ds = (pf * (dp - jnp.sum(pf * dp, axis=-1, keepdims=True))).astype(BF)
                am[rows, lanes] = (joined(mm(ds, kv[:, lanes])) * 0.125).astype(BF)
                dk_c, dv_c = mm_tn(qq, ds), mm_tn(do, prob)
                dk, dv = (dk_c, dv_c) if c == 0 else (dk + dk_c, dv + dv_c)
            dkvt[lanes, :] = dk.astype(BF)
            dkvt[vlanes, :] = dv.astype(BF)

        put_vector(at1[CROSS_QUERY_BIAS], column_total(am, slice(None)))
        matrix_grad(at1[CROSS_QUERY], 6, h2T, am)
        acc[...] = mm_nt(am[...], wide[:, UQ_AT : UQ_AT + D])

        def write_dx1(rows, dv):
            full = rb[rows, :].astype(F32) + dv
            dx[rows, :] = full
            sb_[rows, :] = full.astype(BF)

        sb_ = h2
        norm_backward(x1, acc, V_G2, write_dx1, at1[NORM_TWO_GAIN], at1[NORM_TWO_SHIFT], gf)
        matrix_grad(at1[CROSS_KV], 12, tlT, dkvt, transposed=True)
        kv[...] = dkvt[...].T
        put_vector(at1[CROSS_VALUE_BIAS], column_total(kv, slice(D, 2 * D)))

        def tile_grad(rows):
            keys = mm_nt(kv[rows, 0:D], wide[:, UKV_AT : UKV_AT + D])
            return keys + mm_nt(kv[rows, D : 2 * D], wide[:, UKV_AT + D : UKV_AT + 2 * D])

        dtile[...] = tile_grad(pl.ds(0, PATCH_SENT))[:PATCH]
        dtile_b[...] = tile_grad(pl.ds(PATCH_SLOT, PATCH_SENT)).astype(BF)
        copies["dtile"].start()
        copies["pfx"].wait_recv()
        gf[pl.ds(at1[NORM_THREE_GAIN], LEAD - 12), :] = pfx_in[12:, :]
        copies["lead"].wait_send()
        one.cast(CARRY)
        carry[...] = gf[0:CARRY, :]
        put_vector(at0[SELF_OUT_BIAS], column_total(sb_, slice(None)))
        matrix_grad(at0[SELF_OUT], 6, amT, sb_)
        t1[...] = mm_nt(sb_[...], wide[:, WO_AT : WO_AT + D]).astype(BF)

        one.add_core()
        one.start_y()
        give(0, core_peer)

        @pl.loop(0, 12)
        def _(i):
            c, p = i // 6, i % 6
            rows = pl.ds(al(c, TOK), TOK)
            lanes = pl.ds(al(p, 128), 128)
            klanes, vlanes = pl.ds(al(p, 128) + D, 128), pl.ds(al(p, 128) + 2 * D, 128)
            qq = halves(big1[rows, lanes]) * BF(0.125)
            do = halves(t1[rows, lanes])
            prob = ps[i]
            pf = prob.astype(F32)
            dp = mm_nt(do, big1[rows, vlanes])
            ds = (pf * (dp - jnp.sum(pf * dp, axis=-1, keepdims=True))).astype(BF)
            big2[rows, lanes] = (joined(mm(ds, big1[rows, klanes])) * 0.125).astype(BF)
            big2[rows, klanes] = mm_tn(ds, qq).astype(BF)
            big2[rows, vlanes] = mm_tn(prob, do).astype(BF)

        for j in range(3):
            part = mm_nt(big2[:, D * j : D * j + D], wide[:, D * j : D * j + D])
            acc[...] = part if j == 0 else acc[...] + part

        def write_dx0(rows, dv):
            dx[rows, :] = dx[rows, :] + dv

        norm_backward(xin, acc, V_G1, write_dx0, at0[NORM_ONE_GAIN], at0[NORM_ONE_SHIFT], gf)
        dcap[...] = dx[first, :]
        dcap_b[...] = dx[later, :].astype(BF)
        copies["dcap"].start()
        put_vector(at0[SELF_QUERY_BIAS], column_total(big2, slice(0, D)))
        put_vector(at0[SELF_VALUE_BIAS], column_total(big2, slice(2 * D, 3 * D)))
        matrix_grad(at0[SELF_QKV], 18, h1T, big2)
        gf[pl.ds(at0[NORM_TWO_GAIN], WINDOW - row0[NORM_TWO_GAIN]), :] = carry[
            row0[NORM_TWO_GAIN] - WINDOW + CARRY :, :
        ]
        take(0)
        zero.cast(CARRY)
        zero.add_core()
        rest_of_scatter(one, zero)
        one.sent()
        copies["out"].wait_recv()
        out[...] = ob[...]
        for name in ("dy", "x2", "dcap", "dtile"):
            copies[name].wait_send()
        copies["old"].wait()
        square_sums()

    def mlp_role():
        copies["cap"].start()
        copies["tile"].start()
        copies["meta"].start()
        base = LEAD - weights.shape[0]
        at = {k: base + v for k, v in row0.items()}
        at0 = {k: CARRY - weights.shape[0] + v for k, v in row0.items()}
        at1 = {k: v - WINDOW for k, v in at0.items()}
        one, zero = Scatter(1, 1), Scatter(0, 1)
        dy[later, :] = d_out[...]
        for c in loads:
            c.wait()
        for b in range(4):
            widen(at[MLP_DOWN] + 6 * D * b, 6, W2_AT + D * b)
        copies["lead"].wait_recv()
        widen(at[MLP_UP], 24, W1_AT)
        vector(V_G3, at[NORM_THREE_GAIN], D)
        vector(V_C3, at[NORM_THREE_SHIFT], D)
        vector(V_B1, at[MLP_UP_BIAS], FF)
        vector(V_B2, at[MLP_DOWN_BIAS], D)
        copies["dy"].wait_recv()

        @pl.loop(0, 4)
        def _(b):
            dg = mm_nt(dy[...], wide[:, pl.ds(al(b, D) + W2_AT, D)])
            for j in range(6):
                gf[pl.ds(al(6 * b + j, 256), 256), :] = dg[:, 128 * j : 128 * j + 128]

        copies["x2"].wait_recv()
        norm_forward(rb, h1, V_G3, V_C3)
        acc[...] = jnp.zeros_like(acc)

        @pl.loop(0, 4)
        def _(b):
            cols = pl.ds(al(b, D), D)
            x1[...] = mm(h1[...], wide[:, cols]) + vec[V_B1 : V_B1 + 1, cols]

            @pl.loop(0, 8)
            def _(i):
                rows = pl.ds(al(i, 32), 32)
                for j in range(6):
                    z = x1[rows, 128 * j : 128 * j + 128]
                    phi = 0.5 + 0.5 * lax.erf(z * np.float32(np.sqrt(0.5)))
                    dens = jnp.exp(-0.5 * z * z) * np.float32(1.0 / np.sqrt(2.0 * np.pi))
                    lanes = pl.ds(al(b, D) + 128 * j, 128)
                    big1[rows, lanes] = (z * phi).astype(BF)
                    dg = gf[pl.ds(al(6 * b + j, 256) + al(i, 32), 32), :]
                    big2[rows, lanes] = (dg * (phi + z * dens)).astype(BF)

            acc[...] = acc[...] + mm_nt(big2[:, cols], wide[:, cols])

        def write_dx2(rows, dv):
            sb[rows, :] = (dy[rows, :].astype(F32) + dv).astype(BF)

        norm_backward(rb, acc, V_G3, write_dx2, 12, 18, pfx)
        copies["dx2"].start()

        h1T[...] = h1[...].T
        pfx[0:12, :] = jnp.zeros((12, 128), F32)
        for b in range(4):
            head = mm(h1T[0:8, :], big2[:, D * b : D * b + D])
            for r in range(3):
                for j in range(6):
                    row = 24 + 24 * r + 6 * b + j
                    if row < LEAD:
                        pfx[row : row + 1, :] = head[r : r + 1, 128 * j : 128 * j + 128]
        copies["pfx"].start()
        copies["old"].start()

        acc[...] = rb[...].astype(F32) + vec[V_B2 : V_B2 + 1, :D]

        @pl.loop(0, 4)
        def _(b):
            cols = pl.ds(al(b, D), D)
            acc[...] = acc[...] + mm(big1[:, cols], wide[:, pl.ds(al(b, D) + W2_AT, D)])
            pc[pl.ds(al(b, D), D), 0:256] = big1[:, cols].T

        t1[first, :] = acc[first, :].astype(BF)
        copies["out"].start()
        out[...] = acc[later, :].astype(BF)
        gf[pl.ds(at1[MLP_DOWN_BIAS] + 6, WINDOW + CARRY - at1[MLP_DOWN_BIAS] - 6), :] = jnp.zeros(
            (WINDOW + CARRY - at1[MLP_DOWN_BIAS] - 6, 128), F32
        )
        put_vector(at1[MLP_DOWN_BIAS], column_total(dy, slice(None)))
        for b in range(4):
            matrix_grad(at1[MLP_DOWN] + 6 * D * b, 6, pc.at[pl.ds(D * b, D), pl.ds(0, 256)], dy)
        one.cast(CARRY)
        carry[...] = gf[0:CARRY, :]
        put_vector(at0[MLP_UP_BIAS], column_total(big2, slice(None)))
        matrix_grad(at0[MLP_UP], 24, h1T, big2)
        one.add_core()
        one.start_y()
        give(0, core_peer)
        gf[pl.ds(at0[MLP_DOWN], CARRY), :] = carry[...]
        take(0)
        zero.cast(CARRY)
        zero.add_core()
        rest_of_scatter(one, zero)
        one.sent()
        copies["dtile"].wait_recv()
        dtile[...] = dtile_b[0:PATCH, :].astype(F32)
        copies["dcap"].wait_recv()
        dcap[...] = dcap_b[...].astype(F32)
        for name in ("cap", "tile", "meta", "dx2", "pfx", "out"):
            copies[name].wait_send()
        copies["old"].wait()
        square_sums()

    pl.when(role == 0)(attention_role)
    pl.when(role == 1)(mlp_role)


def pair_call(cap, tiles, d_out, index, valid, length, weights):
    vm = pl.BlockSpec(memory_space=pltpu.VMEM)
    sm = pl.BlockSpec(memory_space=pltpu.SMEM)
    hbm = pl.BlockSpec(memory_space=pl.ANY)
    S = jax.ShapeDtypeStruct
    dma, both = pltpu.SemaphoreType.DMA, 2 * TOK

    def bf(*s):
        return pltpu.VMEM(s, BF)

    def fl(*s):
        return pltpu.VMEM(s, F32)

    return pl.pallas_call(
        pair_kernel,
        in_specs=[vm, vm, vm, sm, sm, sm, hbm],
        out_specs=[hbm, vm, hbm, vm, vm, vm],
        out_shape=[
            S((SHARD, 128), F32),
            S((SEGS, 128), F32),
            S((PADDED, 128), BF),
            S((TOK, D), BF),
            S((TOK, D), F32),
            S((PATCH, D), F32),
        ],
        scratch_shapes=[
            bf(16 * PADDED, 128), bf(D, WIDE), fl(CARRY + WINDOW + 8, 128), bf(12 * both, KEYS),
            bf(12, both, 128), bf(both, FF), bf(both, FF), bf(KEYS, 2 * D), bf(2 * D, KEYS), bf(KEYS, D), bf(D, KEYS),
            *[bf(both, D) for _ in range(10)],
            *[bf(D, both) for _ in range(4)],
            *[fl(both, D) for _ in range(3)],
            fl(16, FF), fl(2, 8, 128), bf(TOK, D), fl(LEAD, 128), fl(LEAD, 128), fl(CARRY, 128),
            bf(TOK, D), bf(PATCH_SENT, D),
            bf(PIECES, 4 * PIECE, 128), bf(PIECES, 2 * PIECE, 128), bf(PIECES, PIECE, 128),
            bf(PIECES, 2, PIECE, 128), bf(PIECES, 2, PIECE, 128), fl(2432, 128), fl(10, SEGS, 128),
            dma((5,)), dma, dma((12,)), dma((12,)),
            *[dma((PIECES,)) for _ in range(6)],
            *[dma((PIECES, 2)) for _ in range(4)],
            pltpu.SemaphoreType.REGULAR((5,)), dma((6,)), dma((6,)),
        ],
        compiler_params=pltpu.CompilerParams(
            collective_id=0, has_side_effects=True, vmem_limit_bytes=63 * 2**20
        ),
    )(cap, tiles, d_out, index, valid, length, weights)


def finish(shard_grad, old_weights, first_moment, second_moment, square_sums):
    shard_rows = shard_grad.shape[0]
    begin_row = lax.axis_index(BOTH) * shard_rows
    seg_starts, seg_ends, decay_flags, seg_entries = segment_table(D, FF)
    row_ids = begin_row + jnp.arange(shard_rows)
    member = (row_ids[:, None] >= seg_starts[None, :]) & (row_ids[:, None] < seg_ends[None, :])
    return adam_step(
        shard_grad, member, decay_flags, old_weights, first_moment, second_moment, square_sums, seg_entries
    )


def pair_body(
    captions, tiles, tile_index, tile_valid, caption_len, weights, first_moment, second_moment, d_out
):
    me, f = lax.axis_index(DP), lax.axis_index(FSDP)
    shard_grad, sums, old, out, caption_grad, tiles_grad = pair_call(
        captions[0], tiles[0], d_out[0], tile_index, tile_valid, caption_len, weights
    )
    own = lax.dynamic_slice_in_dim(weights, ((2 * me + f) % 16) * SHARD, SHARD, 0)
    old = lax.dynamic_slice_in_dim(old, 8 * f, SHARD, 0)
    old_weights = jnp.where(me // 8 == f, own, old).astype(jnp.float32)
    update, new_first, new_second, grad_norm, tensor_rms = finish(
        shard_grad, old_weights, first_moment, second_moment, sums[:21, 0]
    )
    return (
        out[None], caption_grad[None], tiles_grad[None], shard_grad, update, new_first, new_second,
        grad_norm, tensor_rms,
    )


def solution(mesh):
    placed = (
        P(BOTH, None, None),
        P(BOTH, None, None),
        P(BOTH, None),
        P(BOTH, None),
        P(BOTH),
        P(FSDP, None),
        P(BOTH, None),
        P(BOTH, None),
        P(BOTH, None, None),
    )
    return jax.shard_map(
        pair_body if mesh.shape[FSDP] == 2 else body,
        mesh=mesh,
        in_specs=placed,
        out_specs=(
            P(BOTH, None, None),
            P(BOTH, None, None),
            P(BOTH, None, None),
            P(BOTH, None),
            P(BOTH, None),
            P(BOTH, None),
            P(BOTH, None),
            P(),
            P(),
        ),
        check_vma=False,
    )
```

```python
import functools

import jax
import jax.numpy as jnp
import numpy as np
from jax import lax
from jax.experimental import pallas as pl
from jax.experimental.pallas import tpu as pltpu
from jax.sharding import PartitionSpec as P

HEADS = 12
HEAD_DIM = 64
FF = 3072
STEP = 10


EPS_NORM = 1e-05
CLIP_NORM = 1.0
BETA_ONE = 0.9
BETA_TWO = 0.999
LEARN_RATE = 0.01
DECAY_RATE = 0.1
ADAM_EPS = 1e-08
NEG_LARGE = -1e30
(NORM_ONE_GAIN, NORM_ONE_SHIFT, SELF_QKV, SELF_QUERY_BIAS, SELF_VALUE_BIAS, SELF_OUT, SELF_OUT_BIAS, NORM_TWO_GAIN, NORM_TWO_SHIFT, CROSS_QUERY, CROSS_QUERY_BIAS, CROSS_KV, CROSS_VALUE_BIAS, CROSS_OUT, CROSS_OUT_BIAS, NORM_THREE_GAIN, NORM_THREE_SHIFT, MLP_UP, MLP_UP_BIAS, MLP_DOWN, MLP_DOWN_BIAS) = range(21)
DP, FSDP = "dp", "fsdp"
BOTH = (DP, FSDP)
E_BHQK_BKHE_TO_BQHE = "bhqk,bkhe->bqhe"
E_BHQK_BQHE_TO_BKHE = "bhqk,bqhe->bkhe"
E_BLD_BLE_TO_DE = "bld,ble->de"
E_BLD_BLF_TO_DF = "bld,blf->df"
E_BLD_DE_TO_BLE = "bld,de->ble"
E_BLD_DF_TO_BLF = "bld,df->blf"
E_BLD_FD_TO_BLF = "bld,fd->blf"
E_BLE_DE_TO_BLD = "ble,de->bld"
E_BLF_BLD_TO_FD = "blf,bld->fd"
E_BLF_DF_TO_BLD = "blf,df->bld"
E_BLF_FD_TO_BLD = "blf,fd->bld"
E_BQHE_BKHE_TO_BHQK = "bqhe,bkhe->bhqk"
E_CSG_CSPE_TO_GPE = "csg,cspe->gpe"
E_TPD_DE_TO_TPE = "tpd,de->tpe"
E_TPD_TPE_TO_DE = "tpd,tpe->de"
E_TPE_DE_TO_TPD = "tpe,de->tpd"


def for_sending(x):
    return jax.tree.map(lambda a: a.astype(jnp.bfloat16) if a.dtype == jnp.float32 else a, x)


def layout(model_width, hidden_width):
    return [
        (NORM_ONE_GAIN, (model_width,), 0),
        (NORM_ONE_SHIFT, (model_width,), 0),
        (SELF_QKV, (model_width, 3 * model_width), 1),
        (SELF_QUERY_BIAS, (model_width,), 0),
        (SELF_VALUE_BIAS, (model_width,), 0),
        (SELF_OUT, (model_width, model_width), 1),
        (SELF_OUT_BIAS, (model_width,), 0),
        (NORM_TWO_GAIN, (model_width,), 0),
        (NORM_TWO_SHIFT, (model_width,), 0),
        (CROSS_QUERY, (model_width, model_width), 1),
        (CROSS_QUERY_BIAS, (model_width,), 0),
        (CROSS_KV, (model_width, 2 * model_width), 1),
        (CROSS_VALUE_BIAS, (model_width,), 0),
        (CROSS_OUT, (model_width, model_width), 1),
        (CROSS_OUT_BIAS, (model_width,), 0),
        (NORM_THREE_GAIN, (model_width,), 0),
        (NORM_THREE_SHIFT, (model_width,), 0),
        (MLP_UP, (model_width, hidden_width), 1),
        (MLP_UP_BIAS, (hidden_width,), 0),
        (MLP_DOWN, (hidden_width, model_width), 1),
        (MLP_DOWN_BIAS, (model_width,), 0),
    ]


def segment_table(model_width, hidden_width):
    seg_starts = []
    seg_ends = []
    decay_flags = []
    seg_entries = []
    row_at = 0
    for seg_label, seg_shape, seg_flag in layout(model_width, hidden_width):
        item_count = int(np.prod(seg_shape))
        seg_rows = item_count // 128
        seg_starts.append(row_at)
        seg_ends.append(row_at + seg_rows)
        decay_flags.append(seg_flag == 1)
        seg_entries.append(float(item_count))
        row_at = row_at + seg_rows
    return (np.array(seg_starts), np.array(seg_ends), np.array(decay_flags), np.array(seg_entries))


def unpack(flat_rows, model_width, hidden_width):
    vector = flat_rows.reshape(-1)
    tensors = {}
    offset = 0
    for seg_label, seg_shape, seg_flag in layout(model_width, hidden_width):
        item_count = int(np.prod(seg_shape))
        tensors[seg_label] = vector[offset : offset + item_count].reshape(seg_shape)
        offset = offset + item_count
    return tensors


def pack_rows(gradients, model_width, hidden_width, total_rows):
    pieces = [
        gradients[seg_label].reshape(-1, 128)
        for seg_label, seg_shape, seg_flag in layout(model_width, hidden_width)
    ]
    used_rows = sum((tensor_piece.shape[0] for tensor_piece in pieces))
    pieces.append(jnp.zeros((total_rows - used_rows, 128), jnp.float32))
    return jnp.concatenate(pieces, axis=0)


def product(pattern, left_side, right_side):
    return jnp.einsum(pattern, left_side, right_side, preferred_element_type=jnp.float32)


def as_float(tensors, seg_label):
    return tensors[seg_label].astype(jnp.float32)


def column_sums(values):
    return jnp.sum(values.astype(jnp.float32), axis=tuple(range(values.ndim - 1)))


def layer_norm(values, gain_term, offset_term):
    center = values - jnp.mean(values, axis=-1, keepdims=True)
    spread = jnp.mean(center * center, axis=-1, keepdims=True)
    return center * lax.rsqrt(spread + EPS_NORM) * gain_term + offset_term


def gelu_exact(pre_values):
    return jax.nn.gelu(pre_values, approximate=False)


def norm_back(values, tensors, gain, shift, normed_grad, gradients):
    norm_value, norm_pull = jax.vjp(
        layer_norm,
        values,
        as_float(tensors, gain),
        as_float(tensors, shift),
    )
    values_grad, gain_grad, offset_grad = norm_pull(normed_grad)
    gradients[gain] = gain_grad
    gradients[shift] = offset_grad
    return values_grad


def score_block(queries, key_head_split, allowed):
    scores = product(E_BQHE_BKHE_TO_BHQK, queries, key_head_split) * 0.125
    return jnp.where(allowed, scores, NEG_LARGE)


def softmax_forward(queries, key_head_split, allowed):
    scores = score_block(queries, key_head_split, allowed)
    highest = jnp.max(scores, axis=-1, keepdims=True)
    exponent = jnp.exp(scores - highest)
    row_total = jnp.sum(exponent, axis=-1, keepdims=True)
    return (exponent / row_total, highest + jnp.log(row_total))


def attention_backward_pass(queries, key_head_split, values, allowed, log_total, mixed_grad):
    probabilities = jnp.where(
        allowed, jnp.exp(score_block(queries, key_head_split, allowed) - log_total), 0.0
    )
    probs_grad = product(E_BQHE_BKHE_TO_BHQK, mixed_grad, values)
    values_grad = product(E_BHQK_BQHE_TO_BKHE, probabilities.astype(jnp.bfloat16), mixed_grad)
    inner_sum = jnp.sum(probabilities * probs_grad, axis=-1, keepdims=True)
    score_grad = (probabilities * (probs_grad - inner_sum)).astype(jnp.bfloat16)
    queries_grad = product(E_BHQK_BKHE_TO_BQHE, score_grad, key_head_split) * 0.125
    keys_grad = product(E_BHQK_BQHE_TO_BKHE, score_grad, queries) * 0.125
    return (queries_grad, keys_grad, values_grad)


def adam_step(
    gradients,
    member,
    decay_flags,
    old_weights,
    first_moment,
    second_moment,
    square_sums,
    seg_entries,
):
    grad_norm = jnp.sqrt(jnp.sum(square_sums))
    tensor_rms = jnp.sqrt(square_sums / jnp.asarray(seg_entries, dtype=square_sums.dtype))
    clip_scale = jnp.minimum(1.0, CLIP_NORM / (grad_norm + 1e-06))
    clipped = gradients * clip_scale
    new_first = BETA_ONE * first_moment + (1.0 - BETA_ONE) * clipped
    new_second = BETA_TWO * second_moment + (1.0 - BETA_TWO) * clipped * clipped
    first_hat = new_first / (1.0 - BETA_ONE**STEP)
    second_hat = new_second / (1.0 - BETA_TWO**STEP)
    decay_rows = jnp.any(member & decay_flags[None, :], axis=1)
    decayed = jnp.where(decay_rows[:, None], old_weights, 0.0)
    update = -LEARN_RATE * (first_hat / (jnp.sqrt(second_hat) + ADAM_EPS) + DECAY_RATE * decayed)
    return (update, new_first, new_second, grad_norm, tensor_rms)


def body(
    captions,
    tiles,
    tile_index,
    tile_valid,
    caption_len,
    weights,
    first_moment,
    second_moment,
    d_out,
):
    model_width = captions.shape[2]
    hidden_width = FF
    caption_rows = captions.shape[0]
    cap_length = captions.shape[1]
    patch_count = tiles.shape[1]
    own_tiles = tiles.shape[0]
    slot_count = tile_index.shape[1]
    group_size = lax.axis_size(FSDP)
    data_size = lax.axis_size(DP)
    total_rows = weights.shape[0] * group_size
    heads_shape = (caption_rows, cap_length, HEADS, HEAD_DIM)
    key_shape = (caption_rows, slot_count * patch_count, HEADS, HEAD_DIM)
    token_layout_form = (caption_rows, cap_length, model_width)
    tensors = unpack(lax.all_gather(weights, FSDP, axis=0, tiled=True), model_width, hidden_width)
    zero_part = jnp.zeros((model_width,), jnp.bfloat16)
    input_values = captions.astype(jnp.float32)
    normed_one = layer_norm(
        input_values, as_float(tensors, NORM_ONE_GAIN), as_float(tensors, NORM_ONE_SHIFT)
    ).astype(jnp.bfloat16)
    qkv_bias = jnp.concatenate(
        [tensors[SELF_QUERY_BIAS], zero_part, tensors[SELF_VALUE_BIAS]]
    ).astype(jnp.float32)
    packed_qkv = (product(E_BLD_DE_TO_BLE, normed_one, tensors[SELF_QKV]) + qkv_bias).astype(
        jnp.bfloat16
    )
    self_query = packed_qkv[..., :model_width].reshape(heads_shape)
    self_keys = packed_qkv[..., model_width : 2 * model_width].reshape(heads_shape)
    self_values = packed_qkv[..., 2 * model_width :].reshape(heads_shape)
    positions = jnp.arange(cap_length)
    causal = (positions[None, :] <= positions[:, None])[None, None]
    present = (positions[None, :] < caption_len[:, None])[:, None, None, :]
    self_allowed = causal & present
    self_probs, self_log = softmax_forward(self_query, self_keys, self_allowed)
    self_mixed = (
        product(E_BHQK_BKHE_TO_BQHE, self_probs.astype(jnp.bfloat16), self_values)
        .reshape(token_layout_form)
        .astype(jnp.bfloat16)
    )
    first_sum = (
        input_values
        + product(E_BLD_DE_TO_BLE, self_mixed, tensors[SELF_OUT])
        + as_float(tensors, SELF_OUT_BIAS)
    )
    normed_two = layer_norm(
        first_sum, as_float(tensors, NORM_TWO_GAIN), as_float(tensors, NORM_TWO_SHIFT)
    ).astype(jnp.bfloat16)
    cross_queries = (
        (
            product(E_BLD_DE_TO_BLE, normed_two, tensors[CROSS_QUERY])
            + as_float(tensors, CROSS_QUERY_BIAS)
        )
        .astype(jnp.bfloat16)
        .reshape(heads_shape)
    )
    kv_bias = jnp.concatenate([zero_part, tensors[CROSS_VALUE_BIAS]]).astype(jnp.float32)
    kv_weight = tensors[CROSS_KV]
    group_kv = (
        product(E_TPD_DE_TO_TPE, lax.all_gather(tiles, FSDP, axis=0, tiled=True), kv_weight)
        + kv_bias
    ).astype(jnp.bfloat16)
    chosen = jnp.stack(
        [
            jnp.stack(
                [
                    lax.dynamic_index_in_dim(group_kv, tile_index[c, s], 0, keepdims=False)
                    for s in range(slot_count)
                ]
            )
            for c in range(caption_rows)
        ]
    )
    cross_keys = chosen[..., :model_width].reshape(key_shape)
    cross_values = chosen[..., model_width:].reshape(key_shape)
    usable = jnp.repeat(tile_valid > 0, patch_count, axis=1)[:, None, None, :]
    cross_probs, cross_log = softmax_forward(cross_queries, cross_keys, usable)
    cross_mixed = (
        product(E_BHQK_BKHE_TO_BQHE, cross_probs.astype(jnp.bfloat16), cross_values)
        .reshape(token_layout_form)
        .astype(jnp.bfloat16)
    )
    second = (
        first_sum
        + product(E_BLD_DE_TO_BLE, cross_mixed, tensors[CROSS_OUT])
        + as_float(tensors, CROSS_OUT_BIAS)
    )
    normed_three = layer_norm(
        second, as_float(tensors, NORM_THREE_GAIN), as_float(tensors, NORM_THREE_SHIFT)
    ).astype(jnp.bfloat16)
    preact = product(E_BLD_DF_TO_BLF, normed_three, tensors[MLP_UP]) + as_float(
        tensors, MLP_UP_BIAS
    )
    activation = gelu_exact(preact).astype(jnp.bfloat16)
    result = (
        second
        + product(E_BLF_FD_TO_BLD, activation, tensors[MLP_DOWN])
        + as_float(tensors, MLP_DOWN_BIAS)
    ).astype(jnp.bfloat16)
    back_flat = lax.all_gather(weights, FSDP, axis=0, tiled=True)
    tensors = unpack(back_flat, model_width, hidden_width)
    gradients = {}
    out_grad = d_out.astype(jnp.float32)
    gradients[MLP_DOWN] = product(E_BLF_BLD_TO_FD, activation, d_out)
    gradients[MLP_DOWN_BIAS] = column_sums(d_out)
    activ_grad = product(E_BLD_FD_TO_BLF, d_out, tensors[MLP_DOWN])
    gelu_value, gelu_pull = jax.vjp(gelu_exact, preact)
    preact_grad = gelu_pull(activ_grad)[0].astype(jnp.bfloat16)
    gradients[MLP_UP] = product(E_BLD_BLF_TO_DF, normed_three, preact_grad)
    gradients[MLP_UP_BIAS] = column_sums(preact_grad)
    second_grad = out_grad + norm_back(
        second,
        tensors,
        NORM_THREE_GAIN,
        NORM_THREE_SHIFT,
        product(E_BLF_DF_TO_BLD, preact_grad, tensors[MLP_UP]),
        gradients,
    )
    cross_branch = second_grad.astype(jnp.bfloat16)
    gradients[CROSS_OUT] = product(E_BLD_BLE_TO_DE, cross_mixed, cross_branch)
    gradients[CROSS_OUT_BIAS] = column_sums(cross_branch)
    cmixed_grad = (
        product(E_BLE_DE_TO_BLD, cross_branch, tensors[CROSS_OUT])
        .astype(jnp.bfloat16)
        .reshape(heads_shape)
    )
    cquery_grad, ckeys_grad, cvalues_grad = attention_backward_pass(
        cross_queries, cross_keys, cross_values, usable, cross_log, cmixed_grad
    )
    cquery_low = cquery_grad.astype(jnp.bfloat16).reshape(token_layout_form)
    gradients[CROSS_QUERY] = product(E_BLD_BLE_TO_DE, normed_two, cquery_low)
    gradients[CROSS_QUERY_BIAS] = column_sums(cquery_low)
    first_grad = second_grad + norm_back(
        first_sum,
        tensors,
        NORM_TWO_GAIN,
        NORM_TWO_SHIFT,
        product(E_BLE_DE_TO_BLD, cquery_low, tensors[CROSS_QUERY]),
        gradients,
    )
    slot_layout_form = (caption_rows, slot_count, patch_count, model_width)
    slot_grad = jnp.concatenate(
        [ckeys_grad.reshape(slot_layout_form), cvalues_grad.reshape(slot_layout_form)], axis=-1
    )
    picked = (tile_index[:, :, None] == jnp.arange(group_kv.shape[0])[None, None, :]).astype(
        jnp.float32
    )
    group_grad = jnp.einsum(E_CSG_CSPE_TO_GPE, picked, slot_grad, precision=lax.Precision.HIGHEST)
    arrived = lax.all_to_all(
        group_grad.astype(jnp.bfloat16), FSDP, split_axis=0, concat_axis=0, tiled=True
    ).astype(group_grad.dtype)
    own_grad = jnp.sum(arrived.reshape((group_size, own_tiles) + arrived.shape[1:]), axis=0).astype(
        jnp.bfloat16
    )
    gradients[CROSS_KV] = product(E_TPD_TPE_TO_DE, tiles, own_grad)
    gradients[CROSS_VALUE_BIAS] = column_sums(own_grad[..., model_width:])
    tiles_grad = product(E_TPE_DE_TO_TPD, own_grad, tensors[CROSS_KV])
    self_branch = first_grad.astype(jnp.bfloat16)
    gradients[SELF_OUT] = product(E_BLD_BLE_TO_DE, self_mixed, self_branch)
    gradients[SELF_OUT_BIAS] = column_sums(self_branch)
    smixed_grad = (
        product(E_BLE_DE_TO_BLD, self_branch, tensors[SELF_OUT])
        .astype(jnp.bfloat16)
        .reshape(heads_shape)
    )
    self_query_gradient, self_key_gradient, self_value_gradient = attention_backward_pass(
        self_query, self_keys, self_values, self_allowed, self_log, smixed_grad
    )
    qkv_grad = jnp.concatenate(
        [
            self_query_gradient.reshape(token_layout_form),
            self_key_gradient.reshape(token_layout_form),
            self_value_gradient.reshape(token_layout_form),
        ],
        axis=-1,
    ).astype(jnp.bfloat16)
    gradients[SELF_QKV] = product(E_BLD_BLE_TO_DE, normed_one, qkv_grad)
    gradients[SELF_QUERY_BIAS] = column_sums(qkv_grad[..., :model_width])
    gradients[SELF_VALUE_BIAS] = column_sums(qkv_grad[..., 2 * model_width :])
    caption_grad = first_grad + norm_back(
        input_values,
        tensors,
        NORM_ONE_GAIN,
        NORM_ONE_SHIFT,
        product(E_BLE_DE_TO_BLD, qkv_grad, tensors[SELF_QKV]),
        gradients,
    )
    flat_grad = pack_rows(gradients, model_width, hidden_width, total_rows)
    shard_rows = total_rows // (data_size * group_size)
    received = lax.all_to_all(
        for_sending(flat_grad), DP, split_axis=0, concat_axis=0, tiled=True
    ).astype(flat_grad.dtype)
    data_grad = jnp.sum(received.reshape(data_size, group_size * shard_rows, 128), axis=0)
    shard_grad = lax.psum_scatter(
        data_grad.astype(jnp.bfloat16), FSDP, scatter_dimension=0, tiled=True
    ).astype(jnp.float32)
    begin_row = lax.axis_index(BOTH) * shard_rows
    seg_starts, seg_ends, decay_flags, seg_entries = segment_table(model_width, hidden_width)
    row_ids = begin_row + jnp.arange(shard_rows)
    member = (row_ids[:, None] >= seg_starts[None, :]) & (row_ids[:, None] < seg_ends[None, :])
    row_squares = jnp.sum(shard_grad * shard_grad, axis=1)
    part_sums = jnp.sum(jnp.where(member, row_squares[:, None], 0.0), axis=0)
    square_sums = lax.psum(part_sums, BOTH)
    old_weights = lax.dynamic_slice_in_dim(back_flat, begin_row, shard_rows, 0).astype(jnp.float32)
    update, new_first, new_second, grad_norm, tensor_rms = adam_step(
        shard_grad,
        member,
        decay_flags,
        old_weights,
        first_moment,
        second_moment,
        square_sums,
        seg_entries,
    )
    return (
        result,
        caption_grad,
        tiles_grad,
        shard_grad,
        update,
        new_first,
        new_second,
        grad_norm,
        tensor_rms,
    )


D = HEADS * HEAD_DIM
NZ = 4
TOK = 128
PATCH = 196
PATCH_SENT = 208
PATCH_SLOT = 256
KEYS = 2 * PATCH_SLOT
LEAD = 80
BF, F32 = jnp.bfloat16, jnp.float32
MESH = pl.DeviceIdType.MESH
SHARD, PIECES, PIECE = 2312, 5, 464
PADDED = PIECES * PIECE
WINDOW = 8 * SHARD
CARRY = 96
SEGS = 24
QKV_AT, WO_AT, UQ_AT, UKV_AT, UO_AT, WIDE = 0, 2304, 3072, 3840, 5376, 6144
W1_AT, W2_AT = 0, 3072
(V_G1, V_C1, V_BQKV, V_BO, V_G2, V_C2, V_UQ, V_BKV, V_UO, V_G3, V_C3, V_B1, V_B2, V_SUMS) = range(14)


def row_starts():
    starts, at = {}, 0
    for label, shape, _ in layout(D, FF):
        starts[label] = at
        at += int(np.prod(shape)) // 128
    return starts


def mm(a, b):
    return lax.dot_general(a, b, (((1,), (0,)), ((), ())), preferred_element_type=F32)


def mm_nt(a, b):
    return lax.dot_general(a, b, (((1,), (1,)), ((), ())), preferred_element_type=F32)


def mm_tn(a, b):
    return lax.dot_general(a, b, (((0,), (0,)), ((), ())), preferred_element_type=F32)


def al(i, m):
    return pl.multiple_of(i * m, m)


def halves(pair):
    lane = lax.broadcasted_iota(jnp.int32, pair.shape, 1)
    zero = jnp.zeros_like(pair)
    return jnp.concatenate(
        [jnp.where(lane < HEAD_DIM, pair, zero), jnp.where(lane < HEAD_DIM, zero, pair)], axis=0
    )


def joined(stacked):
    n = stacked.shape[0] // 2
    lane = lax.broadcasted_iota(jnp.int32, (n, 128), 1)
    return jnp.where(lane < HEAD_DIM, stacked[:n], stacked[n:])


def normed(v):
    center = v - jnp.mean(v, axis=-1, keepdims=True)
    r = lax.rsqrt(jnp.mean(center * center, axis=-1, keepdims=True) + EPS_NORM)
    return center * r, r


def pair_kernel(
    cap, tiles, d_out, index, valid, length, weights,
    g_out, sums_out, old_out, out, dcap, dtile,
    fw, wide, gf, pc, ps, big1, big2, kv, dkvt, tl, tlT,
    xin, h1, am, h2, q2, a2, sb, rb, dy, t1, h1T, amT, h2T, a2T,
    x1, dx, acc, vec, meta, ob, pfx, pfx_in, carry, dcap_b, dtile_b,
    from_core, from_y, from_x, from_low, from_high, total, sq,
    wsem, gsem, send, recv, core_s, core_r, y_s, y_r, x_s, x_r, up_s, up_r, down_s, down_r, free, sum_s, sum_r,
):
    role = lax.axis_index(FSDP)
    other = 1 - role
    me = lax.axis_index(DP)
    my_z, my_y, my_core = me // 4, (me // 2) % 2, me % 2

    def at_dp(z, y, core):
        return {DP: z * 4 + y * 2 + core, FSDP: role}

    core_peer = at_dp(my_z, my_y, 1 - my_core)
    y_peer = at_dp(my_z, 1 - my_y, my_core)
    x_peer = {DP: me, FSDP: other}
    up_peer = at_dp(jnp.minimum(my_z + 1, NZ - 1), my_y, my_core)
    down_peer = at_dp(jnp.maximum(my_z - 1, 0), my_y, my_core)
    row0 = row_starts()

    cuts = [0, 13856, 18480, 23088, 32320, weights.shape[0]]
    loads = []
    for i in range(5):
        n = cuts[i + 1] - cuts[i]
        loads.append(
            pltpu.make_async_copy(
                weights.at[pl.ds(cuts[i], n)], fw.at[pl.ds(LEAD + cuts[i], n)], wsem.at[i]
            )
        )
    for c in loads:
        c.start()

    def to_other(src, dst, k):
        return pltpu.make_async_remote_copy(
            src_ref=src, dst_ref=dst, send_sem=send.at[k], recv_sem=recv.at[k],
            device_id=x_peer, device_id_type=MESH,
        )

    first, later = pl.ds(0, TOK), pl.ds(TOK, TOK)
    copies = dict(
        cap=to_other(cap, xin.at[later], 0),
        tile=to_other(tl.at[pl.ds(0, PATCH_SENT)], tl.at[pl.ds(PATCH_SLOT, PATCH_SENT)], 1),
        meta=to_other(meta.at[0], meta.at[1], 2),
        dy=to_other(d_out, dy.at[first], 3),
        lead=to_other(fw.at[pl.ds(weights.shape[0], LEAD)], fw.at[pl.ds(0, LEAD)], 4),
        out=to_other(t1.at[first], ob, 7),
        pfx=to_other(pfx, pfx_in, 8),
        old=to_other(
            weights.at[pl.ds(pl.multiple_of(((2 * me + other) % 16) * SHARD - 8 * other, 16), PADDED)], old_out, 9
        ),
        dcap=to_other(dcap_b, dcap_b, 10),
        dtile=to_other(dtile_b, dtile_b, 11),
    )

    def to_other_half(c, k):
        rows = pl.ds(al(c, TOK), TOK)
        return to_other(sb.at[rows], rb.at[rows], k + c)

    def x2_copy(c):
        return to_other_half(c, 12)

    def dx2_copy(c):
        return to_other_half(c, 14)

    tl[...] = jnp.zeros_like(tl)
    tl[0:PATCH, :] = tiles[...]
    counts = []
    for g in range(2):
        named_by = jnp.int32(0)
        for s in range(index.shape[1]):
            named = jnp.where(index[0, s] == g, jnp.int32(1), jnp.int32(0))
            named_by = named_by + jnp.where(valid[0, s] > 0, named, jnp.int32(0))
        counts.append(named_by)
    rows8 = lax.broadcasted_iota(jnp.int32, (8, 128), 0)
    meta[0] = jnp.where(
        rows8 == 0, counts[0], jnp.where(rows8 == 1, counts[1], length[0])
    ).astype(F32)

    barrier = pltpu.get_barrier_semaphore()
    for peer in (core_peer, y_peer, x_peer):
        pl.semaphore_signal(barrier, inc=1, device_id=peer, device_id_type=MESH)
    for step in range(1, NZ):
        peer = at_dp((my_z + step) % NZ, my_y, my_core)
        pl.semaphore_signal(barrier, inc=1, device_id=peer, device_id_type=MESH)
    pl.semaphore_wait(barrier, 3 + NZ - 1)

    def vector(row, at, n, col=0):
        block = fw[pl.ds(at, n // 128), :].astype(F32)
        for j in range(n // 128):
            vec[row : row + 1, col + 128 * j : col + 128 * j + 128] = block[j : j + 1, :]

    def widen(at, k, col, rows=D):
        for j in range(k):
            wide[:, col + 128 * j : col + 128 * j + 128] = fw[pl.ds(at + j, rows, stride=k), :]

    def norm_forward(src, dst, g, c, at=0, n=2 * TOK):
        @pl.loop(0, n // 64)
        def _(i):
            rows = pl.ds(pl.multiple_of(at + 64 * i, 64), 64)
            v, _ = normed(src[rows, :].astype(F32))
            dst[rows, :] = (v * vec[g : g + 1, :D] + vec[c : c + 1, :D]).astype(BF)

    def norm_backward(src, dh, g, write, at=0, n=2 * TOK):
        def step(i, sums):
            rows = pl.ds(pl.multiple_of(at + 64 * i, 64), 64)
            v, r = normed(src[rows, :].astype(F32))
            d = dh[rows, :]
            dn = d * vec[g : g + 1, :D]
            dv = r * (
                dn - jnp.mean(dn, axis=-1, keepdims=True) - v * jnp.mean(dn * v, axis=-1, keepdims=True)
            )
            write(rows, dv)
            return (
                sums[0] + jnp.sum(d * v, axis=0, keepdims=True),
                sums[1] + jnp.sum(d, axis=0, keepdims=True),
            )

        return lax.fori_loop(0, n // 64, step, (jnp.zeros((1, D), F32), jnp.zeros((1, D), F32)))

    def put_vector(at, row, into=gf):
        for j in range(row.shape[1] // 128):
            into[at + j : at + j + 1, :] = row[:, 128 * j : 128 * j + 128]

    def column_total(ref, cols):
        return jnp.sum(ref[:, cols].astype(F32), axis=0, keepdims=True)

    def matrix_grad(at, k, lhs_t, rhs, transposed=False):
        @pl.loop(0, k // 2)
        def _(m):
            cols = pl.ds(al(m, 256), 256)
            res = mm_nt(lhs_t[...], rhs[cols, :]) if transposed else mm(lhs_t[...], rhs[:, cols])
            for half in range(2):
                gf[pl.ds(at + 2 * m + half, D, stride=k), :] = res[:, 128 * half : 128 * half + 128]

    def copy_to(peer, src, dst, ssem, rsem):
        return pltpu.make_async_remote_copy(
            src_ref=src, dst_ref=dst, send_sem=ssem, recv_sem=rsem, device_id=peer, device_id_type=MESH
        )

    def slot(w, s, core, y=0, x=0):
        return pl.multiple_of(((w * PIECES + s) * 8 + core * 4 + y * 2 + x) * PIECE, 16)

    class Scatter:
        def __init__(self, w, x):
            self.w, self.x = w, x

        def core(self, s):
            rows = pl.ds(slot(self.w, s, 1 - my_core), 4 * PIECE)
            return copy_to(core_peer, fw.at[rows], from_core.at[s], core_s.at[self.w, s], core_r.at[self.w, s])

        def y(self, s):
            rows = pl.ds(slot(self.w, s, my_core, 1 - my_y), 2 * PIECE)
            return copy_to(y_peer, fw.at[rows], from_y.at[self.w, s], y_s.at[self.w, s], y_r.at[self.w, s])

        def over(self, s):
            rows = pl.ds(slot(self.w, s, my_core, my_y, 1 - self.x), PIECE)
            return copy_to(x_peer, fw.at[rows], from_x.at[self.w, s], x_s.at[self.w, s], x_r.at[self.w, s])

        def held(self, s, h):
            if h == self.x:
                return fw.at[pl.ds(slot(self.w, s, my_core, my_y, self.x), PIECE)]
            return from_x.at[self.w, s]

        def up(self, s, h):
            return copy_to(
                up_peer, self.held(s, h), from_low.at[self.w, s, h], up_s.at[self.w, s, h], up_r.at[self.w, s, h]
            )

        def down(self, s, h):
            return copy_to(
                down_peer, self.held(s, h), from_high.at[self.w, s, h], down_s.at[self.w, s, h], down_r.at[self.w, s, h]
            )

        def cast(self, first_row):
            @pl.loop(0, PIECES)
            def _(s):
                for k in range(8):
                    j = (k & 2) * 2 + (k & 4) // 2 + (k & 1)
                    src = pl.ds(pl.multiple_of(first_row + j * SHARD + s * PIECE, 8), PIECE)
                    fw[pl.ds(pl.multiple_of(slot(self.w, s, 0) + k * PIECE, 16), PIECE), :] = gf[src, :].astype(BF)
                self.core(s).start()

        def add_core(self):
            @pl.loop(0, PIECES)
            def _(s):
                self.core(s).wait_recv()
                rows = pl.ds(slot(self.w, s, my_core), 4 * PIECE)
                fw[rows, :] = fw[rows, :] + from_core[s]

        def start_y(self):
            @pl.loop(0, PIECES)
            def _(s):
                self.y(s).start()

        def add_y(self, s):
            self.y(s).wait_recv()
            rows = pl.ds(slot(self.w, s, my_core, my_y), 2 * PIECE)
            fw[rows, :] = fw[rows, :] + from_y[self.w, s]
            self.over(s).start()

        def from_ends(self, s):
            self.over(s).wait_recv()
            for h in range(2):
                goal = 2 * h + self.w
                if goal > 0:
                    pl.when(my_z == 0)(self.up(s, h).start)
                if goal < NZ - 1:
                    pl.when(my_z == NZ - 1)(self.down(s, h).start)

        def relay(self, s):
            for h in range(2):
                goal = 2 * h + self.w
                mine = self.held(s, h)
                if goal > 1:

                    @pl.when((my_z > 0) & (my_z < goal))
                    def _():
                        self.up(s, h).wait_recv()
                        mine[...] = mine[...] + from_low[self.w, s, h]
                        self.up(s, h).start()

                if goal < NZ - 2:

                    @pl.when((my_z < NZ - 1) & (my_z > goal))
                    def _():
                        self.down(s, h).wait_recv()
                        mine[...] = mine[...] + from_high[self.w, s, h]
                        self.down(s, h).start()

        def collect(self, s):
            for h in range(2):
                goal = 2 * h + self.w

                @pl.when(my_z == goal)
                def _():
                    whole = self.held(s, h)[...].astype(F32)
                    if goal > 0:
                        self.up(s, h).wait_recv()
                        whole = whole + from_low[self.w, s, h].astype(F32)
                    if goal < NZ - 1:
                        self.down(s, h).wait_recv()
                        whole = whole + from_high[self.w, s, h].astype(F32)
                    total[pl.ds(pl.multiple_of(s * PIECE, 8), PIECE), :] = whole

        def sent(self):
            @pl.loop(0, PIECES)
            def _(s):
                self.core(s).wait_send()
                self.y(s).wait_send()
                self.over(s).wait_send()
                for h in range(2):
                    goal = 2 * h + self.w
                    pl.when(my_z < goal)(self.up(s, h).wait_send)
                    pl.when(my_z > goal)(self.down(s, h).wait_send)

    def rest_of_scatter(one, zero):
        zero.start_y()
        pl.loop(0, PIECES)(one.add_y)
        pl.loop(0, PIECES)(one.from_ends)

        @pl.loop(0, PIECES)
        def _(s):
            zero.add_y(s)
            one.relay(s)
            pl.when(s > 0)(lambda: zero.from_ends(s - 1))

        zero.from_ends(PIECES - 1)
        pl.loop(0, PIECES)(zero.relay)
        pl.loop(0, PIECES)(one.collect)
        pl.loop(0, PIECES)(zero.collect)
        one.sent()
        zero.sent()

    def square_sums():
        total[SHARD:, :] = jnp.zeros((total.shape[0] - SHARD, 128), F32)
        done = pltpu.make_async_copy(total.at[pl.ds(0, SHARD)], g_out, gsem)
        done.start()
        seg = lax.broadcasted_iota(jnp.int32, (SEGS, 1), 0)
        begin = jnp.full((SEGS, 1), 1 << 30, jnp.int32)
        end = begin
        for i, (a, b) in enumerate(zip(*segment_table(D, FF)[:2])):
            begin = jnp.where(seg == i, int(a), begin)
            end = jnp.where(seg == i, int(b), end)
        row = (me * 2 + role) * SHARD + lax.broadcasted_iota(jnp.int32, (SEGS, total.shape[0]), 1)
        member = jnp.where((row >= begin) & (row < end), 1.0, 0.0)
        squares = lax.dot_general(
            member, total[...] * total[...], (((1,), (0,)), ((), ())),
            precision=lax.Precision.HIGHEST, preferred_element_type=F32,
        )
        mine = jnp.broadcast_to(jnp.sum(squares, axis=1, keepdims=True), (SEGS, 128))
        for i, peer in enumerate((core_peer, y_peer, x_peer)):
            sq[2 * i] = mine
            swap = copy_to(peer, sq.at[2 * i], sq.at[2 * i + 1], sum_s.at[i], sum_r.at[i])
            swap.start()
            swap.wait()
            mine = mine + sq[2 * i + 1]
        sq[6] = mine
        sends = []
        for step in range(1, NZ):
            to = at_dp((my_z + step) % NZ, my_y, my_core)
            sends.append(copy_to(to, sq.at[6], sq.at[6 + step], sum_s.at[2 + step], sum_r.at[2 + step]))
            sends[-1].start()
        for c in sends:
            c.wait()
        whole = jnp.zeros((SEGS, 128), F32)
        for z in range(NZ):
            part = mine
            for step in range(1, NZ):
                part = jnp.where((my_z - step + NZ) % NZ == z, sq[6 + step], part)
            whole = whole + part
        sums_out[...] = whole
        done.wait()

    def attention_role():
        at = {k: LEAD + v for k, v in row0.items()}
        at0 = {k: CARRY + v for k, v in row0.items()}
        at1 = {k: CARRY - WINDOW + v for k, v in row0.items()}
        one, zero = Scatter(1, 0), Scatter(0, 0)
        xin[first, :] = cap[...]
        copies["dy"].start()
        loads[0].wait()
        vector(V_G1, at[NORM_ONE_GAIN], D)
        vector(V_C1, at[NORM_ONE_SHIFT], D)
        vec[V_BQKV : V_BQKV + 1, :] = jnp.zeros((1, FF), F32)
        vec[V_BKV : V_BKV + 1, :] = jnp.zeros((1, FF), F32)
        vector(V_BQKV, at[SELF_QUERY_BIAS], D)
        vector(V_BQKV, at[SELF_VALUE_BIAS], D, 2 * D)
        widen(at[SELF_QKV], 18, QKV_AT)
        for c in loads[1:]:
            c.wait()
        copies["lead"].start()
        vector(V_BO, at[SELF_OUT_BIAS], D)
        vector(V_G2, at[NORM_TWO_GAIN], D)
        vector(V_C2, at[NORM_TWO_SHIFT], D)
        vector(V_UQ, at[CROSS_QUERY_BIAS], D)
        vector(V_BKV, at[CROSS_VALUE_BIAS], D, D)
        vector(V_UO, at[CROSS_OUT_BIAS], D)
        widen(at[SELF_OUT], 6, WO_AT)
        widen(at[CROSS_QUERY], 6, UQ_AT)
        widen(at[CROSS_KV], 12, UKV_AT)
        widen(at[CROSS_OUT], 6, UO_AT)

        copies["cap"].wait_recv()
        norm_forward(xin, h1, V_G1, V_C1)

        @pl.loop(0, 3)
        def _(j):
            cols = pl.ds(al(j, D), D)
            big1[:, cols] = (mm(h1[...], wide[:, cols]) + vec[V_BQKV : V_BQKV + 1, cols]).astype(BF)

        copies["meta"].wait_recv()

        @pl.loop(0, 12, unroll=4)
        def _(i):
            c, p = i // 6, i % 6
            rows = pl.ds(al(c, TOK), TOK)
            qq = halves(big1[rows, pl.ds(al(p, 128), 128)]) * BF(0.125)
            k2 = big1[rows, pl.ds(al(p, 128) + D, 128)]
            v2 = big1[rows, pl.ds(al(p, 128) + 2 * D, 128)]
            s = mm_nt(qq, k2)
            row = lax.broadcasted_iota(jnp.int32, s.shape, 0) % TOK
            col = lax.broadcasted_iota(jnp.int32, s.shape, 1)
            present = col.astype(F32) < meta[c][2:3, :]
            s = jnp.where((col <= row) & present, s, NEG_LARGE)
            e = jnp.exp(s - jnp.max(s, axis=-1, keepdims=True))
            prob = (e * (1.0 / jnp.sum(e, axis=-1, keepdims=True))).astype(BF)
            ps[i] = prob
            am[rows, pl.ds(al(p, 128), 128)] = joined(mm(prob, v2)).astype(BF)

        x1[...] = xin[...].astype(F32) + mm(am[...], wide[:, WO_AT : WO_AT + D]) + vec[V_BO : V_BO + 1, :D]
        norm_forward(x1, h2, V_G2, V_C2)
        q2[...] = (mm(h2[...], wide[:, UQ_AT : UQ_AT + D]) + vec[V_UQ : V_UQ + 1, :D]).astype(BF)
        copies["tile"].wait_recv()

        @pl.loop(0, 2)
        def _(j):
            cols = pl.ds(al(j, D), D)
            kv[:, cols] = (
                mm(tl[...], wide[:, pl.ds(al(j, D) + UKV_AT, D)]) + vec[V_BKV : V_BKV + 1, cols]
            ).astype(BF)

        @pl.loop(0, 2)
        def _(c):
            rows = pl.ds(al(c, TOK), TOK)
            col = lax.broadcasted_iota(jnp.int32, (1, KEYS), 1)
            m = meta[c]
            c0 = jnp.concatenate([m[0:1, :]] * (KEYS // 128), axis=1)
            c1 = jnp.concatenate([m[1:2, :]] * (KEYS // 128), axis=1)
            count = jnp.where(col < PATCH, c0, jnp.where(col < PATCH_SLOT, 0.0, c1))
            count = jnp.where(col < PATCH_SLOT + PATCH, count, 0.0)

            @pl.loop(0, 6, unroll=3)
            def _(p):
                qq = halves(q2[rows, pl.ds(al(p, 128), 128)]) * BF(0.125)
                s = mm_nt(qq, kv[:, pl.ds(al(p, 128), 128)])
                s = jnp.where(count > 0.0, s, NEG_LARGE)
                e = jnp.exp(s - jnp.max(s, axis=-1, keepdims=True)) * count
                prob = (e * (1.0 / jnp.sum(e, axis=-1, keepdims=True))).astype(BF)
                pc[pl.ds(al(6 * c + p, 2 * TOK), 2 * TOK), :] = prob
                a2[rows, pl.ds(al(p, 128), 128)] = joined(
                    mm(prob, kv[:, pl.ds(al(p, 128) + D, 128)])
                ).astype(BF)

            sb[rows, :] = (
                x1[rows, :] + mm(a2[rows, :], wide[:, UO_AT : UO_AT + D]) + vec[V_UO : V_UO + 1, :D]
            ).astype(BF)
            x2_copy(c).start()

        copies["old"].start()

        h1T[...] = h1[...].T
        amT[...] = am[...].T
        h2T[...] = h2[...].T
        a2T[...] = a2[...].T
        tlT[...] = tl[...].T

        part_at = at1[CROSS_KV]

        def attend_back(c, p, take_keys):
            rows = pl.ds(c * TOK, TOK)
            lanes, vlanes = pl.ds(al(p, 128), 128), pl.ds(al(p, 128) + D, 128)
            qq = halves(q2[rows, lanes]) * BF(0.125)
            do = halves(t1[rows, lanes])
            prob = pc[pl.ds(al(6 * c + p, 2 * TOK), 2 * TOK), :]
            pf = prob.astype(F32)
            dp = mm_nt(do, kv[:, vlanes])
            ds = (pf * (dp - jnp.sum(pf * dp, axis=-1, keepdims=True))).astype(BF)
            am[rows, lanes] = (joined(mm(ds, kv[:, lanes])) * 0.125).astype(BF)
            take_keys(p, 0, lanes, mm_tn(qq, ds))
            take_keys(p, 1, vlanes, mm_tn(do, prob))

        def part_rows(p, k, j):
            return pl.ds(pl.multiple_of(part_at + ((2 * p + k) * 4 + j) * 128, 8), 128)

        def keep(p, k, lanes, term):
            for j in range(4):
                gf[part_rows(p, k, j), :] = term[:, 128 * j : 128 * j + 128]

        def complete(p, k, lanes, term):
            for j in range(4):
                cols = slice(128 * j, 128 * j + 128)
                dkvt[lanes, cols] = (gf[part_rows(p, k, j), :] + term[:, cols]).astype(BF)

        for c, take_keys in enumerate((keep, complete)):
            rows = pl.ds(c * TOK, TOK)
            dx2_copy(c).wait_recv()
            t1[rows, :] = mm_nt(rb[rows, :], wide[:, UO_AT : UO_AT + D]).astype(BF)
            pl.loop(0, 6, unroll=3)(functools.partial(attend_back, c, take_keys=take_keys))

        put_vector(at1[CROSS_OUT_BIAS], column_total(rb, slice(None)))
        matrix_grad(at1[CROSS_OUT], 6, a2T, rb)
        put_vector(at1[CROSS_QUERY_BIAS], column_total(am, slice(None)))
        matrix_grad(at1[CROSS_QUERY], 6, h2T, am)
        acc[...] = mm_nt(am[...], wide[:, UQ_AT : UQ_AT + D])

        def write_dx1(rows, dv):
            full = rb[rows, :].astype(F32) + dv
            dx[rows, :] = full
            sb_[rows, :] = full.astype(BF)

        sb_ = h2
        gg, gc = norm_backward(x1, acc, V_G2, write_dx1)
        put_vector(at1[NORM_TWO_GAIN], gg)
        put_vector(at1[NORM_TWO_SHIFT], gc)
        matrix_grad(at1[CROSS_KV], 12, tlT, dkvt, transposed=True)
        kv[...] = dkvt[...].T
        put_vector(at1[CROSS_VALUE_BIAS], column_total(kv, slice(D, 2 * D)))

        def tile_grad(rows):
            keys = mm_nt(kv[rows, 0:D], wide[:, UKV_AT : UKV_AT + D])
            return keys + mm_nt(kv[rows, D : 2 * D], wide[:, UKV_AT + D : UKV_AT + 2 * D])

        dtile[...] = tile_grad(pl.ds(0, PATCH_SENT))[:PATCH]
        dtile_b[...] = tile_grad(pl.ds(PATCH_SLOT, PATCH_SENT)).astype(BF)
        copies["dtile"].start()
        copies["pfx"].wait_recv()
        gf[pl.ds(at1[NORM_THREE_GAIN], LEAD - 12), :] = pfx_in[12:, :]
        copies["lead"].wait_send()
        one.cast(CARRY)
        carry[...] = gf[0:CARRY, :]
        put_vector(at0[SELF_OUT_BIAS], column_total(sb_, slice(None)))
        matrix_grad(at0[SELF_OUT], 6, amT, sb_)
        t1[...] = mm_nt(sb_[...], wide[:, WO_AT : WO_AT + D]).astype(BF)

        one.add_core()
        one.start_y()
        pl.semaphore_signal(free, inc=1, device_id=core_peer, device_id_type=MESH)

        @pl.loop(0, 12, unroll=4)
        def _(i):
            c, p = i // 6, i % 6
            rows = pl.ds(al(c, TOK), TOK)
            lanes = pl.ds(al(p, 128), 128)
            klanes, vlanes = pl.ds(al(p, 128) + D, 128), pl.ds(al(p, 128) + 2 * D, 128)
            qq = halves(big1[rows, lanes]) * BF(0.125)
            do = halves(t1[rows, lanes])
            prob = ps[i]
            pf = prob.astype(F32)
            dp = mm_nt(do, big1[rows, vlanes])
            ds = (pf * (dp - jnp.sum(pf * dp, axis=-1, keepdims=True))).astype(BF)
            big2[rows, lanes] = (joined(mm(ds, big1[rows, klanes])) * 0.125).astype(BF)
            big2[rows, klanes] = mm_tn(ds, qq).astype(BF)
            big2[rows, vlanes] = mm_tn(prob, do).astype(BF)

        for j in range(3):
            part = mm_nt(big2[:, D * j : D * j + D], wide[:, D * j : D * j + D])
            acc[...] = part if j == 0 else acc[...] + part

        def write_dx0(rows, dv):
            dx[rows, :] = dx[rows, :] + dv

        gg, gc = norm_backward(xin, acc, V_G1, write_dx0)
        put_vector(at0[NORM_ONE_GAIN], gg)
        put_vector(at0[NORM_ONE_SHIFT], gc)
        dcap[...] = dx[first, :]
        dcap_b[...] = dx[later, :].astype(BF)
        copies["dcap"].start()
        put_vector(at0[SELF_QUERY_BIAS], column_total(big2, slice(0, D)))
        put_vector(at0[SELF_VALUE_BIAS], column_total(big2, slice(2 * D, 3 * D)))
        matrix_grad(at0[SELF_QKV], 18, h1T, big2)
        gf[pl.ds(at0[NORM_TWO_GAIN], WINDOW - row0[NORM_TWO_GAIN]), :] = carry[
            row0[NORM_TWO_GAIN] - WINDOW + CARRY :, :
        ]
        pl.semaphore_wait(free, 1)
        zero.cast(CARRY)
        zero.add_core()
        rest_of_scatter(one, zero)
        copies["out"].wait_recv()
        out[...] = ob[...]
        for name in ("dy", "dcap", "dtile"):
            copies[name].wait_send()
        for c in range(2):
            x2_copy(c).wait_send()
        copies["old"].wait()
        square_sums()

    def mlp_role():
        copies["cap"].start()
        copies["tile"].start()
        copies["meta"].start()
        base = LEAD - weights.shape[0]
        at = {k: base + v for k, v in row0.items()}
        at0 = {k: CARRY - weights.shape[0] + v for k, v in row0.items()}
        at1 = {k: v - WINDOW for k, v in at0.items()}
        one, zero = Scatter(1, 1), Scatter(0, 1)
        dy[later, :] = d_out[...]
        for c in loads:
            c.wait()
        for b in range(4):
            widen(at[MLP_DOWN] + 6 * D * b, 6, W2_AT + D * b)
        copies["lead"].wait_recv()
        widen(at[MLP_UP], 24, W1_AT)
        vector(V_G3, at[NORM_THREE_GAIN], D)
        vector(V_C3, at[NORM_THREE_SHIFT], D)
        vector(V_B1, at[MLP_UP_BIAS], FF)
        vector(V_B2, at[MLP_DOWN_BIAS], D)
        copies["dy"].wait_recv()

        @pl.loop(0, 4)
        def _(b):
            dg = mm_nt(dy[...], wide[:, pl.ds(al(b, D) + W2_AT, D)])
            for j in range(6):
                gf[pl.ds(al(6 * b + j, 256), 256), :] = dg[:, 128 * j : 128 * j + 128]

        def write_dx2(rows, dv):
            sb[rows, :] = (dy[rows, :].astype(F32) + dv).astype(BF)

        vec[V_SUMS : V_SUMS + 2, :] = jnp.zeros((2, FF), F32)

        @pl.loop(0, 2)
        def _(c):
            cap_rows = pl.ds(al(c, TOK), TOK)
            x2_copy(c).wait_recv()
            norm_forward(rb, h1, V_G3, V_C3, c * TOK, TOK)
            acc[cap_rows, :] = jnp.zeros((TOK, D), F32)

            @pl.loop(0, 4)
            def _(b):
                cols = pl.ds(al(b, D), D)
                x1[0:TOK, :] = mm(h1[cap_rows, :], wide[:, cols]) + vec[V_B1 : V_B1 + 1, cols]

                @pl.loop(0, 4)
                def _(i):
                    rows = pl.ds(al(c, TOK) + al(i, 32), 32)
                    for j in range(6):
                        z = x1[pl.ds(al(i, 32), 32), 128 * j : 128 * j + 128]
                        phi = 0.5 + 0.5 * lax.erf(z * np.float32(np.sqrt(0.5)))
                        dens = jnp.exp(-0.5 * z * z) * np.float32(1.0 / np.sqrt(2.0 * np.pi))
                        lanes = pl.ds(al(b, D) + 128 * j, 128)
                        big1[rows, lanes] = (z * phi).astype(BF)
                        dg = gf[pl.ds(al(6 * b + j, 256) + al(c, TOK) + al(i, 32), 32), :]
                        big2[rows, lanes] = (dg * (phi + z * dens)).astype(BF)

                acc[cap_rows, :] = acc[cap_rows, :] + mm_nt(big2[cap_rows, cols], wide[:, cols])

            gg, gc = norm_backward(rb, acc, V_G3, write_dx2, c * TOK, TOK)
            vec[V_SUMS : V_SUMS + 1, :D] = vec[V_SUMS : V_SUMS + 1, :D] + gg
            vec[V_SUMS + 1 : V_SUMS + 2, :D] = vec[V_SUMS + 1 : V_SUMS + 2, :D] + gc
            dx2_copy(c).start()

        put_vector(12, vec[V_SUMS : V_SUMS + 1, :D], pfx)
        put_vector(18, vec[V_SUMS + 1 : V_SUMS + 2, :D], pfx)

        h1T[...] = h1[...].T
        pfx[0:12, :] = jnp.zeros((12, 128), F32)
        for b in range(4):
            head = mm(h1T[0:8, :], big2[:, D * b : D * b + D])
            for r in range(3):
                for j in range(6):
                    row = 24 + 24 * r + 6 * b + j
                    if row < LEAD:
                        pfx[row : row + 1, :] = head[r : r + 1, 128 * j : 128 * j + 128]
        copies["pfx"].start()
        copies["old"].start()

        acc[...] = rb[...].astype(F32) + vec[V_B2 : V_B2 + 1, :D]

        @pl.loop(0, 4)
        def _(b):
            cols = pl.ds(al(b, D), D)
            acc[...] = acc[...] + mm(big1[:, cols], wide[:, pl.ds(al(b, D) + W2_AT, D)])
            pc[pl.ds(al(b, D), D), 0:256] = big1[:, cols].T

        t1[first, :] = acc[first, :].astype(BF)
        copies["out"].start()
        out[...] = acc[later, :].astype(BF)
        gf[pl.ds(at1[MLP_DOWN_BIAS] + 6, WINDOW + CARRY - at1[MLP_DOWN_BIAS] - 6), :] = jnp.zeros(
            (WINDOW + CARRY - at1[MLP_DOWN_BIAS] - 6, 128), F32
        )
        put_vector(at1[MLP_DOWN_BIAS], column_total(dy, slice(None)))
        for b in range(4):
            matrix_grad(at1[MLP_DOWN] + 6 * D * b, 6, pc.at[pl.ds(D * b, D), pl.ds(0, 256)], dy)
        one.cast(CARRY)
        carry[...] = gf[0:CARRY, :]
        put_vector(at0[MLP_UP_BIAS], column_total(big2, slice(None)))
        matrix_grad(at0[MLP_UP], 24, h1T, big2)
        one.add_core()
        one.start_y()
        pl.semaphore_signal(free, inc=1, device_id=core_peer, device_id_type=MESH)
        gf[pl.ds(at0[MLP_DOWN], CARRY), :] = carry[...]
        pl.semaphore_wait(free, 1)
        zero.cast(CARRY)
        zero.add_core()
        rest_of_scatter(one, zero)
        copies["dtile"].wait_recv()
        dtile[...] = dtile_b[0:PATCH, :].astype(F32)
        copies["dcap"].wait_recv()
        dcap[...] = dcap_b[...].astype(F32)
        for name in ("cap", "tile", "meta", "pfx", "out"):
            copies[name].wait_send()
        for c in range(2):
            dx2_copy(c).wait_send()
        copies["old"].wait()
        square_sums()

    pl.when(role == 0)(attention_role)
    pl.when(role == 1)(mlp_role)


def pair_call(cap, tiles, d_out, index, valid, length, weights):
    vm = pl.BlockSpec(memory_space=pltpu.VMEM)
    sm = pl.BlockSpec(memory_space=pltpu.SMEM)
    hbm = pl.BlockSpec(memory_space=pl.ANY)
    S = jax.ShapeDtypeStruct
    dma, both = pltpu.SemaphoreType.DMA, 2 * TOK

    def bf(*s):
        return pltpu.VMEM(s, BF)

    def fl(*s):
        return pltpu.VMEM(s, F32)

    return pl.pallas_call(
        pair_kernel,
        in_specs=[vm, vm, vm, sm, sm, sm, hbm],
        out_specs=[hbm, vm, hbm, vm, vm, vm],
        out_shape=[
            S((SHARD, 128), F32),
            S((SEGS, 128), F32),
            S((PADDED, 128), BF),
            S((TOK, D), BF),
            S((TOK, D), F32),
            S((PATCH, D), F32),
        ],
        scratch_shapes=[
            bf(16 * PADDED, 128), bf(D, WIDE), fl(CARRY + WINDOW + 8, 128), bf(12 * both, KEYS),
            bf(12, both, 128), bf(both, FF), bf(both, FF), bf(KEYS, 2 * D), bf(2 * D, KEYS), bf(KEYS, D), bf(D, KEYS),
            *[bf(both, D) for _ in range(10)],
            *[bf(D, both) for _ in range(4)],
            *[fl(both, D) for _ in range(3)],
            fl(16, FF), fl(2, 8, 128), bf(TOK, D), fl(LEAD, 128), fl(LEAD, 128), fl(CARRY, 128),
            bf(TOK, D), bf(PATCH_SENT, D),
            bf(PIECES, 4 * PIECE, 128), bf(2, PIECES, 2 * PIECE, 128), bf(2, PIECES, PIECE, 128),
            bf(2, PIECES, 2, PIECE, 128), bf(2, PIECES, 2, PIECE, 128), fl(2432, 128), fl(10, SEGS, 128),
            dma((5,)), dma, dma((16,)), dma((16,)),
            *[dma((2, PIECES)) for _ in range(6)],
            *[dma((2, PIECES, 2)) for _ in range(4)],
            pltpu.SemaphoreType.REGULAR, dma((6,)), dma((6,)),
        ],
        compiler_params=pltpu.CompilerParams(
            collective_id=0, has_side_effects=True, vmem_limit_bytes=63 * 2**20
        ),
    )(cap, tiles, d_out, index, valid, length, weights)


def finish(shard_grad, old_weights, first_moment, second_moment, square_sums):
    shard_rows = shard_grad.shape[0]
    begin_row = lax.axis_index(BOTH) * shard_rows
    seg_starts, seg_ends, decay_flags, seg_entries = segment_table(D, FF)
    row_ids = begin_row + jnp.arange(shard_rows)
    member = (row_ids[:, None] >= seg_starts[None, :]) & (row_ids[:, None] < seg_ends[None, :])
    return adam_step(
        shard_grad, member, decay_flags, old_weights, first_moment, second_moment, square_sums, seg_entries
    )


def pair_body(
    captions, tiles, tile_index, tile_valid, caption_len, weights, first_moment, second_moment, d_out
):
    me, f = lax.axis_index(DP), lax.axis_index(FSDP)
    shard_grad, sums, old, out, caption_grad, tiles_grad = pair_call(
        captions[0], tiles[0], d_out[0], tile_index, tile_valid, caption_len, weights
    )
    own = lax.dynamic_slice_in_dim(weights, ((2 * me + f) % 16) * SHARD, SHARD, 0)
    old = lax.dynamic_slice_in_dim(old, 8 * f, SHARD, 0)
    old_weights = jnp.where(me // 8 == f, own, old).astype(jnp.float32)
    update, new_first, new_second, grad_norm, tensor_rms = finish(
        shard_grad, old_weights, first_moment, second_moment, sums[:21, 0]
    )
    return (
        out[None], caption_grad[None], tiles_grad[None], shard_grad, update, new_first, new_second,
        grad_norm, tensor_rms,
    )


def solution(mesh):
    placed = (
        P(BOTH, None, None),
        P(BOTH, None, None),
        P(BOTH, None),
        P(BOTH, None),
        P(BOTH),
        P(FSDP, None),
        P(BOTH, None),
        P(BOTH, None),
        P(BOTH, None, None),
    )
    return jax.shard_map(
        pair_body if mesh.shape[FSDP] == 2 else body,
        mesh=mesh,
        in_specs=placed,
        out_specs=(
            P(BOTH, None, None),
            P(BOTH, None, None),
            P(BOTH, None, None),
            P(BOTH, None),
            P(BOTH, None),
            P(BOTH, None),
            P(BOTH, None),
            P(),
            P(),
        ),
        check_vma=False,
    )
```

```python
import functools

import jax
import jax.numpy as jnp
import numpy as np
from jax import lax
from jax.experimental import pallas as pl
from jax.experimental.pallas import tpu as pltpu
from jax.sharding import PartitionSpec as P

HEADS = 12
HEAD_DIM = 64
FF = 3072
STEP = 10


EPS_NORM = 1e-05
CLIP_NORM = 1.0
BETA_ONE = 0.9
BETA_TWO = 0.999
LEARN_RATE = 0.01
DECAY_RATE = 0.1
ADAM_EPS = 1e-08
NEG_LARGE = -1e30
(NORM_ONE_GAIN, NORM_ONE_SHIFT, SELF_QKV, SELF_QUERY_BIAS, SELF_VALUE_BIAS, SELF_OUT, SELF_OUT_BIAS, NORM_TWO_GAIN, NORM_TWO_SHIFT, CROSS_QUERY, CROSS_QUERY_BIAS, CROSS_KV, CROSS_VALUE_BIAS, CROSS_OUT, CROSS_OUT_BIAS, NORM_THREE_GAIN, NORM_THREE_SHIFT, MLP_UP, MLP_UP_BIAS, MLP_DOWN, MLP_DOWN_BIAS) = range(21)
DP, FSDP = "dp", "fsdp"
BOTH = (DP, FSDP)
E_BHQK_BKHE_TO_BQHE = "bhqk,bkhe->bqhe"
E_BHQK_BQHE_TO_BKHE = "bhqk,bqhe->bkhe"
E_BLD_BLE_TO_DE = "bld,ble->de"
E_BLD_BLF_TO_DF = "bld,blf->df"
E_BLD_DE_TO_BLE = "bld,de->ble"
E_BLD_DF_TO_BLF = "bld,df->blf"
E_BLD_FD_TO_BLF = "bld,fd->blf"
E_BLE_DE_TO_BLD = "ble,de->bld"
E_BLF_BLD_TO_FD = "blf,bld->fd"
E_BLF_DF_TO_BLD = "blf,df->bld"
E_BLF_FD_TO_BLD = "blf,fd->bld"
E_BQHE_BKHE_TO_BHQK = "bqhe,bkhe->bhqk"
E_CSG_CSPE_TO_GPE = "csg,cspe->gpe"
E_TPD_DE_TO_TPE = "tpd,de->tpe"
E_TPD_TPE_TO_DE = "tpd,tpe->de"
E_TPE_DE_TO_TPD = "tpe,de->tpd"


def for_sending(x):
    return jax.tree.map(lambda a: a.astype(jnp.bfloat16) if a.dtype == jnp.float32 else a, x)


def layout(model_width, hidden_width):
    return [
        (NORM_ONE_GAIN, (model_width,), 0),
        (NORM_ONE_SHIFT, (model_width,), 0),
        (SELF_QKV, (model_width, 3 * model_width), 1),
        (SELF_QUERY_BIAS, (model_width,), 0),
        (SELF_VALUE_BIAS, (model_width,), 0),
        (SELF_OUT, (model_width, model_width), 1),
        (SELF_OUT_BIAS, (model_width,), 0),
        (NORM_TWO_GAIN, (model_width,), 0),
        (NORM_TWO_SHIFT, (model_width,), 0),
        (CROSS_QUERY, (model_width, model_width), 1),
        (CROSS_QUERY_BIAS, (model_width,), 0),
        (CROSS_KV, (model_width, 2 * model_width), 1),
        (CROSS_VALUE_BIAS, (model_width,), 0),
        (CROSS_OUT, (model_width, model_width), 1),
        (CROSS_OUT_BIAS, (model_width,), 0),
        (NORM_THREE_GAIN, (model_width,), 0),
        (NORM_THREE_SHIFT, (model_width,), 0),
        (MLP_UP, (model_width, hidden_width), 1),
        (MLP_UP_BIAS, (hidden_width,), 0),
        (MLP_DOWN, (hidden_width, model_width), 1),
        (MLP_DOWN_BIAS, (model_width,), 0),
    ]


def segment_table(model_width, hidden_width):
    seg_starts = []
    seg_ends = []
    decay_flags = []
    seg_entries = []
    row_at = 0
    for seg_label, seg_shape, seg_flag in layout(model_width, hidden_width):
        item_count = int(np.prod(seg_shape))
        seg_rows = item_count // 128
        seg_starts.append(row_at)
        seg_ends.append(row_at + seg_rows)
        decay_flags.append(seg_flag == 1)
        seg_entries.append(float(item_count))
        row_at = row_at + seg_rows
    return (np.array(seg_starts), np.array(seg_ends), np.array(decay_flags), np.array(seg_entries))


def unpack(flat_rows, model_width, hidden_width):
    vector = flat_rows.reshape(-1)
    tensors = {}
    offset = 0
    for seg_label, seg_shape, seg_flag in layout(model_width, hidden_width):
        item_count = int(np.prod(seg_shape))
        tensors[seg_label] = vector[offset : offset + item_count].reshape(seg_shape)
        offset = offset + item_count
    return tensors


def pack_rows(gradients, model_width, hidden_width, total_rows):
    pieces = [
        gradients[seg_label].reshape(-1, 128)
        for seg_label, seg_shape, seg_flag in layout(model_width, hidden_width)
    ]
    used_rows = sum((tensor_piece.shape[0] for tensor_piece in pieces))
    pieces.append(jnp.zeros((total_rows - used_rows, 128), jnp.float32))
    return jnp.concatenate(pieces, axis=0)


def product(pattern, left_side, right_side):
    return jnp.einsum(pattern, left_side, right_side, preferred_element_type=jnp.float32)


def as_float(tensors, seg_label):
    return tensors[seg_label].astype(jnp.float32)


def column_sums(values):
    return jnp.sum(values.astype(jnp.float32), axis=tuple(range(values.ndim - 1)))


def layer_norm(values, gain_term, offset_term):
    center = values - jnp.mean(values, axis=-1, keepdims=True)
    spread = jnp.mean(center * center, axis=-1, keepdims=True)
    return center * lax.rsqrt(spread + EPS_NORM) * gain_term + offset_term


def gelu_exact(pre_values):
    return jax.nn.gelu(pre_values, approximate=False)


def norm_back(values, tensors, gain, shift, normed_grad, gradients):
    norm_value, norm_pull = jax.vjp(
        layer_norm,
        values,
        as_float(tensors, gain),
        as_float(tensors, shift),
    )
    values_grad, gain_grad, offset_grad = norm_pull(normed_grad)
    gradients[gain] = gain_grad
    gradients[shift] = offset_grad
    return values_grad


def score_block(queries, key_head_split, allowed):
    scores = product(E_BQHE_BKHE_TO_BHQK, queries, key_head_split) * 0.125
    return jnp.where(allowed, scores, NEG_LARGE)


def softmax_forward(queries, key_head_split, allowed):
    scores = score_block(queries, key_head_split, allowed)
    highest = jnp.max(scores, axis=-1, keepdims=True)
    exponent = jnp.exp(scores - highest)
    row_total = jnp.sum(exponent, axis=-1, keepdims=True)
    return (exponent / row_total, highest + jnp.log(row_total))


def attention_backward_pass(queries, key_head_split, values, allowed, log_total, mixed_grad):
    probabilities = jnp.where(
        allowed, jnp.exp(score_block(queries, key_head_split, allowed) - log_total), 0.0
    )
    probs_grad = product(E_BQHE_BKHE_TO_BHQK, mixed_grad, values)
    values_grad = product(E_BHQK_BQHE_TO_BKHE, probabilities.astype(jnp.bfloat16), mixed_grad)
    inner_sum = jnp.sum(probabilities * probs_grad, axis=-1, keepdims=True)
    score_grad = (probabilities * (probs_grad - inner_sum)).astype(jnp.bfloat16)
    queries_grad = product(E_BHQK_BKHE_TO_BQHE, score_grad, key_head_split) * 0.125
    keys_grad = product(E_BHQK_BQHE_TO_BKHE, score_grad, queries) * 0.125
    return (queries_grad, keys_grad, values_grad)


def adam_step(
    gradients,
    member,
    decay_flags,
    old_weights,
    first_moment,
    second_moment,
    square_sums,
    seg_entries,
):
    grad_norm = jnp.sqrt(jnp.sum(square_sums))
    tensor_rms = jnp.sqrt(square_sums / jnp.asarray(seg_entries, dtype=square_sums.dtype))
    clip_scale = jnp.minimum(1.0, CLIP_NORM / (grad_norm + 1e-06))
    clipped = gradients * clip_scale
    new_first = BETA_ONE * first_moment + (1.0 - BETA_ONE) * clipped
    new_second = BETA_TWO * second_moment + (1.0 - BETA_TWO) * clipped * clipped
    first_hat = new_first / (1.0 - BETA_ONE**STEP)
    second_hat = new_second / (1.0 - BETA_TWO**STEP)
    decay_rows = jnp.any(member & decay_flags[None, :], axis=1)
    decayed = jnp.where(decay_rows[:, None], old_weights, 0.0)
    update = -LEARN_RATE * (first_hat / (jnp.sqrt(second_hat) + ADAM_EPS) + DECAY_RATE * decayed)
    return (update, new_first, new_second, grad_norm, tensor_rms)


def body(
    captions,
    tiles,
    tile_index,
    tile_valid,
    caption_len,
    weights,
    first_moment,
    second_moment,
    d_out,
):
    model_width = captions.shape[2]
    hidden_width = FF
    caption_rows = captions.shape[0]
    cap_length = captions.shape[1]
    patch_count = tiles.shape[1]
    own_tiles = tiles.shape[0]
    slot_count = tile_index.shape[1]
    group_size = lax.axis_size(FSDP)
    data_size = lax.axis_size(DP)
    total_rows = weights.shape[0] * group_size
    heads_shape = (caption_rows, cap_length, HEADS, HEAD_DIM)
    key_shape = (caption_rows, slot_count * patch_count, HEADS, HEAD_DIM)
    token_layout_form = (caption_rows, cap_length, model_width)
    tensors = unpack(lax.all_gather(weights, FSDP, axis=0, tiled=True), model_width, hidden_width)
    zero_part = jnp.zeros((model_width,), jnp.bfloat16)
    input_values = captions.astype(jnp.float32)
    normed_one = layer_norm(
        input_values, as_float(tensors, NORM_ONE_GAIN), as_float(tensors, NORM_ONE_SHIFT)
    ).astype(jnp.bfloat16)
    qkv_bias = jnp.concatenate(
        [tensors[SELF_QUERY_BIAS], zero_part, tensors[SELF_VALUE_BIAS]]
    ).astype(jnp.float32)
    packed_qkv = (product(E_BLD_DE_TO_BLE, normed_one, tensors[SELF_QKV]) + qkv_bias).astype(
        jnp.bfloat16
    )
    self_query = packed_qkv[..., :model_width].reshape(heads_shape)
    self_keys = packed_qkv[..., model_width : 2 * model_width].reshape(heads_shape)
    self_values = packed_qkv[..., 2 * model_width :].reshape(heads_shape)
    positions = jnp.arange(cap_length)
    causal = (positions[None, :] <= positions[:, None])[None, None]
    present = (positions[None, :] < caption_len[:, None])[:, None, None, :]
    self_allowed = causal & present
    self_probs, self_log = softmax_forward(self_query, self_keys, self_allowed)
    self_mixed = (
        product(E_BHQK_BKHE_TO_BQHE, self_probs.astype(jnp.bfloat16), self_values)
        .reshape(token_layout_form)
        .astype(jnp.bfloat16)
    )
    first_sum = (
        input_values
        + product(E_BLD_DE_TO_BLE, self_mixed, tensors[SELF_OUT])
        + as_float(tensors, SELF_OUT_BIAS)
    )
    normed_two = layer_norm(
        first_sum, as_float(tensors, NORM_TWO_GAIN), as_float(tensors, NORM_TWO_SHIFT)
    ).astype(jnp.bfloat16)
    cross_queries = (
        (
            product(E_BLD_DE_TO_BLE, normed_two, tensors[CROSS_QUERY])
            + as_float(tensors, CROSS_QUERY_BIAS)
        )
        .astype(jnp.bfloat16)
        .reshape(heads_shape)
    )
    kv_bias = jnp.concatenate([zero_part, tensors[CROSS_VALUE_BIAS]]).astype(jnp.float32)
    kv_weight = tensors[CROSS_KV]
    group_kv = (
        product(E_TPD_DE_TO_TPE, lax.all_gather(tiles, FSDP, axis=0, tiled=True), kv_weight)
        + kv_bias
    ).astype(jnp.bfloat16)
    chosen = jnp.stack(
        [
            jnp.stack(
                [
                    lax.dynamic_index_in_dim(group_kv, tile_index[c, s], 0, keepdims=False)
                    for s in range(slot_count)
                ]
            )
            for c in range(caption_rows)
        ]
    )
    cross_keys = chosen[..., :model_width].reshape(key_shape)
    cross_values = chosen[..., model_width:].reshape(key_shape)
    usable = jnp.repeat(tile_valid > 0, patch_count, axis=1)[:, None, None, :]
    cross_probs, cross_log = softmax_forward(cross_queries, cross_keys, usable)
    cross_mixed = (
        product(E_BHQK_BKHE_TO_BQHE, cross_probs.astype(jnp.bfloat16), cross_values)
        .reshape(token_layout_form)
        .astype(jnp.bfloat16)
    )
    second = (
        first_sum
        + product(E_BLD_DE_TO_BLE, cross_mixed, tensors[CROSS_OUT])
        + as_float(tensors, CROSS_OUT_BIAS)
    )
    normed_three = layer_norm(
        second, as_float(tensors, NORM_THREE_GAIN), as_float(tensors, NORM_THREE_SHIFT)
    ).astype(jnp.bfloat16)
    preact = product(E_BLD_DF_TO_BLF, normed_three, tensors[MLP_UP]) + as_float(
        tensors, MLP_UP_BIAS
    )
    activation = gelu_exact(preact).astype(jnp.bfloat16)
    result = (
        second
        + product(E_BLF_FD_TO_BLD, activation, tensors[MLP_DOWN])
        + as_float(tensors, MLP_DOWN_BIAS)
    ).astype(jnp.bfloat16)
    back_flat = lax.all_gather(weights, FSDP, axis=0, tiled=True)
    tensors = unpack(back_flat, model_width, hidden_width)
    gradients = {}
    out_grad = d_out.astype(jnp.float32)
    gradients[MLP_DOWN] = product(E_BLF_BLD_TO_FD, activation, d_out)
    gradients[MLP_DOWN_BIAS] = column_sums(d_out)
    activ_grad = product(E_BLD_FD_TO_BLF, d_out, tensors[MLP_DOWN])
    gelu_value, gelu_pull = jax.vjp(gelu_exact, preact)
    preact_grad = gelu_pull(activ_grad)[0].astype(jnp.bfloat16)
    gradients[MLP_UP] = product(E_BLD_BLF_TO_DF, normed_three, preact_grad)
    gradients[MLP_UP_BIAS] = column_sums(preact_grad)
    second_grad = out_grad + norm_back(
        second,
        tensors,
        NORM_THREE_GAIN,
        NORM_THREE_SHIFT,
        product(E_BLF_DF_TO_BLD, preact_grad, tensors[MLP_UP]),
        gradients,
    )
    cross_branch = second_grad.astype(jnp.bfloat16)
    gradients[CROSS_OUT] = product(E_BLD_BLE_TO_DE, cross_mixed, cross_branch)
    gradients[CROSS_OUT_BIAS] = column_sums(cross_branch)
    cmixed_grad = (
        product(E_BLE_DE_TO_BLD, cross_branch, tensors[CROSS_OUT])
        .astype(jnp.bfloat16)
        .reshape(heads_shape)
    )
    cquery_grad, ckeys_grad, cvalues_grad = attention_backward_pass(
        cross_queries, cross_keys, cross_values, usable, cross_log, cmixed_grad
    )
    cquery_low = cquery_grad.astype(jnp.bfloat16).reshape(token_layout_form)
    gradients[CROSS_QUERY] = product(E_BLD_BLE_TO_DE, normed_two, cquery_low)
    gradients[CROSS_QUERY_BIAS] = column_sums(cquery_low)
    first_grad = second_grad + norm_back(
        first_sum,
        tensors,
        NORM_TWO_GAIN,
        NORM_TWO_SHIFT,
        product(E_BLE_DE_TO_BLD, cquery_low, tensors[CROSS_QUERY]),
        gradients,
    )
    slot_layout_form = (caption_rows, slot_count, patch_count, model_width)
    slot_grad = jnp.concatenate(
        [ckeys_grad.reshape(slot_layout_form), cvalues_grad.reshape(slot_layout_form)], axis=-1
    )
    picked = (tile_index[:, :, None] == jnp.arange(group_kv.shape[0])[None, None, :]).astype(
        jnp.float32
    )
    group_grad = jnp.einsum(E_CSG_CSPE_TO_GPE, picked, slot_grad, precision=lax.Precision.HIGHEST)
    arrived = lax.all_to_all(
        group_grad.astype(jnp.bfloat16), FSDP, split_axis=0, concat_axis=0, tiled=True
    ).astype(group_grad.dtype)
    own_grad = jnp.sum(arrived.reshape((group_size, own_tiles) + arrived.shape[1:]), axis=0).astype(
        jnp.bfloat16
    )
    gradients[CROSS_KV] = product(E_TPD_TPE_TO_DE, tiles, own_grad)
    gradients[CROSS_VALUE_BIAS] = column_sums(own_grad[..., model_width:])
    tiles_grad = product(E_TPE_DE_TO_TPD, own_grad, tensors[CROSS_KV])
    self_branch = first_grad.astype(jnp.bfloat16)
    gradients[SELF_OUT] = product(E_BLD_BLE_TO_DE, self_mixed, self_branch)
    gradients[SELF_OUT_BIAS] = column_sums(self_branch)
    smixed_grad = (
        product(E_BLE_DE_TO_BLD, self_branch, tensors[SELF_OUT])
        .astype(jnp.bfloat16)
        .reshape(heads_shape)
    )
    self_query_gradient, self_key_gradient, self_value_gradient = attention_backward_pass(
        self_query, self_keys, self_values, self_allowed, self_log, smixed_grad
    )
    qkv_grad = jnp.concatenate(
        [
            self_query_gradient.reshape(token_layout_form),
            self_key_gradient.reshape(token_layout_form),
            self_value_gradient.reshape(token_layout_form),
        ],
        axis=-1,
    ).astype(jnp.bfloat16)
    gradients[SELF_QKV] = product(E_BLD_BLE_TO_DE, normed_one, qkv_grad)
    gradients[SELF_QUERY_BIAS] = column_sums(qkv_grad[..., :model_width])
    gradients[SELF_VALUE_BIAS] = column_sums(qkv_grad[..., 2 * model_width :])
    caption_grad = first_grad + norm_back(
        input_values,
        tensors,
        NORM_ONE_GAIN,
        NORM_ONE_SHIFT,
        product(E_BLE_DE_TO_BLD, qkv_grad, tensors[SELF_QKV]),
        gradients,
    )
    flat_grad = pack_rows(gradients, model_width, hidden_width, total_rows)
    shard_rows = total_rows // (data_size * group_size)
    received = lax.all_to_all(
        for_sending(flat_grad), DP, split_axis=0, concat_axis=0, tiled=True
    ).astype(flat_grad.dtype)
    data_grad = jnp.sum(received.reshape(data_size, group_size * shard_rows, 128), axis=0)
    shard_grad = lax.psum_scatter(
        data_grad.astype(jnp.bfloat16), FSDP, scatter_dimension=0, tiled=True
    ).astype(jnp.float32)
    begin_row = lax.axis_index(BOTH) * shard_rows
    seg_starts, seg_ends, decay_flags, seg_entries = segment_table(model_width, hidden_width)
    row_ids = begin_row + jnp.arange(shard_rows)
    member = (row_ids[:, None] >= seg_starts[None, :]) & (row_ids[:, None] < seg_ends[None, :])
    row_squares = jnp.sum(shard_grad * shard_grad, axis=1)
    part_sums = jnp.sum(jnp.where(member, row_squares[:, None], 0.0), axis=0)
    square_sums = lax.psum(part_sums, BOTH)
    old_weights = lax.dynamic_slice_in_dim(back_flat, begin_row, shard_rows, 0).astype(jnp.float32)
    update, new_first, new_second, grad_norm, tensor_rms = adam_step(
        shard_grad,
        member,
        decay_flags,
        old_weights,
        first_moment,
        second_moment,
        square_sums,
        seg_entries,
    )
    return (
        result,
        caption_grad,
        tiles_grad,
        shard_grad,
        update,
        new_first,
        new_second,
        grad_norm,
        tensor_rms,
    )


D = HEADS * HEAD_DIM
NZ = 4
TOK = 128
PATCH = 196
PATCH_SENT = 208
PATCH_SLOT = 256
KEYS = 2 * PATCH_SLOT
LEAD = 80
BF, F32 = jnp.bfloat16, jnp.float32
MESH = pl.DeviceIdType.MESH
SHARD, PIECES, PIECE = 2312, 5, 464
OLD = 2320
PADDED = PIECES * PIECE
WINDOW = 8 * SHARD
CARRY = 96
SEGS = 24
QKV_AT, WO_AT, UQ_AT, UKV_AT, UO_AT, WIDE = 0, 2304, 3072, 3840, 5376, 6144
W1_AT, W2_AT = 0, 3072
(V_G1, V_C1, V_BQKV, V_BO, V_G2, V_C2, V_UQ, V_BKV, V_UO, V_G3, V_C3, V_B1, V_B2, V_SUMS) = range(14)


def row_starts():
    starts, at = {}, 0
    for label, shape, _ in layout(D, FF):
        starts[label] = at
        at += int(np.prod(shape)) // 128
    return starts


def mm(a, b):
    return lax.dot_general(a, b, (((1,), (0,)), ((), ())), preferred_element_type=F32)


def mm_nt(a, b):
    return lax.dot_general(a, b, (((1,), (1,)), ((), ())), preferred_element_type=F32)


def mm_tn(a, b):
    return lax.dot_general(a, b, (((0,), (0,)), ((), ())), preferred_element_type=F32)


def al(i, m):
    return pl.multiple_of(i * m, m)


def halves(pair):
    lane = lax.broadcasted_iota(jnp.int32, pair.shape, 1)
    zero = jnp.zeros_like(pair)
    return jnp.concatenate(
        [jnp.where(lane < HEAD_DIM, pair, zero), jnp.where(lane < HEAD_DIM, zero, pair)], axis=0
    )


def joined(stacked):
    n = stacked.shape[0] // 2
    lane = lax.broadcasted_iota(jnp.int32, (n, 128), 1)
    return jnp.where(lane < HEAD_DIM, stacked[:n], stacked[n:])


def normed(v):
    center = v - jnp.mean(v, axis=-1, keepdims=True)
    r = lax.rsqrt(jnp.mean(center * center, axis=-1, keepdims=True) + EPS_NORM)
    return center * r, r


def pair_kernel(
    cap, tiles, d_out, index, valid, length, weights,
    g_out, sums_out, old_out, out, dcap, dtile,
    fw, wide, gf, pc, ps, big1, big2, kv, dkvt, tl, tlT,
    xin, h1, am, h2, q2, a2, sb, rb, dy, t1, h1T, amT, h2T, a2T,
    x1, dx, acc, vec, meta, ob, pfx, pfx_in, carry, dcap_b, dtile_b,
    from_core, from_y, from_x, from_low, from_high, total, sq,
    wsem, gsem, send, recv, core_s, core_r, y_s, y_r, x_s, x_r, up_s, up_r, down_s, down_r, free, sum_s, sum_r,
):
    role = lax.axis_index(FSDP)
    other = 1 - role
    me = lax.axis_index(DP)
    my_z, my_y, my_core = me // 4, (me // 2) % 2, me % 2

    def at_dp(z, y, core):
        return {DP: z * 4 + y * 2 + core, FSDP: role}

    core_peer = at_dp(my_z, my_y, 1 - my_core)
    y_peer = at_dp(my_z, 1 - my_y, my_core)
    x_peer = {DP: me, FSDP: other}
    up_peer = at_dp(jnp.minimum(my_z + 1, NZ - 1), my_y, my_core)
    down_peer = at_dp(jnp.maximum(my_z - 1, 0), my_y, my_core)
    barrier = pltpu.get_barrier_semaphore()
    for peer in (core_peer, y_peer, x_peer):
        pl.semaphore_signal(barrier, inc=1, device_id=peer, device_id_type=MESH)
    for step in range(1, NZ):
        peer = at_dp((my_z + step) % NZ, my_y, my_core)
        pl.semaphore_signal(barrier, inc=1, device_id=peer, device_id_type=MESH)
    row0 = row_starts()

    cuts = [0, 13856, 18480, 23088, 32320, weights.shape[0]]
    loads = []
    for i in range(5):
        n = cuts[i + 1] - cuts[i]
        loads.append(
            pltpu.make_async_copy(
                weights.at[pl.ds(cuts[i], n)], fw.at[pl.ds(LEAD + cuts[i], n)], wsem.at[i]
            )
        )
    for c in loads:
        c.start()

    def to_other(src, dst, k):
        return pltpu.make_async_remote_copy(
            src_ref=src, dst_ref=dst, send_sem=send.at[k], recv_sem=recv.at[k],
            device_id=x_peer, device_id_type=MESH,
        )

    first, later = pl.ds(0, TOK), pl.ds(TOK, TOK)
    copies = dict(
        cap=to_other(cap, xin.at[later], 0),
        tile=to_other(tl.at[pl.ds(0, PATCH_SENT)], tl.at[pl.ds(PATCH_SLOT, PATCH_SENT)], 1),
        meta=to_other(meta.at[0], meta.at[1], 2),
        dy=to_other(d_out, dy.at[first], 3),
        lead=to_other(fw.at[pl.ds(weights.shape[0], LEAD)], fw.at[pl.ds(0, LEAD)], 4),
        out=to_other(t1.at[first], ob, 7),
        pfx=to_other(pfx, pfx_in, 8),
        old=to_other(
            weights.at[pl.ds(pl.multiple_of(((2 * me + other) % 16) * SHARD - 8 * other, 16), OLD)], old_out, 9
        ),
        dcap=to_other(dcap_b, dcap_b, 10),
        dtile=to_other(dtile_b, dtile_b, 11),
    )

    def to_other_half(c, k):
        rows = pl.ds(al(c, TOK), TOK)
        return to_other(sb.at[rows], rb.at[rows], k + c)

    def x2_copy(c):
        return to_other_half(c, 12)

    def dx2_copy(c):
        return to_other_half(c, 14)

    after = PATCH_SLOT + PATCH_SENT
    tl[0:PATCH_SLOT, :] = jnp.zeros((PATCH_SLOT, D), BF)
    tl[after:, :] = jnp.zeros((KEYS - after, D), BF)
    tl[0:PATCH, :] = tiles[...]
    counts = []
    for g in range(2):
        named_by = jnp.int32(0)
        for s in range(index.shape[1]):
            named = jnp.where(index[0, s] == g, jnp.int32(1), jnp.int32(0))
            named_by = named_by + jnp.where(valid[0, s] > 0, named, jnp.int32(0))
        counts.append(named_by)
    rows8 = lax.broadcasted_iota(jnp.int32, (8, 128), 0)
    meta[0] = jnp.where(
        rows8 == 0, counts[0], jnp.where(rows8 == 1, counts[1], length[0])
    ).astype(F32)

    def all_here():
        pl.semaphore_wait(barrier, 3 + NZ - 1)

    def vector(row, at, n, col=0):
        block = fw[pl.ds(at, n // 128), :].astype(F32)
        for j in range(n // 128):
            vec[row : row + 1, col + 128 * j : col + 128 * j + 128] = block[j : j + 1, :]

    def widen(at, k, col, rows=D):
        for j in range(k):
            wide[:, col + 128 * j : col + 128 * j + 128] = fw[pl.ds(at + j, rows, stride=k), :]

    def norm_forward(src, dst, g, c, at=0, n=2 * TOK):
        @pl.loop(0, n // 64)
        def _(i):
            rows = pl.ds(pl.multiple_of(at + 64 * i, 64), 64)
            v, _ = normed(src[rows, :].astype(F32))
            dst[rows, :] = (v * vec[g : g + 1, :D] + vec[c : c + 1, :D]).astype(BF)

    def norm_backward(src, dh, g, write, at=0, n=2 * TOK):
        def step(i, sums):
            rows = pl.ds(pl.multiple_of(at + 64 * i, 64), 64)
            v, r = normed(src[rows, :].astype(F32))
            d = dh[rows, :]
            dn = d * vec[g : g + 1, :D]
            dv = r * (
                dn - jnp.mean(dn, axis=-1, keepdims=True) - v * jnp.mean(dn * v, axis=-1, keepdims=True)
            )
            write(rows, dv)
            return (
                sums[0] + jnp.sum(d * v, axis=0, keepdims=True),
                sums[1] + jnp.sum(d, axis=0, keepdims=True),
            )

        return lax.fori_loop(0, n // 64, step, (jnp.zeros((1, D), F32), jnp.zeros((1, D), F32)))

    def put_vector(at, row, into=gf):
        for j in range(row.shape[1] // 128):
            into[at + j : at + j + 1, :] = row[:, 128 * j : 128 * j + 128]

    def column_total(ref, cols):
        return jnp.sum(ref[:, cols].astype(F32), axis=0, keepdims=True)

    def matrix_grad(at, k, lhs_t, rhs, transposed=False):
        @pl.loop(0, k // 2, unroll=3)
        def _(m):
            cols = pl.ds(al(m, 256), 256)
            res = mm_nt(lhs_t[...], rhs[cols, :]) if transposed else mm(lhs_t[...], rhs[:, cols])
            for half in range(2):
                gf[pl.ds(at + 2 * m + half, D, stride=k), :] = res[:, 128 * half : 128 * half + 128]

    def copy_to(peer, src, dst, ssem, rsem):
        return pltpu.make_async_remote_copy(
            src_ref=src, dst_ref=dst, send_sem=ssem, recv_sem=rsem, device_id=peer, device_id_type=MESH
        )

    def slot(w, s, core, y=0, x=0):
        return pl.multiple_of(((w * PIECES + s) * 8 + core * 4 + y * 2 + x) * PIECE, 16)

    class Scatter:
        def __init__(self, w, x):
            self.w, self.x = w, x

        def core(self, s):
            rows = pl.ds(slot(self.w, s, 1 - my_core), 4 * PIECE)
            return copy_to(core_peer, fw.at[rows], from_core.at[s], core_s.at[self.w, s], core_r.at[self.w, s])

        def y(self, s):
            rows = pl.ds(slot(self.w, s, my_core, 1 - my_y), 2 * PIECE)
            return copy_to(y_peer, fw.at[rows], from_y.at[self.w, s], y_s.at[self.w, s], y_r.at[self.w, s])

        def over(self, s):
            rows = pl.ds(slot(self.w, s, my_core, my_y, 1 - self.x), PIECE)
            return copy_to(x_peer, fw.at[rows], from_x.at[self.w, s], x_s.at[self.w, s], x_r.at[self.w, s])

        def held(self, s, h):
            if h == self.x:
                return fw.at[pl.ds(slot(self.w, s, my_core, my_y, self.x), PIECE)]
            return from_x.at[self.w, s]

        def up(self, s, h):
            return copy_to(
                up_peer, self.held(s, h), from_low.at[self.w, s, h], up_s.at[self.w, s, h], up_r.at[self.w, s, h]
            )

        def down(self, s, h):
            return copy_to(
                down_peer, self.held(s, h), from_high.at[self.w, s, h], down_s.at[self.w, s, h], down_r.at[self.w, s, h]
            )

        def cast(self, first_row):
            @pl.loop(0, PIECES)
            def _(s):
                for k in range(8):
                    j = (k & 2) * 2 + (k & 4) // 2 + (k & 1)
                    src = pl.ds(pl.multiple_of(first_row + j * SHARD + s * PIECE, 8), PIECE)
                    fw[pl.ds(pl.multiple_of(slot(self.w, s, 0) + k * PIECE, 16), PIECE), :] = gf[src, :].astype(BF)
                self.core(s).start()

        def add_core(self):
            @pl.loop(0, PIECES)
            def _(s):
                self.core(s).wait_recv()
                rows = pl.ds(slot(self.w, s, my_core), 4 * PIECE)
                fw[rows, :] = fw[rows, :] + from_core[s]
                self.y(s).start()

        def add_y(self, s):
            self.y(s).wait_recv()
            rows = pl.ds(slot(self.w, s, my_core, my_y), 2 * PIECE)
            fw[rows, :] = fw[rows, :] + from_y[self.w, s]
            self.over(s).start()

        def from_ends(self, s):
            self.over(s).wait_recv()
            for h in range(2):
                goal = 2 * h + self.w
                if goal > 0:
                    pl.when(my_z == 0)(self.up(s, h).start)
                if goal < NZ - 1:
                    pl.when(my_z == NZ - 1)(self.down(s, h).start)

        def relay(self, s, hop):
            for h in range(2):
                goal = 2 * h + self.w
                mine = self.held(s, h)
                if hop < goal:

                    @pl.when(my_z == hop)
                    def _():
                        self.up(s, h).wait_recv()
                        mine[...] = mine[...] + from_low[self.w, s, h]
                        self.up(s, h).start()

                if NZ - 1 - hop > goal:

                    @pl.when(my_z == NZ - 1 - hop)
                    def _():
                        self.down(s, h).wait_recv()
                        mine[...] = mine[...] + from_high[self.w, s, h]
                        self.down(s, h).start()

        def collect(self, s):
            for h in range(2):
                goal = 2 * h + self.w

                @pl.when(my_z == goal)
                def _():
                    whole = self.held(s, h)[...].astype(F32)
                    if goal > 0:
                        self.up(s, h).wait_recv()
                        whole = whole + from_low[self.w, s, h].astype(F32)
                    if goal < NZ - 1:
                        self.down(s, h).wait_recv()
                        whole = whole + from_high[self.w, s, h].astype(F32)
                    total[pl.ds(pl.multiple_of(s * PIECE, 8), PIECE), :] = whole

        def sent(self):
            @pl.loop(0, PIECES)
            def _(s):
                self.core(s).wait_send()
                self.y(s).wait_send()
                self.over(s).wait_send()
                for h in range(2):
                    goal = 2 * h + self.w
                    pl.when(my_z < goal)(self.up(s, h).wait_send)
                    pl.when(my_z > goal)(self.down(s, h).wait_send)

    def rest_of_scatter(one, zero):
        pl.loop(0, PIECES)(one.add_y)
        pl.loop(0, PIECES)(one.from_ends)

        def step(s, when):
            when(s < PIECES, lambda: zero.add_y(s))
            when(s < PIECES, lambda: one.relay(s, 1))
            when((s > 0) & (s <= PIECES), lambda: one.relay(s - 1, 2))
            when((s > 0) & (s <= PIECES), lambda: zero.from_ends(s - 1))
            when((s > 1) & (s <= PIECES + 1), lambda: zero.relay(s - 2, 1))
            when((s > 2) & (s <= PIECES + 2), lambda: zero.relay(s - 3, 2))

        pl.loop(0, PIECES + 3)(lambda s: step(s, lambda is_so, do: pl.when(is_so)(do)))
        pl.loop(0, PIECES)(one.collect)
        pl.loop(0, PIECES)(zero.collect)
        one.sent()
        zero.sent()

    def square_sums():
        total[SHARD:, :] = jnp.zeros((total.shape[0] - SHARD, 128), F32)
        done = pltpu.make_async_copy(total.at[pl.ds(0, SHARD)], g_out, gsem)
        done.start()
        seg = lax.broadcasted_iota(jnp.int32, (SEGS, 1), 0)
        begin = jnp.full((SEGS, 1), 1 << 30, jnp.int32)
        end = begin
        for i, (a, b) in enumerate(zip(*segment_table(D, FF)[:2])):
            begin = jnp.where(seg == i, int(a), begin)
            end = jnp.where(seg == i, int(b), end)
        row = (me * 2 + role) * SHARD + lax.broadcasted_iota(jnp.int32, (SEGS, total.shape[0]), 1)
        member = jnp.where((row >= begin) & (row < end), 1.0, 0.0)
        squares = lax.dot_general(
            member, total[...] * total[...], (((1,), (0,)), ((), ())),
            precision=lax.Precision.HIGHEST, preferred_element_type=F32,
        )
        mine = jnp.broadcast_to(jnp.sum(squares, axis=1, keepdims=True), (SEGS, 128))
        for i, peer in enumerate((core_peer, y_peer, x_peer)):
            sq[2 * i] = mine
            swap = copy_to(peer, sq.at[2 * i], sq.at[2 * i + 1], sum_s.at[i], sum_r.at[i])
            swap.start()
            swap.wait()
            mine = mine + sq[2 * i + 1]
        sq[6] = mine
        sends = []
        for step in range(1, NZ):
            to = at_dp((my_z + step) % NZ, my_y, my_core)
            sends.append(copy_to(to, sq.at[6], sq.at[6 + step], sum_s.at[2 + step], sum_r.at[2 + step]))
            sends[-1].start()
        for c in sends:
            c.wait()
        whole = jnp.zeros((SEGS, 128), F32)
        for z in range(NZ):
            part = mine
            for step in range(1, NZ):
                part = jnp.where((my_z - step + NZ) % NZ == z, sq[6 + step], part)
            whole = whole + part
        sums_out[...] = whole
        done.wait()

    def attention_role():
        at = {k: LEAD + v for k, v in row0.items()}
        at0 = {k: CARRY + v for k, v in row0.items()}
        at1 = {k: CARRY - WINDOW + v for k, v in row0.items()}
        one, zero = Scatter(1, 0), Scatter(0, 0)
        xin[first, :] = cap[...]
        loads[0].wait()
        vector(V_G1, at[NORM_ONE_GAIN], D)
        vector(V_C1, at[NORM_ONE_SHIFT], D)
        vec[V_BQKV : V_BQKV + 1, :] = jnp.zeros((1, FF), F32)
        vec[V_BKV : V_BKV + 1, :] = jnp.zeros((1, FF), F32)
        vector(V_BQKV, at[SELF_QUERY_BIAS], D)
        vector(V_BQKV, at[SELF_VALUE_BIAS], D, 2 * D)
        widen(at[SELF_QKV], 18, QKV_AT)
        for c in loads[1:]:
            c.wait()
        vector(V_BO, at[SELF_OUT_BIAS], D)
        vector(V_G2, at[NORM_TWO_GAIN], D)
        vector(V_C2, at[NORM_TWO_SHIFT], D)
        vector(V_UQ, at[CROSS_QUERY_BIAS], D)
        vector(V_BKV, at[CROSS_VALUE_BIAS], D, D)
        vector(V_UO, at[CROSS_OUT_BIAS], D)
        widen(at[SELF_OUT], 6, WO_AT)
        widen(at[CROSS_QUERY], 6, UQ_AT)
        widen(at[CROSS_KV], 12, UKV_AT)
        widen(at[CROSS_OUT], 6, UO_AT)
        all_here()
        copies["dy"].start()
        copies["lead"].start()

        copies["cap"].wait_recv()
        norm_forward(xin, h1, V_G1, V_C1)

        for j in range(3):
            cols = slice(D * j, D * j + D)
            big1[:, cols] = (mm(h1[...], wide[:, cols]) + vec[V_BQKV : V_BQKV + 1, cols]).astype(BF)

        copies["meta"].wait_recv()

        @pl.loop(0, 12, unroll=4)
        def _(i):
            c, p = i // 6, i % 6
            rows = pl.ds(al(c, TOK), TOK)
            qq = halves(big1[rows, pl.ds(al(p, 128), 128)]) * BF(0.125)
            k2 = big1[rows, pl.ds(al(p, 128) + D, 128)]
            v2 = big1[rows, pl.ds(al(p, 128) + 2 * D, 128)]
            s = mm_nt(qq, k2)
            row = lax.broadcasted_iota(jnp.int32, s.shape, 0) % TOK
            col = lax.broadcasted_iota(jnp.int32, s.shape, 1)
            present = col.astype(F32) < meta[c][2:3, :]
            s = jnp.where((col <= row) & present, s, NEG_LARGE)
            e = jnp.exp(s - jnp.max(s, axis=-1, keepdims=True))
            prob = (e * (1.0 / jnp.sum(e, axis=-1, keepdims=True))).astype(BF)
            ps[i] = prob
            am[rows, pl.ds(al(p, 128), 128)] = joined(mm(prob, v2)).astype(BF)

        x1[...] = xin[...].astype(F32) + mm(am[...], wide[:, WO_AT : WO_AT + D]) + vec[V_BO : V_BO + 1, :D]
        norm_forward(x1, h2, V_G2, V_C2)
        q2[...] = (mm(h2[...], wide[:, UQ_AT : UQ_AT + D]) + vec[V_UQ : V_UQ + 1, :D]).astype(BF)
        copies["tile"].wait_recv()

        for j in range(2):
            cols = slice(D * j, D * j + D)
            kv[:, cols] = (
                mm(tl[...], wide[:, UKV_AT + D * j : UKV_AT + D * j + D]) + vec[V_BKV : V_BKV + 1, cols]
            ).astype(BF)

        @pl.loop(0, 2)
        def _(c):
            rows = pl.ds(al(c, TOK), TOK)
            col = lax.broadcasted_iota(jnp.int32, (1, KEYS), 1)
            m = meta[c]
            c0 = jnp.concatenate([m[0:1, :]] * (KEYS // 128), axis=1)
            c1 = jnp.concatenate([m[1:2, :]] * (KEYS // 128), axis=1)
            count = jnp.where(col < PATCH, c0, jnp.where(col < PATCH_SLOT, 0.0, c1))
            count = jnp.where(col < PATCH_SLOT + PATCH, count, 0.0)

            @pl.loop(0, 6, unroll=3)
            def _(p):
                qq = halves(q2[rows, pl.ds(al(p, 128), 128)]) * BF(0.125)
                s = mm_nt(qq, kv[:, pl.ds(al(p, 128), 128)])
                s = jnp.where(count > 0.0, s, NEG_LARGE)
                e = jnp.exp(s - jnp.max(s, axis=-1, keepdims=True)) * count
                prob = (e * (1.0 / jnp.sum(e, axis=-1, keepdims=True))).astype(BF)
                pc[pl.ds(al(6 * c + p, 2 * TOK), 2 * TOK), :] = prob
                a2[rows, pl.ds(al(p, 128), 128)] = joined(
                    mm(prob, kv[:, pl.ds(al(p, 128) + D, 128)])
                ).astype(BF)

            sb[rows, :] = (
                x1[rows, :] + mm(a2[rows, :], wide[:, UO_AT : UO_AT + D]) + vec[V_UO : V_UO + 1, :D]
            ).astype(BF)
            x2_copy(c).start()

        copies["old"].start()

        h1T[...] = h1[...].T
        amT[...] = am[...].T
        h2T[...] = h2[...].T
        a2T[...] = a2[...].T
        tlT[...] = tl[...].T

        part_at = at1[CROSS_KV]

        def attend_back(c, p, take_keys):
            rows = pl.ds(c * TOK, TOK)
            lanes, vlanes = pl.ds(al(p, 128), 128), pl.ds(al(p, 128) + D, 128)
            qq = halves(q2[rows, lanes]) * BF(0.125)
            do = halves(t1[rows, lanes])
            prob = pc[pl.ds(al(6 * c + p, 2 * TOK), 2 * TOK), :]
            pf = prob.astype(F32)
            dp = mm_nt(do, kv[:, vlanes])
            ds = (pf * (dp - jnp.sum(pf * dp, axis=-1, keepdims=True))).astype(BF)
            am[rows, lanes] = (joined(mm(ds, kv[:, lanes])) * 0.125).astype(BF)
            take_keys(p, 0, lanes, mm_tn(qq, ds))
            take_keys(p, 1, vlanes, mm_tn(do, prob))

        def part_rows(p, k, j):
            return pl.ds(pl.multiple_of(part_at + ((2 * p + k) * 4 + j) * 128, 8), 128)

        def keep(p, k, lanes, term):
            for j in range(4):
                gf[part_rows(p, k, j), :] = term[:, 128 * j : 128 * j + 128]

        def complete(p, k, lanes, term):
            for j in range(4):
                cols = slice(128 * j, 128 * j + 128)
                dkvt[lanes, cols] = (gf[part_rows(p, k, j), :] + term[:, cols]).astype(BF)

        for c, take_keys in enumerate((keep, complete)):
            rows = pl.ds(c * TOK, TOK)
            dx2_copy(c).wait_recv()
            t1[rows, :] = mm_nt(rb[rows, :], wide[:, UO_AT : UO_AT + D]).astype(BF)
            pl.loop(0, 6, unroll=3)(functools.partial(attend_back, c, take_keys=take_keys))

        put_vector(at1[CROSS_OUT_BIAS], column_total(rb, slice(None)))
        matrix_grad(at1[CROSS_OUT], 6, a2T, rb)
        put_vector(at1[CROSS_QUERY_BIAS], column_total(am, slice(None)))
        matrix_grad(at1[CROSS_QUERY], 6, h2T, am)
        matrix_grad(at1[CROSS_KV], 12, tlT, dkvt, transposed=True)
        kv[...] = dkvt[...].T
        put_vector(at1[CROSS_VALUE_BIAS], column_total(kv, slice(D, 2 * D)))
        copies["pfx"].wait_recv()
        gf[pl.ds(at1[NORM_THREE_GAIN], LEAD - 12), :] = pfx_in[12:, :]
        copies["lead"].wait_send()
        one.cast(CARRY)
        carry[...] = gf[0:CARRY, :]

        def tile_grad(rows):
            return mm_nt(kv[rows, :], wide[:, UKV_AT : UKV_AT + 2 * D])

        dtile[...] = tile_grad(pl.ds(0, PATCH_SENT))[:PATCH]
        dtile_b[...] = tile_grad(pl.ds(PATCH_SLOT, PATCH_SENT)).astype(BF)
        copies["dtile"].start()
        one.add_core()
        pl.semaphore_signal(free, inc=1, device_id=core_peer, device_id_type=MESH)
        acc[...] = mm_nt(am[...], wide[:, UQ_AT : UQ_AT + D])
        e1 = h2

        def write_dx1(rows, dv):
            full = rb[rows, :].astype(F32) + dv
            dx[rows, :] = full
            e1[rows, :] = full.astype(BF)

        gg, gc = norm_backward(x1, acc, V_G2, write_dx1)
        put_vector(at0[NORM_TWO_GAIN], gg)
        put_vector(at0[NORM_TWO_SHIFT], gc)
        put_vector(at0[SELF_OUT_BIAS], column_total(e1, slice(None)))
        matrix_grad(at0[SELF_OUT], 6, amT, e1)
        t1[...] = mm_nt(e1[...], wide[:, WO_AT : WO_AT + D]).astype(BF)

        @pl.loop(0, 12, unroll=4)
        def _(i):
            c, p = i // 6, i % 6
            rows = pl.ds(al(c, TOK), TOK)
            lanes = pl.ds(al(p, 128), 128)
            klanes, vlanes = pl.ds(al(p, 128) + D, 128), pl.ds(al(p, 128) + 2 * D, 128)
            qq = halves(big1[rows, lanes]) * BF(0.125)
            do = halves(t1[rows, lanes])
            prob = ps[i]
            pf = prob.astype(F32)
            dp = mm_nt(do, big1[rows, vlanes])
            ds = (pf * (dp - jnp.sum(pf * dp, axis=-1, keepdims=True))).astype(BF)
            big2[rows, lanes] = (joined(mm(ds, big1[rows, klanes])) * 0.125).astype(BF)
            big2[rows, klanes] = mm_tn(ds, qq).astype(BF)
            big2[rows, vlanes] = mm_tn(prob, do).astype(BF)

        acc[...] = mm_nt(big2[:, : 3 * D], wide[:, : 3 * D])

        def write_dx0(rows, dv):
            dx[rows, :] = dx[rows, :] + dv

        gg, gc = norm_backward(xin, acc, V_G1, write_dx0)
        put_vector(at0[NORM_ONE_GAIN], gg)
        put_vector(at0[NORM_ONE_SHIFT], gc)
        dcap[...] = dx[first, :]
        dcap_b[...] = dx[later, :].astype(BF)
        copies["dcap"].start()
        put_vector(at0[SELF_QUERY_BIAS], column_total(big2, slice(0, D)))
        put_vector(at0[SELF_VALUE_BIAS], column_total(big2, slice(2 * D, 3 * D)))
        matrix_grad(at0[SELF_QKV], 18, h1T, big2)
        gf[pl.ds(at0[CROSS_QUERY], WINDOW - row0[CROSS_QUERY]), :] = carry[
            row0[CROSS_QUERY] - WINDOW + CARRY :, :
        ]
        pl.semaphore_wait(free, 1)
        zero.cast(CARRY)
        zero.add_core()
        rest_of_scatter(one, zero)
        copies["out"].wait_recv()
        out[...] = ob[...]
        for name in ("dy", "dcap", "dtile"):
            copies[name].wait_send()
        for c in range(2):
            x2_copy(c).wait_send()
        copies["old"].wait()
        square_sums()

    def mlp_role():
        all_here()
        copies["meta"].start()
        copies["cap"].start()
        copies["cap"].wait_send()
        copies["tile"].start()
        base = LEAD - weights.shape[0]
        at = {k: base + v for k, v in row0.items()}
        at0 = {k: CARRY - weights.shape[0] + v for k, v in row0.items()}
        at1 = {k: v - WINDOW for k, v in at0.items()}
        one, zero = Scatter(1, 1), Scatter(0, 1)
        dy[later, :] = d_out[...]
        for c in loads:
            c.wait()
        for b in range(4):
            widen(at[MLP_DOWN] + 6 * D * b, 6, W2_AT + D * b)
        copies["lead"].wait_recv()
        widen(at[MLP_UP], 24, W1_AT)
        vector(V_G3, at[NORM_THREE_GAIN], D)
        vector(V_C3, at[NORM_THREE_SHIFT], D)
        vector(V_B1, at[MLP_UP_BIAS], FF)
        vector(V_B2, at[MLP_DOWN_BIAS], D)
        copies["dy"].wait_recv()

        @pl.loop(0, 4)
        def _(b):
            dg = mm_nt(dy[...], wide[:, pl.ds(al(b, D) + W2_AT, D)])
            for j in range(6):
                gf[pl.ds(al(6 * b + j, 256), 256), :] = dg[:, 128 * j : 128 * j + 128]

        def write_dx2(rows, dv):
            sb[rows, :] = (dy[rows, :].astype(F32) + dv).astype(BF)

        vec[V_SUMS : V_SUMS + 2, :] = jnp.zeros((2, FF), F32)

        @pl.loop(0, 2)
        def _(c):
            cap_rows = pl.ds(al(c, TOK), TOK)
            x2_copy(c).wait_recv()
            norm_forward(rb, h1, V_G3, V_C3, c * TOK, TOK)
            z_parts = [x1.at[first], x1.at[later], dx.at[first], dx.at[later]]
            for b in range(4):
                cols = slice(D * b, D * b + D)
                z_parts[b][...] = mm(h1[cap_rows, :], wide[:, cols]) + vec[V_B1 : V_B1 + 1, cols]

            @pl.loop(0, 4)
            def _(i):
                here = pl.ds(al(i, 32), 32)
                rows = pl.ds(al(c, TOK) + al(i, 32), 32)
                for k in range(24):
                    z = z_parts[k // 6][here, 128 * (k % 6) : 128 * (k % 6) + 128]
                    phi = 0.5 + 0.5 * lax.erf(z * np.float32(np.sqrt(0.5)))
                    dens = jnp.exp(-0.5 * z * z) * np.float32(1.0 / np.sqrt(2.0 * np.pi))
                    lanes = slice(128 * k, 128 * k + 128)
                    big1[rows, lanes] = (z * phi).astype(BF)
                    dg = gf[pl.ds(256 * k + al(c, TOK) + al(i, 32), 32), :]
                    big2[rows, lanes] = (dg * (phi + z * dens)).astype(BF)

            acc[cap_rows, :] = mm_nt(big2[cap_rows, :], wide[:, W1_AT : W1_AT + FF])
            gg, gc = norm_backward(rb, acc, V_G3, write_dx2, c * TOK, TOK)
            vec[V_SUMS : V_SUMS + 1, :D] = vec[V_SUMS : V_SUMS + 1, :D] + gg
            vec[V_SUMS + 1 : V_SUMS + 2, :D] = vec[V_SUMS + 1 : V_SUMS + 2, :D] + gc
            dx2_copy(c).start()

        put_vector(12, vec[V_SUMS : V_SUMS + 1, :D], pfx)
        put_vector(18, vec[V_SUMS + 1 : V_SUMS + 2, :D], pfx)

        h1T[...] = h1[...].T
        pfx[0:12, :] = jnp.zeros((12, 128), F32)
        for b in range(4):
            head = mm(h1T[0:8, :], big2[:, D * b : D * b + D])
            for r in range(3):
                for j in range(6):
                    row = 24 + 24 * r + 6 * b + j
                    if row < LEAD:
                        pfx[row : row + 1, :] = head[r : r + 1, 128 * j : 128 * j + 128]
        copies["pfx"].start()
        copies["old"].start()

        acc[...] = rb[...].astype(F32) + vec[V_B2 : V_B2 + 1, :D]
        for b in range(4):
            cols = slice(D * b, D * b + D)
            acc[...] = acc[...] + mm(big1[:, cols], wide[:, W2_AT + D * b : W2_AT + D * b + D])
            pc[D * b : D * b + D, 0:256] = big1[:, cols].T

        t1[first, :] = acc[first, :].astype(BF)
        copies["out"].start()
        out[...] = acc[later, :].astype(BF)
        gf[pl.ds(at1[MLP_DOWN_BIAS] + 6, WINDOW + CARRY - at1[MLP_DOWN_BIAS] - 6), :] = jnp.zeros(
            (WINDOW + CARRY - at1[MLP_DOWN_BIAS] - 6, 128), F32
        )
        put_vector(at1[MLP_DOWN_BIAS], column_total(dy, slice(None)))
        for b in range(4):
            matrix_grad(at1[MLP_DOWN] + 6 * D * b, 6, pc.at[pl.ds(D * b, D), pl.ds(0, 256)], dy)
        one.cast(CARRY)
        carry[...] = gf[0:CARRY, :]
        put_vector(at0[MLP_UP_BIAS], column_total(big2, slice(None)))
        matrix_grad(at0[MLP_UP], 24, h1T, big2)
        one.add_core()
        pl.semaphore_signal(free, inc=1, device_id=core_peer, device_id_type=MESH)
        gf[pl.ds(at0[MLP_DOWN], CARRY), :] = carry[...]
        pl.semaphore_wait(free, 1)
        zero.cast(CARRY)
        zero.add_core()
        rest_of_scatter(one, zero)
        copies["dtile"].wait_recv()
        dtile[...] = dtile_b[0:PATCH, :].astype(F32)
        copies["dcap"].wait_recv()
        dcap[...] = dcap_b[...].astype(F32)
        for name in ("tile", "meta", "pfx", "out"):
            copies[name].wait_send()
        for c in range(2):
            dx2_copy(c).wait_send()
        copies["old"].wait()
        square_sums()

    pl.when(role == 0)(attention_role)
    pl.when(role == 1)(mlp_role)


def pair_call(cap, tiles, d_out, index, valid, length, weights):
    vm = pl.BlockSpec(memory_space=pltpu.VMEM)
    sm = pl.BlockSpec(memory_space=pltpu.SMEM)
    hbm = pl.BlockSpec(memory_space=pl.ANY)
    S = jax.ShapeDtypeStruct
    dma, both = pltpu.SemaphoreType.DMA, 2 * TOK

    def bf(*s):
        return pltpu.VMEM(s, BF)

    def fl(*s):
        return pltpu.VMEM(s, F32)

    return pl.pallas_call(
        pair_kernel,
        in_specs=[vm, vm, vm, sm, sm, sm, hbm],
        out_specs=[hbm, vm, hbm, vm, vm, vm],
        out_shape=[
            S((SHARD, 128), F32),
            S((SEGS, 128), F32),
            S((OLD, 128), BF),
            S((TOK, D), BF),
            S((TOK, D), F32),
            S((PATCH, D), F32),
        ],
        scratch_shapes=[
            bf(16 * PADDED, 128), bf(D, WIDE), fl(CARRY + 7 * SHARD + PADDED, 128), bf(12 * both, KEYS),
            bf(12, both, 128), bf(both, FF), bf(both, FF), bf(KEYS, 2 * D), bf(2 * D, KEYS), bf(KEYS, D), bf(D, KEYS),
            *[bf(both, D) for _ in range(10)],
            *[bf(D, both) for _ in range(4)],
            *[fl(both, D) for _ in range(3)],
            fl(16, FF), fl(2, 8, 128), bf(TOK, D), fl(LEAD, 128), fl(LEAD, 128), fl(CARRY, 128),
            bf(TOK, D), bf(PATCH_SENT, D),
            bf(PIECES, 4 * PIECE, 128), bf(2, PIECES, 2 * PIECE, 128), bf(2, PIECES, PIECE, 128),
            bf(2, PIECES, 2, PIECE, 128), bf(2, PIECES, 2, PIECE, 128), fl(2432, 128), fl(10, SEGS, 128),
            dma((5,)), dma, dma((16,)), dma((16,)),
            *[dma((2, PIECES)) for _ in range(6)],
            *[dma((2, PIECES, 2)) for _ in range(4)],
            pltpu.SemaphoreType.REGULAR, dma((6,)), dma((6,)),
        ],
        compiler_params=pltpu.CompilerParams(
            collective_id=0, has_side_effects=True, vmem_limit_bytes=63 * 2**20
        ),
    )(cap, tiles, d_out, index, valid, length, weights)


def finish(shard_grad, old_weights, first_moment, second_moment, square_sums):
    shard_rows = shard_grad.shape[0]
    begin_row = lax.axis_index(BOTH) * shard_rows
    seg_starts, seg_ends, decay_flags, seg_entries = segment_table(D, FF)
    row_ids = begin_row + jnp.arange(shard_rows)
    member = (row_ids[:, None] >= seg_starts[None, :]) & (row_ids[:, None] < seg_ends[None, :])
    return adam_step(
        shard_grad, member, decay_flags, old_weights, first_moment, second_moment, square_sums, seg_entries
    )


def pair_body(
    captions, tiles, tile_index, tile_valid, caption_len, weights, first_moment, second_moment, d_out
):
    me, f = lax.axis_index(DP), lax.axis_index(FSDP)
    shard_grad, sums, old, out, caption_grad, tiles_grad = pair_call(
        captions[0], tiles[0], d_out[0], tile_index, tile_valid, caption_len, weights
    )
    own = lax.dynamic_slice_in_dim(weights, ((2 * me + f) % 16) * SHARD, SHARD, 0)
    old = lax.dynamic_slice_in_dim(old, 8 * f, SHARD, 0)
    old_weights = jnp.where(me // 8 == f, own, old).astype(jnp.float32)
    update, new_first, new_second, grad_norm, tensor_rms = finish(
        shard_grad, old_weights, first_moment, second_moment, sums[:21, 0]
    )
    return (
        out[None], caption_grad[None], tiles_grad[None], shard_grad, update, new_first, new_second,
        grad_norm, tensor_rms,
    )


def solution(mesh):
    placed = (
        P(BOTH, None, None),
        P(BOTH, None, None),
        P(BOTH, None),
        P(BOTH, None),
        P(BOTH),
        P(FSDP, None),
        P(BOTH, None),
        P(BOTH, None),
        P(BOTH, None, None),
    )
    return jax.shard_map(
        pair_body if mesh.shape[FSDP] == 2 else body,
        mesh=mesh,
        in_specs=placed,
        out_specs=(
            P(BOTH, None, None),
            P(BOTH, None, None),
            P(BOTH, None, None),
            P(BOTH, None),
            P(BOTH, None),
            P(BOTH, None),
            P(BOTH, None),
            P(),
            P(),
        ),
        check_vma=False,
    )
```

```python
import functools

import jax
import jax.numpy as jnp
import numpy as np
from jax import lax
from jax.experimental import pallas as pl
from jax.experimental.pallas import tpu as pltpu
from jax.sharding import PartitionSpec as P

HEADS = 12
HEAD_DIM = 64
FF = 3072
STEP = 10


EPS_NORM = 1e-05
CLIP_NORM = 1.0
BETA_ONE = 0.9
BETA_TWO = 0.999
LEARN_RATE = 0.01
DECAY_RATE = 0.1
ADAM_EPS = 1e-08
NEG_LARGE = -1e30
(NORM_ONE_GAIN, NORM_ONE_SHIFT, SELF_QKV, SELF_QUERY_BIAS, SELF_VALUE_BIAS, SELF_OUT, SELF_OUT_BIAS, NORM_TWO_GAIN, NORM_TWO_SHIFT, CROSS_QUERY, CROSS_QUERY_BIAS, CROSS_KV, CROSS_VALUE_BIAS, CROSS_OUT, CROSS_OUT_BIAS, NORM_THREE_GAIN, NORM_THREE_SHIFT, MLP_UP, MLP_UP_BIAS, MLP_DOWN, MLP_DOWN_BIAS) = range(21)
DP, FSDP = "dp", "fsdp"
BOTH = (DP, FSDP)
E_BHQK_BKHE_TO_BQHE = "bhqk,bkhe->bqhe"
E_BHQK_BQHE_TO_BKHE = "bhqk,bqhe->bkhe"
E_BLD_BLE_TO_DE = "bld,ble->de"
E_BLD_BLF_TO_DF = "bld,blf->df"
E_BLD_DE_TO_BLE = "bld,de->ble"
E_BLD_DF_TO_BLF = "bld,df->blf"
E_BLD_FD_TO_BLF = "bld,fd->blf"
E_BLE_DE_TO_BLD = "ble,de->bld"
E_BLF_BLD_TO_FD = "blf,bld->fd"
E_BLF_DF_TO_BLD = "blf,df->bld"
E_BLF_FD_TO_BLD = "blf,fd->bld"
E_BQHE_BKHE_TO_BHQK = "bqhe,bkhe->bhqk"
E_CSG_CSPE_TO_GPE = "csg,cspe->gpe"
E_TPD_DE_TO_TPE = "tpd,de->tpe"
E_TPD_TPE_TO_DE = "tpd,tpe->de"
E_TPE_DE_TO_TPD = "tpe,de->tpd"


def for_sending(x):
    return jax.tree.map(lambda a: a.astype(jnp.bfloat16) if a.dtype == jnp.float32 else a, x)


def layout(model_width, hidden_width):
    return [
        (NORM_ONE_GAIN, (model_width,), 0),
        (NORM_ONE_SHIFT, (model_width,), 0),
        (SELF_QKV, (model_width, 3 * model_width), 1),
        (SELF_QUERY_BIAS, (model_width,), 0),
        (SELF_VALUE_BIAS, (model_width,), 0),
        (SELF_OUT, (model_width, model_width), 1),
        (SELF_OUT_BIAS, (model_width,), 0),
        (NORM_TWO_GAIN, (model_width,), 0),
        (NORM_TWO_SHIFT, (model_width,), 0),
        (CROSS_QUERY, (model_width, model_width), 1),
        (CROSS_QUERY_BIAS, (model_width,), 0),
        (CROSS_KV, (model_width, 2 * model_width), 1),
        (CROSS_VALUE_BIAS, (model_width,), 0),
        (CROSS_OUT, (model_width, model_width), 1),
        (CROSS_OUT_BIAS, (model_width,), 0),
        (NORM_THREE_GAIN, (model_width,), 0),
        (NORM_THREE_SHIFT, (model_width,), 0),
        (MLP_UP, (model_width, hidden_width), 1),
        (MLP_UP_BIAS, (hidden_width,), 0),
        (MLP_DOWN, (hidden_width, model_width), 1),
        (MLP_DOWN_BIAS, (model_width,), 0),
    ]


def segment_table(model_width, hidden_width):
    seg_starts = []
    seg_ends = []
    decay_flags = []
    seg_entries = []
    row_at = 0
    for seg_label, seg_shape, seg_flag in layout(model_width, hidden_width):
        item_count = int(np.prod(seg_shape))
        seg_rows = item_count // 128
        seg_starts.append(row_at)
        seg_ends.append(row_at + seg_rows)
        decay_flags.append(seg_flag == 1)
        seg_entries.append(float(item_count))
        row_at = row_at + seg_rows
    return (np.array(seg_starts), np.array(seg_ends), np.array(decay_flags), np.array(seg_entries))


def unpack(flat_rows, model_width, hidden_width):
    vector = flat_rows.reshape(-1)
    tensors = {}
    offset = 0
    for seg_label, seg_shape, seg_flag in layout(model_width, hidden_width):
        item_count = int(np.prod(seg_shape))
        tensors[seg_label] = vector[offset : offset + item_count].reshape(seg_shape)
        offset = offset + item_count
    return tensors


def pack_rows(gradients, model_width, hidden_width, total_rows):
    pieces = [
        gradients[seg_label].reshape(-1, 128)
        for seg_label, seg_shape, seg_flag in layout(model_width, hidden_width)
    ]
    used_rows = sum((tensor_piece.shape[0] for tensor_piece in pieces))
    pieces.append(jnp.zeros((total_rows - used_rows, 128), jnp.float32))
    return jnp.concatenate(pieces, axis=0)


def product(pattern, left_side, right_side):
    return jnp.einsum(pattern, left_side, right_side, preferred_element_type=jnp.float32)


def as_float(tensors, seg_label):
    return tensors[seg_label].astype(jnp.float32)


def column_sums(values):
    return jnp.sum(values.astype(jnp.float32), axis=tuple(range(values.ndim - 1)))


def layer_norm(values, gain_term, offset_term):
    center = values - jnp.mean(values, axis=-1, keepdims=True)
    spread = jnp.mean(center * center, axis=-1, keepdims=True)
    return center * lax.rsqrt(spread + EPS_NORM) * gain_term + offset_term


def gelu_exact(pre_values):
    return jax.nn.gelu(pre_values, approximate=False)


def norm_back(values, tensors, gain, shift, normed_grad, gradients):
    norm_value, norm_pull = jax.vjp(
        layer_norm,
        values,
        as_float(tensors, gain),
        as_float(tensors, shift),
    )
    values_grad, gain_grad, offset_grad = norm_pull(normed_grad)
    gradients[gain] = gain_grad
    gradients[shift] = offset_grad
    return values_grad


def score_block(queries, key_head_split, allowed):
    scores = product(E_BQHE_BKHE_TO_BHQK, queries, key_head_split) * 0.125
    return jnp.where(allowed, scores, NEG_LARGE)


def softmax_forward(queries, key_head_split, allowed):
    scores = score_block(queries, key_head_split, allowed)
    highest = jnp.max(scores, axis=-1, keepdims=True)
    exponent = jnp.exp(scores - highest)
    row_total = jnp.sum(exponent, axis=-1, keepdims=True)
    return (exponent / row_total, highest + jnp.log(row_total))


def attention_backward_pass(queries, key_head_split, values, allowed, log_total, mixed_grad):
    probabilities = jnp.where(
        allowed, jnp.exp(score_block(queries, key_head_split, allowed) - log_total), 0.0
    )
    probs_grad = product(E_BQHE_BKHE_TO_BHQK, mixed_grad, values)
    values_grad = product(E_BHQK_BQHE_TO_BKHE, probabilities.astype(jnp.bfloat16), mixed_grad)
    inner_sum = jnp.sum(probabilities * probs_grad, axis=-1, keepdims=True)
    score_grad = (probabilities * (probs_grad - inner_sum)).astype(jnp.bfloat16)
    queries_grad = product(E_BHQK_BKHE_TO_BQHE, score_grad, key_head_split) * 0.125
    keys_grad = product(E_BHQK_BQHE_TO_BKHE, score_grad, queries) * 0.125
    return (queries_grad, keys_grad, values_grad)


def adam_step(
    gradients,
    member,
    decay_flags,
    old_weights,
    first_moment,
    second_moment,
    square_sums,
    seg_entries,
):
    grad_norm = jnp.sqrt(jnp.sum(square_sums))
    tensor_rms = jnp.sqrt(square_sums / jnp.asarray(seg_entries, dtype=square_sums.dtype))
    clip_scale = jnp.minimum(1.0, CLIP_NORM / (grad_norm + 1e-06))
    clipped = gradients * clip_scale
    new_first = BETA_ONE * first_moment + (1.0 - BETA_ONE) * clipped
    new_second = BETA_TWO * second_moment + (1.0 - BETA_TWO) * clipped * clipped
    first_hat = new_first / (1.0 - BETA_ONE**STEP)
    second_hat = new_second / (1.0 - BETA_TWO**STEP)
    decay_rows = jnp.any(member & decay_flags[None, :], axis=1)
    decayed = jnp.where(decay_rows[:, None], old_weights, 0.0)
    update = -LEARN_RATE * (first_hat / (jnp.sqrt(second_hat) + ADAM_EPS) + DECAY_RATE * decayed)
    return (update, new_first, new_second, grad_norm, tensor_rms)


def body(
    captions,
    tiles,
    tile_index,
    tile_valid,
    caption_len,
    weights,
    first_moment,
    second_moment,
    d_out,
):
    model_width = captions.shape[2]
    hidden_width = FF
    caption_rows = captions.shape[0]
    cap_length = captions.shape[1]
    patch_count = tiles.shape[1]
    own_tiles = tiles.shape[0]
    slot_count = tile_index.shape[1]
    group_size = lax.axis_size(FSDP)
    data_size = lax.axis_size(DP)
    total_rows = weights.shape[0] * group_size
    heads_shape = (caption_rows, cap_length, HEADS, HEAD_DIM)
    key_shape = (caption_rows, slot_count * patch_count, HEADS, HEAD_DIM)
    token_layout_form = (caption_rows, cap_length, model_width)
    tensors = unpack(lax.all_gather(weights, FSDP, axis=0, tiled=True), model_width, hidden_width)
    zero_part = jnp.zeros((model_width,), jnp.bfloat16)
    input_values = captions.astype(jnp.float32)
    normed_one = layer_norm(
        input_values, as_float(tensors, NORM_ONE_GAIN), as_float(tensors, NORM_ONE_SHIFT)
    ).astype(jnp.bfloat16)
    qkv_bias = jnp.concatenate(
        [tensors[SELF_QUERY_BIAS], zero_part, tensors[SELF_VALUE_BIAS]]
    ).astype(jnp.float32)
    packed_qkv = (product(E_BLD_DE_TO_BLE, normed_one, tensors[SELF_QKV]) + qkv_bias).astype(
        jnp.bfloat16
    )
    self_query = packed_qkv[..., :model_width].reshape(heads_shape)
    self_keys = packed_qkv[..., model_width : 2 * model_width].reshape(heads_shape)
    self_values = packed_qkv[..., 2 * model_width :].reshape(heads_shape)
    positions = jnp.arange(cap_length)
    causal = (positions[None, :] <= positions[:, None])[None, None]
    present = (positions[None, :] < caption_len[:, None])[:, None, None, :]
    self_allowed = causal & present
    self_probs, self_log = softmax_forward(self_query, self_keys, self_allowed)
    self_mixed = (
        product(E_BHQK_BKHE_TO_BQHE, self_probs.astype(jnp.bfloat16), self_values)
        .reshape(token_layout_form)
        .astype(jnp.bfloat16)
    )
    first_sum = (
        input_values
        + product(E_BLD_DE_TO_BLE, self_mixed, tensors[SELF_OUT])
        + as_float(tensors, SELF_OUT_BIAS)
    )
    normed_two = layer_norm(
        first_sum, as_float(tensors, NORM_TWO_GAIN), as_float(tensors, NORM_TWO_SHIFT)
    ).astype(jnp.bfloat16)
    cross_queries = (
        (
            product(E_BLD_DE_TO_BLE, normed_two, tensors[CROSS_QUERY])
            + as_float(tensors, CROSS_QUERY_BIAS)
        )
        .astype(jnp.bfloat16)
        .reshape(heads_shape)
    )
    kv_bias = jnp.concatenate([zero_part, tensors[CROSS_VALUE_BIAS]]).astype(jnp.float32)
    kv_weight = tensors[CROSS_KV]
    group_kv = (
        product(E_TPD_DE_TO_TPE, lax.all_gather(tiles, FSDP, axis=0, tiled=True), kv_weight)
        + kv_bias
    ).astype(jnp.bfloat16)
    chosen = jnp.stack(
        [
            jnp.stack(
                [
                    lax.dynamic_index_in_dim(group_kv, tile_index[c, s], 0, keepdims=False)
                    for s in range(slot_count)
                ]
            )
            for c in range(caption_rows)
        ]
    )
    cross_keys = chosen[..., :model_width].reshape(key_shape)
    cross_values = chosen[..., model_width:].reshape(key_shape)
    usable = jnp.repeat(tile_valid > 0, patch_count, axis=1)[:, None, None, :]
    cross_probs, cross_log = softmax_forward(cross_queries, cross_keys, usable)
    cross_mixed = (
        product(E_BHQK_BKHE_TO_BQHE, cross_probs.astype(jnp.bfloat16), cross_values)
        .reshape(token_layout_form)
        .astype(jnp.bfloat16)
    )
    second = (
        first_sum
        + product(E_BLD_DE_TO_BLE, cross_mixed, tensors[CROSS_OUT])
        + as_float(tensors, CROSS_OUT_BIAS)
    )
    normed_three = layer_norm(
        second, as_float(tensors, NORM_THREE_GAIN), as_float(tensors, NORM_THREE_SHIFT)
    ).astype(jnp.bfloat16)
    preact = product(E_BLD_DF_TO_BLF, normed_three, tensors[MLP_UP]) + as_float(
        tensors, MLP_UP_BIAS
    )
    activation = gelu_exact(preact).astype(jnp.bfloat16)
    result = (
        second
        + product(E_BLF_FD_TO_BLD, activation, tensors[MLP_DOWN])
        + as_float(tensors, MLP_DOWN_BIAS)
    ).astype(jnp.bfloat16)
    back_flat = lax.all_gather(weights, FSDP, axis=0, tiled=True)
    tensors = unpack(back_flat, model_width, hidden_width)
    gradients = {}
    out_grad = d_out.astype(jnp.float32)
    gradients[MLP_DOWN] = product(E_BLF_BLD_TO_FD, activation, d_out)
    gradients[MLP_DOWN_BIAS] = column_sums(d_out)
    activ_grad = product(E_BLD_FD_TO_BLF, d_out, tensors[MLP_DOWN])
    gelu_value, gelu_pull = jax.vjp(gelu_exact, preact)
    preact_grad = gelu_pull(activ_grad)[0].astype(jnp.bfloat16)
    gradients[MLP_UP] = product(E_BLD_BLF_TO_DF, normed_three, preact_grad)
    gradients[MLP_UP_BIAS] = column_sums(preact_grad)
    second_grad = out_grad + norm_back(
        second,
        tensors,
        NORM_THREE_GAIN,
        NORM_THREE_SHIFT,
        product(E_BLF_DF_TO_BLD, preact_grad, tensors[MLP_UP]),
        gradients,
    )
    cross_branch = second_grad.astype(jnp.bfloat16)
    gradients[CROSS_OUT] = product(E_BLD_BLE_TO_DE, cross_mixed, cross_branch)
    gradients[CROSS_OUT_BIAS] = column_sums(cross_branch)
    cmixed_grad = (
        product(E_BLE_DE_TO_BLD, cross_branch, tensors[CROSS_OUT])
        .astype(jnp.bfloat16)
        .reshape(heads_shape)
    )
    cquery_grad, ckeys_grad, cvalues_grad = attention_backward_pass(
        cross_queries, cross_keys, cross_values, usable, cross_log, cmixed_grad
    )
    cquery_low = cquery_grad.astype(jnp.bfloat16).reshape(token_layout_form)
    gradients[CROSS_QUERY] = product(E_BLD_BLE_TO_DE, normed_two, cquery_low)
    gradients[CROSS_QUERY_BIAS] = column_sums(cquery_low)
    first_grad = second_grad + norm_back(
        first_sum,
        tensors,
        NORM_TWO_GAIN,
        NORM_TWO_SHIFT,
        product(E_BLE_DE_TO_BLD, cquery_low, tensors[CROSS_QUERY]),
        gradients,
    )
    slot_layout_form = (caption_rows, slot_count, patch_count, model_width)
    slot_grad = jnp.concatenate(
        [ckeys_grad.reshape(slot_layout_form), cvalues_grad.reshape(slot_layout_form)], axis=-1
    )
    picked = (tile_index[:, :, None] == jnp.arange(group_kv.shape[0])[None, None, :]).astype(
        jnp.float32
    )
    group_grad = jnp.einsum(E_CSG_CSPE_TO_GPE, picked, slot_grad, precision=lax.Precision.HIGHEST)
    arrived = lax.all_to_all(
        group_grad.astype(jnp.bfloat16), FSDP, split_axis=0, concat_axis=0, tiled=True
    ).astype(group_grad.dtype)
    own_grad = jnp.sum(arrived.reshape((group_size, own_tiles) + arrived.shape[1:]), axis=0).astype(
        jnp.bfloat16
    )
    gradients[CROSS_KV] = product(E_TPD_TPE_TO_DE, tiles, own_grad)
    gradients[CROSS_VALUE_BIAS] = column_sums(own_grad[..., model_width:])
    tiles_grad = product(E_TPE_DE_TO_TPD, own_grad, tensors[CROSS_KV])
    self_branch = first_grad.astype(jnp.bfloat16)
    gradients[SELF_OUT] = product(E_BLD_BLE_TO_DE, self_mixed, self_branch)
    gradients[SELF_OUT_BIAS] = column_sums(self_branch)
    smixed_grad = (
        product(E_BLE_DE_TO_BLD, self_branch, tensors[SELF_OUT])
        .astype(jnp.bfloat16)
        .reshape(heads_shape)
    )
    self_query_gradient, self_key_gradient, self_value_gradient = attention_backward_pass(
        self_query, self_keys, self_values, self_allowed, self_log, smixed_grad
    )
    qkv_grad = jnp.concatenate(
        [
            self_query_gradient.reshape(token_layout_form),
            self_key_gradient.reshape(token_layout_form),
            self_value_gradient.reshape(token_layout_form),
        ],
        axis=-1,
    ).astype(jnp.bfloat16)
    gradients[SELF_QKV] = product(E_BLD_BLE_TO_DE, normed_one, qkv_grad)
    gradients[SELF_QUERY_BIAS] = column_sums(qkv_grad[..., :model_width])
    gradients[SELF_VALUE_BIAS] = column_sums(qkv_grad[..., 2 * model_width :])
    caption_grad = first_grad + norm_back(
        input_values,
        tensors,
        NORM_ONE_GAIN,
        NORM_ONE_SHIFT,
        product(E_BLE_DE_TO_BLD, qkv_grad, tensors[SELF_QKV]),
        gradients,
    )
    flat_grad = pack_rows(gradients, model_width, hidden_width, total_rows)
    shard_rows = total_rows // (data_size * group_size)
    received = lax.all_to_all(
        for_sending(flat_grad), DP, split_axis=0, concat_axis=0, tiled=True
    ).astype(flat_grad.dtype)
    data_grad = jnp.sum(received.reshape(data_size, group_size * shard_rows, 128), axis=0)
    shard_grad = lax.psum_scatter(
        data_grad.astype(jnp.bfloat16), FSDP, scatter_dimension=0, tiled=True
    ).astype(jnp.float32)
    begin_row = lax.axis_index(BOTH) * shard_rows
    seg_starts, seg_ends, decay_flags, seg_entries = segment_table(model_width, hidden_width)
    row_ids = begin_row + jnp.arange(shard_rows)
    member = (row_ids[:, None] >= seg_starts[None, :]) & (row_ids[:, None] < seg_ends[None, :])
    row_squares = jnp.sum(shard_grad * shard_grad, axis=1)
    part_sums = jnp.sum(jnp.where(member, row_squares[:, None], 0.0), axis=0)
    square_sums = lax.psum(part_sums, BOTH)
    old_weights = lax.dynamic_slice_in_dim(back_flat, begin_row, shard_rows, 0).astype(jnp.float32)
    update, new_first, new_second, grad_norm, tensor_rms = adam_step(
        shard_grad,
        member,
        decay_flags,
        old_weights,
        first_moment,
        second_moment,
        square_sums,
        seg_entries,
    )
    return (
        result,
        caption_grad,
        tiles_grad,
        shard_grad,
        update,
        new_first,
        new_second,
        grad_norm,
        tensor_rms,
    )


D = HEADS * HEAD_DIM
NZ = 4
TOK = 128
PATCH = 196
PATCH_SENT = 208
PATCH_SLOT = 256
KEYS = 2 * PATCH_SLOT
LEAD = 80
BF, F32 = jnp.bfloat16, jnp.float32
MESH = pl.DeviceIdType.MESH
SHARD, PIECES, PIECE = 2312, 5, 464
OLD = 2320
PADDED = PIECES * PIECE
WINDOW = 8 * SHARD
CARRY = 96
SEGS = 24
QKV_AT, WO_AT, UQ_AT, UKV_AT, UO_AT, WIDE = 0, 2304, 3072, 3840, 5376, 6144
W1_AT, W2_AT = 0, 3072
(V_G1, V_C1, V_BQKV, V_BO, V_G2, V_C2, V_UQ, V_BKV, V_UO, V_G3, V_C3, V_B1, V_B2, V_SUMS) = range(14)


def row_starts():
    starts, at = {}, 0
    for label, shape, _ in layout(D, FF):
        starts[label] = at
        at += int(np.prod(shape)) // 128
    return starts


def mm(a, b):
    return lax.dot_general(a, b, (((1,), (0,)), ((), ())), preferred_element_type=F32)


def mm_nt(a, b):
    return lax.dot_general(a, b, (((1,), (1,)), ((), ())), preferred_element_type=F32)


def mm_tn(a, b):
    return lax.dot_general(a, b, (((0,), (0,)), ((), ())), preferred_element_type=F32)


def al(i, m):
    return pl.multiple_of(i * m, m)


def halves(pair):
    lane = lax.broadcasted_iota(jnp.int32, pair.shape, 1)
    zero = jnp.zeros_like(pair)
    return jnp.concatenate(
        [jnp.where(lane < HEAD_DIM, pair, zero), jnp.where(lane < HEAD_DIM, zero, pair)], axis=0
    )


def joined(stacked):
    n = stacked.shape[0] // 2
    lane = lax.broadcasted_iota(jnp.int32, (n, 128), 1)
    return jnp.where(lane < HEAD_DIM, stacked[:n], stacked[n:])


def normed(v):
    center = v - jnp.mean(v, axis=-1, keepdims=True)
    r = lax.rsqrt(jnp.mean(center * center, axis=-1, keepdims=True) + EPS_NORM)
    return center * r, r


def pair_kernel(
    cap, tiles, d_out, index, valid, length, weights,
    g_out, sums_out, old_out, out, dcap, dtile,
    fw, wide, gf, pc, ps, big1, big2, kv, dkvt, tl, tlT,
    xin, h1, am, h2, q2, a2, sb, rb, dy, t1, h1T, amT, h2T, a2T,
    x1, dx, acc, vec, meta, ob, pfx, pfx_in, carry, dcap_b, dtile_b,
    from_core, from_y, from_x, from_low, from_high, total, sq,
    wsem, gsem, send, recv, core_s, core_r, y_s, y_r, x_s, x_r, up_s, up_r, down_s, down_r, free, sum_s, sum_r,
):
    role = lax.axis_index(FSDP)
    other = 1 - role
    me = lax.axis_index(DP)
    my_z, my_y, my_core = me // 4, (me // 2) % 2, me % 2

    def at_dp(z, y, core):
        return {DP: z * 4 + y * 2 + core, FSDP: role}

    core_peer = at_dp(my_z, my_y, 1 - my_core)
    y_peer = at_dp(my_z, 1 - my_y, my_core)
    x_peer = {DP: me, FSDP: other}
    up_peer = at_dp(jnp.minimum(my_z + 1, NZ - 1), my_y, my_core)
    down_peer = at_dp(jnp.maximum(my_z - 1, 0), my_y, my_core)
    barrier = pltpu.get_barrier_semaphore()
    for peer in (core_peer, y_peer, x_peer):
        pl.semaphore_signal(barrier, inc=1, device_id=peer, device_id_type=MESH)
    for step in range(1, NZ):
        peer = at_dp((my_z + step) % NZ, my_y, my_core)
        pl.semaphore_signal(barrier, inc=1, device_id=peer, device_id_type=MESH)
    row0 = row_starts()

    cuts = [0, 13856, 18480, 23088, 32320, weights.shape[0]]
    loads = []
    for i in range(5):
        n = cuts[i + 1] - cuts[i]
        loads.append(
            pltpu.make_async_copy(
                weights.at[pl.ds(cuts[i], n)], fw.at[pl.ds(LEAD + cuts[i], n)], wsem.at[i]
            )
        )
    for c in loads:
        c.start()

    def to_other(src, dst, k):
        return pltpu.make_async_remote_copy(
            src_ref=src, dst_ref=dst, send_sem=send.at[k], recv_sem=recv.at[k],
            device_id=x_peer, device_id_type=MESH,
        )

    first, later = pl.ds(0, TOK), pl.ds(TOK, TOK)
    copies = dict(
        cap=to_other(cap, xin.at[later], 0),
        tile=to_other(tl.at[pl.ds(0, PATCH_SENT)], tl.at[pl.ds(PATCH_SLOT, PATCH_SENT)], 1),
        meta=to_other(meta.at[0], meta.at[1], 2),
        dy=to_other(d_out, dy.at[first], 3),
        lead=to_other(fw.at[pl.ds(weights.shape[0], LEAD)], fw.at[pl.ds(0, LEAD)], 4),
        out=to_other(t1.at[first], ob, 7),
        pfx=to_other(pfx, pfx_in, 8),
        old=to_other(
            weights.at[pl.ds(pl.multiple_of(((2 * me + other) % 16) * SHARD - 8 * other, 16), OLD)], old_out, 9
        ),
        dcap=to_other(dcap_b, dcap_b, 10),
        dtile=to_other(dtile_b, dtile_b, 11),
    )

    def to_other_half(c, k):
        rows = pl.ds(al(c, TOK), TOK)
        return to_other(sb.at[rows], rb.at[rows], k + c)

    def x2_copy(c):
        return to_other_half(c, 12)

    def dx2_copy(c):
        return to_other_half(c, 14)

    after = PATCH_SLOT + PATCH_SENT
    tl[0:PATCH_SLOT, :] = jnp.zeros((PATCH_SLOT, D), BF)
    tl[after:, :] = jnp.zeros((KEYS - after, D), BF)
    tl[0:PATCH, :] = tiles[...]
    counts = []
    for g in range(2):
        named_by = jnp.int32(0)
        for s in range(index.shape[1]):
            named = jnp.where(index[0, s] == g, jnp.int32(1), jnp.int32(0))
            named_by = named_by + jnp.where(valid[0, s] > 0, named, jnp.int32(0))
        counts.append(named_by)
    rows8 = lax.broadcasted_iota(jnp.int32, (8, 128), 0)
    meta[0] = jnp.where(
        rows8 == 0, counts[0], jnp.where(rows8 == 1, counts[1], length[0])
    ).astype(F32)

    def all_here():
        pl.semaphore_wait(barrier, 3 + NZ - 1)

    def vector(row, at, n, col=0):
        block = fw[pl.ds(at, n // 128), :].astype(F32)
        for j in range(n // 128):
            vec[row : row + 1, col + 128 * j : col + 128 * j + 128] = block[j : j + 1, :]

    def widen(at, k, col, rows=D):
        for j in range(k):
            wide[:, col + 128 * j : col + 128 * j + 128] = fw[pl.ds(at + j, rows, stride=k), :]

    def norm_forward(src, dst, g, c, at=0, n=2 * TOK):
        @pl.loop(0, n // 64, unroll=2)
        def _(i):
            rows = pl.ds(pl.multiple_of(at + 64 * i, 64), 64)
            v, _ = normed(src[rows, :].astype(F32))
            dst[rows, :] = (v * vec[g : g + 1, :D] + vec[c : c + 1, :D]).astype(BF)

    def norm_backward(src, dh, g, write, at=0, n=2 * TOK):
        def step(i, sums):
            rows = pl.ds(pl.multiple_of(at + 64 * i, 64), 64)
            v, r = normed(src[rows, :].astype(F32))
            d = dh[rows, :]
            dn = d * vec[g : g + 1, :D]
            dv = r * (
                dn - jnp.mean(dn, axis=-1, keepdims=True) - v * jnp.mean(dn * v, axis=-1, keepdims=True)
            )
            write(rows, dv)
            return (
                sums[0] + jnp.sum(d * v, axis=0, keepdims=True),
                sums[1] + jnp.sum(d, axis=0, keepdims=True),
            )

        return lax.fori_loop(0, n // 64, step, (jnp.zeros((1, D), F32), jnp.zeros((1, D), F32)), unroll=2)

    def put_vector(at, row, into=gf):
        for j in range(row.shape[1] // 128):
            into[at + j : at + j + 1, :] = row[:, 128 * j : 128 * j + 128]

    def column_total(ref, cols):
        return jnp.sum(ref[:, cols].astype(F32), axis=0, keepdims=True)

    def matrix_grad(at, k, lhs_t, rhs, transposed=False):
        @pl.loop(0, k // 2, unroll=3)
        def _(m):
            cols = pl.ds(al(m, 256), 256)
            res = mm_nt(lhs_t[...], rhs[cols, :]) if transposed else mm(lhs_t[...], rhs[:, cols])
            for half in range(2):
                gf[pl.ds(at + 2 * m + half, D, stride=k), :] = res[:, 128 * half : 128 * half + 128]

    def copy_to(peer, src, dst, ssem, rsem):
        return pltpu.make_async_remote_copy(
            src_ref=src, dst_ref=dst, send_sem=ssem, recv_sem=rsem, device_id=peer, device_id_type=MESH
        )

    def slot(w, s, core, y=0, x=0):
        return pl.multiple_of(((w * PIECES + s) * 8 + core * 4 + y * 2 + x) * PIECE, 16)

    class Scatter:
        def __init__(self, w, x):
            self.w, self.x = w, x

        def core(self, s):
            rows = pl.ds(slot(self.w, s, 1 - my_core), 4 * PIECE)
            return copy_to(core_peer, fw.at[rows], from_core.at[s], core_s.at[self.w, s], core_r.at[self.w, s])

        def y(self, s):
            rows = pl.ds(slot(self.w, s, my_core, 1 - my_y), 2 * PIECE)
            return copy_to(y_peer, fw.at[rows], from_y.at[self.w, s], y_s.at[self.w, s], y_r.at[self.w, s])

        def over(self, s):
            rows = pl.ds(slot(self.w, s, my_core, my_y, 1 - self.x), PIECE)
            return copy_to(x_peer, fw.at[rows], from_x.at[self.w, s], x_s.at[self.w, s], x_r.at[self.w, s])

        def held(self, s, h):
            if h == self.x:
                return fw.at[pl.ds(slot(self.w, s, my_core, my_y, self.x), PIECE)]
            return from_x.at[self.w, s]

        def up(self, s, h):
            return copy_to(
                up_peer, self.held(s, h), from_low.at[self.w, s, h], up_s.at[self.w, s, h], up_r.at[self.w, s, h]
            )

        def down(self, s, h):
            return copy_to(
                down_peer, self.held(s, h), from_high.at[self.w, s, h], down_s.at[self.w, s, h], down_r.at[self.w, s, h]
            )

        def cast(self, first_row):
            @pl.loop(0, PIECES)
            def _(s):
                for k in range(8):
                    j = (k & 2) * 2 + (k & 4) // 2 + (k & 1)
                    src = pl.ds(pl.multiple_of(first_row + j * SHARD + s * PIECE, 8), PIECE)
                    fw[pl.ds(pl.multiple_of(slot(self.w, s, 0) + k * PIECE, 16), PIECE), :] = gf[src, :].astype(BF)
                self.core(s).start()

        def add_core(self):
            @pl.loop(0, PIECES)
            def _(s):
                self.core(s).wait_recv()
                rows = pl.ds(slot(self.w, s, my_core), 4 * PIECE)
                fw[rows, :] = fw[rows, :] + from_core[s]
                self.y(s).start()

        def add_y(self, s):
            self.y(s).wait_recv()
            rows = pl.ds(slot(self.w, s, my_core, my_y), 2 * PIECE)
            fw[rows, :] = fw[rows, :] + from_y[self.w, s]
            self.over(s).start()

        def from_ends(self, s, h):
            if h != self.x:
                self.over(s).wait_recv()
            goal = 2 * h + self.w
            if goal > 0:
                pl.when(my_z == 0)(self.up(s, h).start)
            if goal < NZ - 1:
                pl.when(my_z == NZ - 1)(self.down(s, h).start)

        def relay(self, s, hop, h):
            goal = 2 * h + self.w
            mine = self.held(s, h)
            if hop < goal:

                @pl.when(my_z == hop)
                def _():
                    self.up(s, h).wait_recv()
                    mine[...] = mine[...] + from_low[self.w, s, h]
                    self.up(s, h).start()

            if NZ - 1 - hop > goal:

                @pl.when(my_z == NZ - 1 - hop)
                def _():
                    self.down(s, h).wait_recv()
                    mine[...] = mine[...] + from_high[self.w, s, h]
                    self.down(s, h).start()

        def step(self, t):
            own, came = self.x, 1 - self.x
            parts = [
                (3, lambda s: self.relay(s, 2, came)),
                (2, lambda s: self.relay(s, 2, own)),
                (2, lambda s: self.relay(s, 1, came)),
                (1, lambda s: self.relay(s, 1, own)),
                (1, lambda s: self.from_ends(s, came)),
                (0, self.add_y),
                (0, lambda s: self.from_ends(s, own)),
            ]
            for lag, part in parts:
                s = t - lag
                if isinstance(t, int):
                    if 0 <= s < PIECES:
                        part(s)
                else:
                    pl.when((s >= 0) & (s < PIECES))(functools.partial(part, s))

        def collect(self, s):
            for h in range(2):
                goal = 2 * h + self.w

                @pl.when(my_z == goal)
                def _():
                    whole = self.held(s, h)[...].astype(F32)
                    if goal > 0:
                        self.up(s, h).wait_recv()
                        whole = whole + from_low[self.w, s, h].astype(F32)
                    if goal < NZ - 1:
                        self.down(s, h).wait_recv()
                        whole = whole + from_high[self.w, s, h].astype(F32)
                    total[pl.ds(pl.multiple_of(s * PIECE, 8), PIECE), :] = whole

        def sent(self):
            @pl.loop(0, PIECES)
            def _(s):
                self.core(s).wait_send()
                self.y(s).wait_send()
                self.over(s).wait_send()
                for h in range(2):
                    goal = 2 * h + self.w
                    pl.when(my_z < goal)(self.up(s, h).wait_send)
                    pl.when(my_z > goal)(self.down(s, h).wait_send)

    def rest_of_scatter(one, zero, begun):
        @pl.loop(begun, 2 * PIECES + 3)
        def _(t):
            one.step(t)
            zero.step(t - PIECES)

        pl.loop(0, PIECES)(one.collect)
        pl.loop(0, PIECES)(zero.collect)
        one.sent()
        zero.sent()

    def square_sums():
        total[SHARD:, :] = jnp.zeros((total.shape[0] - SHARD, 128), F32)
        done = pltpu.make_async_copy(total.at[pl.ds(0, SHARD)], g_out, gsem)
        done.start()
        seg = lax.broadcasted_iota(jnp.int32, (SEGS, 1), 0)
        begin = jnp.full((SEGS, 1), 1 << 30, jnp.int32)
        end = begin
        for i, (a, b) in enumerate(zip(*segment_table(D, FF)[:2])):
            begin = jnp.where(seg == i, int(a), begin)
            end = jnp.where(seg == i, int(b), end)
        row = (me * 2 + role) * SHARD + lax.broadcasted_iota(jnp.int32, (SEGS, total.shape[0]), 1)
        member = jnp.where((row >= begin) & (row < end), 1.0, 0.0).astype(BF)
        square = total[...] * total[...]
        high = square.astype(BF)
        squares = mm(member, high) + mm(member, (square - high.astype(F32)).astype(BF))
        mine = jnp.broadcast_to(jnp.sum(squares, axis=1, keepdims=True), (SEGS, 128))
        for i, peer in enumerate((core_peer, y_peer, x_peer)):
            sq[2 * i] = mine
            swap = copy_to(peer, sq.at[2 * i], sq.at[2 * i + 1], sum_s.at[i], sum_r.at[i])
            swap.start()
            swap.wait()
            mine = mine + sq[2 * i + 1]
        sq[6] = mine
        sends = []
        for step in range(1, NZ):
            to = at_dp((my_z + step) % NZ, my_y, my_core)
            sends.append(copy_to(to, sq.at[6], sq.at[6 + step], sum_s.at[2 + step], sum_r.at[2 + step]))
            sends[-1].start()
        for c in sends:
            c.wait()
        whole = jnp.zeros((SEGS, 128), F32)
        for z in range(NZ):
            part = mine
            for step in range(1, NZ):
                part = jnp.where((my_z - step + NZ) % NZ == z, sq[6 + step], part)
            whole = whole + part
        sums_out[...] = whole
        done.wait()

    def attention_role():
        at = {k: LEAD + v for k, v in row0.items()}
        at0 = {k: CARRY + v for k, v in row0.items()}
        at1 = {k: CARRY - WINDOW + v for k, v in row0.items()}
        one, zero = Scatter(1, 0), Scatter(0, 0)
        xin[first, :] = cap[...]
        loads[0].wait()
        vector(V_G1, at[NORM_ONE_GAIN], D)
        vector(V_C1, at[NORM_ONE_SHIFT], D)
        vec[V_BQKV : V_BQKV + 1, :] = jnp.zeros((1, FF), F32)
        vec[V_BKV : V_BKV + 1, :] = jnp.zeros((1, FF), F32)
        vector(V_BQKV, at[SELF_QUERY_BIAS], D)
        vector(V_BQKV, at[SELF_VALUE_BIAS], D, 2 * D)
        widen(at[SELF_QKV], 18, QKV_AT)
        for c in loads[1:]:
            c.wait()
        vector(V_BO, at[SELF_OUT_BIAS], D)
        vector(V_G2, at[NORM_TWO_GAIN], D)
        vector(V_C2, at[NORM_TWO_SHIFT], D)
        vector(V_UQ, at[CROSS_QUERY_BIAS], D)
        vector(V_BKV, at[CROSS_VALUE_BIAS], D, D)
        vector(V_UO, at[CROSS_OUT_BIAS], D)
        widen(at[SELF_OUT], 6, WO_AT)
        widen(at[CROSS_QUERY], 6, UQ_AT)
        widen(at[CROSS_KV], 12, UKV_AT)
        widen(at[CROSS_OUT], 6, UO_AT)
        all_here()
        copies["dy"].start()
        copies["lead"].start()

        copies["cap"].wait_recv()
        norm_forward(xin, h1, V_G1, V_C1)

        for j in range(3):
            cols = slice(D * j, D * j + D)
            big1[:, cols] = (mm(h1[...], wide[:, cols]) + vec[V_BQKV : V_BQKV + 1, cols]).astype(BF)

        copies["meta"].wait_recv()

        @pl.loop(0, 12, unroll=6)
        def _(i):
            c, p = i // 6, i % 6
            rows = pl.ds(al(c, TOK), TOK)
            qq = halves(big1[rows, pl.ds(al(p, 128), 128)]) * BF(0.125)
            k2 = big1[rows, pl.ds(al(p, 128) + D, 128)]
            v2 = big1[rows, pl.ds(al(p, 128) + 2 * D, 128)]
            s = mm_nt(qq, k2)
            row = lax.broadcasted_iota(jnp.int32, s.shape, 0) % TOK
            col = lax.broadcasted_iota(jnp.int32, s.shape, 1)
            present = col.astype(F32) < meta[c][2:3, :]
            s = jnp.where((col <= row) & present, s, NEG_LARGE)
            e = jnp.exp(s - jnp.max(s, axis=-1, keepdims=True))
            prob = (e * (1.0 / jnp.sum(e, axis=-1, keepdims=True))).astype(BF)
            ps[i] = prob
            am[rows, pl.ds(al(p, 128), 128)] = joined(mm(prob, v2)).astype(BF)

        x1[...] = xin[...].astype(F32) + mm(am[...], wide[:, WO_AT : WO_AT + D]) + vec[V_BO : V_BO + 1, :D]
        norm_forward(x1, h2, V_G2, V_C2)
        q2[...] = (mm(h2[...], wide[:, UQ_AT : UQ_AT + D]) + vec[V_UQ : V_UQ + 1, :D]).astype(BF)
        copies["tile"].wait_recv()

        for j in range(2):
            cols = slice(D * j, D * j + D)
            kv[:, cols] = (
                mm(tl[...], wide[:, UKV_AT + D * j : UKV_AT + D * j + D]) + vec[V_BKV : V_BKV + 1, cols]
            ).astype(BF)

        @pl.loop(0, 2)
        def _(c):
            rows = pl.ds(al(c, TOK), TOK)
            col = lax.broadcasted_iota(jnp.int32, (1, KEYS), 1)
            m = meta[c]
            c0 = jnp.concatenate([m[0:1, :]] * (KEYS // 128), axis=1)
            c1 = jnp.concatenate([m[1:2, :]] * (KEYS // 128), axis=1)
            count = jnp.where(col < PATCH, c0, jnp.where(col < PATCH_SLOT, 0.0, c1))
            count = jnp.where(col < PATCH_SLOT + PATCH, count, 0.0)

            @pl.loop(0, 6, unroll=6)
            def _(p):
                qq = halves(q2[rows, pl.ds(al(p, 128), 128)]) * BF(0.125)
                s = mm_nt(qq, kv[:, pl.ds(al(p, 128), 128)])
                s = jnp.where(count > 0.0, s, NEG_LARGE)
                e = jnp.exp(s - jnp.max(s, axis=-1, keepdims=True)) * count
                prob = (e * (1.0 / jnp.sum(e, axis=-1, keepdims=True))).astype(BF)
                pc[pl.ds(al(6 * c + p, 2 * TOK), 2 * TOK), :] = prob
                a2[rows, pl.ds(al(p, 128), 128)] = joined(
                    mm(prob, kv[:, pl.ds(al(p, 128) + D, 128)])
                ).astype(BF)

            sb[rows, :] = (
                x1[rows, :] + mm(a2[rows, :], wide[:, UO_AT : UO_AT + D]) + vec[V_UO : V_UO + 1, :D]
            ).astype(BF)
            x2_copy(c).start()

        copies["old"].start()

        h1T[...] = h1[...].T
        amT[...] = am[...].T
        h2T[...] = h2[...].T
        a2T[...] = a2[...].T
        tlT[...] = tl[...].T

        part_at = at1[CROSS_KV]

        def attend_back(c, p, take_keys):
            rows = pl.ds(c * TOK, TOK)
            lanes, vlanes = pl.ds(al(p, 128), 128), pl.ds(al(p, 128) + D, 128)
            qq = halves(q2[rows, lanes]) * BF(0.125)
            do = halves(t1[rows, lanes])
            prob = pc[pl.ds(al(6 * c + p, 2 * TOK), 2 * TOK), :]
            pf = prob.astype(F32)
            dp = mm_nt(do, kv[:, vlanes])
            ds = (pf * (dp - jnp.sum(pf * dp, axis=-1, keepdims=True))).astype(BF)
            am[rows, lanes] = (joined(mm(ds, kv[:, lanes])) * 0.125).astype(BF)
            take_keys(p, 0, lanes, mm_tn(qq, ds))
            take_keys(p, 1, vlanes, mm_tn(do, prob))

        def part_rows(p, k, j):
            return pl.ds(pl.multiple_of(part_at + ((2 * p + k) * 4 + j) * 128, 8), 128)

        def keep(p, k, lanes, term):
            for j in range(4):
                gf[part_rows(p, k, j), :] = term[:, 128 * j : 128 * j + 128]

        def complete(p, k, lanes, term):
            for j in range(4):
                cols = slice(128 * j, 128 * j + 128)
                dkvt[lanes, cols] = (gf[part_rows(p, k, j), :] + term[:, cols]).astype(BF)

        for c, take_keys in enumerate((keep, complete)):
            rows = pl.ds(c * TOK, TOK)
            dx2_copy(c).wait_recv()
            t1[rows, :] = mm_nt(rb[rows, :], wide[:, UO_AT : UO_AT + D]).astype(BF)
            pl.loop(0, 6, unroll=6)(functools.partial(attend_back, c, take_keys=take_keys))

        put_vector(at1[CROSS_OUT_BIAS], column_total(rb, slice(None)))
        matrix_grad(at1[CROSS_OUT], 6, a2T, rb)
        put_vector(at1[CROSS_QUERY_BIAS], column_total(am, slice(None)))
        matrix_grad(at1[CROSS_QUERY], 6, h2T, am)
        matrix_grad(at1[CROSS_KV], 12, tlT, dkvt, transposed=True)
        kv[...] = dkvt[...].T
        put_vector(at1[CROSS_VALUE_BIAS], column_total(kv, slice(D, 2 * D)))
        copies["pfx"].wait_recv()
        gf[pl.ds(at1[NORM_THREE_GAIN], LEAD - 12), :] = pfx_in[12:, :]
        copies["lead"].wait_send()
        one.cast(CARRY)
        carry[...] = gf[0:CARRY, :]

        def tile_grad(rows):
            return mm_nt(kv[rows, :], wide[:, UKV_AT : UKV_AT + 2 * D])

        dtile[...] = tile_grad(pl.ds(0, PATCH_SENT))[:PATCH]
        dtile_b[...] = tile_grad(pl.ds(PATCH_SLOT, PATCH_SENT)).astype(BF)
        copies["dtile"].start()
        one.add_core()
        pl.semaphore_signal(free, inc=1, device_id=core_peer, device_id_type=MESH)
        acc[...] = mm_nt(am[...], wide[:, UQ_AT : UQ_AT + D])
        e1 = h2

        def write_dx1(rows, dv):
            full = rb[rows, :].astype(F32) + dv
            dx[rows, :] = full
            e1[rows, :] = full.astype(BF)

        gg, gc = norm_backward(x1, acc, V_G2, write_dx1)
        put_vector(at0[NORM_TWO_GAIN], gg)
        put_vector(at0[NORM_TWO_SHIFT], gc)
        put_vector(at0[SELF_OUT_BIAS], column_total(e1, slice(None)))
        matrix_grad(at0[SELF_OUT], 6, amT, e1)
        t1[...] = mm_nt(e1[...], wide[:, WO_AT : WO_AT + D]).astype(BF)

        @pl.loop(0, 12, unroll=6)
        def _(i):
            c, p = i // 6, i % 6
            rows = pl.ds(al(c, TOK), TOK)
            lanes = pl.ds(al(p, 128), 128)
            klanes, vlanes = pl.ds(al(p, 128) + D, 128), pl.ds(al(p, 128) + 2 * D, 128)
            qq = halves(big1[rows, lanes]) * BF(0.125)
            do = halves(t1[rows, lanes])
            prob = ps[i]
            pf = prob.astype(F32)
            dp = mm_nt(do, big1[rows, vlanes])
            ds = (pf * (dp - jnp.sum(pf * dp, axis=-1, keepdims=True))).astype(BF)
            big2[rows, lanes] = (joined(mm(ds, big1[rows, klanes])) * 0.125).astype(BF)
            big2[rows, klanes] = mm_tn(ds, qq).astype(BF)
            big2[rows, vlanes] = mm_tn(prob, do).astype(BF)

        one.step(0)
        acc[...] = mm_nt(big2[:, : 3 * D], wide[:, : 3 * D])

        def write_dx0(rows, dv):
            dx[rows, :] = dx[rows, :] + dv

        gg, gc = norm_backward(xin, acc, V_G1, write_dx0)
        put_vector(at0[NORM_ONE_GAIN], gg)
        put_vector(at0[NORM_ONE_SHIFT], gc)
        dcap[...] = dx[first, :]
        dcap_b[...] = dx[later, :].astype(BF)
        copies["dcap"].start()
        one.step(1)
        put_vector(at0[SELF_QUERY_BIAS], column_total(big2, slice(0, D)))
        put_vector(at0[SELF_VALUE_BIAS], column_total(big2, slice(2 * D, 3 * D)))
        matrix_grad(at0[SELF_QKV], 18, h1T, big2)
        gf[pl.ds(at0[CROSS_QUERY], WINDOW - row0[CROSS_QUERY]), :] = carry[
            row0[CROSS_QUERY] - WINDOW + CARRY :, :
        ]
        pl.semaphore_wait(free, 1)
        zero.cast(CARRY)
        zero.add_core()
        rest_of_scatter(one, zero, 2)
        copies["out"].wait_recv()
        out[...] = ob[...]
        for name in ("dy", "dcap", "dtile"):
            copies[name].wait_send()
        for c in range(2):
            x2_copy(c).wait_send()
        copies["old"].wait()
        square_sums()

    def mlp_role():
        all_here()
        copies["meta"].start()
        copies["cap"].start()
        copies["cap"].wait_send()
        copies["tile"].start()
        base = LEAD - weights.shape[0]
        at = {k: base + v for k, v in row0.items()}
        at0 = {k: CARRY - weights.shape[0] + v for k, v in row0.items()}
        at1 = {k: v - WINDOW for k, v in at0.items()}
        one, zero = Scatter(1, 1), Scatter(0, 1)
        dy[later, :] = d_out[...]
        for c in loads:
            c.wait()
        for b in range(4):
            widen(at[MLP_DOWN] + 6 * D * b, 6, W2_AT + D * b)
        copies["lead"].wait_recv()
        widen(at[MLP_UP], 24, W1_AT)
        vector(V_G3, at[NORM_THREE_GAIN], D)
        vector(V_C3, at[NORM_THREE_SHIFT], D)
        vector(V_B1, at[MLP_UP_BIAS], FF)
        vector(V_B2, at[MLP_DOWN_BIAS], D)
        copies["dy"].wait_recv()

        @pl.loop(0, 4)
        def _(b):
            dg = mm_nt(dy[...], wide[:, pl.ds(al(b, D) + W2_AT, D)])
            for j in range(6):
                gf[pl.ds(al(6 * b + j, 256), 256), :] = dg[:, 128 * j : 128 * j + 128]

        def write_dx2(rows, dv):
            sb[rows, :] = (dy[rows, :].astype(F32) + dv).astype(BF)

        vec[V_SUMS : V_SUMS + 2, :] = jnp.zeros((2, FF), F32)

        @pl.loop(0, 2)
        def _(c):
            cap_rows = pl.ds(al(c, TOK), TOK)
            x2_copy(c).wait_recv()
            norm_forward(rb, h1, V_G3, V_C3, c * TOK, TOK)
            z_parts = [x1.at[first], x1.at[later], dx.at[first], dx.at[later]]
            for b in range(4):
                cols = slice(D * b, D * b + D)
                z_parts[b][...] = mm(h1[cap_rows, :], wide[:, cols]) + vec[V_B1 : V_B1 + 1, cols]

            @pl.loop(0, 4)
            def _(i):
                here = pl.ds(al(i, 32), 32)
                rows = pl.ds(al(c, TOK) + al(i, 32), 32)
                for k in range(24):
                    z = z_parts[k // 6][here, 128 * (k % 6) : 128 * (k % 6) + 128]
                    phi = 0.5 + 0.5 * lax.erf(z * np.float32(np.sqrt(0.5)))
                    dens = jnp.exp(-0.5 * z * z) * np.float32(1.0 / np.sqrt(2.0 * np.pi))
                    lanes = slice(128 * k, 128 * k + 128)
                    big1[rows, lanes] = (z * phi).astype(BF)
                    dg = gf[pl.ds(256 * k + al(c, TOK) + al(i, 32), 32), :]
                    big2[rows, lanes] = (dg * (phi + z * dens)).astype(BF)

            acc[cap_rows, :] = mm_nt(big2[cap_rows, :], wide[:, W1_AT : W1_AT + FF])
            gg, gc = norm_backward(rb, acc, V_G3, write_dx2, c * TOK, TOK)
            vec[V_SUMS : V_SUMS + 1, :D] = vec[V_SUMS : V_SUMS + 1, :D] + gg
            vec[V_SUMS + 1 : V_SUMS + 2, :D] = vec[V_SUMS + 1 : V_SUMS + 2, :D] + gc
            dx2_copy(c).start()

        put_vector(12, vec[V_SUMS : V_SUMS + 1, :D], pfx)
        put_vector(18, vec[V_SUMS + 1 : V_SUMS + 2, :D], pfx)

        h1T[...] = h1[...].T
        pfx[0:12, :] = jnp.zeros((12, 128), F32)
        for b in range(4):
            head = mm(h1T[0:8, :], big2[:, D * b : D * b + D])
            for r in range(3):
                for j in range(6):
                    row = 24 + 24 * r + 6 * b + j
                    if row < LEAD:
                        pfx[row : row + 1, :] = head[r : r + 1, 128 * j : 128 * j + 128]
        copies["pfx"].start()
        copies["old"].start()

        acc[...] = rb[...].astype(F32) + vec[V_B2 : V_B2 + 1, :D]
        for b in range(4):
            cols = slice(D * b, D * b + D)
            acc[...] = acc[...] + mm(big1[:, cols], wide[:, W2_AT + D * b : W2_AT + D * b + D])
            pc[D * b : D * b + D, 0:256] = big1[:, cols].T

        t1[first, :] = acc[first, :].astype(BF)
        copies["out"].start()
        out[...] = acc[later, :].astype(BF)
        gf[pl.ds(at1[MLP_DOWN_BIAS] + 6, WINDOW + CARRY - at1[MLP_DOWN_BIAS] - 6), :] = jnp.zeros(
            (WINDOW + CARRY - at1[MLP_DOWN_BIAS] - 6, 128), F32
        )
        put_vector(at1[MLP_DOWN_BIAS], column_total(dy, slice(None)))
        for b in range(4):
            matrix_grad(at1[MLP_DOWN] + 6 * D * b, 6, pc.at[pl.ds(D * b, D), pl.ds(0, 256)], dy)
        one.cast(CARRY)
        carry[...] = gf[0:CARRY, :]
        put_vector(at0[MLP_UP_BIAS], column_total(big2, slice(None)))
        matrix_grad(at0[MLP_UP], 24, h1T, big2)
        one.add_core()
        pl.semaphore_signal(free, inc=1, device_id=core_peer, device_id_type=MESH)
        gf[pl.ds(at0[MLP_DOWN], CARRY), :] = carry[...]
        pl.semaphore_wait(free, 1)
        zero.cast(CARRY)
        zero.add_core()
        rest_of_scatter(one, zero, 0)
        copies["dtile"].wait_recv()
        dtile[...] = dtile_b[0:PATCH, :].astype(F32)
        copies["dcap"].wait_recv()
        dcap[...] = dcap_b[...].astype(F32)
        for name in ("tile", "meta", "pfx", "out"):
            copies[name].wait_send()
        for c in range(2):
            dx2_copy(c).wait_send()
        copies["old"].wait()
        square_sums()

    pl.when(role == 0)(attention_role)
    pl.when(role == 1)(mlp_role)


def pair_call(cap, tiles, d_out, index, valid, length, weights):
    vm = pl.BlockSpec(memory_space=pltpu.VMEM)
    sm = pl.BlockSpec(memory_space=pltpu.SMEM)
    hbm = pl.BlockSpec(memory_space=pl.ANY)
    S = jax.ShapeDtypeStruct
    dma, both = pltpu.SemaphoreType.DMA, 2 * TOK

    def bf(*s):
        return pltpu.VMEM(s, BF)

    def fl(*s):
        return pltpu.VMEM(s, F32)

    return pl.pallas_call(
        pair_kernel,
        in_specs=[vm, vm, vm, sm, sm, sm, hbm],
        out_specs=[hbm, vm, hbm, vm, vm, vm],
        out_shape=[
            S((SHARD, 128), F32),
            S((SEGS, 128), F32),
            S((OLD, 128), BF),
            S((TOK, D), BF),
            S((TOK, D), F32),
            S((PATCH, D), F32),
        ],
        scratch_shapes=[
            bf(16 * PADDED, 128), bf(D, WIDE), fl(CARRY + 7 * SHARD + PADDED, 128), bf(12 * both, KEYS),
            bf(12, both, 128), bf(both, FF), bf(both, FF), bf(KEYS, 2 * D), bf(2 * D, KEYS), bf(KEYS, D), bf(D, KEYS),
            *[bf(both, D) for _ in range(10)],
            *[bf(D, both) for _ in range(4)],
            *[fl(both, D) for _ in range(3)],
            fl(16, FF), fl(2, 8, 128), bf(TOK, D), fl(LEAD, 128), fl(LEAD, 128), fl(CARRY, 128),
            bf(TOK, D), bf(PATCH_SENT, D),
            bf(PIECES, 4 * PIECE, 128), bf(2, PIECES, 2 * PIECE, 128), bf(2, PIECES, PIECE, 128),
            bf(2, PIECES, 2, PIECE, 128), bf(2, PIECES, 2, PIECE, 128), fl(2432, 128), fl(10, SEGS, 128),
            dma((5,)), dma, dma((16,)), dma((16,)),
            *[dma((2, PIECES)) for _ in range(6)],
            *[dma((2, PIECES, 2)) for _ in range(4)],
            pltpu.SemaphoreType.REGULAR, dma((6,)), dma((6,)),
        ],
        compiler_params=pltpu.CompilerParams(
            collective_id=0, has_side_effects=True, vmem_limit_bytes=63 * 2**20
        ),
    )(cap, tiles, d_out, index, valid, length, weights)


def finish(shard_grad, old_weights, first_moment, second_moment, square_sums):
    shard_rows = shard_grad.shape[0]
    begin_row = lax.axis_index(BOTH) * shard_rows
    seg_starts, seg_ends, decay_flags, seg_entries = segment_table(D, FF)
    row_ids = begin_row + jnp.arange(shard_rows)
    member = (row_ids[:, None] >= seg_starts[None, :]) & (row_ids[:, None] < seg_ends[None, :])
    return adam_step(
        shard_grad, member, decay_flags, old_weights, first_moment, second_moment, square_sums, seg_entries
    )


def pair_body(
    captions, tiles, tile_index, tile_valid, caption_len, weights, first_moment, second_moment, d_out
):
    me, f = lax.axis_index(DP), lax.axis_index(FSDP)
    shard_grad, sums, old, out, caption_grad, tiles_grad = pair_call(
        captions[0], tiles[0], d_out[0], tile_index, tile_valid, caption_len, weights
    )
    own = lax.dynamic_slice_in_dim(weights, ((2 * me + f) % 16) * SHARD, SHARD, 0)
    old = lax.dynamic_slice_in_dim(old, 8 * f, SHARD, 0)
    old_weights = jnp.where(me // 8 == f, own, old).astype(jnp.float32)
    update, new_first, new_second, grad_norm, tensor_rms = finish(
        shard_grad, old_weights, first_moment, second_moment, sums[:21, 0]
    )
    return (
        out[None], caption_grad[None], tiles_grad[None], shard_grad, update, new_first, new_second,
        grad_norm, tensor_rms,
    )


def solution(mesh):
    placed = (
        P(BOTH, None, None),
        P(BOTH, None, None),
        P(BOTH, None),
        P(BOTH, None),
        P(BOTH),
        P(FSDP, None),
        P(BOTH, None),
        P(BOTH, None),
        P(BOTH, None, None),
    )
    return jax.shard_map(
        pair_body if mesh.shape[FSDP] == 2 else body,
        mesh=mesh,
        in_specs=placed,
        out_specs=(
            P(BOTH, None, None),
            P(BOTH, None, None),
            P(BOTH, None, None),
            P(BOTH, None),
            P(BOTH, None),
            P(BOTH, None),
            P(BOTH, None),
            P(),
            P(),
        ),
        check_vma=False,
    )
```

```python
import functools

import jax
import jax.numpy as jnp
import numpy as np
from jax import lax
from jax.experimental import pallas as pl
from jax.experimental.pallas import tpu as pltpu
from jax.sharding import PartitionSpec as P

HEADS = 12
HEAD_DIM = 64
FF = 3072
STEP = 10


EPS_NORM = 1e-05
CLIP_NORM = 1.0
BETA_ONE = 0.9
BETA_TWO = 0.999
LEARN_RATE = 0.01
DECAY_RATE = 0.1
ADAM_EPS = 1e-08
NEG_LARGE = -1e30
(NORM_ONE_GAIN, NORM_ONE_SHIFT, SELF_QKV, SELF_QUERY_BIAS, SELF_VALUE_BIAS, SELF_OUT, SELF_OUT_BIAS, NORM_TWO_GAIN, NORM_TWO_SHIFT, CROSS_QUERY, CROSS_QUERY_BIAS, CROSS_KV, CROSS_VALUE_BIAS, CROSS_OUT, CROSS_OUT_BIAS, NORM_THREE_GAIN, NORM_THREE_SHIFT, MLP_UP, MLP_UP_BIAS, MLP_DOWN, MLP_DOWN_BIAS) = range(21)
DP, FSDP = "dp", "fsdp"
BOTH = (DP, FSDP)
E_BHQK_BKHE_TO_BQHE = "bhqk,bkhe->bqhe"
E_BHQK_BQHE_TO_BKHE = "bhqk,bqhe->bkhe"
E_BLD_BLE_TO_DE = "bld,ble->de"
E_BLD_BLF_TO_DF = "bld,blf->df"
E_BLD_DE_TO_BLE = "bld,de->ble"
E_BLD_DF_TO_BLF = "bld,df->blf"
E_BLD_FD_TO_BLF = "bld,fd->blf"
E_BLE_DE_TO_BLD = "ble,de->bld"
E_BLF_BLD_TO_FD = "blf,bld->fd"
E_BLF_DF_TO_BLD = "blf,df->bld"
E_BLF_FD_TO_BLD = "blf,fd->bld"
E_BQHE_BKHE_TO_BHQK = "bqhe,bkhe->bhqk"
E_CSG_CSPE_TO_GPE = "csg,cspe->gpe"
E_TPD_DE_TO_TPE = "tpd,de->tpe"
E_TPD_TPE_TO_DE = "tpd,tpe->de"
E_TPE_DE_TO_TPD = "tpe,de->tpd"


def for_sending(x):
    return jax.tree.map(lambda a: a.astype(jnp.bfloat16) if a.dtype == jnp.float32 else a, x)


def layout(model_width, hidden_width):
    return [
        (NORM_ONE_GAIN, (model_width,), 0),
        (NORM_ONE_SHIFT, (model_width,), 0),
        (SELF_QKV, (model_width, 3 * model_width), 1),
        (SELF_QUERY_BIAS, (model_width,), 0),
        (SELF_VALUE_BIAS, (model_width,), 0),
        (SELF_OUT, (model_width, model_width), 1),
        (SELF_OUT_BIAS, (model_width,), 0),
        (NORM_TWO_GAIN, (model_width,), 0),
        (NORM_TWO_SHIFT, (model_width,), 0),
        (CROSS_QUERY, (model_width, model_width), 1),
        (CROSS_QUERY_BIAS, (model_width,), 0),
        (CROSS_KV, (model_width, 2 * model_width), 1),
        (CROSS_VALUE_BIAS, (model_width,), 0),
        (CROSS_OUT, (model_width, model_width), 1),
        (CROSS_OUT_BIAS, (model_width,), 0),
        (NORM_THREE_GAIN, (model_width,), 0),
        (NORM_THREE_SHIFT, (model_width,), 0),
        (MLP_UP, (model_width, hidden_width), 1),
        (MLP_UP_BIAS, (hidden_width,), 0),
        (MLP_DOWN, (hidden_width, model_width), 1),
        (MLP_DOWN_BIAS, (model_width,), 0),
    ]


def segment_table(model_width, hidden_width):
    seg_starts = []
    seg_ends = []
    decay_flags = []
    seg_entries = []
    row_at = 0
    for seg_label, seg_shape, seg_flag in layout(model_width, hidden_width):
        item_count = int(np.prod(seg_shape))
        seg_rows = item_count // 128
        seg_starts.append(row_at)
        seg_ends.append(row_at + seg_rows)
        decay_flags.append(seg_flag == 1)
        seg_entries.append(float(item_count))
        row_at = row_at + seg_rows
    return (np.array(seg_starts), np.array(seg_ends), np.array(decay_flags), np.array(seg_entries))


def unpack(flat_rows, model_width, hidden_width):
    vector = flat_rows.reshape(-1)
    tensors = {}
    offset = 0
    for seg_label, seg_shape, seg_flag in layout(model_width, hidden_width):
        item_count = int(np.prod(seg_shape))
        tensors[seg_label] = vector[offset : offset + item_count].reshape(seg_shape)
        offset = offset + item_count
    return tensors


def pack_rows(gradients, model_width, hidden_width, total_rows):
    pieces = [
        gradients[seg_label].reshape(-1, 128)
        for seg_label, seg_shape, seg_flag in layout(model_width, hidden_width)
    ]
    used_rows = sum((tensor_piece.shape[0] for tensor_piece in pieces))
    pieces.append(jnp.zeros((total_rows - used_rows, 128), jnp.float32))
    return jnp.concatenate(pieces, axis=0)


def product(pattern, left_side, right_side):
    return jnp.einsum(pattern, left_side, right_side, preferred_element_type=jnp.float32)


def as_float(tensors, seg_label):
    return tensors[seg_label].astype(jnp.float32)


def column_sums(values):
    return jnp.sum(values.astype(jnp.float32), axis=tuple(range(values.ndim - 1)))


def layer_norm(values, gain_term, offset_term):
    center = values - jnp.mean(values, axis=-1, keepdims=True)
    spread = jnp.mean(center * center, axis=-1, keepdims=True)
    return center * lax.rsqrt(spread + EPS_NORM) * gain_term + offset_term


def gelu_exact(pre_values):
    return jax.nn.gelu(pre_values, approximate=False)


def norm_back(values, tensors, gain, shift, normed_grad, gradients):
    norm_value, norm_pull = jax.vjp(
        layer_norm,
        values,
        as_float(tensors, gain),
        as_float(tensors, shift),
    )
    values_grad, gain_grad, offset_grad = norm_pull(normed_grad)
    gradients[gain] = gain_grad
    gradients[shift] = offset_grad
    return values_grad


def score_block(queries, key_head_split, allowed):
    scores = product(E_BQHE_BKHE_TO_BHQK, queries, key_head_split) * 0.125
    return jnp.where(allowed, scores, NEG_LARGE)


def softmax_forward(queries, key_head_split, allowed):
    scores = score_block(queries, key_head_split, allowed)
    highest = jnp.max(scores, axis=-1, keepdims=True)
    exponent = jnp.exp(scores - highest)
    row_total = jnp.sum(exponent, axis=-1, keepdims=True)
    return (exponent / row_total, highest + jnp.log(row_total))


def attention_backward_pass(queries, key_head_split, values, allowed, log_total, mixed_grad):
    probabilities = jnp.where(
        allowed, jnp.exp(score_block(queries, key_head_split, allowed) - log_total), 0.0
    )
    probs_grad = product(E_BQHE_BKHE_TO_BHQK, mixed_grad, values)
    values_grad = product(E_BHQK_BQHE_TO_BKHE, probabilities.astype(jnp.bfloat16), mixed_grad)
    inner_sum = jnp.sum(probabilities * probs_grad, axis=-1, keepdims=True)
    score_grad = (probabilities * (probs_grad - inner_sum)).astype(jnp.bfloat16)
    queries_grad = product(E_BHQK_BKHE_TO_BQHE, score_grad, key_head_split) * 0.125
    keys_grad = product(E_BHQK_BQHE_TO_BKHE, score_grad, queries) * 0.125
    return (queries_grad, keys_grad, values_grad)


def adam_step(
    gradients,
    member,
    decay_flags,
    old_weights,
    first_moment,
    second_moment,
    square_sums,
    seg_entries,
):
    grad_norm = jnp.sqrt(jnp.sum(square_sums))
    tensor_rms = jnp.sqrt(square_sums / jnp.asarray(seg_entries, dtype=square_sums.dtype))
    clip_scale = jnp.minimum(1.0, CLIP_NORM / (grad_norm + 1e-06))
    clipped = gradients * clip_scale
    new_first = BETA_ONE * first_moment + (1.0 - BETA_ONE) * clipped
    new_second = BETA_TWO * second_moment + (1.0 - BETA_TWO) * clipped * clipped
    first_hat = new_first / (1.0 - BETA_ONE**STEP)
    second_hat = new_second / (1.0 - BETA_TWO**STEP)
    decay_rows = jnp.any(member & decay_flags[None, :], axis=1)
    decayed = jnp.where(decay_rows[:, None], old_weights, 0.0)
    update = -LEARN_RATE * (first_hat / (jnp.sqrt(second_hat) + ADAM_EPS) + DECAY_RATE * decayed)
    return (update, new_first, new_second, grad_norm, tensor_rms)


def body(
    captions,
    tiles,
    tile_index,
    tile_valid,
    caption_len,
    weights,
    first_moment,
    second_moment,
    d_out,
):
    model_width = captions.shape[2]
    hidden_width = FF
    caption_rows = captions.shape[0]
    cap_length = captions.shape[1]
    patch_count = tiles.shape[1]
    own_tiles = tiles.shape[0]
    slot_count = tile_index.shape[1]
    group_size = lax.axis_size(FSDP)
    data_size = lax.axis_size(DP)
    total_rows = weights.shape[0] * group_size
    heads_shape = (caption_rows, cap_length, HEADS, HEAD_DIM)
    key_shape = (caption_rows, slot_count * patch_count, HEADS, HEAD_DIM)
    token_layout_form = (caption_rows, cap_length, model_width)
    tensors = unpack(lax.all_gather(weights, FSDP, axis=0, tiled=True), model_width, hidden_width)
    zero_part = jnp.zeros((model_width,), jnp.bfloat16)
    input_values = captions.astype(jnp.float32)
    normed_one = layer_norm(
        input_values, as_float(tensors, NORM_ONE_GAIN), as_float(tensors, NORM_ONE_SHIFT)
    ).astype(jnp.bfloat16)
    qkv_bias = jnp.concatenate(
        [tensors[SELF_QUERY_BIAS], zero_part, tensors[SELF_VALUE_BIAS]]
    ).astype(jnp.float32)
    packed_qkv = (product(E_BLD_DE_TO_BLE, normed_one, tensors[SELF_QKV]) + qkv_bias).astype(
        jnp.bfloat16
    )
    self_query = packed_qkv[..., :model_width].reshape(heads_shape)
    self_keys = packed_qkv[..., model_width : 2 * model_width].reshape(heads_shape)
    self_values = packed_qkv[..., 2 * model_width :].reshape(heads_shape)
    positions = jnp.arange(cap_length)
    causal = (positions[None, :] <= positions[:, None])[None, None]
    present = (positions[None, :] < caption_len[:, None])[:, None, None, :]
    self_allowed = causal & present
    self_probs, self_log = softmax_forward(self_query, self_keys, self_allowed)
    self_mixed = (
        product(E_BHQK_BKHE_TO_BQHE, self_probs.astype(jnp.bfloat16), self_values)
        .reshape(token_layout_form)
        .astype(jnp.bfloat16)
    )
    first_sum = (
        input_values
        + product(E_BLD_DE_TO_BLE, self_mixed, tensors[SELF_OUT])
        + as_float(tensors, SELF_OUT_BIAS)
    )
    normed_two = layer_norm(
        first_sum, as_float(tensors, NORM_TWO_GAIN), as_float(tensors, NORM_TWO_SHIFT)
    ).astype(jnp.bfloat16)
    cross_queries = (
        (
            product(E_BLD_DE_TO_BLE, normed_two, tensors[CROSS_QUERY])
            + as_float(tensors, CROSS_QUERY_BIAS)
        )
        .astype(jnp.bfloat16)
        .reshape(heads_shape)
    )
    kv_bias = jnp.concatenate([zero_part, tensors[CROSS_VALUE_BIAS]]).astype(jnp.float32)
    kv_weight = tensors[CROSS_KV]
    group_kv = (
        product(E_TPD_DE_TO_TPE, lax.all_gather(tiles, FSDP, axis=0, tiled=True), kv_weight)
        + kv_bias
    ).astype(jnp.bfloat16)
    chosen = jnp.stack(
        [
            jnp.stack(
                [
                    lax.dynamic_index_in_dim(group_kv, tile_index[c, s], 0, keepdims=False)
                    for s in range(slot_count)
                ]
            )
            for c in range(caption_rows)
        ]
    )
    cross_keys = chosen[..., :model_width].reshape(key_shape)
    cross_values = chosen[..., model_width:].reshape(key_shape)
    usable = jnp.repeat(tile_valid > 0, patch_count, axis=1)[:, None, None, :]
    cross_probs, cross_log = softmax_forward(cross_queries, cross_keys, usable)
    cross_mixed = (
        product(E_BHQK_BKHE_TO_BQHE, cross_probs.astype(jnp.bfloat16), cross_values)
        .reshape(token_layout_form)
        .astype(jnp.bfloat16)
    )
    second = (
        first_sum
        + product(E_BLD_DE_TO_BLE, cross_mixed, tensors[CROSS_OUT])
        + as_float(tensors, CROSS_OUT_BIAS)
    )
    normed_three = layer_norm(
        second, as_float(tensors, NORM_THREE_GAIN), as_float(tensors, NORM_THREE_SHIFT)
    ).astype(jnp.bfloat16)
    preact = product(E_BLD_DF_TO_BLF, normed_three, tensors[MLP_UP]) + as_float(
        tensors, MLP_UP_BIAS
    )
    activation = gelu_exact(preact).astype(jnp.bfloat16)
    result = (
        second
        + product(E_BLF_FD_TO_BLD, activation, tensors[MLP_DOWN])
        + as_float(tensors, MLP_DOWN_BIAS)
    ).astype(jnp.bfloat16)
    back_flat = lax.all_gather(weights, FSDP, axis=0, tiled=True)
    tensors = unpack(back_flat, model_width, hidden_width)
    gradients = {}
    out_grad = d_out.astype(jnp.float32)
    gradients[MLP_DOWN] = product(E_BLF_BLD_TO_FD, activation, d_out)
    gradients[MLP_DOWN_BIAS] = column_sums(d_out)
    activ_grad = product(E_BLD_FD_TO_BLF, d_out, tensors[MLP_DOWN])
    gelu_value, gelu_pull = jax.vjp(gelu_exact, preact)
    preact_grad = gelu_pull(activ_grad)[0].astype(jnp.bfloat16)
    gradients[MLP_UP] = product(E_BLD_BLF_TO_DF, normed_three, preact_grad)
    gradients[MLP_UP_BIAS] = column_sums(preact_grad)
    second_grad = out_grad + norm_back(
        second,
        tensors,
        NORM_THREE_GAIN,
        NORM_THREE_SHIFT,
        product(E_BLF_DF_TO_BLD, preact_grad, tensors[MLP_UP]),
        gradients,
    )
    cross_branch = second_grad.astype(jnp.bfloat16)
    gradients[CROSS_OUT] = product(E_BLD_BLE_TO_DE, cross_mixed, cross_branch)
    gradients[CROSS_OUT_BIAS] = column_sums(cross_branch)
    cmixed_grad = (
        product(E_BLE_DE_TO_BLD, cross_branch, tensors[CROSS_OUT])
        .astype(jnp.bfloat16)
        .reshape(heads_shape)
    )
    cquery_grad, ckeys_grad, cvalues_grad = attention_backward_pass(
        cross_queries, cross_keys, cross_values, usable, cross_log, cmixed_grad
    )
    cquery_low = cquery_grad.astype(jnp.bfloat16).reshape(token_layout_form)
    gradients[CROSS_QUERY] = product(E_BLD_BLE_TO_DE, normed_two, cquery_low)
    gradients[CROSS_QUERY_BIAS] = column_sums(cquery_low)
    first_grad = second_grad + norm_back(
        first_sum,
        tensors,
        NORM_TWO_GAIN,
        NORM_TWO_SHIFT,
        product(E_BLE_DE_TO_BLD, cquery_low, tensors[CROSS_QUERY]),
        gradients,
    )
    slot_layout_form = (caption_rows, slot_count, patch_count, model_width)
    slot_grad = jnp.concatenate(
        [ckeys_grad.reshape(slot_layout_form), cvalues_grad.reshape(slot_layout_form)], axis=-1
    )
    picked = (tile_index[:, :, None] == jnp.arange(group_kv.shape[0])[None, None, :]).astype(
        jnp.float32
    )
    group_grad = jnp.einsum(E_CSG_CSPE_TO_GPE, picked, slot_grad, precision=lax.Precision.HIGHEST)
    arrived = lax.all_to_all(
        group_grad.astype(jnp.bfloat16), FSDP, split_axis=0, concat_axis=0, tiled=True
    ).astype(group_grad.dtype)
    own_grad = jnp.sum(arrived.reshape((group_size, own_tiles) + arrived.shape[1:]), axis=0).astype(
        jnp.bfloat16
    )
    gradients[CROSS_KV] = product(E_TPD_TPE_TO_DE, tiles, own_grad)
    gradients[CROSS_VALUE_BIAS] = column_sums(own_grad[..., model_width:])
    tiles_grad = product(E_TPE_DE_TO_TPD, own_grad, tensors[CROSS_KV])
    self_branch = first_grad.astype(jnp.bfloat16)
    gradients[SELF_OUT] = product(E_BLD_BLE_TO_DE, self_mixed, self_branch)
    gradients[SELF_OUT_BIAS] = column_sums(self_branch)
    smixed_grad = (
        product(E_BLE_DE_TO_BLD, self_branch, tensors[SELF_OUT])
        .astype(jnp.bfloat16)
        .reshape(heads_shape)
    )
    self_query_gradient, self_key_gradient, self_value_gradient = attention_backward_pass(
        self_query, self_keys, self_values, self_allowed, self_log, smixed_grad
    )
    qkv_grad = jnp.concatenate(
        [
            self_query_gradient.reshape(token_layout_form),
            self_key_gradient.reshape(token_layout_form),
            self_value_gradient.reshape(token_layout_form),
        ],
        axis=-1,
    ).astype(jnp.bfloat16)
    gradients[SELF_QKV] = product(E_BLD_BLE_TO_DE, normed_one, qkv_grad)
    gradients[SELF_QUERY_BIAS] = column_sums(qkv_grad[..., :model_width])
    gradients[SELF_VALUE_BIAS] = column_sums(qkv_grad[..., 2 * model_width :])
    caption_grad = first_grad + norm_back(
        input_values,
        tensors,
        NORM_ONE_GAIN,
        NORM_ONE_SHIFT,
        product(E_BLE_DE_TO_BLD, qkv_grad, tensors[SELF_QKV]),
        gradients,
    )
    flat_grad = pack_rows(gradients, model_width, hidden_width, total_rows)
    shard_rows = total_rows // (data_size * group_size)
    received = lax.all_to_all(
        for_sending(flat_grad), DP, split_axis=0, concat_axis=0, tiled=True
    ).astype(flat_grad.dtype)
    data_grad = jnp.sum(received.reshape(data_size, group_size * shard_rows, 128), axis=0)
    shard_grad = lax.psum_scatter(
        data_grad.astype(jnp.bfloat16), FSDP, scatter_dimension=0, tiled=True
    ).astype(jnp.float32)
    begin_row = lax.axis_index(BOTH) * shard_rows
    seg_starts, seg_ends, decay_flags, seg_entries = segment_table(model_width, hidden_width)
    row_ids = begin_row + jnp.arange(shard_rows)
    member = (row_ids[:, None] >= seg_starts[None, :]) & (row_ids[:, None] < seg_ends[None, :])
    row_squares = jnp.sum(shard_grad * shard_grad, axis=1)
    part_sums = jnp.sum(jnp.where(member, row_squares[:, None], 0.0), axis=0)
    square_sums = lax.psum(part_sums, BOTH)
    old_weights = lax.dynamic_slice_in_dim(back_flat, begin_row, shard_rows, 0).astype(jnp.float32)
    update, new_first, new_second, grad_norm, tensor_rms = adam_step(
        shard_grad,
        member,
        decay_flags,
        old_weights,
        first_moment,
        second_moment,
        square_sums,
        seg_entries,
    )
    return (
        result,
        caption_grad,
        tiles_grad,
        shard_grad,
        update,
        new_first,
        new_second,
        grad_norm,
        tensor_rms,
    )


D = HEADS * HEAD_DIM
NZ = 4
TOK = 128
PATCH = 196
PATCH_SENT = 208
PATCH_SLOT = 256
KEYS = 2 * PATCH_SLOT
LEAD = 80
BF, F32 = jnp.bfloat16, jnp.float32
MESH = pl.DeviceIdType.MESH
SHARD, PIECES, PIECE = 2312, 5, 464
OLD = 2320
PADDED = PIECES * PIECE
WINDOW = 8 * SHARD
CARRY = 96
SEGS = 24
QKV_AT, WO_AT, UQ_AT, UKV_AT, UO_AT, WIDE = 0, 2304, 3072, 3840, 5376, 6144
W1_AT, W2_AT = 0, 3072
(V_G1, V_C1, V_BQKV, V_BO, V_G2, V_C2, V_UQ, V_BKV, V_UO, V_G3, V_C3, V_B1, V_B2, V_SUMS) = range(14)


def row_starts():
    starts, at = {}, 0
    for label, shape, _ in layout(D, FF):
        starts[label] = at
        at += int(np.prod(shape)) // 128
    return starts


def mm(a, b):
    return lax.dot_general(a, b, (((1,), (0,)), ((), ())), preferred_element_type=F32)


def mm_nt(a, b):
    return lax.dot_general(a, b, (((1,), (1,)), ((), ())), preferred_element_type=F32)


def mm_tn(a, b):
    return lax.dot_general(a, b, (((0,), (0,)), ((), ())), preferred_element_type=F32)


def al(i, m):
    return pl.multiple_of(i * m, m)


def halves(pair):
    lane = lax.broadcasted_iota(jnp.int32, pair.shape, 1)
    zero = jnp.zeros_like(pair)
    return jnp.concatenate(
        [jnp.where(lane < HEAD_DIM, pair, zero), jnp.where(lane < HEAD_DIM, zero, pair)], axis=0
    )


def joined(stacked):
    n = stacked.shape[0] // 2
    lane = lax.broadcasted_iota(jnp.int32, (n, 128), 1)
    return jnp.where(lane < HEAD_DIM, stacked[:n], stacked[n:])


def normed(v):
    center = v - jnp.mean(v, axis=-1, keepdims=True)
    r = lax.rsqrt(jnp.mean(center * center, axis=-1, keepdims=True) + EPS_NORM)
    return center * r, r


def pair_kernel(
    cap, tiles, d_out, index, valid, length, weights,
    g_out, sums_out, old_out, out, dcap, dtile,
    fw, wide, gf, pc, ps, big1, big2, kv, dkvt, tl, tlT,
    xin, h1, am, h2, q2, a2, sb, rb, dy, t1, h1T, amT, h2T, a2T,
    x1, dx, acc, vec, meta, ob, pfx, pfx_in, carry, dcap_b, dtile_b,
    from_core, from_y, from_x, from_low, from_high, total, sq,
    wsem, gsem, send, recv, core_s, core_r, y_s, y_r, x_s, x_r, up_s, up_r, down_s, down_r, free, sum_s, sum_r,
):
    role = lax.axis_index(FSDP)
    other = 1 - role
    me = lax.axis_index(DP)
    my_z, my_y, my_core = me // 4, (me // 2) % 2, me % 2

    def at_dp(z, y, core):
        return {DP: z * 4 + y * 2 + core, FSDP: role}

    core_peer = at_dp(my_z, my_y, 1 - my_core)
    y_peer = at_dp(my_z, 1 - my_y, my_core)
    x_peer = {DP: me, FSDP: other}
    up_peer = at_dp(jnp.minimum(my_z + 1, NZ - 1), my_y, my_core)
    down_peer = at_dp(jnp.maximum(my_z - 1, 0), my_y, my_core)
    barrier = pltpu.get_barrier_semaphore()
    for peer in (core_peer, y_peer, x_peer):
        pl.semaphore_signal(barrier, inc=1, device_id=peer, device_id_type=MESH)
    for step in range(1, NZ):
        peer = at_dp((my_z + step) % NZ, my_y, my_core)
        pl.semaphore_signal(barrier, inc=1, device_id=peer, device_id_type=MESH)
    row0 = row_starts()

    cuts = [0, 13856, 18480, 23088, 32320, weights.shape[0]]
    loads = []
    for i in range(5):
        n = cuts[i + 1] - cuts[i]
        loads.append(
            pltpu.make_async_copy(
                weights.at[pl.ds(cuts[i], n)], fw.at[pl.ds(LEAD + cuts[i], n)], wsem.at[i]
            )
        )
    for c in loads:
        c.start()

    def to_other(src, dst, k):
        return pltpu.make_async_remote_copy(
            src_ref=src, dst_ref=dst, send_sem=send.at[k], recv_sem=recv.at[k],
            device_id=x_peer, device_id_type=MESH,
        )

    first, later = pl.ds(0, TOK), pl.ds(TOK, TOK)
    copies = dict(
        cap=to_other(cap, xin.at[later], 0),
        tile=to_other(tl.at[pl.ds(0, PATCH_SENT)], tl.at[pl.ds(PATCH_SLOT, PATCH_SENT)], 1),
        meta=to_other(meta.at[0], meta.at[1], 2),
        dy=to_other(d_out, dy.at[first], 3),
        lead=to_other(fw.at[pl.ds(weights.shape[0], LEAD)], fw.at[pl.ds(0, LEAD)], 4),
        out=to_other(t1.at[first], ob, 7),
        pfx=to_other(pfx, pfx_in, 8),
        old=to_other(
            weights.at[pl.ds(pl.multiple_of(((2 * me + other) % 16) * SHARD - 8 * other, 16), OLD)], old_out, 9
        ),
        dcap=to_other(dcap_b, dcap_b, 10),
        dtile=to_other(dtile_b, dtile_b, 11),
    )

    def to_other_half(c, k):
        rows = pl.ds(al(c, TOK), TOK)
        return to_other(sb.at[rows], rb.at[rows], k + c)

    def x2_copy(c):
        return to_other_half(c, 12)

    def dx2_copy(c):
        return to_other_half(c, 14)

    after = PATCH_SLOT + PATCH_SENT
    tl[0:PATCH_SLOT, :] = jnp.zeros((PATCH_SLOT, D), BF)
    tl[after:, :] = jnp.zeros((KEYS - after, D), BF)
    tl[0:PATCH, :] = tiles[...]
    counts = []
    for g in range(2):
        named_by = jnp.int32(0)
        for s in range(index.shape[1]):
            named = jnp.where(index[0, s] == g, jnp.int32(1), jnp.int32(0))
            named_by = named_by + jnp.where(valid[0, s] > 0, named, jnp.int32(0))
        counts.append(named_by)
    rows8 = lax.broadcasted_iota(jnp.int32, (8, 128), 0)
    meta[0] = jnp.where(
        rows8 == 0, counts[0], jnp.where(rows8 == 1, counts[1], length[0])
    ).astype(F32)

    def all_here():
        pl.semaphore_wait(barrier, 3 + NZ - 1)

    def vector(row, at, n, col=0):
        block = fw[pl.ds(at, n // 128), :].astype(F32)
        for j in range(n // 128):
            vec[row : row + 1, col + 128 * j : col + 128 * j + 128] = block[j : j + 1, :]

    def widen(at, k, col, rows=D):
        for j in range(k):
            wide[:, col + 128 * j : col + 128 * j + 128] = fw[pl.ds(at + j, rows, stride=k), :]

    def norm_forward(src, dst, g, c, at=0, n=2 * TOK):
        @pl.loop(0, n // 64, unroll=2)
        def _(i):
            rows = pl.ds(pl.multiple_of(at + 64 * i, 64), 64)
            v, _ = normed(src[rows, :].astype(F32))
            dst[rows, :] = (v * vec[g : g + 1, :D] + vec[c : c + 1, :D]).astype(BF)

    def norm_backward(src, dh, g, write, at=0, n=2 * TOK):
        def step(i, sums):
            rows = pl.ds(pl.multiple_of(at + 64 * i, 64), 64)
            v, r = normed(src[rows, :].astype(F32))
            d = dh[rows, :]
            dn = d * vec[g : g + 1, :D]
            dv = r * (
                dn - jnp.mean(dn, axis=-1, keepdims=True) - v * jnp.mean(dn * v, axis=-1, keepdims=True)
            )
            write(rows, dv)
            return (
                sums[0] + jnp.sum(d * v, axis=0, keepdims=True),
                sums[1] + jnp.sum(d, axis=0, keepdims=True),
            )

        return lax.fori_loop(0, n // 64, step, (jnp.zeros((1, D), F32), jnp.zeros((1, D), F32)), unroll=2)

    def put_vector(at, row, into=gf):
        for j in range(row.shape[1] // 128):
            into[at + j : at + j + 1, :] = row[:, 128 * j : 128 * j + 128]

    def column_total(ref, cols):
        return jnp.sum(ref[:, cols].astype(F32), axis=0, keepdims=True)

    def matrix_grad(at, k, lhs_t, rhs, transposed=False):
        @pl.loop(0, k // 2, unroll=3)
        def _(m):
            cols = pl.ds(al(m, 256), 256)
            res = mm_nt(lhs_t[...], rhs[cols, :]) if transposed else mm(lhs_t[...], rhs[:, cols])
            for half in range(2):
                gf[pl.ds(at + 2 * m + half, D, stride=k), :] = res[:, 128 * half : 128 * half + 128]

    def copy_to(peer, src, dst, ssem, rsem):
        return pltpu.make_async_remote_copy(
            src_ref=src, dst_ref=dst, send_sem=ssem, recv_sem=rsem, device_id=peer, device_id_type=MESH
        )

    def slot(w, s, core, y=0, x=0):
        return pl.multiple_of(((w * PIECES + s) * 8 + core * 4 + y * 2 + x) * PIECE, 16)

    class Scatter:
        def __init__(self, w, x):
            self.w, self.x = w, x

        def core(self, s):
            rows = pl.ds(slot(self.w, s, 1 - my_core), 4 * PIECE)
            return copy_to(core_peer, fw.at[rows], from_core.at[s], core_s.at[self.w, s], core_r.at[self.w, s])

        def y(self, s):
            rows = pl.ds(slot(self.w, s, my_core, 1 - my_y), 2 * PIECE)
            return copy_to(y_peer, fw.at[rows], from_y.at[self.w, s], y_s.at[self.w, s], y_r.at[self.w, s])

        def over(self, s):
            rows = pl.ds(slot(self.w, s, my_core, my_y, 1 - self.x), PIECE)
            return copy_to(x_peer, fw.at[rows], from_x.at[self.w, s], x_s.at[self.w, s], x_r.at[self.w, s])

        def held(self, s, h):
            if h == self.x:
                return fw.at[pl.ds(slot(self.w, s, my_core, my_y, self.x), PIECE)]
            return from_x.at[self.w, s]

        def up(self, s, h):
            return copy_to(
                up_peer, self.held(s, h), from_low.at[self.w, s, h], up_s.at[self.w, s, h], up_r.at[self.w, s, h]
            )

        def down(self, s, h):
            return copy_to(
                down_peer, self.held(s, h), from_high.at[self.w, s, h], down_s.at[self.w, s, h], down_r.at[self.w, s, h]
            )

        def cast(self, first_row):
            @pl.loop(0, PIECES)
            def _(s):
                for k in range(8):
                    j = (k & 2) * 2 + (k & 4) // 2 + (k & 1)
                    src = pl.ds(pl.multiple_of(first_row + j * SHARD + s * PIECE, 8), PIECE)
                    fw[pl.ds(pl.multiple_of(slot(self.w, s, 0) + k * PIECE, 16), PIECE), :] = gf[src, :].astype(BF)
                self.core(s).start()

        def add_core(self):
            @pl.loop(0, PIECES)
            def _(s):
                self.core(s).wait_recv()
                rows = pl.ds(slot(self.w, s, my_core), 4 * PIECE)
                fw[rows, :] = fw[rows, :] + from_core[s]
                self.y(s).start()

        def add_y(self, s):
            self.y(s).wait_recv()
            rows = pl.ds(slot(self.w, s, my_core, my_y), 2 * PIECE)
            fw[rows, :] = fw[rows, :] + from_y[self.w, s]
            self.over(s).start()

        def from_ends(self, s, h):
            if h != self.x:
                self.over(s).wait_recv()
            goal = 2 * h + self.w
            if goal > 0:
                pl.when(my_z == 0)(self.up(s, h).start)
            if goal < NZ - 1:
                pl.when(my_z == NZ - 1)(self.down(s, h).start)

        def relay(self, s, hop, h):
            goal = 2 * h + self.w
            mine = self.held(s, h)
            if hop < goal:

                @pl.when(my_z == hop)
                def _():
                    self.up(s, h).wait_recv()
                    mine[...] = mine[...] + from_low[self.w, s, h]
                    self.up(s, h).start()

            if NZ - 1 - hop > goal:

                @pl.when(my_z == NZ - 1 - hop)
                def _():
                    self.down(s, h).wait_recv()
                    mine[...] = mine[...] + from_high[self.w, s, h]
                    self.down(s, h).start()

        def step(self, t):
            own, came = self.x, 1 - self.x
            parts = [
                (3, lambda s: self.relay(s, 2, came)),
                (2, lambda s: self.relay(s, 2, own)),
                (2, lambda s: self.relay(s, 1, came)),
                (1, lambda s: self.relay(s, 1, own)),
                (1, lambda s: self.from_ends(s, came)),
                (0, self.add_y),
                (0, lambda s: self.from_ends(s, own)),
            ]
            for lag, part in parts:
                s = t - lag
                if isinstance(t, int):
                    if 0 <= s < PIECES:
                        part(s)
                else:
                    pl.when((s >= 0) & (s < PIECES))(functools.partial(part, s))

        def collect(self, s):
            for h in range(2):
                goal = 2 * h + self.w

                @pl.when(my_z == goal)
                def _():
                    whole = self.held(s, h)[...].astype(F32)
                    if goal > 0:
                        self.up(s, h).wait_recv()
                        whole = whole + from_low[self.w, s, h].astype(F32)
                    if goal < NZ - 1:
                        self.down(s, h).wait_recv()
                        whole = whole + from_high[self.w, s, h].astype(F32)
                    total[pl.ds(pl.multiple_of(s * PIECE, 8), PIECE), :] = whole

        def sent(self):
            @pl.loop(0, PIECES)
            def _(s):
                self.core(s).wait_send()
                self.y(s).wait_send()
                self.over(s).wait_send()
                for h in range(2):
                    goal = 2 * h + self.w
                    pl.when(my_z < goal)(self.up(s, h).wait_send)
                    pl.when(my_z > goal)(self.down(s, h).wait_send)

    def rest_of_scatter(one, zero, begun):
        @pl.loop(begun, 2 * PIECES + 3)
        def _(t):
            one.step(t)
            zero.step(t - PIECES)

        pl.loop(0, PIECES)(one.collect)
        pl.loop(0, PIECES)(zero.collect)
        one.sent()
        zero.sent()

    def square_sums():
        total[SHARD:, :] = jnp.zeros((total.shape[0] - SHARD, 128), F32)
        done = pltpu.make_async_copy(total.at[pl.ds(0, OLD)], g_out, gsem)
        done.start()
        seg = lax.broadcasted_iota(jnp.int32, (SEGS, 1), 0)
        begin = jnp.full((SEGS, 1), 1 << 30, jnp.int32)
        end = begin
        for i, (a, b) in enumerate(zip(*segment_table(D, FF)[:2])):
            begin = jnp.where(seg == i, int(a), begin)
            end = jnp.where(seg == i, int(b), end)
        row = (me * 2 + role) * SHARD + lax.broadcasted_iota(jnp.int32, (SEGS, total.shape[0]), 1)
        member = jnp.where((row >= begin) & (row < end), 1.0, 0.0).astype(BF)
        square = total[...] * total[...]
        high = square.astype(BF)
        squares = mm(member, high) + mm(member, (square - high.astype(F32)).astype(BF))
        mine = jnp.broadcast_to(jnp.sum(squares, axis=1, keepdims=True), (SEGS, 128))
        for i, peer in enumerate((core_peer, y_peer, x_peer)):
            sq[2 * i] = mine
            swap = copy_to(peer, sq.at[2 * i], sq.at[2 * i + 1], sum_s.at[i], sum_r.at[i])
            swap.start()
            swap.wait()
            mine = mine + sq[2 * i + 1]
        sq[6] = mine
        sends = []
        for step in range(1, NZ):
            to = at_dp((my_z + step) % NZ, my_y, my_core)
            sends.append(copy_to(to, sq.at[6], sq.at[6 + step], sum_s.at[2 + step], sum_r.at[2 + step]))
            sends[-1].start()
        for c in sends:
            c.wait()
        whole = jnp.zeros((SEGS, 128), F32)
        for z in range(NZ):
            part = mine
            for step in range(1, NZ):
                part = jnp.where((my_z - step + NZ) % NZ == z, sq[6 + step], part)
            whole = whole + part
        sums_out[...] = whole
        done.wait()

    def attention_role():
        at = {k: LEAD + v for k, v in row0.items()}
        at0 = {k: CARRY + v for k, v in row0.items()}
        at1 = {k: CARRY - WINDOW + v for k, v in row0.items()}
        one, zero = Scatter(1, 0), Scatter(0, 0)
        xin[first, :] = cap[...]
        loads[0].wait()
        vector(V_G1, at[NORM_ONE_GAIN], D)
        vector(V_C1, at[NORM_ONE_SHIFT], D)
        vec[V_BQKV : V_BQKV + 1, :] = jnp.zeros((1, FF), F32)
        vec[V_BKV : V_BKV + 1, :] = jnp.zeros((1, FF), F32)
        vector(V_BQKV, at[SELF_QUERY_BIAS], D)
        vector(V_BQKV, at[SELF_VALUE_BIAS], D, 2 * D)
        widen(at[SELF_QKV], 18, QKV_AT)
        for c in loads[1:]:
            c.wait()
        vector(V_BO, at[SELF_OUT_BIAS], D)
        vector(V_G2, at[NORM_TWO_GAIN], D)
        vector(V_C2, at[NORM_TWO_SHIFT], D)
        vector(V_UQ, at[CROSS_QUERY_BIAS], D)
        vector(V_BKV, at[CROSS_VALUE_BIAS], D, D)
        vector(V_UO, at[CROSS_OUT_BIAS], D)
        widen(at[SELF_OUT], 6, WO_AT)
        widen(at[CROSS_QUERY], 6, UQ_AT)
        widen(at[CROSS_KV], 12, UKV_AT)
        widen(at[CROSS_OUT], 6, UO_AT)
        all_here()
        copies["dy"].start()
        copies["lead"].start()

        copies["cap"].wait_recv()
        norm_forward(xin, h1, V_G1, V_C1)

        for j in range(3):
            cols = slice(D * j, D * j + D)
            big1[:, cols] = (mm(h1[...], wide[:, cols]) + vec[V_BQKV : V_BQKV + 1, cols]).astype(BF)

        copies["meta"].wait_recv()

        @pl.loop(0, 12, unroll=6)
        def _(i):
            c, p = i // 6, i % 6
            rows = pl.ds(al(c, TOK), TOK)
            qq = halves(big1[rows, pl.ds(al(p, 128), 128)]) * BF(0.125)
            k2 = big1[rows, pl.ds(al(p, 128) + D, 128)]
            v2 = big1[rows, pl.ds(al(p, 128) + 2 * D, 128)]
            s = mm_nt(qq, k2)
            row = lax.broadcasted_iota(jnp.int32, s.shape, 0) % TOK
            col = lax.broadcasted_iota(jnp.int32, s.shape, 1)
            present = col.astype(F32) < meta[c][2:3, :]
            s = jnp.where((col <= row) & present, s, NEG_LARGE)
            e = jnp.exp(s - jnp.max(s, axis=-1, keepdims=True))
            prob = (e * (1.0 / jnp.sum(e, axis=-1, keepdims=True))).astype(BF)
            ps[i] = prob
            am[rows, pl.ds(al(p, 128), 128)] = joined(mm(prob, v2)).astype(BF)

        x1[...] = xin[...].astype(F32) + mm(am[...], wide[:, WO_AT : WO_AT + D]) + vec[V_BO : V_BO + 1, :D]
        norm_forward(x1, h2, V_G2, V_C2)
        q2[...] = (mm(h2[...], wide[:, UQ_AT : UQ_AT + D]) + vec[V_UQ : V_UQ + 1, :D]).astype(BF)
        copies["tile"].wait_recv()

        for j in range(2):
            cols = slice(D * j, D * j + D)
            kv[:, cols] = (
                mm(tl[...], wide[:, UKV_AT + D * j : UKV_AT + D * j + D]) + vec[V_BKV : V_BKV + 1, cols]
            ).astype(BF)

        @pl.loop(0, 2)
        def _(c):
            rows = pl.ds(al(c, TOK), TOK)
            col = lax.broadcasted_iota(jnp.int32, (1, KEYS), 1)
            m = meta[c]
            c0 = jnp.concatenate([m[0:1, :]] * (KEYS // 128), axis=1)
            c1 = jnp.concatenate([m[1:2, :]] * (KEYS // 128), axis=1)
            count = jnp.where(col < PATCH, c0, jnp.where(col < PATCH_SLOT, 0.0, c1))
            count = jnp.where(col < PATCH_SLOT + PATCH, count, 0.0)

            @pl.loop(0, 6, unroll=6)
            def _(p):
                qq = halves(q2[rows, pl.ds(al(p, 128), 128)]) * BF(0.125)
                s = mm_nt(qq, kv[:, pl.ds(al(p, 128), 128)])
                s = jnp.where(count > 0.0, s, NEG_LARGE)
                e = jnp.exp(s - jnp.max(s, axis=-1, keepdims=True)) * count
                prob = (e * (1.0 / jnp.sum(e, axis=-1, keepdims=True))).astype(BF)
                pc[pl.ds(al(6 * c + p, 2 * TOK), 2 * TOK), :] = prob
                a2[rows, pl.ds(al(p, 128), 128)] = joined(
                    mm(prob, kv[:, pl.ds(al(p, 128) + D, 128)])
                ).astype(BF)

            sb[rows, :] = (
                x1[rows, :] + mm(a2[rows, :], wide[:, UO_AT : UO_AT + D]) + vec[V_UO : V_UO + 1, :D]
            ).astype(BF)
            x2_copy(c).start()

        copies["old"].start()

        h1T[...] = h1[...].T
        amT[...] = am[...].T
        h2T[...] = h2[...].T
        a2T[...] = a2[...].T
        tlT[...] = tl[...].T

        part_at = at1[CROSS_KV]

        def attend_back(c, p, take_keys):
            rows = pl.ds(c * TOK, TOK)
            lanes, vlanes = pl.ds(al(p, 128), 128), pl.ds(al(p, 128) + D, 128)
            qq = halves(q2[rows, lanes]) * BF(0.125)
            do = halves(t1[rows, lanes])
            prob = pc[pl.ds(al(6 * c + p, 2 * TOK), 2 * TOK), :]
            pf = prob.astype(F32)
            dp = mm_nt(do, kv[:, vlanes])
            ds = (pf * (dp - jnp.sum(pf * dp, axis=-1, keepdims=True))).astype(BF)
            am[rows, lanes] = (joined(mm(ds, kv[:, lanes])) * 0.125).astype(BF)
            take_keys(p, 0, lanes, mm_tn(qq, ds))
            take_keys(p, 1, vlanes, mm_tn(do, prob))

        def part_rows(p, k, j):
            return pl.ds(pl.multiple_of(part_at + ((2 * p + k) * 4 + j) * 128, 8), 128)

        def keep(p, k, lanes, term):
            for j in range(4):
                gf[part_rows(p, k, j), :] = term[:, 128 * j : 128 * j + 128]

        def complete(p, k, lanes, term):
            for j in range(4):
                cols = slice(128 * j, 128 * j + 128)
                dkvt[lanes, cols] = (gf[part_rows(p, k, j), :] + term[:, cols]).astype(BF)

        for c, take_keys in enumerate((keep, complete)):
            rows = pl.ds(c * TOK, TOK)
            dx2_copy(c).wait_recv()
            t1[rows, :] = mm_nt(rb[rows, :], wide[:, UO_AT : UO_AT + D]).astype(BF)
            pl.loop(0, 6, unroll=6)(functools.partial(attend_back, c, take_keys=take_keys))

        put_vector(at1[CROSS_OUT_BIAS], column_total(rb, slice(None)))
        matrix_grad(at1[CROSS_OUT], 6, a2T, rb)
        put_vector(at1[CROSS_QUERY_BIAS], column_total(am, slice(None)))
        matrix_grad(at1[CROSS_QUERY], 6, h2T, am)
        matrix_grad(at1[CROSS_KV], 12, tlT, dkvt, transposed=True)
        kv[...] = dkvt[...].T
        put_vector(at1[CROSS_VALUE_BIAS], column_total(kv, slice(D, 2 * D)))
        copies["pfx"].wait_recv()
        gf[pl.ds(at1[NORM_THREE_GAIN], LEAD - 12), :] = pfx_in[12:, :]
        copies["lead"].wait_send()
        one.cast(CARRY)
        carry[...] = gf[0:CARRY, :]

        def tile_grad(rows):
            return mm_nt(kv[rows, :], wide[:, UKV_AT : UKV_AT + 2 * D])

        dtile[:, 0, :] = tile_grad(pl.ds(0, PATCH_SENT))[:PATCH]
        dtile_b[...] = tile_grad(pl.ds(PATCH_SLOT, PATCH_SENT)).astype(BF)
        copies["dtile"].start()
        one.add_core()
        pl.semaphore_signal(free, inc=1, device_id=core_peer, device_id_type=MESH)
        acc[...] = mm_nt(am[...], wide[:, UQ_AT : UQ_AT + D])
        e1 = h2

        def write_dx1(rows, dv):
            full = rb[rows, :].astype(F32) + dv
            dx[rows, :] = full
            e1[rows, :] = full.astype(BF)

        gg, gc = norm_backward(x1, acc, V_G2, write_dx1)
        put_vector(at0[NORM_TWO_GAIN], gg)
        put_vector(at0[NORM_TWO_SHIFT], gc)
        put_vector(at0[SELF_OUT_BIAS], column_total(e1, slice(None)))
        matrix_grad(at0[SELF_OUT], 6, amT, e1)
        t1[...] = mm_nt(e1[...], wide[:, WO_AT : WO_AT + D]).astype(BF)

        @pl.loop(0, 12, unroll=6)
        def _(i):
            c, p = i // 6, i % 6
            rows = pl.ds(al(c, TOK), TOK)
            lanes = pl.ds(al(p, 128), 128)
            klanes, vlanes = pl.ds(al(p, 128) + D, 128), pl.ds(al(p, 128) + 2 * D, 128)
            qq = halves(big1[rows, lanes]) * BF(0.125)
            do = halves(t1[rows, lanes])
            prob = ps[i]
            pf = prob.astype(F32)
            dp = mm_nt(do, big1[rows, vlanes])
            ds = (pf * (dp - jnp.sum(pf * dp, axis=-1, keepdims=True))).astype(BF)
            big2[rows, lanes] = (joined(mm(ds, big1[rows, klanes])) * 0.125).astype(BF)
            big2[rows, klanes] = mm_tn(ds, qq).astype(BF)
            big2[rows, vlanes] = mm_tn(prob, do).astype(BF)

        one.step(0)
        acc[...] = mm_nt(big2[:, : 3 * D], wide[:, : 3 * D])

        def write_dx0(rows, dv):
            dx[rows, :] = dx[rows, :] + dv

        gg, gc = norm_backward(xin, acc, V_G1, write_dx0)
        put_vector(at0[NORM_ONE_GAIN], gg)
        put_vector(at0[NORM_ONE_SHIFT], gc)
        dcap[...] = dx[first, :]
        dcap_b[...] = dx[later, :].astype(BF)
        copies["dcap"].start()
        one.step(1)
        put_vector(at0[SELF_QUERY_BIAS], column_total(big2, slice(0, D)))
        put_vector(at0[SELF_VALUE_BIAS], column_total(big2, slice(2 * D, 3 * D)))
        matrix_grad(at0[SELF_QKV], 18, h1T, big2)
        gf[pl.ds(at0[CROSS_QUERY], WINDOW - row0[CROSS_QUERY]), :] = carry[
            row0[CROSS_QUERY] - WINDOW + CARRY :, :
        ]
        pl.semaphore_wait(free, 1)
        zero.cast(CARRY)
        one.step(2)
        zero.add_core()
        rest_of_scatter(one, zero, 3)
        copies["out"].wait_recv()
        out[...] = ob[...]
        for name in ("dy", "dcap", "dtile"):
            copies[name].wait_send()
        for c in range(2):
            x2_copy(c).wait_send()
        copies["old"].wait()
        square_sums()

    def mlp_role():
        all_here()
        copies["meta"].start()
        copies["cap"].start()
        copies["cap"].wait_send()
        copies["tile"].start()
        base = LEAD - weights.shape[0]
        at = {k: base + v for k, v in row0.items()}
        at0 = {k: CARRY - weights.shape[0] + v for k, v in row0.items()}
        at1 = {k: v - WINDOW for k, v in at0.items()}
        one, zero = Scatter(1, 1), Scatter(0, 1)
        dy[later, :] = d_out[...]
        for c in loads:
            c.wait()
        for b in range(4):
            widen(at[MLP_DOWN] + 6 * D * b, 6, W2_AT + D * b)
        copies["lead"].wait_recv()
        widen(at[MLP_UP], 24, W1_AT)
        vector(V_G3, at[NORM_THREE_GAIN], D)
        vector(V_C3, at[NORM_THREE_SHIFT], D)
        vector(V_B1, at[MLP_UP_BIAS], FF)
        vector(V_B2, at[MLP_DOWN_BIAS], D)
        copies["dy"].wait_recv()

        @pl.loop(0, 4)
        def _(b):
            dg = mm_nt(dy[...], wide[:, pl.ds(al(b, D) + W2_AT, D)])
            for j in range(6):
                gf[pl.ds(al(6 * b + j, 256), 256), :] = dg[:, 128 * j : 128 * j + 128]

        def write_dx2(rows, dv):
            sb[rows, :] = (dy[rows, :].astype(F32) + dv).astype(BF)

        vec[V_SUMS : V_SUMS + 2, :] = jnp.zeros((2, FF), F32)

        @pl.loop(0, 2)
        def _(c):
            cap_rows = pl.ds(al(c, TOK), TOK)
            x2_copy(c).wait_recv()
            norm_forward(rb, h1, V_G3, V_C3, c * TOK, TOK)
            z_parts = [x1.at[first], x1.at[later], dx.at[first], dx.at[later]]
            for b in range(4):
                cols = slice(D * b, D * b + D)
                z_parts[b][...] = mm(h1[cap_rows, :], wide[:, cols]) + vec[V_B1 : V_B1 + 1, cols]

            @pl.loop(0, 4)
            def _(i):
                here = pl.ds(al(i, 32), 32)
                rows = pl.ds(al(c, TOK) + al(i, 32), 32)
                for k in range(24):
                    z = z_parts[k // 6][here, 128 * (k % 6) : 128 * (k % 6) + 128]
                    phi = 0.5 + 0.5 * lax.erf(z * np.float32(np.sqrt(0.5)))
                    dens = jnp.exp(-0.5 * z * z) * np.float32(1.0 / np.sqrt(2.0 * np.pi))
                    lanes = slice(128 * k, 128 * k + 128)
                    big1[rows, lanes] = (z * phi).astype(BF)
                    dg = gf[pl.ds(256 * k + al(c, TOK) + al(i, 32), 32), :]
                    big2[rows, lanes] = (dg * (phi + z * dens)).astype(BF)

            acc[cap_rows, :] = mm_nt(big2[cap_rows, :], wide[:, W1_AT : W1_AT + FF])
            gg, gc = norm_backward(rb, acc, V_G3, write_dx2, c * TOK, TOK)
            vec[V_SUMS : V_SUMS + 1, :D] = vec[V_SUMS : V_SUMS + 1, :D] + gg
            vec[V_SUMS + 1 : V_SUMS + 2, :D] = vec[V_SUMS + 1 : V_SUMS + 2, :D] + gc
            dx2_copy(c).start()

        put_vector(12, vec[V_SUMS : V_SUMS + 1, :D], pfx)
        put_vector(18, vec[V_SUMS + 1 : V_SUMS + 2, :D], pfx)

        h1T[...] = h1[...].T
        pfx[0:12, :] = jnp.zeros((12, 128), F32)
        for b in range(4):
            head = mm(h1T[0:8, :], big2[:, D * b : D * b + D])
            for r in range(3):
                for j in range(6):
                    row = 24 + 24 * r + 6 * b + j
                    if row < LEAD:
                        pfx[row : row + 1, :] = head[r : r + 1, 128 * j : 128 * j + 128]
        copies["pfx"].start()
        copies["old"].start()

        acc[...] = rb[...].astype(F32) + vec[V_B2 : V_B2 + 1, :D]
        for b in range(4):
            cols = slice(D * b, D * b + D)
            acc[...] = acc[...] + mm(big1[:, cols], wide[:, W2_AT + D * b : W2_AT + D * b + D])
            pc[D * b : D * b + D, 0:256] = big1[:, cols].T

        t1[first, :] = acc[first, :].astype(BF)
        copies["out"].start()
        out[...] = acc[later, :].astype(BF)
        gf[pl.ds(at1[MLP_DOWN_BIAS] + 6, WINDOW + CARRY - at1[MLP_DOWN_BIAS] - 6), :] = jnp.zeros(
            (WINDOW + CARRY - at1[MLP_DOWN_BIAS] - 6, 128), F32
        )
        put_vector(at1[MLP_DOWN_BIAS], column_total(dy, slice(None)))
        for b in range(4):
            matrix_grad(at1[MLP_DOWN] + 6 * D * b, 6, pc.at[pl.ds(D * b, D), pl.ds(0, 256)], dy)
        one.cast(CARRY)
        carry[...] = gf[0:CARRY, :]
        put_vector(at0[MLP_UP_BIAS], column_total(big2, slice(None)))
        matrix_grad(at0[MLP_UP], 24, h1T, big2)
        one.add_core()
        pl.semaphore_signal(free, inc=1, device_id=core_peer, device_id_type=MESH)
        gf[pl.ds(at0[MLP_DOWN], CARRY), :] = carry[...]
        pl.semaphore_wait(free, 1)
        zero.cast(CARRY)
        zero.add_core()
        rest_of_scatter(one, zero, 0)
        copies["dtile"].wait_recv()
        dtile[:, 0, :] = dtile_b[0:PATCH, :].astype(F32)
        copies["dcap"].wait_recv()
        dcap[...] = dcap_b[...].astype(F32)
        for name in ("tile", "meta", "pfx", "out"):
            copies[name].wait_send()
        for c in range(2):
            dx2_copy(c).wait_send()
        copies["old"].wait()
        square_sums()

    pl.when(role == 0)(attention_role)
    pl.when(role == 1)(mlp_role)


def pair_call(cap, tiles, d_out, index, valid, length, weights):
    vm = pl.BlockSpec(memory_space=pltpu.VMEM)
    sm = pl.BlockSpec(memory_space=pltpu.SMEM)
    hbm = pl.BlockSpec(memory_space=pl.ANY)
    S = jax.ShapeDtypeStruct
    dma, both = pltpu.SemaphoreType.DMA, 2 * TOK

    def bf(*s):
        return pltpu.VMEM(s, BF)

    def fl(*s):
        return pltpu.VMEM(s, F32)

    return pl.pallas_call(
        pair_kernel,
        in_specs=[vm, vm, vm, sm, sm, sm, hbm],
        out_specs=[hbm, vm, hbm, vm, vm, vm],
        out_shape=[
            S((OLD, 128), F32),
            S((SEGS, 128), F32),
            S((OLD, 128), BF),
            S((TOK, D), BF),
            S((TOK, D), F32),
            S((PATCH, 1, D), F32),
        ],
        scratch_shapes=[
            bf(16 * PADDED, 128), bf(D, WIDE), fl(CARRY + 7 * SHARD + PADDED, 128), bf(12 * both, KEYS),
            bf(12, both, 128), bf(both, FF), bf(both, FF), bf(KEYS, 2 * D), bf(2 * D, KEYS), bf(KEYS, D), bf(D, KEYS),
            *[bf(both, D) for _ in range(10)],
            *[bf(D, both) for _ in range(4)],
            *[fl(both, D) for _ in range(3)],
            fl(16, FF), fl(2, 8, 128), bf(TOK, D), fl(LEAD, 128), fl(LEAD, 128), fl(CARRY, 128),
            bf(TOK, D), bf(PATCH_SENT, D),
            bf(PIECES, 4 * PIECE, 128), bf(2, PIECES, 2 * PIECE, 128), bf(2, PIECES, PIECE, 128),
            bf(2, PIECES, 2, PIECE, 128), bf(2, PIECES, 2, PIECE, 128), fl(2432, 128), fl(10, SEGS, 128),
            dma((5,)), dma, dma((16,)), dma((16,)),
            *[dma((2, PIECES)) for _ in range(6)],
            *[dma((2, PIECES, 2)) for _ in range(4)],
            pltpu.SemaphoreType.REGULAR, dma((6,)), dma((6,)),
        ],
        compiler_params=pltpu.CompilerParams(
            collective_id=0, has_side_effects=True, vmem_limit_bytes=63 * 2**20
        ),
    )(cap, tiles, d_out, index, valid, length, weights)


def pair_update(grads, old_weights, first_moment, second_moment, square_sums):
    seg_starts, seg_ends, decay_flags, seg_entries = segment_table(D, FF)
    grad_norm = jnp.sqrt(jnp.sum(square_sums))
    tensor_rms = jnp.sqrt(square_sums / jnp.asarray(seg_entries, dtype=square_sums.dtype))
    clipped = grads * jnp.minimum(1.0, CLIP_NORM / (grad_norm + 1e-06))
    new_first = BETA_ONE * first_moment + (1.0 - BETA_ONE) * clipped
    new_second = BETA_TWO * second_moment + (1.0 - BETA_TWO) * clipped * clipped
    first_hat = new_first / (1.0 - BETA_ONE**STEP)
    second_hat = new_second / (1.0 - BETA_TWO**STEP)
    row = lax.axis_index(BOTH) * SHARD + lax.broadcasted_iota(jnp.int32, grads.shape, 0)
    decays = row < 0
    for start, end, decay in zip(seg_starts, seg_ends, decay_flags):
        if decay:
            decays = decays | ((row >= int(start)) & (row < int(end)))
    decayed = jnp.where(decays, old_weights, 0.0)
    update = -LEARN_RATE * (first_hat / (jnp.sqrt(second_hat) + ADAM_EPS) + DECAY_RATE * decayed)
    return (update, new_first, new_second, grad_norm, tensor_rms)


def pair_body(
    captions, tiles, tile_index, tile_valid, caption_len, weights, first_moment, second_moment, d_out
):
    me, f = lax.axis_index(DP), lax.axis_index(FSDP)
    padded, sums, old, out, caption_grad, tiles_grad = pair_call(
        captions[0], tiles[0], d_out[0], tile_index, tile_valid, caption_len, weights
    )
    shard_grad = padded[:SHARD]
    own = lax.dynamic_slice_in_dim(weights, ((2 * me + f) % 16) * SHARD, SHARD, 0)
    old = lax.dynamic_slice_in_dim(old, 8 * f, SHARD, 0)
    old_weights = jnp.where(me // 8 == f, own, old).astype(jnp.float32)
    update, new_first, new_second, grad_norm, tensor_rms = pair_update(
        shard_grad, old_weights, first_moment, second_moment, sums[:21, 0]
    )
    return (
        out[None], caption_grad[None], jnp.swapaxes(tiles_grad, 0, 1), shard_grad, update, new_first, new_second,
        grad_norm, tensor_rms,
    )


def solution(mesh):
    placed = (
        P(BOTH, None, None),
        P(BOTH, None, None),
        P(BOTH, None),
        P(BOTH, None),
        P(BOTH),
        P(FSDP, None),
        P(BOTH, None),
        P(BOTH, None),
        P(BOTH, None, None),
    )
    return jax.shard_map(
        pair_body if mesh.shape[FSDP] == 2 else body,
        mesh=mesh,
        in_specs=placed,
        out_specs=(
            P(BOTH, None, None),
            P(BOTH, None, None),
            P(BOTH, None, None),
            P(BOTH, None),
            P(BOTH, None),
            P(BOTH, None),
            P(BOTH, None),
            P(),
            P(),
        ),
        check_vma=False,
    )
```

```python
import functools

import jax
import jax.numpy as jnp
import numpy as np
from jax import lax
from jax.experimental import pallas as pl
from jax.experimental.pallas import tpu as pltpu
from jax.sharding import PartitionSpec as P

HEADS = 12
HEAD_DIM = 64
FF = 3072
STEP = 10


EPS_NORM = 1e-05
CLIP_NORM = 1.0
BETA_ONE = 0.9
BETA_TWO = 0.999
LEARN_RATE = 0.01
DECAY_RATE = 0.1
ADAM_EPS = 1e-08
NEG_LARGE = -1e30
(NORM_ONE_GAIN, NORM_ONE_SHIFT, SELF_QKV, SELF_QUERY_BIAS, SELF_VALUE_BIAS, SELF_OUT, SELF_OUT_BIAS, NORM_TWO_GAIN, NORM_TWO_SHIFT, CROSS_QUERY, CROSS_QUERY_BIAS, CROSS_KV, CROSS_VALUE_BIAS, CROSS_OUT, CROSS_OUT_BIAS, NORM_THREE_GAIN, NORM_THREE_SHIFT, MLP_UP, MLP_UP_BIAS, MLP_DOWN, MLP_DOWN_BIAS) = range(21)
DP, FSDP = "dp", "fsdp"
BOTH = (DP, FSDP)
E_BHQK_BKHE_TO_BQHE = "bhqk,bkhe->bqhe"
E_BHQK_BQHE_TO_BKHE = "bhqk,bqhe->bkhe"
E_BLD_BLE_TO_DE = "bld,ble->de"
E_BLD_BLF_TO_DF = "bld,blf->df"
E_BLD_DE_TO_BLE = "bld,de->ble"
E_BLD_DF_TO_BLF = "bld,df->blf"
E_BLD_FD_TO_BLF = "bld,fd->blf"
E_BLE_DE_TO_BLD = "ble,de->bld"
E_BLF_BLD_TO_FD = "blf,bld->fd"
E_BLF_DF_TO_BLD = "blf,df->bld"
E_BLF_FD_TO_BLD = "blf,fd->bld"
E_BQHE_BKHE_TO_BHQK = "bqhe,bkhe->bhqk"
E_CSG_CSPE_TO_GPE = "csg,cspe->gpe"
E_TPD_DE_TO_TPE = "tpd,de->tpe"
E_TPD_TPE_TO_DE = "tpd,tpe->de"
E_TPE_DE_TO_TPD = "tpe,de->tpd"


def for_sending(x):
    return jax.tree.map(lambda a: a.astype(jnp.bfloat16) if a.dtype == jnp.float32 else a, x)


def layout(model_width, hidden_width):
    return [
        (NORM_ONE_GAIN, (model_width,), 0),
        (NORM_ONE_SHIFT, (model_width,), 0),
        (SELF_QKV, (model_width, 3 * model_width), 1),
        (SELF_QUERY_BIAS, (model_width,), 0),
        (SELF_VALUE_BIAS, (model_width,), 0),
        (SELF_OUT, (model_width, model_width), 1),
        (SELF_OUT_BIAS, (model_width,), 0),
        (NORM_TWO_GAIN, (model_width,), 0),
        (NORM_TWO_SHIFT, (model_width,), 0),
        (CROSS_QUERY, (model_width, model_width), 1),
        (CROSS_QUERY_BIAS, (model_width,), 0),
        (CROSS_KV, (model_width, 2 * model_width), 1),
        (CROSS_VALUE_BIAS, (model_width,), 0),
        (CROSS_OUT, (model_width, model_width), 1),
        (CROSS_OUT_BIAS, (model_width,), 0),
        (NORM_THREE_GAIN, (model_width,), 0),
        (NORM_THREE_SHIFT, (model_width,), 0),
        (MLP_UP, (model_width, hidden_width), 1),
        (MLP_UP_BIAS, (hidden_width,), 0),
        (MLP_DOWN, (hidden_width, model_width), 1),
        (MLP_DOWN_BIAS, (model_width,), 0),
    ]


def segment_table(model_width, hidden_width):
    seg_starts = []
    seg_ends = []
    decay_flags = []
    seg_entries = []
    row_at = 0
    for seg_label, seg_shape, seg_flag in layout(model_width, hidden_width):
        item_count = int(np.prod(seg_shape))
        seg_rows = item_count // 128
        seg_starts.append(row_at)
        seg_ends.append(row_at + seg_rows)
        decay_flags.append(seg_flag == 1)
        seg_entries.append(float(item_count))
        row_at = row_at + seg_rows
    return (np.array(seg_starts), np.array(seg_ends), np.array(decay_flags), np.array(seg_entries))


def unpack(flat_rows, model_width, hidden_width):
    vector = flat_rows.reshape(-1)
    tensors = {}
    offset = 0
    for seg_label, seg_shape, seg_flag in layout(model_width, hidden_width):
        item_count = int(np.prod(seg_shape))
        tensors[seg_label] = vector[offset : offset + item_count].reshape(seg_shape)
        offset = offset + item_count
    return tensors


def pack_rows(gradients, model_width, hidden_width, total_rows):
    pieces = [
        gradients[seg_label].reshape(-1, 128)
        for seg_label, seg_shape, seg_flag in layout(model_width, hidden_width)
    ]
    used_rows = sum((tensor_piece.shape[0] for tensor_piece in pieces))
    pieces.append(jnp.zeros((total_rows - used_rows, 128), jnp.float32))
    return jnp.concatenate(pieces, axis=0)


def product(pattern, left_side, right_side):
    return jnp.einsum(pattern, left_side, right_side, preferred_element_type=jnp.float32)


def as_float(tensors, seg_label):
    return tensors[seg_label].astype(jnp.float32)


def column_sums(values):
    return jnp.sum(values.astype(jnp.float32), axis=tuple(range(values.ndim - 1)))


def layer_norm(values, gain_term, offset_term):
    center = values - jnp.mean(values, axis=-1, keepdims=True)
    spread = jnp.mean(center * center, axis=-1, keepdims=True)
    return center * lax.rsqrt(spread + EPS_NORM) * gain_term + offset_term


def gelu_exact(pre_values):
    return jax.nn.gelu(pre_values, approximate=False)


def norm_back(values, tensors, gain, shift, normed_grad, gradients):
    norm_value, norm_pull = jax.vjp(
        layer_norm,
        values,
        as_float(tensors, gain),
        as_float(tensors, shift),
    )
    values_grad, gain_grad, offset_grad = norm_pull(normed_grad)
    gradients[gain] = gain_grad
    gradients[shift] = offset_grad
    return values_grad


def score_block(queries, key_head_split, allowed):
    scores = product(E_BQHE_BKHE_TO_BHQK, queries, key_head_split) * 0.125
    return jnp.where(allowed, scores, NEG_LARGE)


def softmax_forward(queries, key_head_split, allowed):
    scores = score_block(queries, key_head_split, allowed)
    highest = jnp.max(scores, axis=-1, keepdims=True)
    exponent = jnp.exp(scores - highest)
    row_total = jnp.sum(exponent, axis=-1, keepdims=True)
    return (exponent / row_total, highest + jnp.log(row_total))


def attention_backward_pass(queries, key_head_split, values, allowed, log_total, mixed_grad):
    probabilities = jnp.where(
        allowed, jnp.exp(score_block(queries, key_head_split, allowed) - log_total), 0.0
    )
    probs_grad = product(E_BQHE_BKHE_TO_BHQK, mixed_grad, values)
    values_grad = product(E_BHQK_BQHE_TO_BKHE, probabilities.astype(jnp.bfloat16), mixed_grad)
    inner_sum = jnp.sum(probabilities * probs_grad, axis=-1, keepdims=True)
    score_grad = (probabilities * (probs_grad - inner_sum)).astype(jnp.bfloat16)
    queries_grad = product(E_BHQK_BKHE_TO_BQHE, score_grad, key_head_split) * 0.125
    keys_grad = product(E_BHQK_BQHE_TO_BKHE, score_grad, queries) * 0.125
    return (queries_grad, keys_grad, values_grad)


def adam_step(
    gradients,
    member,
    decay_flags,
    old_weights,
    first_moment,
    second_moment,
    square_sums,
    seg_entries,
):
    grad_norm = jnp.sqrt(jnp.sum(square_sums))
    tensor_rms = jnp.sqrt(square_sums / jnp.asarray(seg_entries, dtype=square_sums.dtype))
    clip_scale = jnp.minimum(1.0, CLIP_NORM / (grad_norm + 1e-06))
    clipped = gradients * clip_scale
    new_first = BETA_ONE * first_moment + (1.0 - BETA_ONE) * clipped
    new_second = BETA_TWO * second_moment + (1.0 - BETA_TWO) * clipped * clipped
    first_hat = new_first / (1.0 - BETA_ONE**STEP)
    second_hat = new_second / (1.0 - BETA_TWO**STEP)
    decay_rows = jnp.any(member & decay_flags[None, :], axis=1)
    decayed = jnp.where(decay_rows[:, None], old_weights, 0.0)
    update = -LEARN_RATE * (first_hat / (jnp.sqrt(second_hat) + ADAM_EPS) + DECAY_RATE * decayed)
    return (update, new_first, new_second, grad_norm, tensor_rms)


def body(
    captions,
    tiles,
    tile_index,
    tile_valid,
    caption_len,
    weights,
    first_moment,
    second_moment,
    d_out,
):
    model_width = captions.shape[2]
    hidden_width = FF
    caption_rows = captions.shape[0]
    cap_length = captions.shape[1]
    patch_count = tiles.shape[1]
    own_tiles = tiles.shape[0]
    slot_count = tile_index.shape[1]
    group_size = lax.axis_size(FSDP)
    data_size = lax.axis_size(DP)
    total_rows = weights.shape[0] * group_size
    heads_shape = (caption_rows, cap_length, HEADS, HEAD_DIM)
    key_shape = (caption_rows, slot_count * patch_count, HEADS, HEAD_DIM)
    token_layout_form = (caption_rows, cap_length, model_width)
    tensors = unpack(lax.all_gather(weights, FSDP, axis=0, tiled=True), model_width, hidden_width)
    zero_part = jnp.zeros((model_width,), jnp.bfloat16)
    input_values = captions.astype(jnp.float32)
    normed_one = layer_norm(
        input_values, as_float(tensors, NORM_ONE_GAIN), as_float(tensors, NORM_ONE_SHIFT)
    ).astype(jnp.bfloat16)
    qkv_bias = jnp.concatenate(
        [tensors[SELF_QUERY_BIAS], zero_part, tensors[SELF_VALUE_BIAS]]
    ).astype(jnp.float32)
    packed_qkv = (product(E_BLD_DE_TO_BLE, normed_one, tensors[SELF_QKV]) + qkv_bias).astype(
        jnp.bfloat16
    )
    self_query = packed_qkv[..., :model_width].reshape(heads_shape)
    self_keys = packed_qkv[..., model_width : 2 * model_width].reshape(heads_shape)
    self_values = packed_qkv[..., 2 * model_width :].reshape(heads_shape)
    positions = jnp.arange(cap_length)
    causal = (positions[None, :] <= positions[:, None])[None, None]
    present = (positions[None, :] < caption_len[:, None])[:, None, None, :]
    self_allowed = causal & present
    self_probs, self_log = softmax_forward(self_query, self_keys, self_allowed)
    self_mixed = (
        product(E_BHQK_BKHE_TO_BQHE, self_probs.astype(jnp.bfloat16), self_values)
        .reshape(token_layout_form)
        .astype(jnp.bfloat16)
    )
    first_sum = (
        input_values
        + product(E_BLD_DE_TO_BLE, self_mixed, tensors[SELF_OUT])
        + as_float(tensors, SELF_OUT_BIAS)
    )
    normed_two = layer_norm(
        first_sum, as_float(tensors, NORM_TWO_GAIN), as_float(tensors, NORM_TWO_SHIFT)
    ).astype(jnp.bfloat16)
    cross_queries = (
        (
            product(E_BLD_DE_TO_BLE, normed_two, tensors[CROSS_QUERY])
            + as_float(tensors, CROSS_QUERY_BIAS)
        )
        .astype(jnp.bfloat16)
        .reshape(heads_shape)
    )
    kv_bias = jnp.concatenate([zero_part, tensors[CROSS_VALUE_BIAS]]).astype(jnp.float32)
    kv_weight = tensors[CROSS_KV]
    group_kv = (
        product(E_TPD_DE_TO_TPE, lax.all_gather(tiles, FSDP, axis=0, tiled=True), kv_weight)
        + kv_bias
    ).astype(jnp.bfloat16)
    chosen = jnp.stack(
        [
            jnp.stack(
                [
                    lax.dynamic_index_in_dim(group_kv, tile_index[c, s], 0, keepdims=False)
                    for s in range(slot_count)
                ]
            )
            for c in range(caption_rows)
        ]
    )
    cross_keys = chosen[..., :model_width].reshape(key_shape)
    cross_values = chosen[..., model_width:].reshape(key_shape)
    usable = jnp.repeat(tile_valid > 0, patch_count, axis=1)[:, None, None, :]
    cross_probs, cross_log = softmax_forward(cross_queries, cross_keys, usable)
    cross_mixed = (
        product(E_BHQK_BKHE_TO_BQHE, cross_probs.astype(jnp.bfloat16), cross_values)
        .reshape(token_layout_form)
        .astype(jnp.bfloat16)
    )
    second = (
        first_sum
        + product(E_BLD_DE_TO_BLE, cross_mixed, tensors[CROSS_OUT])
        + as_float(tensors, CROSS_OUT_BIAS)
    )
    normed_three = layer_norm(
        second, as_float(tensors, NORM_THREE_GAIN), as_float(tensors, NORM_THREE_SHIFT)
    ).astype(jnp.bfloat16)
    preact = product(E_BLD_DF_TO_BLF, normed_three, tensors[MLP_UP]) + as_float(
        tensors, MLP_UP_BIAS
    )
    activation = gelu_exact(preact).astype(jnp.bfloat16)
    result = (
        second
        + product(E_BLF_FD_TO_BLD, activation, tensors[MLP_DOWN])
        + as_float(tensors, MLP_DOWN_BIAS)
    ).astype(jnp.bfloat16)
    back_flat = lax.all_gather(weights, FSDP, axis=0, tiled=True)
    tensors = unpack(back_flat, model_width, hidden_width)
    gradients = {}
    out_grad = d_out.astype(jnp.float32)
    gradients[MLP_DOWN] = product(E_BLF_BLD_TO_FD, activation, d_out)
    gradients[MLP_DOWN_BIAS] = column_sums(d_out)
    activ_grad = product(E_BLD_FD_TO_BLF, d_out, tensors[MLP_DOWN])
    gelu_value, gelu_pull = jax.vjp(gelu_exact, preact)
    preact_grad = gelu_pull(activ_grad)[0].astype(jnp.bfloat16)
    gradients[MLP_UP] = product(E_BLD_BLF_TO_DF, normed_three, preact_grad)
    gradients[MLP_UP_BIAS] = column_sums(preact_grad)
    second_grad = out_grad + norm_back(
        second,
        tensors,
        NORM_THREE_GAIN,
        NORM_THREE_SHIFT,
        product(E_BLF_DF_TO_BLD, preact_grad, tensors[MLP_UP]),
        gradients,
    )
    cross_branch = second_grad.astype(jnp.bfloat16)
    gradients[CROSS_OUT] = product(E_BLD_BLE_TO_DE, cross_mixed, cross_branch)
    gradients[CROSS_OUT_BIAS] = column_sums(cross_branch)
    cmixed_grad = (
        product(E_BLE_DE_TO_BLD, cross_branch, tensors[CROSS_OUT])
        .astype(jnp.bfloat16)
        .reshape(heads_shape)
    )
    cquery_grad, ckeys_grad, cvalues_grad = attention_backward_pass(
        cross_queries, cross_keys, cross_values, usable, cross_log, cmixed_grad
    )
    cquery_low = cquery_grad.astype(jnp.bfloat16).reshape(token_layout_form)
    gradients[CROSS_QUERY] = product(E_BLD_BLE_TO_DE, normed_two, cquery_low)
    gradients[CROSS_QUERY_BIAS] = column_sums(cquery_low)
    first_grad = second_grad + norm_back(
        first_sum,
        tensors,
        NORM_TWO_GAIN,
        NORM_TWO_SHIFT,
        product(E_BLE_DE_TO_BLD, cquery_low, tensors[CROSS_QUERY]),
        gradients,
    )
    slot_layout_form = (caption_rows, slot_count, patch_count, model_width)
    slot_grad = jnp.concatenate(
        [ckeys_grad.reshape(slot_layout_form), cvalues_grad.reshape(slot_layout_form)], axis=-1
    )
    picked = (tile_index[:, :, None] == jnp.arange(group_kv.shape[0])[None, None, :]).astype(
        jnp.float32
    )
    group_grad = jnp.einsum(E_CSG_CSPE_TO_GPE, picked, slot_grad, precision=lax.Precision.HIGHEST)
    arrived = lax.all_to_all(
        group_grad.astype(jnp.bfloat16), FSDP, split_axis=0, concat_axis=0, tiled=True
    ).astype(group_grad.dtype)
    own_grad = jnp.sum(arrived.reshape((group_size, own_tiles) + arrived.shape[1:]), axis=0).astype(
        jnp.bfloat16
    )
    gradients[CROSS_KV] = product(E_TPD_TPE_TO_DE, tiles, own_grad)
    gradients[CROSS_VALUE_BIAS] = column_sums(own_grad[..., model_width:])
    tiles_grad = product(E_TPE_DE_TO_TPD, own_grad, tensors[CROSS_KV])
    self_branch = first_grad.astype(jnp.bfloat16)
    gradients[SELF_OUT] = product(E_BLD_BLE_TO_DE, self_mixed, self_branch)
    gradients[SELF_OUT_BIAS] = column_sums(self_branch)
    smixed_grad = (
        product(E_BLE_DE_TO_BLD, self_branch, tensors[SELF_OUT])
        .astype(jnp.bfloat16)
        .reshape(heads_shape)
    )
    self_query_gradient, self_key_gradient, self_value_gradient = attention_backward_pass(
        self_query, self_keys, self_values, self_allowed, self_log, smixed_grad
    )
    qkv_grad = jnp.concatenate(
        [
            self_query_gradient.reshape(token_layout_form),
            self_key_gradient.reshape(token_layout_form),
            self_value_gradient.reshape(token_layout_form),
        ],
        axis=-1,
    ).astype(jnp.bfloat16)
    gradients[SELF_QKV] = product(E_BLD_BLE_TO_DE, normed_one, qkv_grad)
    gradients[SELF_QUERY_BIAS] = column_sums(qkv_grad[..., :model_width])
    gradients[SELF_VALUE_BIAS] = column_sums(qkv_grad[..., 2 * model_width :])
    caption_grad = first_grad + norm_back(
        input_values,
        tensors,
        NORM_ONE_GAIN,
        NORM_ONE_SHIFT,
        product(E_BLE_DE_TO_BLD, qkv_grad, tensors[SELF_QKV]),
        gradients,
    )
    flat_grad = pack_rows(gradients, model_width, hidden_width, total_rows)
    shard_rows = total_rows // (data_size * group_size)
    received = lax.all_to_all(
        for_sending(flat_grad), DP, split_axis=0, concat_axis=0, tiled=True
    ).astype(flat_grad.dtype)
    data_grad = jnp.sum(received.reshape(data_size, group_size * shard_rows, 128), axis=0)
    shard_grad = lax.psum_scatter(
        data_grad.astype(jnp.bfloat16), FSDP, scatter_dimension=0, tiled=True
    ).astype(jnp.float32)
    begin_row = lax.axis_index(BOTH) * shard_rows
    seg_starts, seg_ends, decay_flags, seg_entries = segment_table(model_width, hidden_width)
    row_ids = begin_row + jnp.arange(shard_rows)
    member = (row_ids[:, None] >= seg_starts[None, :]) & (row_ids[:, None] < seg_ends[None, :])
    row_squares = jnp.sum(shard_grad * shard_grad, axis=1)
    part_sums = jnp.sum(jnp.where(member, row_squares[:, None], 0.0), axis=0)
    square_sums = lax.psum(part_sums, BOTH)
    old_weights = lax.dynamic_slice_in_dim(back_flat, begin_row, shard_rows, 0).astype(jnp.float32)
    update, new_first, new_second, grad_norm, tensor_rms = adam_step(
        shard_grad,
        member,
        decay_flags,
        old_weights,
        first_moment,
        second_moment,
        square_sums,
        seg_entries,
    )
    return (
        result,
        caption_grad,
        tiles_grad,
        shard_grad,
        update,
        new_first,
        new_second,
        grad_norm,
        tensor_rms,
    )


D = HEADS * HEAD_DIM
NZ = 4
TOK = 128
PATCH = 196
PATCH_SENT = 208
PATCH_SLOT = 256
KEYS = 2 * PATCH_SLOT
LEAD = 80
BF, F32 = jnp.bfloat16, jnp.float32
MESH = pl.DeviceIdType.MESH
SHARD, PIECES, PIECE = 2312, 5, 464
OLD = 2320
PADDED = PIECES * PIECE
WINDOW = 8 * SHARD
CARRY = 96
SEGS = 24
QKV_AT, WO_AT, UQ_AT, UKV_AT, UO_AT, WIDE = 0, 2304, 3072, 3840, 5376, 6144
W1_AT, W2_AT = 0, 3072
(V_G1, V_C1, V_BQKV, V_BO, V_G2, V_C2, V_UQ, V_BKV, V_UO, V_G3, V_C3, V_B1, V_B2, V_SUMS) = range(14)


def row_starts():
    starts, at = {}, 0
    for label, shape, _ in layout(D, FF):
        starts[label] = at
        at += int(np.prod(shape)) // 128
    return starts


def mm(a, b):
    return lax.dot_general(a, b, (((1,), (0,)), ((), ())), preferred_element_type=F32)


def mm_nt(a, b):
    return lax.dot_general(a, b, (((1,), (1,)), ((), ())), preferred_element_type=F32)


def mm_tn(a, b):
    return lax.dot_general(a, b, (((0,), (0,)), ((), ())), preferred_element_type=F32)


def al(i, m):
    return pl.multiple_of(i * m, m)


def halves(pair):
    lane = lax.broadcasted_iota(jnp.int32, pair.shape, 1)
    zero = jnp.zeros_like(pair)
    return jnp.concatenate(
        [jnp.where(lane < HEAD_DIM, pair, zero), jnp.where(lane < HEAD_DIM, zero, pair)], axis=0
    )


def joined(stacked):
    n = stacked.shape[0] // 2
    lane = lax.broadcasted_iota(jnp.int32, (n, 128), 1)
    return jnp.where(lane < HEAD_DIM, stacked[:n], stacked[n:])


def normed(v):
    center = v - jnp.mean(v, axis=-1, keepdims=True)
    r = lax.rsqrt(jnp.mean(center * center, axis=-1, keepdims=True) + EPS_NORM)
    return center * r, r


def pair_kernel(
    cap, tiles, d_out, index, valid, length, weights,
    g_out, sums_out, old_out, out, dcap, dtile,
    fw, wide, gf, pc, ps, big1, big2, kv, dkvt, tl, tlT,
    xin, h1, am, h2, q2, a2, sb, rb, dy, t1, h1T, amT, h2T, a2T,
    x1, dx, acc, vec, meta, ob, pfx, pfx_in, carry, dcap_b, dtile_b,
    from_core, from_y, from_x, from_low, from_high, total, sq,
    wsem, gsem, send, recv, core_s, core_r, y_s, y_r, x_s, x_r, up_s, up_r, down_s, down_r, free, sum_s, sum_r,
):
    role = lax.axis_index(FSDP)
    other = 1 - role
    me = lax.axis_index(DP)
    my_z, my_y, my_core = me // 4, (me // 2) % 2, me % 2

    def at_dp(z, y, core):
        return {DP: z * 4 + y * 2 + core, FSDP: role}

    core_peer = at_dp(my_z, my_y, 1 - my_core)
    y_peer = at_dp(my_z, 1 - my_y, my_core)
    x_peer = {DP: me, FSDP: other}
    up_peer = at_dp(jnp.minimum(my_z + 1, NZ - 1), my_y, my_core)
    down_peer = at_dp(jnp.maximum(my_z - 1, 0), my_y, my_core)
    barrier = pltpu.get_barrier_semaphore()
    cube = []
    for k in range(1, 8):
        core = 1 - my_core if k & 1 else my_core
        y = 1 - my_y if k & 2 else my_y
        cube.append({DP: my_z * 4 + y * 2 + core, FSDP: other if k & 4 else role})
    for peer in cube:
        pl.semaphore_signal(barrier, inc=1, device_id=peer, device_id_type=MESH)
    for step in range(1, NZ):
        peer = at_dp((my_z + step) % NZ, my_y, my_core)
        pl.semaphore_signal(barrier, inc=1, device_id=peer, device_id_type=MESH)
    row0 = row_starts()

    cuts = [0, 13856, 18480, 23088, 32320, weights.shape[0]]
    loads = []
    for i in range(5):
        n = cuts[i + 1] - cuts[i]
        loads.append(
            pltpu.make_async_copy(
                weights.at[pl.ds(cuts[i], n)], fw.at[pl.ds(LEAD + cuts[i], n)], wsem.at[i]
            )
        )
    for c in loads:
        c.start()

    def to_other(src, dst, k):
        return pltpu.make_async_remote_copy(
            src_ref=src, dst_ref=dst, send_sem=send.at[k], recv_sem=recv.at[k],
            device_id=x_peer, device_id_type=MESH,
        )

    first, later = pl.ds(0, TOK), pl.ds(TOK, TOK)
    copies = dict(
        cap=to_other(cap, xin.at[later], 0),
        tile=to_other(tl.at[pl.ds(0, PATCH_SENT)], tl.at[pl.ds(PATCH_SLOT, PATCH_SENT)], 1),
        meta=to_other(meta.at[0], meta.at[1], 2),
        dy=to_other(d_out, dy.at[first], 3),
        lead=to_other(fw.at[pl.ds(weights.shape[0], LEAD)], fw.at[pl.ds(0, LEAD)], 4),
        out=to_other(t1.at[first], ob, 7),
        pfx=to_other(pfx, pfx_in, 8),
        old=to_other(
            weights.at[pl.ds(pl.multiple_of(((2 * me + other) % 16) * SHARD - 8 * other, 16), OLD)], old_out, 9
        ),
        dcap=to_other(dcap_b, dcap_b, 10),
        dtile=to_other(dtile_b, dtile_b, 11),
    )

    def to_other_half(c, k):
        rows = pl.ds(al(c, TOK), TOK)
        return to_other(sb.at[rows], rb.at[rows], k + c)

    def x2_copy(c):
        return to_other_half(c, 12)

    def dx2_copy(c):
        return to_other_half(c, 14)

    after = PATCH_SLOT + PATCH_SENT
    tl[0:PATCH_SLOT, :] = jnp.zeros((PATCH_SLOT, D), BF)
    tl[after:, :] = jnp.zeros((KEYS - after, D), BF)
    tl[0:PATCH, :] = tiles[...]
    counts = []
    for g in range(2):
        named_by = jnp.int32(0)
        for s in range(index.shape[1]):
            named = jnp.where(index[0, s] == g, jnp.int32(1), jnp.int32(0))
            named_by = named_by + jnp.where(valid[0, s] > 0, named, jnp.int32(0))
        counts.append(named_by)
    rows8 = lax.broadcasted_iota(jnp.int32, (8, 128), 0)
    meta[0] = jnp.where(
        rows8 == 0, counts[0], jnp.where(rows8 == 1, counts[1], length[0])
    ).astype(F32)

    def all_here():
        pl.semaphore_wait(barrier, len(cube) + NZ - 1)

    def vector(row, at, n, col=0):
        block = fw[pl.ds(at, n // 128), :].astype(F32)
        for j in range(n // 128):
            vec[row : row + 1, col + 128 * j : col + 128 * j + 128] = block[j : j + 1, :]

    def widen(at, k, col, rows=D):
        for j in range(k):
            wide[:, col + 128 * j : col + 128 * j + 128] = fw[pl.ds(at + j, rows, stride=k), :]

    def norm_forward(src, dst, g, c, at=0, n=2 * TOK):
        @pl.loop(0, n // 64, unroll=2)
        def _(i):
            rows = pl.ds(pl.multiple_of(at + 64 * i, 64), 64)
            v, _ = normed(src[rows, :].astype(F32))
            dst[rows, :] = (v * vec[g : g + 1, :D] + vec[c : c + 1, :D]).astype(BF)

    def norm_backward(src, dh, g, write, at=0, n=2 * TOK):
        def step(i, sums):
            rows = pl.ds(pl.multiple_of(at + 64 * i, 64), 64)
            v, r = normed(src[rows, :].astype(F32))
            d = dh[rows, :]
            dn = d * vec[g : g + 1, :D]
            dv = r * (
                dn - jnp.mean(dn, axis=-1, keepdims=True) - v * jnp.mean(dn * v, axis=-1, keepdims=True)
            )
            write(rows, dv)
            return (
                sums[0] + jnp.sum(d * v, axis=0, keepdims=True),
                sums[1] + jnp.sum(d, axis=0, keepdims=True),
            )

        return lax.fori_loop(0, n // 64, step, (jnp.zeros((1, D), F32), jnp.zeros((1, D), F32)), unroll=2)

    def put_vector(at, row, into=gf):
        for j in range(row.shape[1] // 128):
            into[at + j : at + j + 1, :] = row[:, 128 * j : 128 * j + 128]

    def column_total(ref, cols):
        return jnp.sum(ref[:, cols].astype(F32), axis=0, keepdims=True)

    def matrix_grad(at, k, lhs_t, rhs, transposed=False):
        @pl.loop(0, k // 2, unroll=3)
        def _(m):
            cols = pl.ds(al(m, 256), 256)
            res = mm_nt(lhs_t[...], rhs[cols, :]) if transposed else mm(lhs_t[...], rhs[:, cols])
            for half in range(2):
                gf[pl.ds(at + 2 * m + half, D, stride=k), :] = res[:, 128 * half : 128 * half + 128]

    def copy_to(peer, src, dst, ssem, rsem):
        return pltpu.make_async_remote_copy(
            src_ref=src, dst_ref=dst, send_sem=ssem, recv_sem=rsem, device_id=peer, device_id_type=MESH
        )

    def slot(w, s, core, y=0, x=0):
        return pl.multiple_of(((w * PIECES + s) * 8 + core * 4 + y * 2 + x) * PIECE, 16)

    class Scatter:
        def __init__(self, w, x):
            self.w, self.x = w, x

        def core(self, s):
            rows = pl.ds(slot(self.w, s, 1 - my_core), 4 * PIECE)
            return copy_to(core_peer, fw.at[rows], from_core.at[s], core_s.at[self.w, s], core_r.at[self.w, s])

        def y(self, s):
            rows = pl.ds(slot(self.w, s, my_core, 1 - my_y), 2 * PIECE)
            return copy_to(y_peer, fw.at[rows], from_y.at[self.w, s], y_s.at[self.w, s], y_r.at[self.w, s])

        def over(self, s):
            rows = pl.ds(slot(self.w, s, my_core, my_y, 1 - self.x), PIECE)
            return copy_to(x_peer, fw.at[rows], from_x.at[self.w, s], x_s.at[self.w, s], x_r.at[self.w, s])

        def held(self, s, h):
            if h == self.x:
                return fw.at[pl.ds(slot(self.w, s, my_core, my_y, self.x), PIECE)]
            return from_x.at[self.w, s]

        def up(self, s, h):
            return copy_to(
                up_peer, self.held(s, h), from_low.at[self.w, s, h], up_s.at[self.w, s, h], up_r.at[self.w, s, h]
            )

        def down(self, s, h):
            return copy_to(
                down_peer, self.held(s, h), from_high.at[self.w, s, h], down_s.at[self.w, s, h], down_r.at[self.w, s, h]
            )

        def cast(self, first_row):
            @pl.loop(0, PIECES)
            def _(s):
                for k in range(8):
                    j = (k & 2) * 2 + (k & 4) // 2 + (k & 1)
                    src = pl.ds(pl.multiple_of(first_row + j * SHARD + s * PIECE, 8), PIECE)
                    fw[pl.ds(pl.multiple_of(slot(self.w, s, 0) + k * PIECE, 16), PIECE), :] = gf[src, :].astype(BF)
                self.core(s).start()

        def add_core(self):
            @pl.loop(0, PIECES)
            def _(s):
                self.core(s).wait_recv()
                rows = pl.ds(slot(self.w, s, my_core), 4 * PIECE)
                fw[rows, :] = fw[rows, :] + from_core[s]
                self.y(s).start()

        def add_y(self, s):
            self.y(s).wait_recv()
            rows = pl.ds(slot(self.w, s, my_core, my_y), 2 * PIECE)
            fw[rows, :] = fw[rows, :] + from_y[self.w, s]
            self.over(s).start()

        def from_ends(self, s, h):
            if h != self.x:
                self.over(s).wait_recv()
            goal = 2 * h + self.w
            if goal > 0:
                pl.when(my_z == 0)(self.up(s, h).start)
            if goal < NZ - 1:
                pl.when(my_z == NZ - 1)(self.down(s, h).start)

        def relay(self, s, hop, h):
            goal = 2 * h + self.w
            mine = self.held(s, h)
            if hop < goal:

                @pl.when(my_z == hop)
                def _():
                    self.up(s, h).wait_recv()
                    mine[...] = mine[...] + from_low[self.w, s, h]
                    self.up(s, h).start()

            if NZ - 1 - hop > goal:

                @pl.when(my_z == NZ - 1 - hop)
                def _():
                    self.down(s, h).wait_recv()
                    mine[...] = mine[...] + from_high[self.w, s, h]
                    self.down(s, h).start()

        def step(self, t):
            own, came = self.x, 1 - self.x
            parts = [
                (3, lambda s: self.relay(s, 2, came)),
                (2, lambda s: self.relay(s, 2, own)),
                (2, lambda s: self.relay(s, 1, came)),
                (1, lambda s: self.relay(s, 1, own)),
                (1, lambda s: self.from_ends(s, came)),
                (0, self.add_y),
                (0, lambda s: self.from_ends(s, own)),
            ]
            for lag, part in parts:
                s = t - lag
                if isinstance(t, int):
                    if 0 <= s < PIECES:
                        part(s)
                else:
                    pl.when((s >= 0) & (s < PIECES))(functools.partial(part, s))

        def collect(self, s):
            for h in range(2):
                goal = 2 * h + self.w

                @pl.when(my_z == goal)
                def _():
                    whole = self.held(s, h)[...].astype(F32)
                    if goal > 0:
                        self.up(s, h).wait_recv()
                        whole = whole + from_low[self.w, s, h].astype(F32)
                    if goal < NZ - 1:
                        self.down(s, h).wait_recv()
                        whole = whole + from_high[self.w, s, h].astype(F32)
                    total[pl.ds(pl.multiple_of(s * PIECE, 8), PIECE), :] = whole

        def sent(self):
            @pl.loop(0, PIECES)
            def _(s):
                self.core(s).wait_send()
                self.y(s).wait_send()
                self.over(s).wait_send()
                for h in range(2):
                    goal = 2 * h + self.w
                    pl.when(my_z < goal)(self.up(s, h).wait_send)
                    pl.when(my_z > goal)(self.down(s, h).wait_send)

    def rest_of_scatter(one, zero, begun):
        @pl.loop(begun, 2 * PIECES + 3)
        def _(t):
            one.step(t)
            zero.step(t - PIECES)

        pl.loop(0, PIECES)(one.collect)
        pl.loop(0, PIECES)(zero.collect)
        one.sent()
        zero.sent()

    def square_sums():
        total[SHARD:, :] = jnp.zeros((total.shape[0] - SHARD, 128), F32)
        done = pltpu.make_async_copy(total.at[pl.ds(0, OLD)], g_out, gsem)
        done.start()
        seg = lax.broadcasted_iota(jnp.int32, (SEGS, 1), 0)
        begin = jnp.full((SEGS, 1), 1 << 30, jnp.int32)
        end = begin
        for i, (a, b) in enumerate(zip(*segment_table(D, FF)[:2])):
            begin = jnp.where(seg == i, int(a), begin)
            end = jnp.where(seg == i, int(b), end)
        row = (me * 2 + role) * SHARD + lax.broadcasted_iota(jnp.int32, (SEGS, total.shape[0]), 1)
        member = jnp.where((row >= begin) & (row < end), 1.0, 0.0).astype(BF)
        square = total[...] * total[...]
        high = square.astype(BF)
        squares = mm(member, high) + mm(member, (square - high.astype(F32)).astype(BF))
        mine = jnp.broadcast_to(jnp.sum(squares, axis=1, keepdims=True), (SEGS, 128))
        sq[0] = mine
        swaps = [copy_to(p, sq.at[0], sq.at[k], sum_s.at[k], sum_r.at[k]) for k, p in enumerate(cube, 1)]
        for c in swaps:
            c.start()
        for c in swaps:
            c.wait()
        mine = jnp.zeros((SEGS, 128), F32)
        for k in range(8):
            core = 1 - my_core if k & 1 else my_core
            y = 1 - my_y if k & 2 else my_y
            mine = mine + sq[core + 2 * y + 4 * (1 - role if k & 4 else role)]
        sq[8] = mine
        sends = []
        for step in range(1, NZ):
            to = at_dp((my_z + step) % NZ, my_y, my_core)
            sends.append(copy_to(to, sq.at[8], sq.at[8 + step], sum_s.at[7 + step], sum_r.at[7 + step]))
            sends[-1].start()
        for c in sends:
            c.wait()
        whole = jnp.zeros((SEGS, 128), F32)
        for z in range(NZ):
            part = mine
            for step in range(1, NZ):
                part = jnp.where((my_z - step + NZ) % NZ == z, sq[8 + step], part)
            whole = whole + part
        sums_out[...] = whole
        done.wait()

    def attention_role():
        at = {k: LEAD + v for k, v in row0.items()}
        at0 = {k: CARRY + v for k, v in row0.items()}
        at1 = {k: CARRY - WINDOW + v for k, v in row0.items()}
        one, zero = Scatter(1, 0), Scatter(0, 0)
        xin[first, :] = cap[...]
        loads[0].wait()
        vector(V_G1, at[NORM_ONE_GAIN], D)
        vector(V_C1, at[NORM_ONE_SHIFT], D)
        vec[V_BQKV : V_BQKV + 1, :] = jnp.zeros((1, FF), F32)
        vec[V_BKV : V_BKV + 1, :] = jnp.zeros((1, FF), F32)
        vector(V_BQKV, at[SELF_QUERY_BIAS], D)
        vector(V_BQKV, at[SELF_VALUE_BIAS], D, 2 * D)
        widen(at[SELF_QKV], 18, QKV_AT)
        for c in loads[1:]:
            c.wait()
        vector(V_BO, at[SELF_OUT_BIAS], D)
        vector(V_G2, at[NORM_TWO_GAIN], D)
        vector(V_C2, at[NORM_TWO_SHIFT], D)
        vector(V_UQ, at[CROSS_QUERY_BIAS], D)
        vector(V_BKV, at[CROSS_VALUE_BIAS], D, D)
        vector(V_UO, at[CROSS_OUT_BIAS], D)
        widen(at[SELF_OUT], 6, WO_AT)
        widen(at[CROSS_QUERY], 6, UQ_AT)
        widen(at[CROSS_KV], 12, UKV_AT)
        widen(at[CROSS_OUT], 6, UO_AT)
        all_here()
        copies["dy"].start()
        copies["lead"].start()

        copies["cap"].wait_recv()
        norm_forward(xin, h1, V_G1, V_C1)

        for j in range(3):
            cols = slice(D * j, D * j + D)
            big1[:, cols] = (mm(h1[...], wide[:, cols]) + vec[V_BQKV : V_BQKV + 1, cols]).astype(BF)

        copies["meta"].wait_recv()

        @pl.loop(0, 12, unroll=6)
        def _(i):
            c, p = i // 6, i % 6
            rows = pl.ds(al(c, TOK), TOK)
            qq = halves(big1[rows, pl.ds(al(p, 128), 128)]) * BF(0.125)
            k2 = big1[rows, pl.ds(al(p, 128) + D, 128)]
            v2 = big1[rows, pl.ds(al(p, 128) + 2 * D, 128)]
            s = mm_nt(qq, k2)
            row = lax.broadcasted_iota(jnp.int32, s.shape, 0) % TOK
            col = lax.broadcasted_iota(jnp.int32, s.shape, 1)
            present = col.astype(F32) < meta[c][2:3, :]
            s = jnp.where((col <= row) & present, s, NEG_LARGE)
            e = jnp.exp(s - jnp.max(s, axis=-1, keepdims=True))
            prob = (e * (1.0 / jnp.sum(e, axis=-1, keepdims=True))).astype(BF)
            ps[i] = prob
            am[rows, pl.ds(al(p, 128), 128)] = joined(mm(prob, v2)).astype(BF)

        x1[...] = xin[...].astype(F32) + mm(am[...], wide[:, WO_AT : WO_AT + D]) + vec[V_BO : V_BO + 1, :D]
        norm_forward(x1, h2, V_G2, V_C2)
        q2[...] = (mm(h2[...], wide[:, UQ_AT : UQ_AT + D]) + vec[V_UQ : V_UQ + 1, :D]).astype(BF)
        copies["tile"].wait_recv()

        for j in range(2):
            cols = slice(D * j, D * j + D)
            kv[:, cols] = (
                mm(tl[...], wide[:, UKV_AT + D * j : UKV_AT + D * j + D]) + vec[V_BKV : V_BKV + 1, cols]
            ).astype(BF)

        @pl.loop(0, 2)
        def _(c):
            rows = pl.ds(al(c, TOK), TOK)
            col = lax.broadcasted_iota(jnp.int32, (1, KEYS), 1)
            m = meta[c]
            c0 = jnp.concatenate([m[0:1, :]] * (KEYS // 128), axis=1)
            c1 = jnp.concatenate([m[1:2, :]] * (KEYS // 128), axis=1)
            count = jnp.where(col < PATCH, c0, jnp.where(col < PATCH_SLOT, 0.0, c1))
            count = jnp.where(col < PATCH_SLOT + PATCH, count, 0.0)

            @pl.loop(0, 6, unroll=6)
            def _(p):
                qq = halves(q2[rows, pl.ds(al(p, 128), 128)]) * BF(0.125)
                s = mm_nt(qq, kv[:, pl.ds(al(p, 128), 128)])
                s = jnp.where(count > 0.0, s, NEG_LARGE)
                e = jnp.exp(s - jnp.max(s, axis=-1, keepdims=True)) * count
                prob = (e * (1.0 / jnp.sum(e, axis=-1, keepdims=True))).astype(BF)
                pc[pl.ds(al(6 * c + p, 2 * TOK), 2 * TOK), :] = prob
                a2[rows, pl.ds(al(p, 128), 128)] = joined(
                    mm(prob, kv[:, pl.ds(al(p, 128) + D, 128)])
                ).astype(BF)

            sb[rows, :] = (
                x1[rows, :] + mm(a2[rows, :], wide[:, UO_AT : UO_AT + D]) + vec[V_UO : V_UO + 1, :D]
            ).astype(BF)
            x2_copy(c).start()

        copies["old"].start()

        h1T[...] = h1[...].T
        amT[...] = am[...].T
        h2T[...] = h2[...].T
        a2T[...] = a2[...].T
        tlT[...] = tl[...].T

        part_at = at1[CROSS_KV]

        def attend_back(c, p, take_keys):
            rows = pl.ds(c * TOK, TOK)
            lanes, vlanes = pl.ds(al(p, 128), 128), pl.ds(al(p, 128) + D, 128)
            qq = halves(q2[rows, lanes]) * BF(0.125)
            do = halves(t1[rows, lanes])
            prob = pc[pl.ds(al(6 * c + p, 2 * TOK), 2 * TOK), :]
            pf = prob.astype(F32)
            dp = mm_nt(do, kv[:, vlanes])
            ds = (pf * (dp - jnp.sum(pf * dp, axis=-1, keepdims=True))).astype(BF)
            am[rows, lanes] = (joined(mm(ds, kv[:, lanes])) * 0.125).astype(BF)
            take_keys(p, 0, lanes, mm_tn(qq, ds))
            take_keys(p, 1, vlanes, mm_tn(do, prob))

        def part_rows(p, k, j):
            return pl.ds(pl.multiple_of(part_at + ((2 * p + k) * 4 + j) * 128, 8), 128)

        def keep(p, k, lanes, term):
            for j in range(4):
                gf[part_rows(p, k, j), :] = term[:, 128 * j : 128 * j + 128]

        def complete(p, k, lanes, term):
            for j in range(4):
                cols = slice(128 * j, 128 * j + 128)
                dkvt[lanes, cols] = (gf[part_rows(p, k, j), :] + term[:, cols]).astype(BF)

        for c, take_keys in enumerate((keep, complete)):
            rows = pl.ds(c * TOK, TOK)
            dx2_copy(c).wait_recv()
            t1[rows, :] = mm_nt(rb[rows, :], wide[:, UO_AT : UO_AT + D]).astype(BF)
            pl.loop(0, 6, unroll=6)(functools.partial(attend_back, c, take_keys=take_keys))

        put_vector(at1[CROSS_OUT_BIAS], column_total(rb, slice(None)))
        matrix_grad(at1[CROSS_OUT], 6, a2T, rb)
        put_vector(at1[CROSS_QUERY_BIAS], column_total(am, slice(None)))
        matrix_grad(at1[CROSS_QUERY], 6, h2T, am)
        matrix_grad(at1[CROSS_KV], 12, tlT, dkvt, transposed=True)
        kv[...] = dkvt[...].T
        put_vector(at1[CROSS_VALUE_BIAS], column_total(kv, slice(D, 2 * D)))
        copies["pfx"].wait_recv()
        gf[pl.ds(at1[NORM_THREE_GAIN], LEAD - 12), :] = pfx_in[12:, :]
        copies["lead"].wait_send()
        one.cast(CARRY)
        carry[...] = gf[0:CARRY, :]

        def tile_grad(rows):
            return mm_nt(kv[rows, :], wide[:, UKV_AT : UKV_AT + 2 * D])

        dtile[:, 0, :] = tile_grad(pl.ds(0, PATCH_SENT))[:PATCH]
        dtile_b[...] = tile_grad(pl.ds(PATCH_SLOT, PATCH_SENT)).astype(BF)
        copies["dtile"].start()
        one.add_core()
        pl.semaphore_signal(free, inc=1, device_id=core_peer, device_id_type=MESH)
        acc[...] = mm_nt(am[...], wide[:, UQ_AT : UQ_AT + D])
        e1 = h2

        def write_dx1(rows, dv):
            full = rb[rows, :].astype(F32) + dv
            dx[rows, :] = full
            e1[rows, :] = full.astype(BF)

        gg, gc = norm_backward(x1, acc, V_G2, write_dx1)
        put_vector(at0[NORM_TWO_GAIN], gg)
        put_vector(at0[NORM_TWO_SHIFT], gc)
        put_vector(at0[SELF_OUT_BIAS], column_total(e1, slice(None)))
        matrix_grad(at0[SELF_OUT], 6, amT, e1)
        t1[...] = mm_nt(e1[...], wide[:, WO_AT : WO_AT + D]).astype(BF)

        @pl.loop(0, 12, unroll=6)
        def _(i):
            c, p = i // 6, i % 6
            rows = pl.ds(al(c, TOK), TOK)
            lanes = pl.ds(al(p, 128), 128)
            klanes, vlanes = pl.ds(al(p, 128) + D, 128), pl.ds(al(p, 128) + 2 * D, 128)
            qq = halves(big1[rows, lanes]) * BF(0.125)
            do = halves(t1[rows, lanes])
            prob = ps[i]
            pf = prob.astype(F32)
            dp = mm_nt(do, big1[rows, vlanes])
            ds = (pf * (dp - jnp.sum(pf * dp, axis=-1, keepdims=True))).astype(BF)
            big2[rows, lanes] = (joined(mm(ds, big1[rows, klanes])) * 0.125).astype(BF)
            big2[rows, klanes] = mm_tn(ds, qq).astype(BF)
            big2[rows, vlanes] = mm_tn(prob, do).astype(BF)

        one.step(0)
        acc[...] = mm_nt(big2[:, : 3 * D], wide[:, : 3 * D])

        def write_dx0(rows, dv):
            dx[rows, :] = dx[rows, :] + dv

        gg, gc = norm_backward(xin, acc, V_G1, write_dx0)
        put_vector(at0[NORM_ONE_GAIN], gg)
        put_vector(at0[NORM_ONE_SHIFT], gc)
        dcap[...] = dx[first, :]
        dcap_b[...] = dx[later, :].astype(BF)
        copies["dcap"].start()
        one.step(1)
        put_vector(at0[SELF_QUERY_BIAS], column_total(big2, slice(0, D)))
        put_vector(at0[SELF_VALUE_BIAS], column_total(big2, slice(2 * D, 3 * D)))
        matrix_grad(at0[SELF_QKV], 18, h1T, big2)
        gf[pl.ds(at0[CROSS_QUERY], WINDOW - row0[CROSS_QUERY]), :] = carry[
            row0[CROSS_QUERY] - WINDOW + CARRY :, :
        ]
        pl.semaphore_wait(free, 1)
        zero.cast(CARRY)
        one.step(2)
        zero.add_core()
        rest_of_scatter(one, zero, 3)
        copies["out"].wait_recv()
        out[...] = ob[...]
        for name in ("dy", "dcap", "dtile"):
            copies[name].wait_send()
        for c in range(2):
            x2_copy(c).wait_send()
        copies["old"].wait()
        square_sums()

    def mlp_role():
        all_here()
        copies["meta"].start()
        copies["cap"].start()
        copies["cap"].wait_send()
        copies["tile"].start()
        base = LEAD - weights.shape[0]
        at = {k: base + v for k, v in row0.items()}
        at0 = {k: CARRY - weights.shape[0] + v for k, v in row0.items()}
        at1 = {k: v - WINDOW for k, v in at0.items()}
        one, zero = Scatter(1, 1), Scatter(0, 1)
        dy[later, :] = d_out[...]
        for c in loads:
            c.wait()
        for b in range(4):
            widen(at[MLP_DOWN] + 6 * D * b, 6, W2_AT + D * b)
        copies["lead"].wait_recv()
        widen(at[MLP_UP], 24, W1_AT)
        vector(V_G3, at[NORM_THREE_GAIN], D)
        vector(V_C3, at[NORM_THREE_SHIFT], D)
        vector(V_B1, at[MLP_UP_BIAS], FF)
        vector(V_B2, at[MLP_DOWN_BIAS], D)
        copies["dy"].wait_recv()

        @pl.loop(0, 4)
        def _(b):
            dg = mm_nt(dy[...], wide[:, pl.ds(al(b, D) + W2_AT, D)])
            for j in range(6):
                gf[pl.ds(al(6 * b + j, 256), 256), :] = dg[:, 128 * j : 128 * j + 128]

        def write_dx2(rows, dv):
            sb[rows, :] = (dy[rows, :].astype(F32) + dv).astype(BF)

        vec[V_SUMS : V_SUMS + 2, :] = jnp.zeros((2, FF), F32)

        @pl.loop(0, 2)
        def _(c):
            cap_rows = pl.ds(al(c, TOK), TOK)
            x2_copy(c).wait_recv()
            norm_forward(rb, h1, V_G3, V_C3, c * TOK, TOK)
            z_parts = [x1.at[first], x1.at[later], dx.at[first], dx.at[later]]
            for b in range(4):
                cols = slice(D * b, D * b + D)
                z_parts[b][...] = mm(h1[cap_rows, :], wide[:, cols]) + vec[V_B1 : V_B1 + 1, cols]

            @pl.loop(0, 4)
            def _(i):
                here = pl.ds(al(i, 32), 32)
                rows = pl.ds(al(c, TOK) + al(i, 32), 32)
                for k in range(24):
                    z = z_parts[k // 6][here, 128 * (k % 6) : 128 * (k % 6) + 128]
                    phi = 0.5 + 0.5 * lax.erf(z * np.float32(np.sqrt(0.5)))
                    dens = jnp.exp(-0.5 * z * z) * np.float32(1.0 / np.sqrt(2.0 * np.pi))
                    lanes = slice(128 * k, 128 * k + 128)
                    big1[rows, lanes] = (z * phi).astype(BF)
                    dg = gf[pl.ds(256 * k + al(c, TOK) + al(i, 32), 32), :]
                    big2[rows, lanes] = (dg * (phi + z * dens)).astype(BF)

            acc[cap_rows, :] = mm_nt(big2[cap_rows, :], wide[:, W1_AT : W1_AT + FF])
            gg, gc = norm_backward(rb, acc, V_G3, write_dx2, c * TOK, TOK)
            vec[V_SUMS : V_SUMS + 1, :D] = vec[V_SUMS : V_SUMS + 1, :D] + gg
            vec[V_SUMS + 1 : V_SUMS + 2, :D] = vec[V_SUMS + 1 : V_SUMS + 2, :D] + gc
            dx2_copy(c).start()

        put_vector(12, vec[V_SUMS : V_SUMS + 1, :D], pfx)
        put_vector(18, vec[V_SUMS + 1 : V_SUMS + 2, :D], pfx)

        h1T[...] = h1[...].T
        pfx[0:12, :] = jnp.zeros((12, 128), F32)
        for b in range(4):
            head = mm(h1T[0:8, :], big2[:, D * b : D * b + D])
            for r in range(3):
                for j in range(6):
                    row = 24 + 24 * r + 6 * b + j
                    if row < LEAD:
                        pfx[row : row + 1, :] = head[r : r + 1, 128 * j : 128 * j + 128]
        copies["pfx"].start()
        copies["old"].start()

        acc[...] = rb[...].astype(F32) + vec[V_B2 : V_B2 + 1, :D]
        for b in range(4):
            cols = slice(D * b, D * b + D)
            acc[...] = acc[...] + mm(big1[:, cols], wide[:, W2_AT + D * b : W2_AT + D * b + D])
            pc[D * b : D * b + D, 0:256] = big1[:, cols].T

        t1[first, :] = acc[first, :].astype(BF)
        copies["out"].start()
        out[...] = acc[later, :].astype(BF)
        gf[pl.ds(at1[MLP_DOWN_BIAS] + 6, WINDOW + CARRY - at1[MLP_DOWN_BIAS] - 6), :] = jnp.zeros(
            (WINDOW + CARRY - at1[MLP_DOWN_BIAS] - 6, 128), F32
        )
        put_vector(at1[MLP_DOWN_BIAS], column_total(dy, slice(None)))
        for b in range(4):
            matrix_grad(at1[MLP_DOWN] + 6 * D * b, 6, pc.at[pl.ds(D * b, D), pl.ds(0, 256)], dy)
        one.cast(CARRY)
        carry[...] = gf[0:CARRY, :]
        put_vector(at0[MLP_UP_BIAS], column_total(big2, slice(None)))
        matrix_grad(at0[MLP_UP], 24, h1T, big2)
        one.add_core()
        pl.semaphore_signal(free, inc=1, device_id=core_peer, device_id_type=MESH)
        gf[pl.ds(at0[MLP_DOWN], CARRY), :] = carry[...]
        pl.semaphore_wait(free, 1)
        zero.cast(CARRY)
        zero.add_core()
        rest_of_scatter(one, zero, 0)
        copies["dtile"].wait_recv()
        dtile[:, 0, :] = dtile_b[0:PATCH, :].astype(F32)
        copies["dcap"].wait_recv()
        dcap[...] = dcap_b[...].astype(F32)
        for name in ("tile", "meta", "pfx", "out"):
            copies[name].wait_send()
        for c in range(2):
            dx2_copy(c).wait_send()
        copies["old"].wait()
        square_sums()

    pl.when(role == 0)(attention_role)
    pl.when(role == 1)(mlp_role)


def pair_call(cap, tiles, d_out, index, valid, length, weights):
    vm = pl.BlockSpec(memory_space=pltpu.VMEM)
    sm = pl.BlockSpec(memory_space=pltpu.SMEM)
    hbm = pl.BlockSpec(memory_space=pl.ANY)
    S = jax.ShapeDtypeStruct
    dma, both = pltpu.SemaphoreType.DMA, 2 * TOK

    def bf(*s):
        return pltpu.VMEM(s, BF)

    def fl(*s):
        return pltpu.VMEM(s, F32)

    return pl.pallas_call(
        pair_kernel,
        in_specs=[vm, vm, vm, sm, sm, sm, hbm],
        out_specs=[hbm, vm, hbm, vm, vm, vm],
        out_shape=[
            S((OLD, 128), F32),
            S((SEGS, 128), F32),
            S((OLD, 128), BF),
            S((TOK, D), BF),
            S((TOK, D), F32),
            S((PATCH, 1, D), F32),
        ],
        scratch_shapes=[
            bf(16 * PADDED, 128), bf(D, WIDE), fl(CARRY + 7 * SHARD + PADDED, 128), bf(12 * both, KEYS),
            bf(12, both, 128), bf(both, FF), bf(both, FF), bf(KEYS, 2 * D), bf(2 * D, KEYS), bf(KEYS, D), bf(D, KEYS),
            *[bf(both, D) for _ in range(10)],
            *[bf(D, both) for _ in range(4)],
            *[fl(both, D) for _ in range(3)],
            fl(16, FF), fl(2, 8, 128), bf(TOK, D), fl(LEAD, 128), fl(LEAD, 128), fl(CARRY, 128),
            bf(TOK, D), bf(PATCH_SENT, D),
            bf(PIECES, 4 * PIECE, 128), bf(2, PIECES, 2 * PIECE, 128), bf(2, PIECES, PIECE, 128),
            bf(2, PIECES, 2, PIECE, 128), bf(2, PIECES, 2, PIECE, 128), fl(2432, 128), fl(8 + NZ, SEGS, 128),
            dma((5,)), dma, dma((16,)), dma((16,)),
            *[dma((2, PIECES)) for _ in range(6)],
            *[dma((2, PIECES, 2)) for _ in range(4)],
            pltpu.SemaphoreType.REGULAR, dma((7 + NZ,)), dma((7 + NZ,)),
        ],
        compiler_params=pltpu.CompilerParams(
            collective_id=0, has_side_effects=True, vmem_limit_bytes=63 * 2**20
        ),
    )(cap, tiles, d_out, index, valid, length, weights)


def pair_update(grads, old_weights, first_moment, second_moment, square_sums):
    seg_starts, seg_ends, decay_flags, seg_entries = segment_table(D, FF)
    grad_norm = jnp.sqrt(jnp.sum(square_sums))
    tensor_rms = jnp.sqrt(square_sums / jnp.asarray(seg_entries, dtype=square_sums.dtype))
    clipped = grads * jnp.minimum(1.0, CLIP_NORM / (grad_norm + 1e-06))
    new_first = BETA_ONE * first_moment + (1.0 - BETA_ONE) * clipped
    new_second = BETA_TWO * second_moment + (1.0 - BETA_TWO) * clipped * clipped
    first_hat = new_first / (1.0 - BETA_ONE**STEP)
    second_hat = new_second / (1.0 - BETA_TWO**STEP)
    row = lax.axis_index(BOTH) * SHARD + lax.broadcasted_iota(jnp.int32, grads.shape, 0)
    decays = row < 0
    for start, end, decay in zip(seg_starts, seg_ends, decay_flags):
        if decay:
            decays = decays | ((row >= int(start)) & (row < int(end)))
    decayed = jnp.where(decays, old_weights, 0.0)
    update = -LEARN_RATE * (first_hat / (jnp.sqrt(second_hat) + ADAM_EPS) + DECAY_RATE * decayed)
    return (update, new_first, new_second, grad_norm, tensor_rms)


def pair_body(
    captions, tiles, tile_index, tile_valid, caption_len, weights, first_moment, second_moment, d_out
):
    me, f = lax.axis_index(DP), lax.axis_index(FSDP)
    padded, sums, old, out, caption_grad, tiles_grad = pair_call(
        captions[0], tiles[0], d_out[0], tile_index, tile_valid, caption_len, weights
    )
    shard_grad = padded[:SHARD]
    own = lax.dynamic_slice_in_dim(weights, ((2 * me + f) % 16) * SHARD, SHARD, 0)
    old = lax.dynamic_slice_in_dim(old, 8 * f, SHARD, 0)
    old_weights = jnp.where(me // 8 == f, own, old).astype(jnp.float32)
    update, new_first, new_second, grad_norm, tensor_rms = pair_update(
        shard_grad, old_weights, first_moment, second_moment, sums[:21, 0]
    )
    return (
        out[None], caption_grad[None], jnp.swapaxes(tiles_grad, 0, 1), shard_grad, update, new_first, new_second,
        grad_norm, tensor_rms,
    )


def solution(mesh):
    placed = (
        P(BOTH, None, None),
        P(BOTH, None, None),
        P(BOTH, None),
        P(BOTH, None),
        P(BOTH),
        P(FSDP, None),
        P(BOTH, None),
        P(BOTH, None),
        P(BOTH, None, None),
    )
    return jax.shard_map(
        pair_body if mesh.shape[FSDP] == 2 else body,
        mesh=mesh,
        in_specs=placed,
        out_specs=(
            P(BOTH, None, None),
            P(BOTH, None, None),
            P(BOTH, None, None),
            P(BOTH, None),
            P(BOTH, None),
            P(BOTH, None),
            P(BOTH, None),
            P(),
            P(),
        ),
        check_vma=False,
    )
```

```python
import functools

import jax
import jax.numpy as jnp
import numpy as np
from jax import lax
from jax.experimental import pallas as pl
from jax.experimental.pallas import tpu as pltpu
from jax.sharding import PartitionSpec as P

HEADS = 12
HEAD_DIM = 64
FF = 3072
STEP = 10


EPS_NORM = 1e-05
CLIP_NORM = 1.0
BETA_ONE = 0.9
BETA_TWO = 0.999
LEARN_RATE = 0.01
DECAY_RATE = 0.1
ADAM_EPS = 1e-08
NEG_LARGE = -1e30
(NORM_ONE_GAIN, NORM_ONE_SHIFT, SELF_QKV, SELF_QUERY_BIAS, SELF_VALUE_BIAS, SELF_OUT, SELF_OUT_BIAS, NORM_TWO_GAIN, NORM_TWO_SHIFT, CROSS_QUERY, CROSS_QUERY_BIAS, CROSS_KV, CROSS_VALUE_BIAS, CROSS_OUT, CROSS_OUT_BIAS, NORM_THREE_GAIN, NORM_THREE_SHIFT, MLP_UP, MLP_UP_BIAS, MLP_DOWN, MLP_DOWN_BIAS) = range(21)
DP, FSDP = "dp", "fsdp"
BOTH = (DP, FSDP)
E_BHQK_BKHE_TO_BQHE = "bhqk,bkhe->bqhe"
E_BHQK_BQHE_TO_BKHE = "bhqk,bqhe->bkhe"
E_BLD_BLE_TO_DE = "bld,ble->de"
E_BLD_BLF_TO_DF = "bld,blf->df"
E_BLD_DE_TO_BLE = "bld,de->ble"
E_BLD_DF_TO_BLF = "bld,df->blf"
E_BLD_FD_TO_BLF = "bld,fd->blf"
E_BLE_DE_TO_BLD = "ble,de->bld"
E_BLF_BLD_TO_FD = "blf,bld->fd"
E_BLF_DF_TO_BLD = "blf,df->bld"
E_BLF_FD_TO_BLD = "blf,fd->bld"
E_BQHE_BKHE_TO_BHQK = "bqhe,bkhe->bhqk"
E_CSG_CSPE_TO_GPE = "csg,cspe->gpe"
E_TPD_DE_TO_TPE = "tpd,de->tpe"
E_TPD_TPE_TO_DE = "tpd,tpe->de"
E_TPE_DE_TO_TPD = "tpe,de->tpd"


def for_sending(x):
    return jax.tree.map(lambda a: a.astype(jnp.bfloat16) if a.dtype == jnp.float32 else a, x)


def layout(model_width, hidden_width):
    return [
        (NORM_ONE_GAIN, (model_width,), 0),
        (NORM_ONE_SHIFT, (model_width,), 0),
        (SELF_QKV, (model_width, 3 * model_width), 1),
        (SELF_QUERY_BIAS, (model_width,), 0),
        (SELF_VALUE_BIAS, (model_width,), 0),
        (SELF_OUT, (model_width, model_width), 1),
        (SELF_OUT_BIAS, (model_width,), 0),
        (NORM_TWO_GAIN, (model_width,), 0),
        (NORM_TWO_SHIFT, (model_width,), 0),
        (CROSS_QUERY, (model_width, model_width), 1),
        (CROSS_QUERY_BIAS, (model_width,), 0),
        (CROSS_KV, (model_width, 2 * model_width), 1),
        (CROSS_VALUE_BIAS, (model_width,), 0),
        (CROSS_OUT, (model_width, model_width), 1),
        (CROSS_OUT_BIAS, (model_width,), 0),
        (NORM_THREE_GAIN, (model_width,), 0),
        (NORM_THREE_SHIFT, (model_width,), 0),
        (MLP_UP, (model_width, hidden_width), 1),
        (MLP_UP_BIAS, (hidden_width,), 0),
        (MLP_DOWN, (hidden_width, model_width), 1),
        (MLP_DOWN_BIAS, (model_width,), 0),
    ]


def segment_table(model_width, hidden_width):
    seg_starts = []
    seg_ends = []
    decay_flags = []
    seg_entries = []
    row_at = 0
    for seg_label, seg_shape, seg_flag in layout(model_width, hidden_width):
        item_count = int(np.prod(seg_shape))
        seg_rows = item_count // 128
        seg_starts.append(row_at)
        seg_ends.append(row_at + seg_rows)
        decay_flags.append(seg_flag == 1)
        seg_entries.append(float(item_count))
        row_at = row_at + seg_rows
    return (np.array(seg_starts), np.array(seg_ends), np.array(decay_flags), np.array(seg_entries))


def unpack(flat_rows, model_width, hidden_width):
    vector = flat_rows.reshape(-1)
    tensors = {}
    offset = 0
    for seg_label, seg_shape, seg_flag in layout(model_width, hidden_width):
        item_count = int(np.prod(seg_shape))
        tensors[seg_label] = vector[offset : offset + item_count].reshape(seg_shape)
        offset = offset + item_count
    return tensors


def pack_rows(gradients, model_width, hidden_width, total_rows):
    pieces = [
        gradients[seg_label].reshape(-1, 128)
        for seg_label, seg_shape, seg_flag in layout(model_width, hidden_width)
    ]
    used_rows = sum((tensor_piece.shape[0] for tensor_piece in pieces))
    pieces.append(jnp.zeros((total_rows - used_rows, 128), jnp.float32))
    return jnp.concatenate(pieces, axis=0)


def product(pattern, left_side, right_side):
    return jnp.einsum(pattern, left_side, right_side, preferred_element_type=jnp.float32)


def as_float(tensors, seg_label):
    return tensors[seg_label].astype(jnp.float32)


def column_sums(values):
    return jnp.sum(values.astype(jnp.float32), axis=tuple(range(values.ndim - 1)))


def layer_norm(values, gain_term, offset_term):
    center = values - jnp.mean(values, axis=-1, keepdims=True)
    spread = jnp.mean(center * center, axis=-1, keepdims=True)
    return center * lax.rsqrt(spread + EPS_NORM) * gain_term + offset_term


def gelu_exact(pre_values):
    return jax.nn.gelu(pre_values, approximate=False)


def norm_back(values, tensors, gain, shift, normed_grad, gradients):
    norm_value, norm_pull = jax.vjp(
        layer_norm,
        values,
        as_float(tensors, gain),
        as_float(tensors, shift),
    )
    values_grad, gain_grad, offset_grad = norm_pull(normed_grad)
    gradients[gain] = gain_grad
    gradients[shift] = offset_grad
    return values_grad


def score_block(queries, key_head_split, allowed):
    scores = product(E_BQHE_BKHE_TO_BHQK, queries, key_head_split) * 0.125
    return jnp.where(allowed, scores, NEG_LARGE)


def softmax_forward(queries, key_head_split, allowed):
    scores = score_block(queries, key_head_split, allowed)
    highest = jnp.max(scores, axis=-1, keepdims=True)
    exponent = jnp.exp(scores - highest)
    row_total = jnp.sum(exponent, axis=-1, keepdims=True)
    return (exponent / row_total, highest + jnp.log(row_total))


def attention_backward_pass(queries, key_head_split, values, allowed, log_total, mixed_grad):
    probabilities = jnp.where(
        allowed, jnp.exp(score_block(queries, key_head_split, allowed) - log_total), 0.0
    )
    probs_grad = product(E_BQHE_BKHE_TO_BHQK, mixed_grad, values)
    values_grad = product(E_BHQK_BQHE_TO_BKHE, probabilities.astype(jnp.bfloat16), mixed_grad)
    inner_sum = jnp.sum(probabilities * probs_grad, axis=-1, keepdims=True)
    score_grad = (probabilities * (probs_grad - inner_sum)).astype(jnp.bfloat16)
    queries_grad = product(E_BHQK_BKHE_TO_BQHE, score_grad, key_head_split) * 0.125
    keys_grad = product(E_BHQK_BQHE_TO_BKHE, score_grad, queries) * 0.125
    return (queries_grad, keys_grad, values_grad)


def adam_step(
    gradients,
    member,
    decay_flags,
    old_weights,
    first_moment,
    second_moment,
    square_sums,
    seg_entries,
):
    grad_norm = jnp.sqrt(jnp.sum(square_sums))
    tensor_rms = jnp.sqrt(square_sums / jnp.asarray(seg_entries, dtype=square_sums.dtype))
    clip_scale = jnp.minimum(1.0, CLIP_NORM / (grad_norm + 1e-06))
    clipped = gradients * clip_scale
    new_first = BETA_ONE * first_moment + (1.0 - BETA_ONE) * clipped
    new_second = BETA_TWO * second_moment + (1.0 - BETA_TWO) * clipped * clipped
    first_hat = new_first / (1.0 - BETA_ONE**STEP)
    second_hat = new_second / (1.0 - BETA_TWO**STEP)
    decay_rows = jnp.any(member & decay_flags[None, :], axis=1)
    decayed = jnp.where(decay_rows[:, None], old_weights, 0.0)
    update = -LEARN_RATE * (first_hat / (jnp.sqrt(second_hat) + ADAM_EPS) + DECAY_RATE * decayed)
    return (update, new_first, new_second, grad_norm, tensor_rms)


def body(
    captions,
    tiles,
    tile_index,
    tile_valid,
    caption_len,
    weights,
    first_moment,
    second_moment,
    d_out,
):
    model_width = captions.shape[2]
    hidden_width = FF
    caption_rows = captions.shape[0]
    cap_length = captions.shape[1]
    patch_count = tiles.shape[1]
    own_tiles = tiles.shape[0]
    slot_count = tile_index.shape[1]
    group_size = lax.axis_size(FSDP)
    data_size = lax.axis_size(DP)
    total_rows = weights.shape[0] * group_size
    heads_shape = (caption_rows, cap_length, HEADS, HEAD_DIM)
    key_shape = (caption_rows, slot_count * patch_count, HEADS, HEAD_DIM)
    token_layout_form = (caption_rows, cap_length, model_width)
    tensors = unpack(lax.all_gather(weights, FSDP, axis=0, tiled=True), model_width, hidden_width)
    zero_part = jnp.zeros((model_width,), jnp.bfloat16)
    input_values = captions.astype(jnp.float32)
    normed_one = layer_norm(
        input_values, as_float(tensors, NORM_ONE_GAIN), as_float(tensors, NORM_ONE_SHIFT)
    ).astype(jnp.bfloat16)
    qkv_bias = jnp.concatenate(
        [tensors[SELF_QUERY_BIAS], zero_part, tensors[SELF_VALUE_BIAS]]
    ).astype(jnp.float32)
    packed_qkv = (product(E_BLD_DE_TO_BLE, normed_one, tensors[SELF_QKV]) + qkv_bias).astype(
        jnp.bfloat16
    )
    self_query = packed_qkv[..., :model_width].reshape(heads_shape)
    self_keys = packed_qkv[..., model_width : 2 * model_width].reshape(heads_shape)
    self_values = packed_qkv[..., 2 * model_width :].reshape(heads_shape)
    positions = jnp.arange(cap_length)
    causal = (positions[None, :] <= positions[:, None])[None, None]
    present = (positions[None, :] < caption_len[:, None])[:, None, None, :]
    self_allowed = causal & present
    self_probs, self_log = softmax_forward(self_query, self_keys, self_allowed)
    self_mixed = (
        product(E_BHQK_BKHE_TO_BQHE, self_probs.astype(jnp.bfloat16), self_values)
        .reshape(token_layout_form)
        .astype(jnp.bfloat16)
    )
    first_sum = (
        input_values
        + product(E_BLD_DE_TO_BLE, self_mixed, tensors[SELF_OUT])
        + as_float(tensors, SELF_OUT_BIAS)
    )
    normed_two = layer_norm(
        first_sum, as_float(tensors, NORM_TWO_GAIN), as_float(tensors, NORM_TWO_SHIFT)
    ).astype(jnp.bfloat16)
    cross_queries = (
        (
            product(E_BLD_DE_TO_BLE, normed_two, tensors[CROSS_QUERY])
            + as_float(tensors, CROSS_QUERY_BIAS)
        )
        .astype(jnp.bfloat16)
        .reshape(heads_shape)
    )
    kv_bias = jnp.concatenate([zero_part, tensors[CROSS_VALUE_BIAS]]).astype(jnp.float32)
    kv_weight = tensors[CROSS_KV]
    group_kv = (
        product(E_TPD_DE_TO_TPE, lax.all_gather(tiles, FSDP, axis=0, tiled=True), kv_weight)
        + kv_bias
    ).astype(jnp.bfloat16)
    chosen = jnp.stack(
        [
            jnp.stack(
                [
                    lax.dynamic_index_in_dim(group_kv, tile_index[c, s], 0, keepdims=False)
                    for s in range(slot_count)
                ]
            )
            for c in range(caption_rows)
        ]
    )
    cross_keys = chosen[..., :model_width].reshape(key_shape)
    cross_values = chosen[..., model_width:].reshape(key_shape)
    usable = jnp.repeat(tile_valid > 0, patch_count, axis=1)[:, None, None, :]
    cross_probs, cross_log = softmax_forward(cross_queries, cross_keys, usable)
    cross_mixed = (
        product(E_BHQK_BKHE_TO_BQHE, cross_probs.astype(jnp.bfloat16), cross_values)
        .reshape(token_layout_form)
        .astype(jnp.bfloat16)
    )
    second = (
        first_sum
        + product(E_BLD_DE_TO_BLE, cross_mixed, tensors[CROSS_OUT])
        + as_float(tensors, CROSS_OUT_BIAS)
    )
    normed_three = layer_norm(
        second, as_float(tensors, NORM_THREE_GAIN), as_float(tensors, NORM_THREE_SHIFT)
    ).astype(jnp.bfloat16)
    preact = product(E_BLD_DF_TO_BLF, normed_three, tensors[MLP_UP]) + as_float(
        tensors, MLP_UP_BIAS
    )
    activation = gelu_exact(preact).astype(jnp.bfloat16)
    result = (
        second
        + product(E_BLF_FD_TO_BLD, activation, tensors[MLP_DOWN])
        + as_float(tensors, MLP_DOWN_BIAS)
    ).astype(jnp.bfloat16)
    back_flat = lax.all_gather(weights, FSDP, axis=0, tiled=True)
    tensors = unpack(back_flat, model_width, hidden_width)
    gradients = {}
    out_grad = d_out.astype(jnp.float32)
    gradients[MLP_DOWN] = product(E_BLF_BLD_TO_FD, activation, d_out)
    gradients[MLP_DOWN_BIAS] = column_sums(d_out)
    activ_grad = product(E_BLD_FD_TO_BLF, d_out, tensors[MLP_DOWN])
    gelu_value, gelu_pull = jax.vjp(gelu_exact, preact)
    preact_grad = gelu_pull(activ_grad)[0].astype(jnp.bfloat16)
    gradients[MLP_UP] = product(E_BLD_BLF_TO_DF, normed_three, preact_grad)
    gradients[MLP_UP_BIAS] = column_sums(preact_grad)
    second_grad = out_grad + norm_back(
        second,
        tensors,
        NORM_THREE_GAIN,
        NORM_THREE_SHIFT,
        product(E_BLF_DF_TO_BLD, preact_grad, tensors[MLP_UP]),
        gradients,
    )
    cross_branch = second_grad.astype(jnp.bfloat16)
    gradients[CROSS_OUT] = product(E_BLD_BLE_TO_DE, cross_mixed, cross_branch)
    gradients[CROSS_OUT_BIAS] = column_sums(cross_branch)
    cmixed_grad = (
        product(E_BLE_DE_TO_BLD, cross_branch, tensors[CROSS_OUT])
        .astype(jnp.bfloat16)
        .reshape(heads_shape)
    )
    cquery_grad, ckeys_grad, cvalues_grad = attention_backward_pass(
        cross_queries, cross_keys, cross_values, usable, cross_log, cmixed_grad
    )
    cquery_low = cquery_grad.astype(jnp.bfloat16).reshape(token_layout_form)
    gradients[CROSS_QUERY] = product(E_BLD_BLE_TO_DE, normed_two, cquery_low)
    gradients[CROSS_QUERY_BIAS] = column_sums(cquery_low)
    first_grad = second_grad + norm_back(
        first_sum,
        tensors,
        NORM_TWO_GAIN,
        NORM_TWO_SHIFT,
        product(E_BLE_DE_TO_BLD, cquery_low, tensors[CROSS_QUERY]),
        gradients,
    )
    slot_layout_form = (caption_rows, slot_count, patch_count, model_width)
    slot_grad = jnp.concatenate(
        [ckeys_grad.reshape(slot_layout_form), cvalues_grad.reshape(slot_layout_form)], axis=-1
    )
    picked = (tile_index[:, :, None] == jnp.arange(group_kv.shape[0])[None, None, :]).astype(
        jnp.float32
    )
    group_grad = jnp.einsum(E_CSG_CSPE_TO_GPE, picked, slot_grad, precision=lax.Precision.HIGHEST)
    arrived = lax.all_to_all(
        group_grad.astype(jnp.bfloat16), FSDP, split_axis=0, concat_axis=0, tiled=True
    ).astype(group_grad.dtype)
    own_grad = jnp.sum(arrived.reshape((group_size, own_tiles) + arrived.shape[1:]), axis=0).astype(
        jnp.bfloat16
    )
    gradients[CROSS_KV] = product(E_TPD_TPE_TO_DE, tiles, own_grad)
    gradients[CROSS_VALUE_BIAS] = column_sums(own_grad[..., model_width:])
    tiles_grad = product(E_TPE_DE_TO_TPD, own_grad, tensors[CROSS_KV])
    self_branch = first_grad.astype(jnp.bfloat16)
    gradients[SELF_OUT] = product(E_BLD_BLE_TO_DE, self_mixed, self_branch)
    gradients[SELF_OUT_BIAS] = column_sums(self_branch)
    smixed_grad = (
        product(E_BLE_DE_TO_BLD, self_branch, tensors[SELF_OUT])
        .astype(jnp.bfloat16)
        .reshape(heads_shape)
    )
    self_query_gradient, self_key_gradient, self_value_gradient = attention_backward_pass(
        self_query, self_keys, self_values, self_allowed, self_log, smixed_grad
    )
    qkv_grad = jnp.concatenate(
        [
            self_query_gradient.reshape(token_layout_form),
            self_key_gradient.reshape(token_layout_form),
            self_value_gradient.reshape(token_layout_form),
        ],
        axis=-1,
    ).astype(jnp.bfloat16)
    gradients[SELF_QKV] = product(E_BLD_BLE_TO_DE, normed_one, qkv_grad)
    gradients[SELF_QUERY_BIAS] = column_sums(qkv_grad[..., :model_width])
    gradients[SELF_VALUE_BIAS] = column_sums(qkv_grad[..., 2 * model_width :])
    caption_grad = first_grad + norm_back(
        input_values,
        tensors,
        NORM_ONE_GAIN,
        NORM_ONE_SHIFT,
        product(E_BLE_DE_TO_BLD, qkv_grad, tensors[SELF_QKV]),
        gradients,
    )
    flat_grad = pack_rows(gradients, model_width, hidden_width, total_rows)
    shard_rows = total_rows // (data_size * group_size)
    received = lax.all_to_all(
        for_sending(flat_grad), DP, split_axis=0, concat_axis=0, tiled=True
    ).astype(flat_grad.dtype)
    data_grad = jnp.sum(received.reshape(data_size, group_size * shard_rows, 128), axis=0)
    shard_grad = lax.psum_scatter(
        data_grad.astype(jnp.bfloat16), FSDP, scatter_dimension=0, tiled=True
    ).astype(jnp.float32)
    begin_row = lax.axis_index(BOTH) * shard_rows
    seg_starts, seg_ends, decay_flags, seg_entries = segment_table(model_width, hidden_width)
    row_ids = begin_row + jnp.arange(shard_rows)
    member = (row_ids[:, None] >= seg_starts[None, :]) & (row_ids[:, None] < seg_ends[None, :])
    row_squares = jnp.sum(shard_grad * shard_grad, axis=1)
    part_sums = jnp.sum(jnp.where(member, row_squares[:, None], 0.0), axis=0)
    square_sums = lax.psum(part_sums, BOTH)
    old_weights = lax.dynamic_slice_in_dim(back_flat, begin_row, shard_rows, 0).astype(jnp.float32)
    update, new_first, new_second, grad_norm, tensor_rms = adam_step(
        shard_grad,
        member,
        decay_flags,
        old_weights,
        first_moment,
        second_moment,
        square_sums,
        seg_entries,
    )
    return (
        result,
        caption_grad,
        tiles_grad,
        shard_grad,
        update,
        new_first,
        new_second,
        grad_norm,
        tensor_rms,
    )


D = HEADS * HEAD_DIM
NZ = 4
TOK = 128
PATCH = 196
PATCH_SENT = 208
PATCH_SLOT = 256
KEYS = 2 * PATCH_SLOT
LEAD = 80
BF, F32 = jnp.bfloat16, jnp.float32
MESH = pl.DeviceIdType.MESH
SHARD, PIECES, PIECE = 2312, 5, 464
OLD = 2320
PADDED = PIECES * PIECE
WINDOW = 8 * SHARD
CARRY = 96
SEGS = 24
QKV_AT, WO_AT, UQ_AT, UKV_AT, UO_AT, WIDE = 0, 2304, 3072, 3840, 5376, 6144
W1_AT, W2_AT = 0, 3072
(V_G1, V_C1, V_BQKV, V_BO, V_G2, V_C2, V_UQ, V_BKV, V_UO, V_G3, V_C3, V_B1, V_B2, V_SUMS) = range(14)


def row_starts():
    starts, at = {}, 0
    for label, shape, _ in layout(D, FF):
        starts[label] = at
        at += int(np.prod(shape)) // 128
    return starts


def mm(a, b):
    return lax.dot_general(a, b, (((1,), (0,)), ((), ())), preferred_element_type=F32)


def mm_nt(a, b):
    return lax.dot_general(a, b, (((1,), (1,)), ((), ())), preferred_element_type=F32)


def mm_tn(a, b):
    return lax.dot_general(a, b, (((0,), (0,)), ((), ())), preferred_element_type=F32)


def al(i, m):
    return pl.multiple_of(i * m, m)


def halves(pair):
    lane = lax.broadcasted_iota(jnp.int32, pair.shape, 1)
    zero = jnp.zeros_like(pair)
    return jnp.concatenate(
        [jnp.where(lane < HEAD_DIM, pair, zero), jnp.where(lane < HEAD_DIM, zero, pair)], axis=0
    )


def joined(stacked):
    n = stacked.shape[0] // 2
    lane = lax.broadcasted_iota(jnp.int32, (n, 128), 1)
    return jnp.where(lane < HEAD_DIM, stacked[:n], stacked[n:])


def normed(v):
    center = v - jnp.mean(v, axis=-1, keepdims=True)
    r = lax.rsqrt(jnp.mean(center * center, axis=-1, keepdims=True) + EPS_NORM)
    return center * r, r


def pair_kernel(
    cap, tiles, d_out, index, valid, length, weights,
    g_out, sums_out, old_out, out, dcap, dtile,
    fw, wide, gf, pc, ps, big1, big2, kv, dkvt, tl, tlT,
    xin, h1, am, h2, q2, a2, sb, rb, dy, t1, h1T, amT, h2T, a2T,
    x1, dx, acc, vec, meta, ob, pfx, pfx_in, carry, dcap_b, dtile_b,
    from_core, from_y, from_x, from_low, from_high, total, sq,
    wsem, gsem, send, recv, core_s, core_r, y_s, y_r, x_s, x_r, up_s, up_r, down_s, down_r, free, sum_s, sum_r,
):
    role = lax.axis_index(FSDP)
    other = 1 - role
    me = lax.axis_index(DP)
    my_z, my_y, my_core = me // 4, (me // 2) % 2, me % 2

    def at_dp(z, y, core):
        return {DP: z * 4 + y * 2 + core, FSDP: role}

    core_peer = at_dp(my_z, my_y, 1 - my_core)
    y_peer = at_dp(my_z, 1 - my_y, my_core)
    x_peer = {DP: me, FSDP: other}
    up_peer = at_dp(jnp.minimum(my_z + 1, NZ - 1), my_y, my_core)
    down_peer = at_dp(jnp.maximum(my_z - 1, 0), my_y, my_core)
    barrier = pltpu.get_barrier_semaphore()
    cube = []
    for k in range(1, 8):
        core = 1 - my_core if k & 1 else my_core
        y = 1 - my_y if k & 2 else my_y
        cube.append({DP: my_z * 4 + y * 2 + core, FSDP: other if k & 4 else role})
    for peer in cube:
        pl.semaphore_signal(barrier, inc=1, device_id=peer, device_id_type=MESH)
    for step in range(1, NZ):
        peer = at_dp((my_z + step) % NZ, my_y, my_core)
        pl.semaphore_signal(barrier, inc=1, device_id=peer, device_id_type=MESH)
    row0 = row_starts()

    cuts = [0, 13856, 18480, 23088, 32320, weights.shape[0]]
    loads = []
    for i in range(5):
        n = cuts[i + 1] - cuts[i]
        loads.append(
            pltpu.make_async_copy(
                weights.at[pl.ds(cuts[i], n)], fw.at[pl.ds(LEAD + cuts[i], n)], wsem.at[i]
            )
        )
    for c in loads:
        c.start()

    def to_other(src, dst, k):
        return pltpu.make_async_remote_copy(
            src_ref=src, dst_ref=dst, send_sem=send.at[k], recv_sem=recv.at[k],
            device_id=x_peer, device_id_type=MESH,
        )

    first, later = pl.ds(0, TOK), pl.ds(TOK, TOK)
    copies = dict(
        cap=to_other(cap, xin.at[later], 0),
        tile=to_other(tl.at[pl.ds(0, PATCH_SENT)], tl.at[pl.ds(PATCH_SLOT, PATCH_SENT)], 1),
        meta=to_other(meta.at[0], meta.at[1], 2),
        dy=to_other(d_out, dy.at[first], 3),
        lead=to_other(fw.at[pl.ds(weights.shape[0], LEAD)], fw.at[pl.ds(0, LEAD)], 4),
        out=to_other(t1.at[first], ob, 7),
        pfx=to_other(pfx, pfx_in, 8),
        old=to_other(
            weights.at[pl.ds(pl.multiple_of(((2 * me + other) % 16) * SHARD - 8 * other, 16), OLD)], old_out, 9
        ),
        dcap=to_other(dcap_b, dcap_b, 10),
        dtile=to_other(dtile_b, dtile_b, 11),
    )

    def to_other_half(c, k):
        rows = pl.ds(al(c, TOK), TOK)
        return to_other(sb.at[rows], rb.at[rows], k + c)

    def x2_copy(c):
        return to_other_half(c, 12)

    def dx2_copy(c):
        return to_other_half(c, 14)

    after = PATCH_SLOT + PATCH_SENT
    tl[0:PATCH_SLOT, :] = jnp.zeros((PATCH_SLOT, D), BF)
    tl[after:, :] = jnp.zeros((KEYS - after, D), BF)
    tl[0:PATCH, :] = tiles[...]
    counts = []
    for g in range(2):
        named_by = jnp.int32(0)
        for s in range(index.shape[1]):
            named = jnp.where(index[0, s] == g, jnp.int32(1), jnp.int32(0))
            named_by = named_by + jnp.where(valid[0, s] > 0, named, jnp.int32(0))
        counts.append(named_by)
    rows8 = lax.broadcasted_iota(jnp.int32, (8, 128), 0)
    meta[0] = jnp.where(
        rows8 == 0, counts[0], jnp.where(rows8 == 1, counts[1], length[0])
    ).astype(F32)

    def all_here():
        pl.semaphore_wait(barrier, len(cube) + NZ - 1)

    def vector(row, at, n, col=0):
        block = fw[pl.ds(at, n // 128), :].astype(F32)
        for j in range(n // 128):
            vec[row : row + 1, col + 128 * j : col + 128 * j + 128] = block[j : j + 1, :]

    def widen(at, k, col, rows=D):
        for j in range(k):
            wide[:, col + 128 * j : col + 128 * j + 128] = fw[pl.ds(at + j, rows, stride=k), :]

    def norm_forward(src, dst, g, c, at=0, n=2 * TOK):
        @pl.loop(0, n // 64, unroll=2)
        def _(i):
            rows = pl.ds(pl.multiple_of(at + 64 * i, 64), 64)
            v, _ = normed(src[rows, :].astype(F32))
            dst[rows, :] = (v * vec[g : g + 1, :D] + vec[c : c + 1, :D]).astype(BF)

    def norm_backward(src, dh, g, write, at=0, n=2 * TOK):
        def step(i, sums):
            rows = pl.ds(pl.multiple_of(at + 64 * i, 64), 64)
            v, r = normed(src[rows, :].astype(F32))
            d = dh[rows, :]
            dn = d * vec[g : g + 1, :D]
            dv = r * (
                dn - jnp.mean(dn, axis=-1, keepdims=True) - v * jnp.mean(dn * v, axis=-1, keepdims=True)
            )
            write(rows, dv)
            return (
                sums[0] + jnp.sum(d * v, axis=0, keepdims=True),
                sums[1] + jnp.sum(d, axis=0, keepdims=True),
            )

        return lax.fori_loop(0, n // 64, step, (jnp.zeros((1, D), F32), jnp.zeros((1, D), F32)), unroll=2)

    def put_vector(at, row, into=gf):
        for j in range(row.shape[1] // 128):
            into[at + j : at + j + 1, :] = row[:, 128 * j : 128 * j + 128]

    def column_total(ref, cols):
        return jnp.sum(ref[:, cols].astype(F32), axis=0, keepdims=True)

    def matrix_grad(at, k, lhs_t, rhs, transposed=False):
        @pl.loop(0, k // 2, unroll=3)
        def _(m):
            cols = pl.ds(al(m, 256), 256)
            res = mm_nt(lhs_t[...], rhs[cols, :]) if transposed else mm(lhs_t[...], rhs[:, cols])
            for half in range(2):
                gf[pl.ds(at + 2 * m + half, D, stride=k), :] = res[:, 128 * half : 128 * half + 128]

    def copy_to(peer, src, dst, ssem, rsem):
        return pltpu.make_async_remote_copy(
            src_ref=src, dst_ref=dst, send_sem=ssem, recv_sem=rsem, device_id=peer, device_id_type=MESH
        )

    def slot(w, s, core, y=0, x=0):
        return pl.multiple_of(((w * PIECES + s) * 8 + core * 4 + y * 2 + x) * PIECE, 16)

    class Scatter:
        def __init__(self, w, x):
            self.w, self.x = w, x

        def core(self, s):
            rows = pl.ds(slot(self.w, s, 1 - my_core), 4 * PIECE)
            return copy_to(core_peer, fw.at[rows], from_core.at[s], core_s.at[self.w, s], core_r.at[self.w, s])

        def y(self, s):
            rows = pl.ds(slot(self.w, s, my_core, 1 - my_y), 2 * PIECE)
            return copy_to(y_peer, fw.at[rows], from_y.at[self.w, s], y_s.at[self.w, s], y_r.at[self.w, s])

        def over(self, s):
            rows = pl.ds(slot(self.w, s, my_core, my_y, 1 - self.x), PIECE)
            return copy_to(x_peer, fw.at[rows], from_x.at[self.w, s], x_s.at[self.w, s], x_r.at[self.w, s])

        def held(self, s, h):
            if h == self.x:
                return fw.at[pl.ds(slot(self.w, s, my_core, my_y, self.x), PIECE)]
            return from_x.at[self.w, s]

        def up(self, s, h):
            return copy_to(
                up_peer, self.held(s, h), from_low.at[self.w, s, h], up_s.at[self.w, s, h], up_r.at[self.w, s, h]
            )

        def down(self, s, h):
            return copy_to(
                down_peer, self.held(s, h), from_high.at[self.w, s, h], down_s.at[self.w, s, h], down_r.at[self.w, s, h]
            )

        def cast(self, first_row):
            @pl.loop(0, PIECES)
            def _(s):
                for k in range(8):
                    j = (k & 2) * 2 + (k & 4) // 2 + (k & 1)
                    src = pl.ds(pl.multiple_of(first_row + j * SHARD + s * PIECE, 8), PIECE)
                    fw[pl.ds(pl.multiple_of(slot(self.w, s, 0) + k * PIECE, 16), PIECE), :] = gf[src, :].astype(BF)
                self.core(s).start()

        def add_core(self):
            @pl.loop(0, PIECES)
            def _(s):
                self.core(s).wait_recv()
                rows = pl.ds(slot(self.w, s, my_core), 4 * PIECE)
                fw[rows, :] = fw[rows, :] + from_core[s]
                self.y(s).start()

        def add_y(self, s):
            self.y(s).wait_recv()
            rows = pl.ds(slot(self.w, s, my_core, my_y), 2 * PIECE)
            fw[rows, :] = fw[rows, :] + from_y[self.w, s]
            self.over(s).start()

        def from_ends(self, s, h):
            if h != self.x:
                self.over(s).wait_recv()
            goal = 2 * h + self.w
            if goal > 0:
                pl.when(my_z == 0)(self.up(s, h).start)
            if goal < NZ - 1:
                pl.when(my_z == NZ - 1)(self.down(s, h).start)

        def relay(self, s, hop, h):
            goal = 2 * h + self.w
            mine = self.held(s, h)
            if hop < goal:

                @pl.when(my_z == hop)
                def _():
                    self.up(s, h).wait_recv()
                    mine[...] = mine[...] + from_low[self.w, s, h]
                    self.up(s, h).start()

            if NZ - 1 - hop > goal:

                @pl.when(my_z == NZ - 1 - hop)
                def _():
                    self.down(s, h).wait_recv()
                    mine[...] = mine[...] + from_high[self.w, s, h]
                    self.down(s, h).start()

        def step(self, t):
            own, came = self.x, 1 - self.x
            parts = [
                (3, lambda s: self.relay(s, 2, came)),
                (2, lambda s: self.relay(s, 2, own)),
                (2, lambda s: self.relay(s, 1, came)),
                (1, lambda s: self.relay(s, 1, own)),
                (1, lambda s: self.from_ends(s, came)),
                (0, self.add_y),
                (0, lambda s: self.from_ends(s, own)),
            ]
            for lag, part in parts:
                s = t - lag
                if isinstance(t, int):
                    if 0 <= s < PIECES:
                        part(s)
                else:
                    pl.when((s >= 0) & (s < PIECES))(functools.partial(part, s))

        def collect(self, s):
            for h in range(2):
                goal = 2 * h + self.w

                @pl.when(my_z == goal)
                def _():
                    whole = self.held(s, h)[...].astype(F32)
                    if goal > 0:
                        self.up(s, h).wait_recv()
                        whole = whole + from_low[self.w, s, h].astype(F32)
                    if goal < NZ - 1:
                        self.down(s, h).wait_recv()
                        whole = whole + from_high[self.w, s, h].astype(F32)
                    total[pl.ds(pl.multiple_of(s * PIECE, 8), PIECE), :] = whole

        def sent(self):
            @pl.loop(0, PIECES)
            def _(s):
                self.core(s).wait_send()
                self.y(s).wait_send()
                self.over(s).wait_send()
                for h in range(2):
                    goal = 2 * h + self.w
                    pl.when(my_z < goal)(self.up(s, h).wait_send)
                    pl.when(my_z > goal)(self.down(s, h).wait_send)

    def rest_of_scatter(one, zero, begun):
        @pl.loop(begun, 2 * PIECES + 3)
        def _(t):
            one.step(t)
            zero.step(t - PIECES)

        pl.loop(0, PIECES)(one.collect)
        pl.loop(0, PIECES)(zero.collect)
        one.sent()
        zero.sent()

    def square_sums():
        total[SHARD:, :] = jnp.zeros((total.shape[0] - SHARD, 128), F32)
        done = pltpu.make_async_copy(total.at[pl.ds(0, OLD)], g_out, gsem)
        done.start()
        seg = lax.broadcasted_iota(jnp.int32, (SEGS, 1), 0)
        begin = jnp.full((SEGS, 1), 1 << 30, jnp.int32)
        end = begin
        for i, (a, b) in enumerate(zip(*segment_table(D, FF)[:2])):
            begin = jnp.where(seg == i, int(a), begin)
            end = jnp.where(seg == i, int(b), end)
        row = (me * 2 + role) * SHARD + lax.broadcasted_iota(jnp.int32, (SEGS, total.shape[0]), 1)
        member = jnp.where((row >= begin) & (row < end), 1.0, 0.0).astype(BF)
        square = total[...] * total[...]
        high = square.astype(BF)
        squares = mm(member, high) + mm(member, (square - high.astype(F32)).astype(BF))
        mine = jnp.broadcast_to(jnp.sum(squares, axis=1, keepdims=True), (SEGS, 128))
        sq[0] = mine
        swaps = [copy_to(p, sq.at[0], sq.at[k], sum_s.at[k], sum_r.at[k]) for k, p in enumerate(cube, 1)]
        for c in swaps:
            c.start()
        for c in swaps:
            c.wait()
        mine = jnp.zeros((SEGS, 128), F32)
        for k in range(8):
            core = 1 - my_core if k & 1 else my_core
            y = 1 - my_y if k & 2 else my_y
            mine = mine + sq[core + 2 * y + 4 * (1 - role if k & 4 else role)]
        sq[8] = mine
        sends = []
        for step in range(1, NZ):
            to = at_dp((my_z + step) % NZ, my_y, my_core)
            sends.append(copy_to(to, sq.at[8], sq.at[8 + step], sum_s.at[7 + step], sum_r.at[7 + step]))
            sends[-1].start()
        for c in sends:
            c.wait()
        whole = jnp.zeros((SEGS, 128), F32)
        for z in range(NZ):
            part = mine
            for step in range(1, NZ):
                part = jnp.where((my_z - step + NZ) % NZ == z, sq[8 + step], part)
            whole = whole + part
        sums_out[...] = whole
        done.wait()

    def attention_role():
        at = {k: LEAD + v for k, v in row0.items()}
        at0 = {k: CARRY + v for k, v in row0.items()}
        at1 = {k: CARRY - WINDOW + v for k, v in row0.items()}
        one, zero = Scatter(1, 0), Scatter(0, 0)
        xin[first, :] = cap[...]
        loads[0].wait()
        vector(V_G1, at[NORM_ONE_GAIN], D)
        vector(V_C1, at[NORM_ONE_SHIFT], D)
        vec[V_BQKV : V_BQKV + 1, :] = jnp.zeros((1, FF), F32)
        vec[V_BKV : V_BKV + 1, :] = jnp.zeros((1, FF), F32)
        vector(V_BQKV, at[SELF_QUERY_BIAS], D)
        vector(V_BQKV, at[SELF_VALUE_BIAS], D, 2 * D)
        widen(at[SELF_QKV], 18, QKV_AT)
        for c in loads[1:]:
            c.wait()
        vector(V_BO, at[SELF_OUT_BIAS], D)
        vector(V_G2, at[NORM_TWO_GAIN], D)
        vector(V_C2, at[NORM_TWO_SHIFT], D)
        vector(V_UQ, at[CROSS_QUERY_BIAS], D)
        vector(V_BKV, at[CROSS_VALUE_BIAS], D, D)
        vector(V_UO, at[CROSS_OUT_BIAS], D)
        widen(at[SELF_OUT], 6, WO_AT)
        widen(at[CROSS_QUERY], 6, UQ_AT)
        widen(at[CROSS_KV], 12, UKV_AT)
        widen(at[CROSS_OUT], 6, UO_AT)
        all_here()
        copies["dy"].start()
        copies["lead"].start()

        copies["cap"].wait_recv()
        norm_forward(xin, h1, V_G1, V_C1)

        for j in range(3):
            cols = slice(D * j, D * j + D)
            big1[:, cols] = (mm(h1[...], wide[:, cols]) + vec[V_BQKV : V_BQKV + 1, cols]).astype(BF)

        copies["meta"].wait_recv()

        @pl.loop(0, 12, unroll=6)
        def _(i):
            c, p = i // 6, i % 6
            rows = pl.ds(al(c, TOK), TOK)
            qq = halves(big1[rows, pl.ds(al(p, 128), 128)]) * BF(0.125)
            k2 = big1[rows, pl.ds(al(p, 128) + D, 128)]
            v2 = big1[rows, pl.ds(al(p, 128) + 2 * D, 128)]
            s = mm_nt(qq, k2)
            row = lax.broadcasted_iota(jnp.int32, s.shape, 0) % TOK
            col = lax.broadcasted_iota(jnp.int32, s.shape, 1)
            present = col.astype(F32) < meta[c][2:3, :]
            s = jnp.where((col <= row) & present, s, NEG_LARGE)
            e = jnp.exp(s - jnp.max(s, axis=-1, keepdims=True))
            prob = (e * (1.0 / jnp.sum(e, axis=-1, keepdims=True))).astype(BF)
            ps[i] = prob
            am[rows, pl.ds(al(p, 128), 128)] = joined(mm(prob, v2)).astype(BF)

        x1[...] = xin[...].astype(F32) + mm(am[...], wide[:, WO_AT : WO_AT + D]) + vec[V_BO : V_BO + 1, :D]
        norm_forward(x1, h2, V_G2, V_C2)
        q2[...] = (mm(h2[...], wide[:, UQ_AT : UQ_AT + D]) + vec[V_UQ : V_UQ + 1, :D]).astype(BF)
        copies["tile"].wait_recv()

        for j in range(2):
            cols = slice(D * j, D * j + D)
            kv[:, cols] = (
                mm(tl[...], wide[:, UKV_AT + D * j : UKV_AT + D * j + D]) + vec[V_BKV : V_BKV + 1, cols]
            ).astype(BF)

        @pl.loop(0, 2)
        def _(c):
            rows = pl.ds(al(c, TOK), TOK)
            col = lax.broadcasted_iota(jnp.int32, (1, KEYS), 1)
            m = meta[c]
            c0 = jnp.concatenate([m[0:1, :]] * (KEYS // 128), axis=1)
            c1 = jnp.concatenate([m[1:2, :]] * (KEYS // 128), axis=1)
            count = jnp.where(col < PATCH, c0, jnp.where(col < PATCH_SLOT, 0.0, c1))
            count = jnp.where(col < PATCH_SLOT + PATCH, count, 0.0)

            @pl.loop(0, 6, unroll=6)
            def _(p):
                qq = halves(q2[rows, pl.ds(al(p, 128), 128)]) * BF(0.125)
                s = mm_nt(qq, kv[:, pl.ds(al(p, 128), 128)])
                s = jnp.where(count > 0.0, s, NEG_LARGE)
                e = jnp.exp(s - jnp.max(s, axis=-1, keepdims=True)) * count
                prob = (e * (1.0 / jnp.sum(e, axis=-1, keepdims=True))).astype(BF)
                pc[pl.ds(al(6 * c + p, 2 * TOK), 2 * TOK), :] = prob
                a2[rows, pl.ds(al(p, 128), 128)] = joined(
                    mm(prob, kv[:, pl.ds(al(p, 128) + D, 128)])
                ).astype(BF)

            sb[rows, :] = (
                x1[rows, :] + mm(a2[rows, :], wide[:, UO_AT : UO_AT + D]) + vec[V_UO : V_UO + 1, :D]
            ).astype(BF)
            x2_copy(c).start()

        copies["old"].start()

        h1T[...] = h1[...].T
        amT[...] = am[...].T
        h2T[...] = h2[...].T
        a2T[...] = a2[...].T
        tlT[...] = tl[...].T

        part_at = at1[CROSS_KV]

        def attend_back(c, p, take_keys):
            rows = pl.ds(c * TOK, TOK)
            lanes, vlanes = pl.ds(al(p, 128), 128), pl.ds(al(p, 128) + D, 128)
            qq = halves(q2[rows, lanes]) * BF(0.125)
            do = halves(t1[rows, lanes])
            prob = pc[pl.ds(al(6 * c + p, 2 * TOK), 2 * TOK), :]
            pf = prob.astype(F32)
            dp = mm_nt(do, kv[:, vlanes])
            ds = (pf * (dp - jnp.sum(pf * dp, axis=-1, keepdims=True))).astype(BF)
            am[rows, lanes] = (joined(mm(ds, kv[:, lanes])) * 0.125).astype(BF)
            take_keys(p, 0, lanes, mm_tn(qq, ds))
            take_keys(p, 1, vlanes, mm_tn(do, prob))

        def part_rows(p, k, j):
            return pl.ds(pl.multiple_of(part_at + ((2 * p + k) * 4 + j) * 128, 8), 128)

        def keep(p, k, lanes, term):
            for j in range(4):
                gf[part_rows(p, k, j), :] = term[:, 128 * j : 128 * j + 128]

        def complete(p, k, lanes, term):
            for j in range(4):
                cols = slice(128 * j, 128 * j + 128)
                dkvt[lanes, cols] = (gf[part_rows(p, k, j), :] + term[:, cols]).astype(BF)

        for c, take_keys in enumerate((keep, complete)):
            rows = pl.ds(c * TOK, TOK)
            dx2_copy(c).wait_recv()
            t1[rows, :] = mm_nt(rb[rows, :], wide[:, UO_AT : UO_AT + D]).astype(BF)
            pl.loop(0, 6, unroll=6)(functools.partial(attend_back, c, take_keys=take_keys))

        put_vector(at1[CROSS_OUT_BIAS], column_total(rb, slice(None)))
        matrix_grad(at1[CROSS_OUT], 6, a2T, rb)
        put_vector(at1[CROSS_QUERY_BIAS], column_total(am, slice(None)))
        matrix_grad(at1[CROSS_QUERY], 6, h2T, am)
        matrix_grad(at1[CROSS_KV], 12, tlT, dkvt, transposed=True)
        kv[...] = dkvt[...].T
        put_vector(at1[CROSS_VALUE_BIAS], column_total(kv, slice(D, 2 * D)))
        copies["pfx"].wait_recv()
        gf[pl.ds(at1[NORM_THREE_GAIN], LEAD - 12), :] = pfx_in[12:, :]
        copies["lead"].wait_send()
        one.cast(CARRY)
        carry[...] = gf[0:CARRY, :]

        one.add_core()
        pl.semaphore_signal(free, inc=1, device_id=core_peer, device_id_type=MESH)

        def tile_grad(rows):
            return mm_nt(kv[rows, :], wide[:, UKV_AT : UKV_AT + 2 * D])

        dtile[:, 0, :] = tile_grad(pl.ds(0, PATCH_SENT))[:PATCH]
        dtile_b[...] = tile_grad(pl.ds(PATCH_SLOT, PATCH_SENT)).astype(BF)
        copies["dtile"].start()
        acc[...] = mm_nt(am[...], wide[:, UQ_AT : UQ_AT + D])
        e1 = h2

        def write_dx1(rows, dv):
            full = rb[rows, :].astype(F32) + dv
            dx[rows, :] = full
            e1[rows, :] = full.astype(BF)

        gg, gc = norm_backward(x1, acc, V_G2, write_dx1)
        put_vector(at0[NORM_TWO_GAIN], gg)
        put_vector(at0[NORM_TWO_SHIFT], gc)
        put_vector(at0[SELF_OUT_BIAS], column_total(e1, slice(None)))
        matrix_grad(at0[SELF_OUT], 6, amT, e1)
        t1[...] = mm_nt(e1[...], wide[:, WO_AT : WO_AT + D]).astype(BF)

        @pl.loop(0, 12, unroll=6)
        def _(i):
            c, p = i // 6, i % 6
            rows = pl.ds(al(c, TOK), TOK)
            lanes = pl.ds(al(p, 128), 128)
            klanes, vlanes = pl.ds(al(p, 128) + D, 128), pl.ds(al(p, 128) + 2 * D, 128)
            qq = halves(big1[rows, lanes]) * BF(0.125)
            do = halves(t1[rows, lanes])
            prob = ps[i]
            pf = prob.astype(F32)
            dp = mm_nt(do, big1[rows, vlanes])
            ds = (pf * (dp - jnp.sum(pf * dp, axis=-1, keepdims=True))).astype(BF)
            big2[rows, lanes] = (joined(mm(ds, big1[rows, klanes])) * 0.125).astype(BF)
            big2[rows, klanes] = mm_tn(ds, qq).astype(BF)
            big2[rows, vlanes] = mm_tn(prob, do).astype(BF)

        one.step(0)
        acc[...] = mm_nt(big2[:, : 3 * D], wide[:, : 3 * D])

        def write_dx0(rows, dv):
            dx[rows, :] = dx[rows, :] + dv

        gg, gc = norm_backward(xin, acc, V_G1, write_dx0)
        put_vector(at0[NORM_ONE_GAIN], gg)
        put_vector(at0[NORM_ONE_SHIFT], gc)
        dcap[...] = dx[first, :]
        dcap_b[...] = dx[later, :].astype(BF)
        copies["dcap"].start()
        one.step(1)
        put_vector(at0[SELF_QUERY_BIAS], column_total(big2, slice(0, D)))
        put_vector(at0[SELF_VALUE_BIAS], column_total(big2, slice(2 * D, 3 * D)))
        matrix_grad(at0[SELF_QKV], 18, h1T, big2)
        gf[pl.ds(at0[CROSS_QUERY], WINDOW - row0[CROSS_QUERY]), :] = carry[
            row0[CROSS_QUERY] - WINDOW + CARRY :, :
        ]
        pl.semaphore_wait(free, 1)
        zero.cast(CARRY)
        one.step(2)
        zero.add_core()
        rest_of_scatter(one, zero, 3)
        copies["out"].wait_recv()
        out[...] = ob[...]
        for name in ("dy", "dcap", "dtile"):
            copies[name].wait_send()
        for c in range(2):
            x2_copy(c).wait_send()
        copies["old"].wait()
        square_sums()

    def mlp_role():
        all_here()
        copies["meta"].start()
        copies["cap"].start()
        copies["cap"].wait_send()
        copies["tile"].start()
        base = LEAD - weights.shape[0]
        at = {k: base + v for k, v in row0.items()}
        at0 = {k: CARRY - weights.shape[0] + v for k, v in row0.items()}
        at1 = {k: v - WINDOW for k, v in at0.items()}
        one, zero = Scatter(1, 1), Scatter(0, 1)
        dy[later, :] = d_out[...]
        for c in loads:
            c.wait()
        for b in range(4):
            widen(at[MLP_DOWN] + 6 * D * b, 6, W2_AT + D * b)
        copies["lead"].wait_recv()
        widen(at[MLP_UP], 24, W1_AT)
        vector(V_G3, at[NORM_THREE_GAIN], D)
        vector(V_C3, at[NORM_THREE_SHIFT], D)
        vector(V_B1, at[MLP_UP_BIAS], FF)
        vector(V_B2, at[MLP_DOWN_BIAS], D)
        copies["dy"].wait_recv()

        @pl.loop(0, 4)
        def _(b):
            dg = mm_nt(dy[...], wide[:, pl.ds(al(b, D) + W2_AT, D)])
            for j in range(6):
                gf[pl.ds(al(6 * b + j, 256), 256), :] = dg[:, 128 * j : 128 * j + 128]

        def write_dx2(rows, dv):
            sb[rows, :] = (dy[rows, :].astype(F32) + dv).astype(BF)

        vec[V_SUMS : V_SUMS + 2, :] = jnp.zeros((2, FF), F32)

        @pl.loop(0, 2)
        def _(c):
            cap_rows = pl.ds(al(c, TOK), TOK)
            x2_copy(c).wait_recv()
            norm_forward(rb, h1, V_G3, V_C3, c * TOK, TOK)
            z_parts = [x1.at[first], x1.at[later], dx.at[first], dx.at[later]]
            for b in range(4):
                cols = slice(D * b, D * b + D)
                z_parts[b][...] = mm(h1[cap_rows, :], wide[:, cols]) + vec[V_B1 : V_B1 + 1, cols]

            @pl.loop(0, 4)
            def _(i):
                here = pl.ds(al(i, 32), 32)
                rows = pl.ds(al(c, TOK) + al(i, 32), 32)
                for k in range(24):
                    z = z_parts[k // 6][here, 128 * (k % 6) : 128 * (k % 6) + 128]
                    phi = 0.5 + 0.5 * lax.erf(z * np.float32(np.sqrt(0.5)))
                    dens = jnp.exp(-0.5 * z * z) * np.float32(1.0 / np.sqrt(2.0 * np.pi))
                    lanes = slice(128 * k, 128 * k + 128)
                    big1[rows, lanes] = (z * phi).astype(BF)
                    dg = gf[pl.ds(256 * k + al(c, TOK) + al(i, 32), 32), :]
                    big2[rows, lanes] = (dg * (phi + z * dens)).astype(BF)

            acc[cap_rows, :] = mm_nt(big2[cap_rows, :], wide[:, W1_AT : W1_AT + FF])
            gg, gc = norm_backward(rb, acc, V_G3, write_dx2, c * TOK, TOK)
            vec[V_SUMS : V_SUMS + 1, :D] = vec[V_SUMS : V_SUMS + 1, :D] + gg
            vec[V_SUMS + 1 : V_SUMS + 2, :D] = vec[V_SUMS + 1 : V_SUMS + 2, :D] + gc
            dx2_copy(c).start()

        put_vector(12, vec[V_SUMS : V_SUMS + 1, :D], pfx)
        put_vector(18, vec[V_SUMS + 1 : V_SUMS + 2, :D], pfx)

        h1T[...] = h1[...].T
        pfx[0:12, :] = jnp.zeros((12, 128), F32)
        for b in range(4):
            head = mm(h1T[0:8, :], big2[:, D * b : D * b + D])
            for r in range(3):
                for j in range(6):
                    row = 24 + 24 * r + 6 * b + j
                    if row < LEAD:
                        pfx[row : row + 1, :] = head[r : r + 1, 128 * j : 128 * j + 128]
        copies["pfx"].start()
        copies["old"].start()

        acc[...] = rb[...].astype(F32) + vec[V_B2 : V_B2 + 1, :D]
        for b in range(4):
            cols = slice(D * b, D * b + D)
            acc[...] = acc[...] + mm(big1[:, cols], wide[:, W2_AT + D * b : W2_AT + D * b + D])
            pc[D * b : D * b + D, 0:256] = big1[:, cols].T

        t1[first, :] = acc[first, :].astype(BF)
        copies["out"].start()
        out[...] = acc[later, :].astype(BF)
        gf[pl.ds(at1[MLP_DOWN_BIAS] + 6, WINDOW + CARRY - at1[MLP_DOWN_BIAS] - 6), :] = jnp.zeros(
            (WINDOW + CARRY - at1[MLP_DOWN_BIAS] - 6, 128), F32
        )
        put_vector(at1[MLP_DOWN_BIAS], column_total(dy, slice(None)))
        for b in range(4):
            matrix_grad(at1[MLP_DOWN] + 6 * D * b, 6, pc.at[pl.ds(D * b, D), pl.ds(0, 256)], dy)
        one.cast(CARRY)
        carry[...] = gf[0:CARRY, :]
        put_vector(at0[MLP_UP_BIAS], column_total(big2, slice(None)))
        matrix_grad(at0[MLP_UP], 24, h1T, big2)
        one.add_core()
        pl.semaphore_signal(free, inc=1, device_id=core_peer, device_id_type=MESH)
        gf[pl.ds(at0[MLP_DOWN], CARRY), :] = carry[...]
        pl.semaphore_wait(free, 1)
        zero.cast(CARRY)
        zero.add_core()
        rest_of_scatter(one, zero, 0)
        copies["dtile"].wait_recv()
        dtile[:, 0, :] = dtile_b[0:PATCH, :].astype(F32)
        copies["dcap"].wait_recv()
        dcap[...] = dcap_b[...].astype(F32)
        for name in ("tile", "meta", "pfx", "out"):
            copies[name].wait_send()
        for c in range(2):
            dx2_copy(c).wait_send()
        copies["old"].wait()
        square_sums()

    pl.when(role == 0)(attention_role)
    pl.when(role == 1)(mlp_role)


def pair_call(cap, tiles, d_out, index, valid, length, weights):
    vm = pl.BlockSpec(memory_space=pltpu.VMEM)
    sm = pl.BlockSpec(memory_space=pltpu.SMEM)
    hbm = pl.BlockSpec(memory_space=pl.ANY)
    S = jax.ShapeDtypeStruct
    dma, both = pltpu.SemaphoreType.DMA, 2 * TOK

    def bf(*s):
        return pltpu.VMEM(s, BF)

    def fl(*s):
        return pltpu.VMEM(s, F32)

    return pl.pallas_call(
        pair_kernel,
        in_specs=[vm, vm, vm, sm, sm, sm, hbm],
        out_specs=[hbm, vm, hbm, vm, vm, vm],
        out_shape=[
            S((OLD, 128), F32),
            S((SEGS, 128), F32),
            S((OLD, 128), BF),
            S((TOK, D), BF),
            S((TOK, D), F32),
            S((PATCH, 1, D), F32),
        ],
        scratch_shapes=[
            bf(16 * PADDED, 128), bf(D, WIDE), fl(CARRY + 7 * SHARD + PADDED, 128), bf(12 * both, KEYS),
            bf(12, both, 128), bf(both, FF), bf(both, FF), bf(KEYS, 2 * D), bf(2 * D, KEYS), bf(KEYS, D), bf(D, KEYS),
            *[bf(both, D) for _ in range(10)],
            *[bf(D, both) for _ in range(4)],
            *[fl(both, D) for _ in range(3)],
            fl(16, FF), fl(2, 8, 128), bf(TOK, D), fl(LEAD, 128), fl(LEAD, 128), fl(CARRY, 128),
            bf(TOK, D), bf(PATCH_SENT, D),
            bf(PIECES, 4 * PIECE, 128), bf(2, PIECES, 2 * PIECE, 128), bf(2, PIECES, PIECE, 128),
            bf(2, PIECES, 2, PIECE, 128), bf(2, PIECES, 2, PIECE, 128), fl(2432, 128), fl(8 + NZ, SEGS, 128),
            dma((5,)), dma, dma((16,)), dma((16,)),
            *[dma((2, PIECES)) for _ in range(6)],
            *[dma((2, PIECES, 2)) for _ in range(4)],
            pltpu.SemaphoreType.REGULAR, dma((7 + NZ,)), dma((7 + NZ,)),
        ],
        compiler_params=pltpu.CompilerParams(
            collective_id=0, has_side_effects=True, vmem_limit_bytes=63 * 2**20
        ),
    )(cap, tiles, d_out, index, valid, length, weights)


def pair_update(grads, old_weights, first_moment, second_moment, square_sums):
    seg_starts, seg_ends, decay_flags, seg_entries = segment_table(D, FF)
    grad_norm = jnp.sqrt(jnp.sum(square_sums))
    tensor_rms = jnp.sqrt(square_sums / jnp.asarray(seg_entries, dtype=square_sums.dtype))
    clipped = grads * jnp.minimum(1.0, CLIP_NORM / (grad_norm + 1e-06))
    new_first = BETA_ONE * first_moment + (1.0 - BETA_ONE) * clipped
    new_second = BETA_TWO * second_moment + (1.0 - BETA_TWO) * clipped * clipped
    first_hat = new_first / (1.0 - BETA_ONE**STEP)
    second_hat = new_second / (1.0 - BETA_TWO**STEP)
    row = lax.axis_index(BOTH) * SHARD + lax.broadcasted_iota(jnp.int32, grads.shape, 0)
    decays = row < 0
    for start, end, decay in zip(seg_starts, seg_ends, decay_flags):
        if decay:
            decays = decays | ((row >= int(start)) & (row < int(end)))
    decayed = jnp.where(decays, old_weights, 0.0)
    update = -LEARN_RATE * (first_hat / (jnp.sqrt(second_hat) + ADAM_EPS) + DECAY_RATE * decayed)
    return (update, new_first, new_second, grad_norm, tensor_rms)


def pair_body(
    captions, tiles, tile_index, tile_valid, caption_len, weights, first_moment, second_moment, d_out
):
    me, f = lax.axis_index(DP), lax.axis_index(FSDP)
    padded, sums, old, out, caption_grad, tiles_grad = pair_call(
        captions[0], tiles[0], d_out[0], tile_index, tile_valid, caption_len, weights
    )
    shard_grad = padded[:SHARD]
    own = lax.dynamic_slice_in_dim(weights, ((2 * me + f) % 16) * SHARD, SHARD, 0)
    old = lax.dynamic_slice_in_dim(old, 8 * f, SHARD, 0)
    old_weights = jnp.where(me // 8 == f, own, old).astype(jnp.float32)
    update, new_first, new_second, grad_norm, tensor_rms = pair_update(
        shard_grad, old_weights, first_moment, second_moment, sums[:21, 0]
    )
    return (
        out[None], caption_grad[None], jnp.swapaxes(tiles_grad, 0, 1), shard_grad, update, new_first, new_second,
        grad_norm, tensor_rms,
    )


def solution(mesh):
    placed = (
        P(BOTH, None, None),
        P(BOTH, None, None),
        P(BOTH, None),
        P(BOTH, None),
        P(BOTH),
        P(FSDP, None),
        P(BOTH, None),
        P(BOTH, None),
        P(BOTH, None, None),
    )
    return jax.shard_map(
        pair_body if mesh.shape[FSDP] == 2 else body,
        mesh=mesh,
        in_specs=placed,
        out_specs=(
            P(BOTH, None, None),
            P(BOTH, None, None),
            P(BOTH, None, None),
            P(BOTH, None),
            P(BOTH, None),
            P(BOTH, None),
            P(BOTH, None),
            P(),
            P(),
        ),
        check_vma=False,
    )
```
